32 devices in a mesh: dp: 2 (over x), blk: 4 (over z), head: 4 (over y, core).
Axes of the slice: x: 2, y: 2, z: 4, core: 2. Of those that a mesh axis runs over, the one named last changes fastest.
Arguments:
- tokens: bfloat16 [2, 2048, 768], P('dp', ('blk', 'head')), may hold values from -6 to 6
- order: int32 [2, 2048], P('dp', ('blk', 'head')), may hold values from 0 to 2047, each once within a row
- expert_ids: int32 [2, 2048, 1], replicated, may hold values from 0 to 7
- norm1_gain: bfloat16 [768], P(('dp', 'blk', 'head')), may hold values from 0.5 to 1.5
- w_query: bfloat16 [768, 768], P(('dp', 'blk', 'head')), may hold values from -0.3125 to 0.3125
- w_key: bfloat16 [768, 768], P(('dp', 'blk', 'head')), may hold values from -0.3125 to 0.3125
- w_value: bfloat16 [768, 768], P(('dp', 'blk', 'head')), may hold values from -0.21875 to 0.21875
- w_attn_out: bfloat16 [768, 768], P(('dp', 'blk', 'head')), may hold values from -1.25 to 1.25
- rel_table: bfloat16 [384], P(('dp', 'blk', 'head')), may hold values from -3 to 3
- norm2_gain: bfloat16 [768], P(('dp', 'blk', 'head')), may hold values from 0.5 to 1.5
- w_router: bfloat16 [768, 8], P(('dp', 'blk', 'head')), may hold values from -0.15625 to 0.15625
- w_in: bfloat16 [8, 768, 3072], P(('dp', 'blk')), may hold values from -0.21875 to 0.21875
- w_out: bfloat16 [8, 3072, 768], P(('dp', 'blk')), may hold values from -3.5 to 3.5
- cotangent: bfloat16 [2, 2048, 768], P('dp', ('blk', 'head')), may hold values from -6 to 6
Outputs:
- layer_out: bfloat16 [2, 2048, 768], P('dp', ('blk', 'head'))
- grad_tokens: bfloat16 [2, 2048, 768], P('dp', ('blk', 'head'))
- grad_norm1_gain: float32 [768], P(('dp', 'blk', 'head'))
- grad_w_query: float32 [768, 768], P(('dp', 'blk', 'head'))
- grad_w_key: float32 [768, 768], P(('dp', 'blk', 'head'))
- grad_w_value: float32 [768, 768], P(('dp', 'blk', 'head'))
- grad_w_attn_out: float32 [768, 768], P(('dp', 'blk', 'head'))
- grad_rel_table: float32 [384], P(('dp', 'blk', 'head'))
- grad_norm2_gain: float32 [768], P(('dp', 'blk', 'head'))
- grad_w_router: float32 [768, 8], P(('dp', 'blk', 'head'))
- grad_w_in: float32 [8, 768, 3072], P(('dp', 'blk'))
- grad_w_out: float32 [8, 3072, 768], P(('dp', 'blk'))
The draws below stay inside these ranges and needn't reach their ends.
Inputs may be any that keep to these rules, and one draw needn't show every extreme that they name: `expert_ids`: every expert is named by some token. `order`: within each sequence every value appears once.
All inputs are finite; a program needn't handle non-finite values.
Results may differ from the reference program's by a relative error of at most 0.033.
Values may be sent and summed in bfloat16 or wider, within the bound.
A program may use at most 192 MiB of HBM per device.

```python
import jax
import jax.numpy as jnp
from jax import lax

D = 768
HEAD_COUNT = 12
HEAD_SIZE = 64
FF = 3072
BUCKETS = 32
BLOCK = 256
SEQUENCE_LENGTH = 2048
SEQ_DEV = 1
EXPERTS = 8
SEQUENCE_COUNT = 2
PIECE = 128
CAP = 20
N_DP = 2
N_BLK = 4
N_HEAD = 4


def steps_of(own_key, extent, cuts, low, largest):
    gain, own = 1.0, jax.random.fold_in(own_key, 6)
    for axis_at, blocks in cuts:
        steps = jnp.exp(jax.random.uniform(jax.random.fold_in(own, axis_at), (blocks,), jnp.float32, low / len(cuts), largest / len(cuts)))
        gain = gain * jnp.repeat(steps, extent[axis_at] // blocks).reshape([-1 if axis == axis_at else 1 for axis in range(len(extent))])
    return gain


def choose_distinct(own_key, rows, number_of, top, lift):
    ranking = jax.random.permutation(jax.random.fold_in(own_key, 1), number_of)
    pull = ranking
    for power in range(3):
        pull = pull * pull // number_of
    pull = pull * lift // number_of
    tickets = jax.random.randint(jax.random.fold_in(own_key, 2), (rows, number_of), 0, 4096) + pull
    holders = jax.random.permutation(jax.random.fold_in(own_key, 3), rows)[jnp.arange(number_of) % rows]
    tickets = jnp.where(jnp.arange(rows)[:, None] == holders[None, :], 1 << 14, tickets)
    merit = tickets * number_of + jnp.arange(number_of)
    return lax.top_k(merit.astype(jnp.int32), top)[1].astype(jnp.int32)


def noise(rng, shape, width, bound, cuts=(), kind=jnp.bfloat16):
    result = jax.random.normal(rng, shape, jnp.float32) * width
    if len(cuts) > 0:
        result = steps_of(rng, shape, cuts, -0.22, 0.18) * result
    return jnp.clip(result, min=-bound, max=bound).astype(kind)


def setup_inputs(seed: int = 0) -> dict:
    key_of = jax.random.split(jax.random.key(seed), 15)
    tokens = noise(key_of[0], (SEQUENCE_COUNT, SEQUENCE_LENGTH, D), 1.0, 6.0, ((0, 2), (1, 16)))
    order = jax.vmap(lambda own: jax.random.permutation(own, SEQUENCE_LENGTH))(jax.random.split(key_of[1], SEQUENCE_COUNT)).reshape((SEQUENCE_COUNT, SEQUENCE_LENGTH)).astype(jnp.int32)
    expert_ids = choose_distinct(key_of[2], SEQUENCE_COUNT * SEQUENCE_LENGTH, EXPERTS, 1, 1024).reshape((SEQUENCE_COUNT, SEQUENCE_LENGTH, 1))
    norm1_gain = jnp.clip(1.0 + 0.1 * jax.random.normal(key_of[3], (D,), jnp.float32), 0.5, 1.5).astype(jnp.bfloat16)
    w_query = noise(key_of[4], (D, D), (D // 2) ** -0.5, 0.3125, ((0, 32),))
    w_key = noise(key_of[5], (D, D), (D // 2) ** -0.5, 0.3125, ((0, 32),))
    w_value = noise(key_of[6], (D, D), D ** -0.5, 0.21875, ((0, 32),))
    w_attn_out = noise(key_of[7], (D, D), (D // 32) ** -0.5, 1.25, ((0, 32),))
    rel_table = noise(key_of[8], (HEAD_COUNT * BUCKETS,), 0.5, 3.0, ((0, 32),))
    norm2_gain = jnp.clip(1.0 + 0.1 * jax.random.normal(key_of[9], (D,), jnp.float32), 0.5, 1.5).astype(jnp.bfloat16)
    w_router = noise(key_of[10], (D, EXPERTS), (2 * D) ** -0.5, 0.15625, ((0, 32),))
    w_in = noise(key_of[11], (EXPERTS, D, FF), D ** -0.5, 0.21875, ((0, 8),))
    w_out = noise(key_of[12], (EXPERTS, FF, D), (max(1, FF // 1024)) ** -0.5, 3.5, ((0, 8),))
    cotangent = noise(key_of[13], (SEQUENCE_COUNT, SEQUENCE_LENGTH, D), 1.0, 6.0, ((0, 2), (1, 16)))
    return {"tokens": tokens, "order": order, "expert_ids": expert_ids, "norm1_gain": norm1_gain, "w_query": w_query, "w_key": w_key, "w_value": w_value, "w_attn_out": w_attn_out, "rel_table": rel_table, "norm2_gain": norm2_gain, "w_router": w_router, "w_in": w_in, "w_out": w_out, "cotangent": cotangent}


EPSILON = 1e-06
AUX_WEIGHT = 1.0
MASKED = -1e+30
HIGH_PRECISION = lax.Precision.HIGHEST
LIMITS = (1, 2, 3, 4, 5, 6, 7, 8, 12, 16, 23, 32, 46, 64, 91)

@jax.custom_vjp
def low_precision(v):
    return lax.optimization_barrier(v.astype(jnp.bfloat16)).astype(jnp.float32)

@jax.custom_vjp
def low_precision_backward(v):
    return v

def low_keep(v):
    return (low_precision(v), None)

def low_pass(kept, grad):
    return (grad,)

def back_keep(v):
    return (v, None)

def back_low(kept, grad):
    return (low_precision(grad),)
low_precision.defvjp(low_keep, low_pass)
low_precision_backward.defvjp(back_keep, back_low)

def bucket_of(distance, half_count):
    magnitude = jnp.abs(distance)
    bucket = jnp.zeros(distance.shape, jnp.int32)
    for threshold in LIMITS:
        bucket = bucket + (magnitude >= threshold).astype(jnp.int32)
    return bucket + half_count * (distance > 0).astype(jnp.int32)

def norm(values, gain_vec):
    return values * lax.rsqrt(lax.optimization_barrier(jnp.mean(values * values, axis=-1, keepdims=True)) + EPSILON) * gain_vec

def to_groups(values):
    trailing = values.shape[2:]
    pieces = values.reshape((N_DP, SEQ_DEV, N_BLK * N_HEAD, PIECE) + trailing)
    return jnp.swapaxes(pieces, 1, 2).reshape((N_DP * N_BLK * N_HEAD, SEQ_DEV * PIECE) + trailing)

def from_groups(values):
    trailing = values.shape[2:]
    pieces = values.reshape((N_DP, N_BLK * N_HEAD, SEQ_DEV, PIECE) + trailing)
    return jnp.swapaxes(pieces, 1, 2).reshape((SEQUENCE_COUNT, SEQUENCE_LENGTH) + trailing)

def attention_block(query_rows, key_seq, value_seq, table_heads, start_row):
    query_pos = start_row + jnp.arange(query_rows.shape[0], dtype=jnp.int32)
    key_pos = jnp.arange(key_seq.shape[0], dtype=jnp.int32)
    distance = key_pos[None, :] - query_pos[:, None]
    bias_all = jnp.take(table_heads, bucket_of(distance, BUCKETS // 2), axis=1)
    scores = jnp.einsum('qhd,khd->hqk', query_rows, key_seq, precision=HIGH_PRECISION) * HEAD_SIZE ** (-0.5) + bias_all
    scores = low_precision_backward(scores)
    allowed = key_pos[None, :] // BLOCK <= query_pos[:, None] // BLOCK
    scores = jnp.where(allowed[None], scores, MASKED)
    attn_weights = low_precision(jax.nn.softmax(scores, axis=-1))
    return jnp.einsum('hqk,khd->qhd', attn_weights, value_seq, precision=HIGH_PRECISION)

def reference(tokens, order, expert_ids, norm1_gain, w_query, w_key, w_value, w_attn_out, rel_table, norm2_gain, w_router, w_in, w_out, cotangent):
    ids_all = expert_ids[:, :, 0]
    columns = jnp.arange(EXPERTS, dtype=jnp.int32)
    tallies = lax.optimization_barrier(jnp.sum((ids_all.reshape(-1, 1) == columns[None, :]).astype(jnp.float32), axis=0))
    seq_local = (jnp.arange(SEQUENCE_COUNT, dtype=jnp.int32) % SEQ_DEV)[:, None]
    priority = to_groups(order * SEQ_DEV + seq_local)
    group_ids = to_groups(ids_all)
    earlier = (priority[:, None, :] < priority[:, :, None]) & (group_ids[:, None, :] == group_ids[:, :, None])
    queue_rank = lax.optimization_barrier(jnp.sum(earlier.astype(jnp.int32), axis=-1))
    kept = (queue_rank < CAP).astype(jnp.float32)
    slot_rank = jnp.minimum(queue_rank, CAP - 1)
    group_total = N_DP * N_BLK * N_HEAD
    group_index = jnp.broadcast_to(jnp.arange(group_total, dtype=jnp.int32)[:, None], queue_rank.shape)

    def forward(x_in, gain_one, weight_q, weight_k, weight_v, output_weight, table_flat, gain_two, router_weight, weight_in, weight_out):
        normed_input = low_precision(norm(x_in, gain_one))

        def project(weight_matrix):
            return low_precision(low_precision_backward(jnp.einsum('ivp,pq->ivq', normed_input, weight_matrix, precision=HIGH_PRECISION))).reshape(SEQUENCE_COUNT, SEQUENCE_LENGTH, HEAD_COUNT, HEAD_SIZE)
        query_all = project(weight_q)
        key_all = project(weight_k)
        value_all = project(weight_v)
        table_heads = table_flat.reshape(HEAD_COUNT, BUCKETS)
        row_block = min(512, SEQUENCE_LENGTH)

        def per_sequence(inputs):
            query_seq, key_seq, value_seq = inputs

            def per_block(block_index):
                start_row = block_index * row_block
                query_rows = lax.dynamic_slice_in_dim(query_seq, start_row, row_block, 0)
                return attention_block(query_rows, key_seq, value_seq, table_heads, start_row)
            return lax.map(jax.checkpoint(per_block), jnp.arange(SEQUENCE_LENGTH // row_block, dtype=jnp.int32)).reshape(SEQUENCE_LENGTH, HEAD_COUNT, HEAD_SIZE)
        attended_values = lax.map(per_sequence, (query_all, key_all, value_all))
        attended_values = low_precision(low_precision_backward(attended_values.reshape(SEQUENCE_COUNT, SEQUENCE_LENGTH, D)))
        attention_output = low_precision_backward(jnp.einsum('ivp,pq->ivq', attended_values, output_weight, precision=HIGH_PRECISION))
        middle = x_in + attention_output
        routed_tokens = low_precision(norm(middle, gain_two))
        router_logits = low_precision_backward(jnp.einsum('ivp,pq->ivq', routed_tokens, router_weight, precision=HIGH_PRECISION))
        router_probs = jax.nn.softmax(router_logits, axis=-1)
        gate_value = jnp.take_along_axis(router_probs, expert_ids, axis=-1)[..., 0]
        outgoing = to_groups(low_precision_backward(routed_tokens))
        buffer = jnp.zeros((group_total, EXPERTS, CAP, D), jnp.float32).at[group_index, group_ids, slot_rank].add(outgoing * kept[..., None])

        def expert_apply(inputs):
            rows_in, weight_first, weight_second = inputs
            pre_act = low_precision_backward(jnp.einsum('gcd,df->gcf', rows_in, weight_first, precision=HIGH_PRECISION))
            hidden = low_precision(low_precision_backward(jax.nn.gelu(pre_act, approximate=False)))
            return low_precision(low_precision_backward(jnp.einsum('gcf,fd->gcd', hidden, weight_second, precision=HIGH_PRECISION)))
        expert_out = lax.map(jax.checkpoint(expert_apply), (jnp.swapaxes(buffer, 0, 1), weight_in, weight_out))
        expert_rows = expert_out[group_ids, group_index, slot_rank] * kept[..., None]
        layer_out = middle + gate_value[..., None] * from_groups(expert_rows)
        balance = EXPERTS * jnp.sum(tallies / (SEQUENCE_COUNT * SEQUENCE_LENGTH) * lax.optimization_barrier(jnp.mean(router_probs, axis=(0, 1))))
        return (layer_out, balance)
    primal = (tokens.astype(jnp.float32), norm1_gain.astype(jnp.float32), w_query.astype(jnp.float32), w_key.astype(jnp.float32), w_value.astype(jnp.float32), w_attn_out.astype(jnp.float32), rel_table.astype(jnp.float32), norm2_gain.astype(jnp.float32), w_router.astype(jnp.float32), w_in.astype(jnp.float32), w_out.astype(jnp.float32))
    (layer_out, balance), pull_back = jax.vjp(forward, *primal)
    grads = pull_back((cotangent.astype(jnp.float32), jnp.float32(AUX_WEIGHT * SEQUENCE_COUNT * SEQUENCE_LENGTH)))
    return (layer_out.astype(jnp.bfloat16), grads[0].astype(jnp.bfloat16), grads[1], grads[2], grads[3], grads[4], grads[5], grads[6], grads[7], grads[8], grads[9], grads[10])
```

```python
import functools

import jax
import jax.numpy as jnp
import numpy as np
from jax import lax
from jax.experimental import pallas as pl
from jax.experimental.pallas import tpu as pltpu
from jax.sharding import PartitionSpec as P

HEAD_COUNT = 12
HEAD_SIZE = 64
BUCKETS = 32
BLOCK = 256
EPSILON = 1e-06
AUX_WEIGHT = 1.0
LIMITS = (1, 2, 3, 4, 5, 6, 7, 8, 12, 16, 23, 32, 46, 64, 91)
INV_ROOT_TWO = 0.7071067811865476
INV_ROOT_TWO_PI = 0.3989422804014327
LANES = 128
MESH = pl.DeviceIdType.MESH
F32 = jnp.float32
BF16 = jnp.bfloat16


class Sizes:
    def __init__(self, n_dp, n_blk, n_head, rows, width, experts, hidden, piece):
        self.n_dp, self.n_blk, self.n_head = n_dp, n_blk, n_head
        self.ndev = n_dp * n_blk * n_head
        self.ns = n_blk * n_head
        self.R, self.D, self.E, self.FF, self.PT = rows, width, experts, hidden, piece
        self.S = piece * self.ns
        self.nq = self.S // BLOCK
        self.hb = HEAD_COUNT // n_blk
        self.cap = (5 * piece + 4 * experts - 1) // (4 * experts)
        self.cap8 = (self.cap + 7) // 8 * 8
        self.SB = 2 * self.cap8
        self.NG = n_dp * n_blk
        self.RL = HEAD_COUNT * BUCKETS // self.ndev
        assert self.hb <= n_head and self.hb * n_blk == HEAD_COUNT
        assert experts == self.NG and n_head == 4


def nt(a, b):
    return lax.dot_general(a, b, (((1,), (1,)), ((), ())), preferred_element_type=F32)


def tn(a, b):
    return lax.dot_general(a, b, (((0,), (0,)), ((), ())), preferred_element_type=F32)


def nn(a, b):
    return jnp.dot(a, b, preferred_element_type=F32)


def place():
    return lax.axis_index("dp"), lax.axis_index("blk"), lax.axis_index("head")


def signal(device):
    pl.semaphore_signal(
        pltpu.get_barrier_semaphore(), inc=1, device_id=device, device_id_type=MESH
    )


def await_barrier(count):
    pl.semaphore_wait(pltpu.get_barrier_semaphore(), count)


def remote(src, dst, send, recv, device):
    return pltpu.make_async_remote_copy(
        src_ref=src, dst_ref=dst, send_sem=send, recv_sem=recv, device_id=device, device_id_type=MESH
    )


def flatten_rows(blocks):
    count, rows, lanes = blocks.shape
    wide = blocks.astype(F32)
    if rows % 8 == 0:
        return wide.reshape(count * rows, lanes)
    return jnp.concatenate([wide[i] for i in range(count)], axis=0)


def split_rows(dst_ref, values, rows):
    count = values.shape[0] // rows
    if rows % 8 == 0:
        dst_ref[...] = values.reshape(count, rows, values.shape[1]).astype(dst_ref.dtype)
    else:
        for i in range(count):
            dst_ref[i] = values[i * rows : (i + 1) * rows].astype(dst_ref.dtype)


def normal_parts(v):
    bell = jnp.exp(-0.5 * v * v)
    t = 1.0 / (1.0 + (0.3275911 * INV_ROOT_TWO) * jnp.abs(v))
    poly = t * (
        0.254829592
        + t * (-0.284496736 + t * (1.421413741 + t * (-1.453152027 + t * 1.061405429)))
    )
    tail = 0.5 * poly * bell
    return jnp.where(v >= 0, 1.0 - tail, tail), bell


def gather_kernel(z, x_ref, w_ref, xg_ref, wg_ref, xs, xr, ws, wr, loc):
    d, b, h = place()
    nb, nh, nd = z.n_blk, z.n_head, z.n_dp
    hy = lax.rem(h + 2, nh)
    hc = h + 1 - 2 * lax.rem(h, 2)
    hyc = lax.rem(hc + 2, nh)
    zpeers = [lax.rem(b + k, nb) for k in range(1, nb)]
    zfrom = [lax.rem(b + nb - k, nb) for k in range(1, nb)]
    dpeers = [lax.rem(d + k, nd) for k in range(1, nd)]
    dfrom = [lax.rem(d + nd - k, nd) for k in range(1, nd)]
    for p in zpeers:
        signal((d, p, h))
    signal((d, b, hy))
    signal((d, b, hc))
    for p in dpeers:
        signal((p, b, h))

    def xslot(bb, hh):
        return bb * nh + hh

    def wslot(dd, bb, hh):
        return (dd * nb + bb) * nh + hh

    own_x = xslot(b, h)
    own_w = wslot(d, b, h)
    cx = pltpu.make_async_copy(x_ref, xg_ref.at[own_x], loc.at[0])
    cw = pltpu.make_async_copy(w_ref, wg_ref.at[own_w], loc.at[1])
    cx.start()
    cw.start()
    await_barrier(nb - 1 + 2 + nd - 1)
    sent = []

    def send_x(src, slot, device):
        c = remote(src, xg_ref.at[slot], xs.at[len(sent_x)], xr.at[slot], device)
        sent_x.append(c)
        c.start()

    def send_w(src, slot, device):
        c = remote(src, wg_ref.at[slot], ws.at[len(sent_w)], wr.at[slot], device)
        sent_w.append(c)
        c.start()

    sent_x, sent_w = [], []

    def got_x(slot):
        remote(xg_ref.at[slot], xg_ref.at[slot], xs.at[0], xr.at[slot], (d, b, hc)).wait_recv()

    def got_w(slot):
        remote(wg_ref.at[slot], wg_ref.at[slot], ws.at[0], wr.at[slot], (d, b, hc)).wait_recv()

    for p in zpeers:
        send_x(x_ref, own_x, (d, p, h))
    send_x(x_ref, own_x, (d, b, hy))
    send_x(x_ref, own_x, (d, b, hc))
    for p in dpeers:
        send_w(w_ref, own_w, (p, b, h))
    for p in zpeers:
        send_w(w_ref, own_w, (d, p, h))
    send_w(w_ref, own_w, (d, b, hy))
    send_w(w_ref, own_w, (d, b, hc))
    for f in zfrom:
        slot = xslot(f, h)
        got_x(slot)
        send_x(xg_ref.at[slot], slot, (d, b, hy))
        send_x(xg_ref.at[slot], slot, (d, b, hc))
    for f in zfrom:
        slot = wslot(d, f, h)
        got_w(slot)
        for p in dpeers:
            send_w(wg_ref.at[slot], slot, (p, b, h))
        send_w(wg_ref.at[slot], slot, (d, b, hy))
        send_w(wg_ref.at[slot], slot, (d, b, hc))
    for f in [b] + zfrom:
        slot = xslot(f, hy)
        got_x(slot)
        send_x(xg_ref.at[slot], slot, (d, b, hc))
    for f in [b] + zfrom:
        slot = wslot(d, f, hy)
        got_w(slot)
        for p in dpeers:
            send_w(wg_ref.at[slot], slot, (p, b, h))
        send_w(wg_ref.at[slot], slot, (d, b, hc))
    for g in dfrom:
        for hh in (h, hy):
            for f in [b] + zfrom:
                slot = wslot(g, f, hh)
                got_w(slot)
                send_w(wg_ref.at[slot], slot, (d, b, hc))
    for hh in (hc, hyc):
        for f in [b] + zfrom:
            got_x(xslot(f, hh))
    for g in [d] + dfrom:
        for hh in (hc, hyc):
            for f in [b] + zfrom:
                got_w(wslot(g, f, hh))
    cx.wait()
    cw.wait()
    for c in sent_x + sent_w:
        c.wait_send()


def gather(z, x, w):
    nb, nh, nd = z.n_blk, z.n_head, z.n_dp
    count_x = (nb - 1) + 2 + 2 * (nb - 1) + nb
    count_w = (nd - 1) + (nb - 1) + 2 + (nb - 1) * (nd + 1) + nb * nd + (nd - 1) * 2 * nb
    return pl.pallas_call(
        functools.partial(gather_kernel, z),
        out_shape=(
            jax.ShapeDtypeStruct((z.ns,) + x.shape, x.dtype),
            jax.ShapeDtypeStruct((z.ndev,) + w.shape, w.dtype),
        ),
        in_specs=[pl.BlockSpec(memory_space=pl.ANY)] * 2,
        out_specs=(pl.BlockSpec(memory_space=pl.ANY),) * 2,
        scratch_shapes=[
            pltpu.SemaphoreType.DMA((count_x,)),
            pltpu.SemaphoreType.DMA((z.ns,)),
            pltpu.SemaphoreType.DMA((count_w,)),
            pltpu.SemaphoreType.DMA((z.ndev,)),
            pltpu.SemaphoreType.DMA((2,)),
        ],
        compiler_params=pltpu.CompilerParams(collective_id=0, has_side_effects=True),
        name="gather_inputs",
    )(x, w)


def bias_tile(table, shift):
    i = lax.broadcasted_iota(jnp.int32, (BLOCK, BLOCK), 0)
    j = lax.broadcasted_iota(jnp.int32, (BLOCK, BLOCK), 1)
    dist = j - i + shift
    mag = jnp.abs(dist)
    half = BUCKETS // 2
    out = jnp.broadcast_to(table[0:1, 0:1], (BLOCK, BLOCK))
    for n, limit in enumerate(LIMITS):
        low = table[n + 1 : n + 2, 0:1]
        if shift == 0:
            high = table[half + n + 1 : half + n + 2, 0:1]
            out = jnp.where(mag >= limit, jnp.where(dist > 0, high, low), out)
        else:
            out = jnp.where(mag >= limit, low, out)
    return out


def forward_kernel(
    z, entry_ref, x_ref, w_ref, normed_ref, qkv_ref, p_ref, att_ref,
    slab, wh, gain, far, bias_d, bias_s, k_scr, v_scr, s_scr, sem,
):
    step = pl.program_id(0)
    D = z.D

    @pl.when(step == 0)
    def _():
        d, b, h = place()
        hd = b * z.hb + jnp.minimum(h, z.hb - 1)
        pair = hd // 2
        copies = []
        for m in range(3):
            at = pl.ds(pl.multiple_of(m * D + pair * LANES, LANES), LANES)
            copies.append(pltpu.make_async_copy(w_ref.at[:, :, at], slab.at[m], sem.at[m]))
        copies.append(
            pltpu.make_async_copy(w_ref.at[:, :, pl.ds(4 * D, LANES)], slab.at[3], sem.at[3])
        )
        for c in copies:
            c.start()
        for c in copies:
            c.wait()
        odd = lax.rem(hd, 2) == 1
        for m in range(3):
            rows = flatten_rows(slab[m])
            own = jnp.where(odd, rows[:, HEAD_SIZE:], rows[:, :HEAD_SIZE])
            if m == 0:
                own = own * HEAD_SIZE ** (-0.5)
            wh[:, m * HEAD_SIZE : (m + 1) * HEAD_SIZE] = own.astype(BF16)
        misc = flatten_rows(slab[3])
        gain[...] = jnp.transpose(misc)[z.E : z.E + 1, :]
        wanted = hd * BUCKETS + lax.broadcasted_iota(jnp.int32, (BUCKETS, D), 0)
        pick = (entry_ref[...] == wanted).astype(BF16)
        table = nn(pick, misc.astype(BF16))[:, z.E + 2 : z.E + 3]
        bias_d[...] = bias_tile(table, 0)
        bias_s[...] = bias_tile(table, -BLOCK)
        far[...] = table[BUCKETS // 2 - 1 : BUCKETS // 2, 0:1]

    x = x_ref[...].astype(F32)
    inverse = lax.rsqrt(jnp.mean(x * x, axis=-1, keepdims=True) + EPSILON)
    normed = (x * inverse * gain[...]).astype(BF16)
    normed_ref[...] = normed
    qkv = nn(normed, wh[...]).astype(BF16)
    qkv_ref[...] = qkv
    here = pl.ds(pl.multiple_of(step * BLOCK, BLOCK), BLOCK)
    q = qkv[:, :HEAD_SIZE]
    k_scr[here, :] = qkv[:, HEAD_SIZE : 2 * HEAD_SIZE]
    v_scr[here, :] = qkv[:, 2 * HEAD_SIZE :]

    def at(j):
        return pl.ds(pl.multiple_of(j * BLOCK, BLOCK), BLOCK)

    def score(j, bias, top):
        s = nt(q, k_scr[at(j), :]) + bias
        s_scr[:, at(j)] = s
        return jnp.maximum(top, jnp.max(s, axis=-1, keepdims=True))

    top = jnp.full((BLOCK, 1), -1e30, F32)
    top = lax.fori_loop(0, step - 1, lambda j, t: score(j, far[...], t), top)
    top = lax.fori_loop(
        jnp.maximum(step - 1, 0), step, lambda j, t: score(j, bias_s[...], t), top
    )
    top = score(step, bias_d[...], top)

    def exps(j, total):
        e = jnp.exp(s_scr[:, at(j)] - top)
        s_scr[:, at(j)] = e
        return total + jnp.sum(e, axis=-1, keepdims=True)

    total = lax.fori_loop(0, step + 1, exps, jnp.zeros((BLOCK, 1), F32))
    scale = 1.0 / total

    def values(j, acc):
        p = (s_scr[:, at(j)] * scale).astype(BF16)
        p_ref[0, :, at(j)] = p
        return acc + nn(p, v_scr[at(j), :])

    acc = lax.fori_loop(0, step + 1, values, jnp.zeros((BLOCK, HEAD_SIZE), F32))
    att_ref[...] = acc.astype(BF16)


def attention_forward(z, entries, xg, wg):
    D, S, HS = z.D, z.S, HEAD_SIZE
    row = lambda i: (i, 0)
    return pl.pallas_call(
        functools.partial(forward_kernel, z),
        grid=(z.nq,),
        out_shape=(
            jax.ShapeDtypeStruct((S, D), BF16),
            jax.ShapeDtypeStruct((S, 3 * HS), BF16),
            jax.ShapeDtypeStruct((z.nq, BLOCK, S), BF16),
            jax.ShapeDtypeStruct((S, HS), BF16),
        ),
        in_specs=[
            pl.BlockSpec((1, D), lambda i: (0, 0)),
            pl.BlockSpec((BLOCK, D), row),
            pl.BlockSpec(memory_space=pl.ANY),
        ],
        out_specs=(
            pl.BlockSpec((BLOCK, D), row),
            pl.BlockSpec((BLOCK, 3 * HS), row),
            pl.BlockSpec((1, BLOCK, S), lambda i: (i, 0, 0)),
            pl.BlockSpec((BLOCK, HS), row),
        ),
        scratch_shapes=[
            pltpu.VMEM((4, z.ndev, z.R, LANES), BF16),
            pltpu.VMEM((D, 3 * HS), BF16),
            pltpu.VMEM((1, D), F32),
            pltpu.VMEM((1, 1), F32),
            pltpu.VMEM((BLOCK, BLOCK), F32),
            pltpu.VMEM((BLOCK, BLOCK), F32),
            pltpu.VMEM((S, HS), BF16),
            pltpu.VMEM((S, HS), BF16),
            pltpu.VMEM((BLOCK, S), F32),
            pltpu.SemaphoreType.DMA((4,)),
        ],
        compiler_params=pltpu.CompilerParams(
            dimension_semantics=("arbitrary",), vmem_limit_bytes=48 * 1024 * 1024
        ),
        name="attention_forward",
    )(entries, xg.reshape(S, D), wg)


def middle_kernel(
    z, att_ref, x_ref, w_ref, order_ref, ids_ref, win_ref, wout_ref, cot_ref,
    layer_ref, gmid_ref, gatt_ref, dwo_ref, all_ref,
    win, wout, wo3, misc3, att_in, disp, exp_in, ret, back, route, att_cat, out_acc, gg_acc,
    loc, att_s, att_r, dis_s, dis_r, ret_s, ret_r, all_s, all_r,
):
    d, b, h = place()
    nb, nh, nd, ns = z.n_blk, z.n_head, z.n_dp, z.ns
    D, E, PT, SB, NG = z.D, z.E, z.PT, z.SB, z.NG
    s = b * nh + h
    me = d * ns + s
    g = d * nb + b
    hd = b * z.hb + jnp.minimum(h, z.hb - 1)
    active = h < z.hb
    hy = lax.rem(h + 2, nh)
    hc = h + 1 - 2 * lax.rem(h, 2)
    hyc = lax.rem(hc + 2, nh)

    def seq_peer(k):
        t = lax.rem(s + k, ns)
        return t, (d, t // nh, lax.rem(t, nh))

    def exp_peer(k):
        e = lax.rem(g + k, NG)
        return e, (e // nb, lax.rem(e, nb), h)

    def exp_from(k):
        e = lax.rem(g + NG - k, NG)
        return e, (e // nb, lax.rem(e, nb), h)

    for k in range(1, ns):
        signal(seq_peer(k)[1])
    for k in range(1, nd):
        for kb in range(nb):
            signal((lax.rem(d + k, nd), lax.rem(b + kb, nb), h))

    local = [
        pltpu.make_async_copy(w_ref.at[:, :, pl.ds(3 * D, D)], wo3, loc.at[0]),
        pltpu.make_async_copy(w_ref.at[:, :, pl.ds(4 * D, LANES)], misc3, loc.at[1]),
        pltpu.make_async_copy(win_ref.at[0], win, loc.at[2]),
        pltpu.make_async_copy(wout_ref.at[0], wout, loc.at[3]),
    ]
    for c in local:
        c.start()
    await_barrier(ns - 1 + (nd - 1) * nb)

    def send_att(k):
        t, device = seq_peer(k)
        return remote(att_ref.at[t], att_in.at[hd], att_s.at[k], att_r.at[hd], device)

    @pl.when(active)
    def _():
        for k in range(1, ns):
            send_att(k).start()
        own = pltpu.make_async_copy(att_ref.at[s], att_in.at[hd], loc.at[4])
        own.start()
        own.wait()

    ids_row = ids_ref[pl.ds(me, 1), :]
    order_row = order_ref[...]
    ids_col = jnp.transpose(jnp.broadcast_to(ids_row, (PT, PT)))
    order_col = jnp.transpose(jnp.broadcast_to(order_row, (PT, PT)))
    earlier = (order_col < order_row) & (ids_col == ids_row)
    rank = jnp.sum(earlier.astype(jnp.int32), axis=0, keepdims=True)
    ids2 = jnp.concatenate([ids_row, ids_row], axis=1)
    rank2 = jnp.concatenate([rank, rank], axis=1)
    kk = lax.broadcasted_iota(jnp.int32, (SB, 2 * PT), 0)
    cc = lax.broadcasted_iota(jnp.int32, (SB, 2 * PT), 1)
    low = kk >= z.cap8
    kept = jnp.where(low, kk - z.cap8, kk)
    base = (rank2 == kept) & (kept < z.cap) & (low.astype(jnp.int32) == (cc >= PT).astype(jnp.int32))
    lane = lax.broadcasted_iota(jnp.int32, (1, LANES), 1)
    share = jnp.zeros((1, LANES), F32)
    ids_all = ids_ref[...]
    for e in range(E):
        route[e * SB : (e + 1) * SB, :] = (base & (ids2 == e)).astype(BF16)
        count = jnp.sum((ids_all == e).astype(F32), axis=1, keepdims=True)
        count = jnp.sum(count, axis=0, keepdims=True)
        share = share + jnp.where(lane == e, count, 0.0)
    share = share * (AUX_WEIGHT * E / (ids_all.shape[0] * ids_all.shape[1]))
    chosen = (ids_col[:, :1] == lane)

    local[0].wait()
    local[1].wait()
    wo = flatten_rows(wo3[...]).astype(BF16)
    misc = flatten_rows(misc3[...])
    router = misc.astype(BF16)
    gain = jnp.transpose(misc)[E + 1 : E + 2, :]
    x = x_ref[...].astype(F32)
    cot = cot_ref[...].astype(F32)

    for n in range(HEAD_COUNT):

        @pl.when(jnp.logical_not(active & (hd == n)))
        def _():
            remote(
                att_in.at[n], att_in.at[n], att_s.at[0], att_r.at[n], (d, b, hc)
            ).wait_recv()

        att_cat[:, n * HEAD_SIZE : (n + 1) * HEAD_SIZE] = att_in[n]
    att = att_cat[...]
    middle = x + nn(att, wo)
    inverse = lax.rsqrt(jnp.mean(middle * middle, axis=-1, keepdims=True) + EPSILON)
    routed = (middle * inverse * gain).astype(BF16)
    logits = jnp.where(lane < E, nn(routed, router), -1e30)
    exps = jnp.exp(logits - jnp.max(logits, axis=-1, keepdims=True))
    probs = exps / jnp.sum(exps, axis=-1, keepdims=True)
    gate = jnp.sum(jnp.where(chosen, probs, 0.0), axis=-1, keepdims=True)
    stacked = jnp.concatenate([routed, (gate * cot).astype(BF16)], axis=0)
    disp[...] = nn(route[...], stacked).reshape(E, SB, D).astype(BF16)

    def send_disp(k):
        e, device = exp_peer(k)
        return remote(disp.at[e], exp_in.at[g], dis_s.at[k], dis_r.at[g], device)

    for k in range(1, NG):
        send_disp(k).start()
    exp_in[g] = disp[g]
    local[2].wait()
    local[3].wait()
    for k in range(1, NG):
        e, device = exp_from(k)
        remote(exp_in.at[e], exp_in.at[e], dis_s.at[0], dis_r.at[e], device).wait_recv()
    to_y = remote(exp_in, all_ref.at[h], all_s.at[0], all_r.at[h], (d, b, hy))
    to_c = remote(exp_in, all_ref.at[h], all_s.at[1], all_r.at[h], (d, b, hc))
    to_me = pltpu.make_async_copy(exp_in, all_ref.at[h], loc.at[5])
    to_y.start()
    to_c.start()
    to_me.start()
    slots = exp_in[...].astype(F32)
    rows_in = slots[:, : z.cap8].reshape(NG * z.cap8, D).astype(BF16)
    grad_out = slots[:, z.cap8 :].reshape(NG * z.cap8, D).astype(BF16)
    out_acc[...] = jnp.zeros_like(out_acc)
    gg_acc[...] = jnp.zeros_like(gg_acc)
    chunk = D

    def ff_step(c, carry):
        at = pl.ds(pl.multiple_of(c * chunk, chunk), chunk)
        w1 = win[:, at]
        w2 = wout[at, :]
        pre = nn(rows_in, w1)
        phi, bell = normal_parts(pre)
        hidden = (pre * phi).astype(BF16)
        out_acc[...] += nn(hidden, w2)
        gh = nt(grad_out, w2).astype(BF16).astype(F32)
        gp = (gh * (phi + pre * bell * INV_ROOT_TWO_PI)).astype(BF16)
        gg_acc[...] += nt(gp, w1)
        return carry

    lax.fori_loop(0, z.FF // chunk, ff_step, 0)
    both = jnp.concatenate(
        [out_acc[...].reshape(NG, z.cap8, D), gg_acc[...].reshape(NG, z.cap8, D)], axis=1
    )
    ret[...] = both.astype(BF16)

    def send_ret(k):
        e, device = exp_peer(k)
        return remote(ret.at[e], back.at[g], ret_s.at[k], ret_r.at[g], device)

    for k in range(1, NG):
        send_ret(k).start()
    back[g] = ret[g]
    remote(
        all_ref.at[hy], all_ref.at[hy], all_s.at[0], all_r.at[hy], (d, b, hy)
    ).wait_recv()
    on_c = remote(all_ref.at[hy], all_ref.at[hy], all_s.at[2], all_r.at[hy], (d, b, hc))
    on_c.start()
    for k in range(1, NG):
        e, device = exp_from(k)
        remote(back.at[e], back.at[e], ret_s.at[0], ret_r.at[e], device).wait_recv()
    comb = tn(route[...], back[...].reshape(E * SB, D))
    expert_rows = comb[:PT]
    grad_routed = comb[PT:]
    layer_ref[...] = (middle + gate * expert_rows).astype(BF16)
    grad_gate = jnp.sum(cot * expert_rows, axis=-1, keepdims=True)
    grad_probs = jnp.where(chosen, grad_gate, 0.0) + share
    inner = jnp.sum(probs * grad_probs, axis=-1, keepdims=True)
    grad_logits = (probs * (grad_probs - inner)).astype(BF16)
    grad_routed = grad_routed + nt(grad_logits, router)
    scaled = grad_routed * gain
    mean = jnp.mean(scaled * middle, axis=-1, keepdims=True)
    gmid = cot + inverse * scaled - middle * (inverse * inverse * inverse) * mean
    gmid_ref[...] = gmid
    low_mid = gmid.astype(BF16)
    gatt = nt(low_mid, wo).astype(BF16)
    for n in range(HEAD_COUNT):
        gatt_ref[n] = gatt[:, n * HEAD_SIZE : (n + 1) * HEAD_SIZE]
    term = grad_routed * middle * inverse
    high = term.astype(BF16)
    rest = (term - high.astype(F32)).astype(BF16)
    ones = jnp.broadcast_to((lane == E).astype(BF16), (PT, LANES))
    small = tn(routed, grad_logits) + tn(high, ones) + tn(rest, ones)
    split_rows(dwo_ref, jnp.concatenate([tn(att, low_mid), small], axis=1), z.R)

    to_me.wait()
    for hh in (hc, hyc):
        remote(
            all_ref.at[hh], all_ref.at[hh], all_s.at[0], all_r.at[hh], (d, b, hc)
        ).wait_recv()
    for c in (to_y, to_c, on_c):
        c.wait_send()
    for k in range(1, NG):
        send_disp(k).wait_send()
        send_ret(k).wait_send()

    @pl.when(active)
    def _():
        for k in range(1, ns):
            send_att(k).wait_send()


def middle_part(z, att, x, wg, order, ids, w_in, w_out, cot):
    D, PT, SB, NG, E = z.D, z.PT, z.SB, z.NG, z.E
    dma = pltpu.SemaphoreType.DMA
    vmem = pl.BlockSpec(memory_space=pltpu.VMEM)
    hbm = pl.BlockSpec(memory_space=pl.ANY)
    return pl.pallas_call(
        functools.partial(middle_kernel, z),
        out_shape=(
            jax.ShapeDtypeStruct((PT, D), BF16),
            jax.ShapeDtypeStruct((PT, D), F32),
            jax.ShapeDtypeStruct((HEAD_COUNT, PT, HEAD_SIZE), BF16),
            jax.ShapeDtypeStruct((z.ndev, z.R, D + LANES), BF16),
            jax.ShapeDtypeStruct((z.n_head, NG, SB, D), BF16),
        ),
        in_specs=[hbm, vmem, hbm, vmem, vmem, hbm, hbm, vmem],
        out_specs=(vmem, vmem, vmem, vmem, hbm),
        scratch_shapes=[
            pltpu.VMEM((D, z.FF), BF16),
            pltpu.VMEM((z.FF, D), BF16),
            pltpu.VMEM((z.ndev, z.R, D), BF16),
            pltpu.VMEM((z.ndev, z.R, LANES), BF16),
            pltpu.VMEM((HEAD_COUNT, PT, HEAD_SIZE), BF16),
            pltpu.VMEM((E, SB, D), BF16),
            pltpu.VMEM((NG, SB, D), BF16),
            pltpu.VMEM((NG, SB, D), BF16),
            pltpu.VMEM((E, SB, D), BF16),
            pltpu.VMEM((E * SB, 2 * PT), BF16),
            pltpu.VMEM((PT, D), BF16),
            pltpu.VMEM((NG * z.cap8, D), F32),
            pltpu.VMEM((NG * z.cap8, D), F32),
            dma((6,)),
            dma((z.ns,)),
            dma((HEAD_COUNT,)),
            dma((NG,)),
            dma((NG,)),
            dma((NG,)),
            dma((NG,)),
            dma((3,)),
            dma((z.n_head,)),
        ],
        compiler_params=pltpu.CompilerParams(
            collective_id=1, has_side_effects=True, vmem_limit_bytes=56 * 1024 * 1024
        ),
        name="experts_and_norms",
    )(att.reshape(z.ns, PT, HEAD_SIZE), x, wg, order, ids, w_in, w_out, cot)


def backward_kernel(
    z, gatt_ref, dwo_ref, normed_ref, qkv_ref, p_ref, att_ref, wg_ref, w_ref, x_ref, gmid_ref,
    gtok_ref, gain1_ref, gq_ref, gk_ref, gv_ref, go_ref, table_ref, gain2_ref, router_ref,
    w3, wfull, misc3, normed, qkv, probs, att, do_in, grad_cat, dkv, dqkv, dw, dw3, diag, sub, far,
    dq_in, dw_in, rs_in,
    loc, do_s, do_r, dq_s, dq_r, dw_s, dw_r, rs_s, rs_r,
):
    d, b, h = place()
    nb, nh, nd, ns, nv = z.n_blk, z.n_head, z.n_dp, z.ns, z.ndev
    D, R, PT, HS, E = z.D, z.R, z.PT, HEAD_SIZE, z.E
    s = b * nh + h
    me = d * ns + s
    hd = b * z.hb + jnp.minimum(h, z.hb - 1)
    active = h < z.hb

    def any_peer(k):
        t = lax.rem(me + k, nv)
        return t, (t // ns, lax.rem(t // nh, nb), lax.rem(t, nh))

    def greet(k, carry):
        signal(any_peer(k)[1])
        return carry

    lax.fori_loop(1, nv, greet, 0)
    local = [
        pltpu.make_async_copy(normed_ref, normed, loc.at[0]),
        pltpu.make_async_copy(qkv_ref, qkv, loc.at[1]),
        pltpu.make_async_copy(att_ref, att, loc.at[2]),
        pltpu.make_async_copy(p_ref, probs, loc.at[3]),
        pltpu.make_async_copy(wg_ref.at[:, :, pl.ds(0, 3 * D)], w3, loc.at[4]),
        pltpu.make_async_copy(wg_ref.at[:, :, pl.ds(4 * D, LANES)], misc3, loc.at[5]),
    ]
    for c in local:
        c.start()
    await_barrier(nv - 1)

    def send_do(n):
        hb, hh = n // z.hb, n % z.hb
        return remote(gatt_ref.at[n], do_in.at[s], do_s.at[n], do_r.at[s], (d, hb, hh))

    for n in range(HEAD_COUNT):
        mine = active & (hd == n)

        @pl.when(jnp.logical_not(mine))
        def _():
            send_do(n).start()

        @pl.when(mine)
        def _():
            do_in[s] = gatt_ref[n]

    def send_rs(k):
        t, device = any_peer(k)
        return remote(dwo_ref.at[t], rs_in.at[me], rs_s.at[k], rs_r.at[me], device)

    def start_rs(k, carry):
        send_rs(k).start()
        return carry

    lax.fori_loop(1, nv, start_rs, 0)
    rs_in[me] = dwo_ref[me]
    for c in local:
        c.wait()

    def send_dq(t):
        return remote(
            dqkv.at[t], dq_in.at[hd], dq_s.at[t], dq_r.at[hd], (d, t // nh, lax.rem(t, nh))
        )

    def send_dw(k):
        t, device = any_peer(k)
        slot = d * HEAD_COUNT + hd
        return remote(dw3.at[t], dw_in.at[slot], dw_s.at[k], dw_r.at[slot], device)

    per = BLOCK // PT

    @pl.when(active)
    def _():
        def got_do(k, carry):
            t = lax.rem(s + k, ns)
            remote(
                do_in.at[t], do_in.at[t], do_s.at[0], do_r.at[t], (d, t // nh, lax.rem(t, nh))
            ).wait_recv()
            return carry

        lax.fori_loop(1, ns, got_do, 0)
        dkv[...] = jnp.zeros_like(dkv)
        dw[...] = jnp.zeros_like(dw)
        diag[...] = jnp.zeros_like(diag)
        sub[...] = jnp.zeros_like(sub)
        far[...] = jnp.zeros_like(far)

        def at(j):
            return pl.ds(pl.multiple_of(j * BLOCK, BLOCK), BLOCK)

        def row_block(step, carry):
            i = z.nq - 1 - step
            do = do_in[pl.ds(i * per, per)].reshape(BLOCK, HS)
            delta = jnp.sum(do.astype(F32) * att[at(i), :].astype(F32), axis=-1, keepdims=True)
            q = qkv[at(i), :HS]

            def tile(j, dq):
                k = qkv[at(j), HS : 2 * HS]
                v = qkv[at(j), 2 * HS :]
                p = probs[i, :, at(j)]
                ds = (p.astype(F32) * (nt(do, v) - delta)).astype(BF16)
                dkv[at(j), :HS] += tn(ds, q)
                dkv[at(j), HS:] += tn(p, do)
                return dq + nn(ds, k), ds.astype(F32)

            def far_tile(j, dq):
                dq, ds = tile(j, dq)
                far[...] += jnp.sum(ds, axis=0, keepdims=True)
                return dq

            def sub_tile(j, dq):
                dq, ds = tile(j, dq)
                sub[...] += ds
                return dq

            dq = lax.fori_loop(0, i - 1, far_tile, jnp.zeros((BLOCK, HS), F32))
            dq = lax.fori_loop(jnp.maximum(i - 1, 0), i, sub_tile, dq)
            dq, ds = tile(i, dq)
            diag[...] += ds
            dq = dq * HS ** (-0.5)
            parts = jnp.concatenate([dq, dkv[at(i), :]], axis=1).astype(BF16)
            dw[...] += tn(normed[at(i), :], parts)
            dqkv[pl.ds(i * per, per)] = parts.reshape(per, PT, 3 * HS)
            for u in range(per):
                t = i * per + u

                @pl.when(t != s)
                def _():
                    send_dq(t).start()

                @pl.when(t == s)
                def _():
                    dq_in[hd] = dqkv[t]

            return carry

        lax.fori_loop(0, z.nq, row_block, 0)

        ii = lax.broadcasted_iota(jnp.int32, (BLOCK, BLOCK), 0)
        jj = lax.broadcasted_iota(jnp.int32, (BLOCK, BLOCK), 1)
        lane = lax.broadcasted_iota(jnp.int32, (1, HS), 1)
        sums = jnp.zeros((1, HS), F32)
        half = BUCKETS // 2
        bounds = (0,) + LIMITS + (1 << 30,)
        tile_d, tile_s = diag[...], sub[...]

        def total(values):
            return jnp.sum(jnp.sum(values, axis=0, keepdims=True), axis=1, keepdims=True)

        for n in range(half):
            lo, hi = bounds[n], bounds[n + 1]
            dist = ii - jj
            part = total(
                jnp.where((dist >= lo) & (dist < hi), tile_d, 0.0)
                + jnp.where((dist + BLOCK >= lo) & (dist + BLOCK < hi), tile_s, 0.0)
            )
            if n == half - 1:
                part = part + jnp.sum(far[...], axis=1, keepdims=True)
            sums = sums + jnp.where(lane == n, part, 0.0)
            if n > 0:
                part = total(jnp.where((-dist >= lo) & (-dist < hi), tile_d, 0.0))
                sums = sums + jnp.where(lane == half + n, part, 0.0)
        wide = jnp.concatenate([dw[...], jnp.broadcast_to(sums, (D, HS))], axis=1)
        split_rows(dw3, wide, R)

        def start_dw(k, carry):
            send_dw(k).start()
            return carry

        lax.fori_loop(1, nv, start_dw, 0)
        dw_in[d * HEAD_COUNT + hd] = dw3[me]

    wfull[...] = flatten_rows(w3[...]).astype(BF16)
    gain = jnp.transpose(flatten_rows(misc3[...]))[E : E + 1, :]
    for n in range(HEAD_COUNT):

        @pl.when(jnp.logical_not(active & (hd == n)))
        def _():
            remote(
                dq_in.at[n], dq_in.at[n], dq_s.at[0], dq_r.at[n], (d, n // z.hb, n % z.hb)
            ).wait_recv()

        part = dq_in[n]
        for m in range(3):
            grad_cat[:, m * D + n * HS : m * D + (n + 1) * HS] = part[:, m * HS : (m + 1) * HS]
    grad_normed = nt(grad_cat[...], wfull[...])
    x = x_ref[...].astype(F32)
    inverse = lax.rsqrt(jnp.mean(x * x, axis=-1, keepdims=True) + EPSILON)
    scaled = grad_normed * gain
    mean = jnp.mean(scaled * x, axis=-1, keepdims=True)
    grad_in = inverse * scaled - x * (inverse * inverse * inverse) * mean
    gtok_ref[...] = (gmid_ref[...] + grad_in).astype(BF16)

    def got_rs(k, carry):
        t, device = any_peer(k)
        remote(rs_in.at[t], rs_in.at[t], rs_s.at[0], rs_r.at[t], device).wait_recv()
        return carry

    lax.fori_loop(1, nv, got_rs, 0)
    acc = lax.fori_loop(
        0, nv, lambda t, a: a + rs_in[t].astype(F32), jnp.zeros((R, D + LANES), F32)
    )
    go_ref[...] = acc[:, :D]
    router_ref[...] = acc[:, D : D + E]
    gain2_ref[...] = acc[:, D + E : D + E + 1]

    for dd in range(nd):
        for n in range(HEAD_COUNT):

            @pl.when(jnp.logical_not(active & (hd == n) & (d == dd)))
            def _():
                slot = dd * HEAD_COUNT + n
                remote(
                    dw_in.at[slot], dw_in.at[slot], dw_s.at[0], dw_r.at[slot],
                    (dd, n // z.hb, n % z.hb),
                ).wait_recv()

    lane = lax.broadcasted_iota(jnp.int32, (1, BUCKETS), 1)
    slot_lane = lax.broadcasted_iota(jnp.int32, (1, z.RL), 1)
    own_table = jnp.zeros((1, z.RL), F32)
    first = jnp.zeros((R, 1), F32)
    w_own = w_ref[...].astype(F32)
    for n in range(HEAD_COUNT):
        part = dw_in[n].astype(F32)
        for dd in range(1, nd):
            part = part + dw_in[dd * HEAD_COUNT + n].astype(F32)
        for m, out in enumerate((gq_ref, gk_ref, gv_ref)):
            cols = part[:, m * HS : (m + 1) * HS]
            out[:, n * HS : (n + 1) * HS] = cols
            first = first + jnp.sum(
                cols * w_own[:, m * D + n * HS : m * D + (n + 1) * HS], axis=-1, keepdims=True
            )
        line = part[0:1, 3 * HS : 3 * HS + BUCKETS]
        for k in range(z.RL):
            hit = lane + n * BUCKETS == me * z.RL + k
            value = jnp.sum(jnp.where(hit, line, 0.0), axis=1, keepdims=True)
            own_table = own_table + jnp.where(slot_lane == k, value, 0.0)
    gain1_ref[...] = first / w_own[:, 4 * D + E : 4 * D + E + 1]
    table_ref[...] = own_table

    def sent_rs(k, carry):
        send_rs(k).wait_send()
        return carry

    lax.fori_loop(1, nv, sent_rs, 0)
    for n in range(HEAD_COUNT):

        @pl.when(jnp.logical_not(active & (hd == n)))
        def _():
            send_do(n).wait_send()

    @pl.when(active)
    def _():
        def sent_dq(k, carry):
            send_dq(lax.rem(s + k, ns)).wait_send()
            return carry

        lax.fori_loop(1, ns, sent_dq, 0)

        def sent_dw(k, carry):
            send_dw(k).wait_send()
            return carry

        lax.fori_loop(1, nv, sent_dw, 0)


def attention_backward(z, gatt, dwo, normed, qkv, probs, att, wg, w_own, x, gmid):
    D, R, PT, S, HS, E = z.D, z.R, z.PT, z.S, HEAD_SIZE, z.E
    dma = pltpu.SemaphoreType.DMA
    vmem = pl.BlockSpec(memory_space=pltpu.VMEM)
    hbm = pl.BlockSpec(memory_space=pl.ANY)
    return pl.pallas_call(
        functools.partial(backward_kernel, z),
        out_shape=(
            jax.ShapeDtypeStruct((PT, D), BF16),
            jax.ShapeDtypeStruct((R, 1), F32),
            jax.ShapeDtypeStruct((R, D), F32),
            jax.ShapeDtypeStruct((R, D), F32),
            jax.ShapeDtypeStruct((R, D), F32),
            jax.ShapeDtypeStruct((R, D), F32),
            jax.ShapeDtypeStruct((1, z.RL), F32),
            jax.ShapeDtypeStruct((R, 1), F32),
            jax.ShapeDtypeStruct((R, E), F32),
        ),
        in_specs=[vmem, vmem, hbm, hbm, hbm, hbm, hbm, vmem, vmem, vmem],
        out_specs=(vmem,) * 9,
        scratch_shapes=[
            pltpu.VMEM((z.ndev, R, 3 * D), BF16),
            pltpu.VMEM((D, 3 * D), BF16),
            pltpu.VMEM((z.ndev, R, LANES), BF16),
            pltpu.VMEM((S, D), BF16),
            pltpu.VMEM((S, 3 * HS), BF16),
            pltpu.VMEM((z.nq, BLOCK, S), BF16),
            pltpu.VMEM((S, HS), BF16),
            pltpu.VMEM((z.ns, PT, HS), BF16),
            pltpu.VMEM((PT, 3 * D), BF16),
            pltpu.VMEM((S, 2 * HS), F32),
            pltpu.VMEM((z.ns, PT, 3 * HS), BF16),
            pltpu.VMEM((D, 3 * HS), F32),
            pltpu.VMEM((z.ndev, R, 4 * HS), BF16),
            pltpu.VMEM((BLOCK, BLOCK), F32),
            pltpu.VMEM((BLOCK, BLOCK), F32),
            pltpu.VMEM((1, BLOCK), F32),
            pltpu.VMEM((HEAD_COUNT, PT, 3 * HS), BF16),
            pltpu.VMEM((z.n_dp * HEAD_COUNT, R, 4 * HS), BF16),
            pltpu.VMEM((z.ndev, R, D + LANES), BF16),
            dma((6,)),
            dma((HEAD_COUNT,)),
            dma((z.ns,)),
            dma((z.ns,)),
            dma((HEAD_COUNT,)),
            dma((z.ndev,)),
            dma((z.n_dp * HEAD_COUNT,)),
            dma((z.ndev,)),
            dma((z.ndev,)),
        ],
        compiler_params=pltpu.CompilerParams(
            collective_id=2, has_side_effects=True, vmem_limit_bytes=58 * 1024 * 1024
        ),
        name="attention_backward",
    )(
        gatt, dwo, normed, qkv, probs, att, wg, w_own, x, gmid
    )


def expert_kernel(z, slots_ref, win_ref, wout_ref, gin_ref, gout_ref, rows_in, rows_t, grad_out):
    @pl.when(pl.program_id(0) == 0)
    def _():
        for n in range(z.n_head):
            slots = slots_ref[n].astype(F32)
            at = slice(n * z.NG * z.cap8, (n + 1) * z.NG * z.cap8)
            rows = slots[:, : z.cap8].reshape(z.NG * z.cap8, z.D)
            rows_in[at, :] = rows.astype(BF16)
            grad_out[at, :] = slots[:, z.cap8 :].reshape(z.NG * z.cap8, z.D).astype(BF16)
        rows_t[...] = jnp.transpose(rows_in[...])

    w1 = win_ref[0]
    w2 = wout_ref[0]
    pre = nn(rows_in[...], w1)
    phi, bell = normal_parts(pre)
    hidden = (pre * phi).astype(BF16)
    gh = nt(grad_out[...], w2).astype(BF16).astype(F32)
    gp = (gh * (phi + pre * bell * INV_ROOT_TWO_PI)).astype(BF16)
    gin_ref[0] = nn(rows_t[...], gp)
    gout_ref[0] = tn(hidden, grad_out[...])


def expert_weights(z, slots, w_in, w_out):
    chunk = 512
    total = z.n_head * z.NG * z.cap8
    in_chunk = pl.BlockSpec((1, z.D, chunk), lambda i: (0, 0, i))
    out_chunk = pl.BlockSpec((1, chunk, z.D), lambda i: (0, i, 0))
    return pl.pallas_call(
        functools.partial(expert_kernel, z),
        grid=(z.FF // chunk,),
        out_shape=(
            jax.ShapeDtypeStruct((1, z.D, z.FF), F32),
            jax.ShapeDtypeStruct((1, z.FF, z.D), F32),
        ),
        in_specs=[pl.BlockSpec(memory_space=pltpu.VMEM), in_chunk, out_chunk],
        out_specs=(in_chunk, out_chunk),
        scratch_shapes=[
            pltpu.VMEM((total, z.D), BF16),
            pltpu.VMEM((z.D, total), BF16),
            pltpu.VMEM((total, z.D), BF16),
        ],
        compiler_params=pltpu.CompilerParams(
            dimension_semantics=("arbitrary",), vmem_limit_bytes=48 * 1024 * 1024
        ),
        name="expert_weight_grads",
    )(slots, w_in, w_out)


def local(
    sizes,
    tokens,
    order,
    expert_ids,
    norm1_gain,
    w_query,
    w_key,
    w_value,
    w_attn_out,
    rel_table,
    norm2_gain,
    w_router,
    w_in,
    w_out,
    cotangent,
):
    R, D = w_query.shape
    E = w_router.shape[1]
    z = Sizes(*sizes, R, D, E, w_in.shape[2], tokens.shape[1])
    rel = jnp.pad(rel_table, (0, R - rel_table.shape[0]))
    misc = jnp.concatenate(
        [w_router, norm1_gain[:, None], norm2_gain[:, None], rel[:, None]], axis=1
    )
    misc = jnp.pad(misc, ((0, 0), (0, LANES - misc.shape[1])))
    w_own = jnp.concatenate([w_query, w_key, w_value, w_attn_out, misc], axis=1)
    row = np.arange(D)
    entries = np.where(row % R < z.RL, row // R * z.RL + row % R, -1).astype(np.int32)[None, :]
    ids = expert_ids.reshape(-1, z.PT)
    x = tokens.reshape(z.PT, D)
    cot = cotangent.reshape(z.PT, D)

    xg, wg = gather(z, x, w_own)
    normed, qkv, probs, att = attention_forward(z, jnp.asarray(entries), xg, wg)
    layer, gmid, gatt, dwo, slots = middle_part(z, att, x, wg, order, ids, w_in, w_out, cot)
    gtok, gain1, gq, gk, gv, go, table, gain2, router = attention_backward(
        z, gatt, dwo, normed, qkv, probs, att, wg, w_own, x, gmid
    )
    g_in, g_out = expert_weights(z, slots, w_in, w_out)
    return (
        layer.reshape(tokens.shape),
        gtok.reshape(tokens.shape),
        gain1.reshape(R),
        gq,
        gk,
        gv,
        go,
        table.reshape(z.RL),
        gain2.reshape(R),
        router,
        g_in,
        g_out,
    )


def solution(mesh):
    everywhere = ("dp", "blk", "head")
    rows, table = P(everywhere), P(everywhere, None)
    tokens = P("dp", ("blk", "head"), None)
    expert = P(("dp", "blk"), None, None)
    in_specs = (
        tokens,
        P("dp", ("blk", "head")),
        P(),
        rows,
        table,
        table,
        table,
        table,
        rows,
        rows,
        table,
        expert,
        expert,
        tokens,
    )
    out_specs = (
        tokens, tokens, rows, table, table, table, table, rows, rows, table, expert, expert
    )
    sizes = (mesh.shape["dp"], mesh.shape["blk"], mesh.shape["head"])
    return jax.shard_map(
        functools.partial(local, sizes),
        mesh=mesh,
        in_specs=in_specs,
        out_specs=out_specs,
        check_vma=False,
    )
```

```python
import functools
import itertools

import jax
import jax.numpy as jnp
import numpy as np
from jax import lax
from jax.experimental import pallas as pl
from jax.experimental.pallas import tpu as pltpu
from jax.sharding import PartitionSpec as P

HEAD_COUNT = 12
HEAD_SIZE = 64
BUCKETS = 32
BLOCK = 256
EPSILON = 1e-06
AUX_WEIGHT = 1.0
LIMITS = (1, 2, 3, 4, 5, 6, 7, 8, 12, 16, 23, 32, 46, 64, 91)
INV_ROOT_TWO = 0.7071067811865476
INV_ROOT_TWO_PI = 0.3989422804014327
LANES = 128
MESH = pl.DeviceIdType.MESH
F32 = jnp.float32
BF16 = jnp.bfloat16


class Sizes:
    def __init__(self, n_dp, n_blk, n_head, rows, width, experts, hidden, piece):
        self.n_dp, self.n_blk, self.n_head = n_dp, n_blk, n_head
        self.ndev = n_dp * n_blk * n_head
        self.ns = n_blk * n_head
        self.R, self.D, self.E, self.FF, self.PT = rows, width, experts, hidden, piece
        self.S = piece * self.ns
        self.nq = self.S // BLOCK
        self.hb = HEAD_COUNT // n_blk
        self.cap = (5 * piece + 4 * experts - 1) // (4 * experts)
        self.cap8 = (self.cap + 7) // 8 * 8
        self.NG = n_dp * n_blk
        self.RL = HEAD_COUNT * BUCKETS // self.ndev
        assert self.hb <= n_head and self.hb * n_blk == HEAD_COUNT
        assert experts == self.NG and n_head == 4


def nt(a, b):
    return lax.dot_general(a, b, (((1,), (1,)), ((), ())), preferred_element_type=F32)


def tn(a, b):
    return lax.dot_general(a, b, (((0,), (0,)), ((), ())), preferred_element_type=F32)


def nn(a, b):
    return jnp.dot(a, b, preferred_element_type=F32)


def place():
    return lax.axis_index("dp"), lax.axis_index("blk"), lax.axis_index("head")


def signal(device):
    pl.semaphore_signal(
        pltpu.get_barrier_semaphore(), inc=1, device_id=device, device_id_type=MESH
    )


def await_barrier(count):
    pl.semaphore_wait(pltpu.get_barrier_semaphore(), count)


def remote(src, dst, send, recv, device):
    return pltpu.make_async_remote_copy(
        src_ref=src, dst_ref=dst, send_sem=send, recv_sem=recv, device_id=device, device_id_type=MESH
    )


def flatten_rows(blocks):
    count, rows, lanes = blocks.shape
    wide = blocks.astype(F32)
    if rows % 8 == 0:
        return wide.reshape(count * rows, lanes)
    return jnp.concatenate([wide[i] for i in range(count)], axis=0)


def split_rows(dst_ref, values, rows):
    count = values.shape[0] // rows
    if rows % 8 == 0:
        dst_ref[...] = values.reshape(count, rows, values.shape[1]).astype(dst_ref.dtype)
    else:
        for i in range(count):
            dst_ref[i] = values[i * rows : (i + 1) * rows].astype(dst_ref.dtype)


def normal_parts(v):
    bell = jnp.exp(-0.5 * v * v)
    t = 1.0 / (1.0 + (0.3275911 * INV_ROOT_TWO) * jnp.abs(v))
    poly = t * (
        0.254829592
        + t * (-0.284496736 + t * (1.421413741 + t * (-1.453152027 + t * 1.061405429)))
    )
    tail = 0.5 * poly * bell
    return jnp.where(v >= 0, 1.0 - tail, tail), bell


def bias_tile(table, shift):
    j = lax.broadcasted_iota(jnp.int32, (BLOCK, BLOCK), 0)
    i = lax.broadcasted_iota(jnp.int32, (BLOCK, BLOCK), 1)
    dist = j - i + shift
    mag = jnp.abs(dist)
    half = BUCKETS // 2
    out = jnp.broadcast_to(table[0:1, 0:1], (BLOCK, BLOCK))
    for n, limit in enumerate(LIMITS):
        low = table[n + 1 : n + 2, 0:1]
        if shift == 0:
            high = table[half + n + 1 : half + n + 2, 0:1]
            out = jnp.where(mag >= limit, jnp.where(dist > 0, high, low), out)
        else:
            out = jnp.where(mag >= limit, low, out)
    return out


class Spread:
    def __init__(self, z, src, dst, send, recv, y_first, lanes):
        self.z, self.src, self.dst, self.send, self.recv = z, src, dst, send, recv
        self.lanes = lanes
        d, b, h = place()
        self.at = (d, b, h)
        nb, nh, nd = z.n_blk, z.n_head, z.n_dp
        self.hy = lax.rem(h + 2, nh)
        self.hc = h + 1 - 2 * lax.rem(h, 2)
        self.hyc = lax.rem(self.hc + 2, nh)
        self.zto = [lax.rem(b + k, nb) for k in range(1, nb)]
        self.zfrom = [lax.rem(b + nb - k, nb) for k in range(1, nb)]
        dto = [lax.rem(d + k, nd) for k in range(1, nd)]
        dfrom = [lax.rem(d + nd - k, nd) for k in range(1, nd)]
        ys = ([(d, self.hy)], [(d, self.hy)])
        xs = ([(p, h) for p in dto], [(p, h) for p in dfrom])
        self.first, self.second = (ys, xs) if y_first else (xs, ys)
        if y_first:
            self.second_slots = [(p, hh) for p in dfrom for hh in (h, self.hy)]
        else:
            self.second_slots = [(p, self.hy) for p in [d] + dfrom]
        self.core_slots = [(p, hh) for p in [d] + dfrom for hh in (self.hc, self.hyc)]
        self.copies = []

    def slot(self, dd, bb, hh):
        return (dd * self.z.n_blk + bb) * self.z.n_head + hh

    def put(self, own, slot, device):
        src = self.src if own else self.dst.at[slot, :, self.lanes]
        c = remote(
            src, self.dst.at[slot, :, self.lanes], self.send.at[len(self.copies)],
            self.recv.at[slot], device,
        )
        self.copies.append(c)
        c.start()

    def got(self, slot):
        ref = self.dst.at[slot, :, self.lanes]
        d, b, h = self.at
        remote(ref, ref, self.send.at[0], self.recv.at[slot], (d, b, self.hc)).wait_recv()

    def steps(self):
        d, b, h = self.at

        def begin():
            mine = self.slot(d, b, h)
            for p in self.zto:
                self.put(True, mine, (d, p, h))
            for dd, hh in self.first[0] + self.second[0] + [(d, self.hc)]:
                self.put(True, mine, (dd, b, hh))

        def blk_arrival(f):
            slot = self.slot(d, f, h)
            self.got(slot)
            for dd, hh in self.first[0] + self.second[0] + [(d, self.hc)]:
                self.put(False, slot, (dd, b, hh))

        def first_arrival(p, f):
            slot = self.slot(p[0], f, p[1])
            self.got(slot)
            for dd, hh in self.second[0] + [(d, self.hc)]:
                self.put(False, slot, (dd, b, hh))

        def second_arrival(p, f):
            slot = self.slot(p[0], f, p[1])
            self.got(slot)
            self.put(False, slot, (d, b, self.hc))

        out = [begin]
        for f in self.zfrom:
            out.append(functools.partial(blk_arrival, f))
        for p in self.first[1]:
            for f in [b] + self.zfrom:
                out.append(functools.partial(first_arrival, p, f))
        for p in self.second_slots:
            for f in [b] + self.zfrom:
                out.append(functools.partial(second_arrival, p, f))
        return out

    def finish(self):
        d, b, h = self.at
        for p in self.core_slots:
            for f in [b] + self.zfrom:
                self.got(self.slot(p[0], f, p[1]))
        for c in self.copies:
            c.wait_send()


def spread_copies(z, y_first):
    nb, nd = z.n_blk, z.n_dp
    peers = 1 + nd - 1 + 1
    first = 1 if y_first else nd - 1
    second = peers - 1 - first
    second_slots = 2 * (nd - 1) if y_first else nd
    return nb - 1 + peers + (nb - 1) * peers + first * nb * (second + 1) + second_slots * nb


def forward_kernel(
    z, entry_ref, x_ref, wq_ref, wk_ref, wv_ref, wo_ref, router_ref, rows_ref, rel_ref,
    wg_ref, normed_ref, qkv_ref, p_ref, attl_ref, att_out,
    w_own, slices, slices_in, xg, wh, bias_d, bias_s, normed, qkv, v_t, s_scr, p_scr, attl, att_scr,
    xs, xr, ss, sr, was, war, wbs, wbr, ats, atr, loc,
):
    d, b, h = place()
    nb, nh, nd, ns, nv = z.n_blk, z.n_head, z.n_dp, z.ns, z.ndev
    D, R, E, PT, HS = z.D, z.R, z.E, z.PT, HEAD_SIZE
    s = b * nh + h
    me = d * ns + s
    hd = b * z.hb + jnp.minimum(h, z.hb - 1)
    active = h < z.hb
    hy = lax.rem(h + 2, nh)
    hc = h + 1 - 2 * lax.rem(h, 2)
    hyc = lax.rem(hc + 2, nh)

    def any_peer(k):
        t = lax.rem(me + k, nv)
        return t, (t // ns, lax.rem(t // nh, nb), lax.rem(t, nh))

    def greet(k, carry):
        signal(any_peer(k)[1])
        return carry

    lax.fori_loop(1, nv, greet, 0)

    eye = lax.broadcasted_iota(jnp.int32, (R, R), 0) == lax.broadcasted_iota(jnp.int32, (R, R), 1)
    row_of = lax.broadcasted_iota(jnp.int32, (LANES, R), 0)
    gains = jnp.where(
        row_of == E, rows_ref[0:1, :], jnp.where(row_of == E + 1, rows_ref[1:2, :], 0.0)
    )
    gains = jnp.where(row_of == E + 2, rel_ref[...], gains)
    misc = nt(eye.astype(BF16), gains.astype(BF16))
    lane = lax.broadcasted_iota(jnp.int32, (R, LANES), 1)
    w_own[:, 4 * D :] = misc.astype(BF16)
    w_own[:, 4 * D : 4 * D + E] = router_ref[...]
    for m, ref in enumerate((wq_ref, wk_ref, wv_ref, wo_ref)):
        w_own[:, m * D : (m + 1) * D] = ref[...]
    for n in range(HEAD_COUNT):
        at = slice(n * HS, (n + 1) * HS)
        slices[n] = jnp.concatenate(
            [wq_ref[:, at], wk_ref[:, at], wv_ref[:, at], misc[:, E : E + HS].astype(BF16)], axis=1
        )
    save_w = pltpu.make_async_copy(w_own, wg_ref.at[me], loc.at[0])
    save_w.start()
    await_barrier(nv - 1)

    def send_slice(dd, n):
        k = dd * HEAD_COUNT + n
        return remote(
            slices.at[n], slices_in.at[me], ss.at[k], sr.at[me], (dd, n // z.hb, n % z.hb)
        )

    def is_me(dd, n):
        return active & (hd == n) & (d == dd)

    def for_slices(action):
        for dd in range(nd):
            for n in range(HEAD_COUNT):
                pl.when(jnp.logical_not(is_me(dd, n)))(functools.partial(action, dd, n))

    copies = []

    def xslot(bb, hh):
        return bb * nh + hh

    def put(src, slot, device):
        c = remote(src, xg.at[slot], xs.at[len(copies)], xr.at[slot], device)
        copies.append(c)
        c.start()

    def got(slot):
        remote(xg.at[slot], xg.at[slot], xs.at[0], xr.at[slot], (d, b, hc)).wait_recv()

    zto = [lax.rem(b + k, nb) for k in range(1, nb)]
    zfrom = [lax.rem(b + nb - k, nb) for k in range(1, nb)]
    for p in zto:
        put(x_ref, s, (d, p, h))
    put(x_ref, s, (d, b, hy))
    put(x_ref, s, (d, b, hc))
    for_slices(lambda dd, n: send_slice(dd, n).start())
    xg[s] = x_ref[...]

    @pl.when(active)
    def _():
        slices_in[me] = slices[hd]

    for f in zfrom:
        slot = xslot(f, h)
        got(slot)
        put(xg.at[slot], slot, (d, b, hy))
        put(xg.at[slot], slot, (d, b, hc))
    for f in [b] + zfrom:
        slot = xslot(f, hy)
        got(slot)
        put(xg.at[slot], slot, (d, b, hc))

    cut = 2 * D
    part_a = Spread(
        z, w_own.at[:, pl.ds(0, cut)], wg_ref, was, war, True, pl.ds(0, cut)
    )
    part_b = Spread(
        z, w_own.at[:, pl.ds(cut, 2 * D + LANES)], wg_ref, wbs, wbr, False,
        pl.ds(cut, 2 * D + LANES),
    )
    spread_steps = [
        step
        for pair in itertools.zip_longest(part_b.steps(), part_a.steps())
        for step in pair
        if step is not None
    ]

    def run_steps(count):
        for _ in range(min(count, len(spread_steps))):
            spread_steps.pop(0)()

    run_steps(2)

    @pl.when(active)
    def _():
        def got_slice(k, carry):
            t, device = any_peer(k)
            remote(slices_in.at[t], slices_in.at[t], ss.at[0], sr.at[t], device).wait_recv()
            return carry

        lax.fori_loop(1, nv, got_slice, 0)

    for f in [b] + zfrom:
        got(xslot(f, hc))
        got(xslot(f, hyc))

    rows = flatten_rows(slices_in[...])
    wh[:, : 2 * HS] = rows[:, : 2 * HS].astype(BF16)
    wh[:, :HS] = (rows[:, :HS] * HS ** (-0.5)).astype(BF16)
    wh[:, 2 * HS :] = rows[:, 2 * HS : 3 * HS].astype(BF16)
    gain = jnp.transpose(rows[:, LANES:])[HS : HS + 1, :]
    wanted = hd * BUCKETS + lax.broadcasted_iota(jnp.int32, (BUCKETS, D), 0)
    pick = (entry_ref[...] == wanted).astype(BF16)
    table = nn(pick, rows[:, LANES:].astype(BF16))[:, HS + 2 : HS + 3]
    bias_d[...] = bias_tile(table, 0)
    bias_s[...] = bias_tile(table, -BLOCK)
    far = table[BUCKETS // 2 - 1 : BUCKETS // 2, 0:1]
    per = BLOCK // PT
    half = BLOCK // 2

    def send_att(t):
        return remote(
            att_scr.at[t], att_out.at[hd], ats.at[t], atr.at[hd], (d, t // nh, t % nh)
        )

    for i in range(z.nq):
        run_steps(5)

        @pl.when(active)
        def _():
            here = slice(i * BLOCK, (i + 1) * BLOCK)
            x = xg[i * per : (i + 1) * per].reshape(BLOCK, D).astype(F32)
            inverse = lax.rsqrt(jnp.mean(x * x, axis=-1, keepdims=True) + EPSILON)
            low = (x * inverse * gain).astype(BF16)
            normed[here, :] = low
            mixed = nn(low, wh[...])
            qkv[here, :] = mixed.astype(BF16)
            v_t[:, here] = jnp.transpose(mixed[:, 2 * HS :]).astype(BF16)
            q = qkv[here, :HS]
            top = jnp.full((8, BLOCK), -1e30, F32)
            for j in range(i + 1):
                for u in range(2):
                    at = slice(j * BLOCK + u * half, j * BLOCK + (u + 1) * half)
                    part = slice(u * half, (u + 1) * half)
                    if j == i:
                        bias = bias_d[part, :]
                    elif j == i - 1:
                        bias = bias_s[part, :]
                    else:
                        bias = far
                    sc = nt(qkv[at, HS : 2 * HS], q) + bias
                    s_scr[at, :] = sc
                    top = jnp.maximum(top, jnp.max(sc.reshape(half // 8, 8, BLOCK), axis=0))
            top = jnp.max(top, axis=0, keepdims=True)
            total = jnp.zeros((8, BLOCK), F32)
            acc = jnp.zeros((HS, BLOCK), F32)
            for j in range(i + 1):
                for u in range(2):
                    at = slice(j * BLOCK + u * half, j * BLOCK + (u + 1) * half)
                    e = jnp.exp(s_scr[at, :] - top)
                    total = total + jnp.sum(e.reshape(half // 8, 8, BLOCK), axis=0)
                    p_scr[i, at, :] = e.astype(BF16)
                at = slice(j * BLOCK, (j + 1) * BLOCK)
                acc = acc + nn(v_t[:, at], p_scr[i, at, :])
            total = jnp.sum(total, axis=0, keepdims=True)
            both = jnp.concatenate([acc, jnp.broadcast_to(total, (HS, BLOCK))], axis=0)
            both = jnp.transpose(both)
            inv = 1.0 / both[:, HS:]
            att = (both[:, :HS] * inv).astype(BF16)
            attl[here, :] = jnp.concatenate([att.astype(F32), inv], axis=1)
            att_scr[i * per : (i + 1) * per] = att.reshape(per, PT, HS)
            to = slice(0, (i + 1) * BLOCK)
            pltpu.make_async_copy(p_scr.at[i, to], p_ref.at[i, to], loc.at[4 + i]).start()
            for u in range(per):
                t = i * per + u

                @pl.when(t != s)
                def _():
                    send_att(t).start()

                @pl.when(t == s)
                def _():
                    att_out[hd] = att_scr[t]

    @pl.when(active)
    def _():
        pltpu.make_async_copy(normed, normed_ref, loc.at[1]).start()
        pltpu.make_async_copy(qkv, qkv_ref, loc.at[2]).start()
        pltpu.make_async_copy(attl, attl_ref, loc.at[3]).start()

    run_steps(len(spread_steps))
    for n in range(HEAD_COUNT):

        @pl.when(jnp.logical_not(active & (hd == n)))
        def _():
            remote(
                att_out.at[n], att_out.at[n], ats.at[0], atr.at[n], (d, n // z.hb, n % z.hb)
            ).wait_recv()

    part_a.finish()
    part_b.finish()
    save_w.wait()
    for c in copies:
        c.wait_send()
    for_slices(lambda dd, n: send_slice(dd, n).wait_send())

    @pl.when(active)
    def _():
        pltpu.make_async_copy(normed, normed_ref, loc.at[1]).wait()
        pltpu.make_async_copy(qkv, qkv_ref, loc.at[2]).wait()
        pltpu.make_async_copy(attl, attl_ref, loc.at[3]).wait()
        for i in range(z.nq):
            to = slice(0, (i + 1) * BLOCK)
            pltpu.make_async_copy(p_scr.at[i, to], p_ref.at[i, to], loc.at[4 + i]).wait()
        for t in range(ns):

            @pl.when(t != s)
            def _():
                send_att(t).wait_send()


def attention_forward(z, entries, x, weights, router, rows, rel):
    D, S, HS, R, PT = z.D, z.S, HEAD_SIZE, z.R, z.PT
    nb = z.n_blk
    dma = pltpu.SemaphoreType.DMA
    vmem = pl.BlockSpec(memory_space=pltpu.VMEM)
    hbm = pl.BlockSpec(memory_space=pl.ANY)
    wide = 4 * D + LANES
    return pl.pallas_call(
        functools.partial(forward_kernel, z),
        out_shape=(
            jax.ShapeDtypeStruct((z.ndev, R, wide), BF16),
            jax.ShapeDtypeStruct((S, D), BF16),
            jax.ShapeDtypeStruct((S, 3 * HS), BF16),
            jax.ShapeDtypeStruct((z.nq, S, BLOCK), BF16),
            jax.ShapeDtypeStruct((S, 2 * HS), F32),
            jax.ShapeDtypeStruct((HEAD_COUNT, PT, HS), BF16),
        ),
        in_specs=[vmem] * 9,
        out_specs=(hbm, hbm, hbm, hbm, hbm, vmem),
        scratch_shapes=[
            pltpu.VMEM((R, wide), BF16),
            pltpu.VMEM((HEAD_COUNT, R, 4 * HS), BF16),
            pltpu.VMEM((z.ndev, R, 4 * HS), BF16),
            pltpu.VMEM((z.ns, PT, D), BF16),
            pltpu.VMEM((D, 3 * HS), BF16),
            pltpu.VMEM((BLOCK, BLOCK), F32),
            pltpu.VMEM((BLOCK, BLOCK), F32),
            pltpu.VMEM((S, D), BF16),
            pltpu.VMEM((S, 3 * HS), BF16),
            pltpu.VMEM((HS, S), BF16),
            pltpu.VMEM((S, BLOCK), F32),
            pltpu.VMEM((z.nq, S, BLOCK), BF16),
            pltpu.VMEM((S, 2 * HS), F32),
            pltpu.VMEM((z.ns, PT, HS), BF16),
            dma((nb - 1 + 2 + 2 * (nb - 1) + nb,)),
            dma((z.ns,)),
            dma((z.n_dp * HEAD_COUNT,)),
            dma((z.ndev,)),
            dma((spread_copies(z, True),)),
            dma((z.ndev,)),
            dma((spread_copies(z, False),)),
            dma((z.ndev,)),
            dma((z.ns,)),
            dma((HEAD_COUNT,)),
            dma((4 + z.nq,)),
        ],
        compiler_params=pltpu.CompilerParams(
            collective_id=0, has_side_effects=True, vmem_limit_bytes=48 * 1024 * 1024
        ),
        name="attention_forward",
    )(entries, x, *weights, router, rows, rel)


def middle_kernel(
    z, att_in, x_ref, w_ref, order_ref, ids_ref, win_ref, wout_ref, cot_ref,
    layer_ref, gmid_ref, gatt_ref, dwo_ref, all_ref,
    win, wout, wo3, misc3, disp, exp_in, ret, back, route, att_cat, pre_scr, out_acc, gg_acc,
    loc, dis_s, dis_r, ret_s, ret_r, all_s, all_r,
):
    d, b, h = place()
    nb, nh, nd, ns = z.n_blk, z.n_head, z.n_dp, z.ns
    D, E, PT, NG, C8 = z.D, z.E, z.PT, z.NG, z.cap8
    me = d * ns + b * nh + h
    g = d * nb + b
    hy = lax.rem(h + 2, nh)
    hc = h + 1 - 2 * lax.rem(h, 2)
    hyc = lax.rem(hc + 2, nh)

    def exp_peer(k):
        e = lax.rem(g + k, NG)
        return e, (e // nb, lax.rem(e, nb), h)

    def exp_from(k):
        e = lax.rem(g + NG - k, NG)
        return e, (e // nb, lax.rem(e, nb), h)

    for k in range(1, NG):
        signal(exp_peer(k)[1])
    signal((d, b, hy))
    signal((d, b, hc))
    local = [
        pltpu.make_async_copy(w_ref.at[:, :, pl.ds(3 * D, D)], wo3, loc.at[0]),
        pltpu.make_async_copy(w_ref.at[:, :, pl.ds(4 * D, LANES)], misc3, loc.at[1]),
        pltpu.make_async_copy(win_ref.at[0], win, loc.at[2]),
        pltpu.make_async_copy(wout_ref.at[0], wout, loc.at[3]),
    ]
    for c in local:
        c.start()

    ids_row = ids_ref[pl.ds(me, 1), :]
    order_row = order_ref[...]
    ids_col = jnp.transpose(jnp.broadcast_to(ids_row, (PT, PT)))
    order_col = jnp.transpose(jnp.broadcast_to(order_row, (PT, PT)))
    earlier = (order_col < order_row) & (ids_col == ids_row)
    rank = jnp.sum(earlier.astype(jnp.int32), axis=0, keepdims=True)
    slot = lax.broadcasted_iota(jnp.int32, (C8, PT), 0)
    base = (rank == slot) & (slot < z.cap)
    lane = lax.broadcasted_iota(jnp.int32, (1, LANES), 1)
    share = jnp.zeros((1, LANES), F32)
    ids_all = ids_ref[...]
    for e in range(E):
        route[e * C8 : (e + 1) * C8, :] = (base & (ids_row == e)).astype(F32)
        count = jnp.sum((ids_all == e).astype(F32), axis=1, keepdims=True)
        count = jnp.sum(count, axis=0, keepdims=True)
        share = share + jnp.where(lane == e, count, 0.0)
    share = share * (AUX_WEIGHT * E / (ids_all.shape[0] * ids_all.shape[1]))
    chosen = ids_col[:, :1] == lane
    picks = route[...].astype(BF16)

    x = x_ref[...].astype(F32)
    cot = cot_ref[...].astype(F32)
    for n in range(HEAD_COUNT):
        att_cat[:, n * HEAD_SIZE : (n + 1) * HEAD_SIZE] = att_in[n]
    att = att_cat[...]
    local[0].wait()
    local[1].wait()
    wo = flatten_rows(wo3[...]).astype(BF16)
    misc = flatten_rows(misc3[...])
    router = misc.astype(BF16)
    gain = jnp.transpose(misc)[E + 1 : E + 2, :]
    middle = x + nn(att, wo)
    inverse = lax.rsqrt(jnp.mean(middle * middle, axis=-1, keepdims=True) + EPSILON)
    routed = (middle * inverse * gain).astype(BF16)
    await_barrier(NG - 1 + 2)

    def send_disp(part, k):
        e, device = exp_peer(k)
        at = part * NG
        return remote(
            disp.at[part, e], exp_in.at[part, g], dis_s.at[at + k], dis_r.at[at + g], device
        )

    def dispatch(part, values):
        disp[part] = nn(picks, values).reshape(E, C8, D).astype(BF16)
        for k in range(1, NG):
            send_disp(part, k).start()
        exp_in[part, g] = disp[part, g]

    def arrivals(part):
        for k in range(1, NG):
            e, device = exp_from(k)
            ref = exp_in.at[part, e]
            remote(ref, ref, dis_s.at[0], dis_r.at[part * NG + e], device).wait_recv()

    def send_ret(part, k):
        e, device = exp_peer(k)
        at = part * NG
        return remote(
            ret.at[part, e], back.at[part, g], ret_s.at[at + k], ret_r.at[at + g], device
        )

    def give_back(part, values):
        ret[part] = values.reshape(NG, C8, D).astype(BF16)
        for k in range(1, NG):
            send_ret(part, k).start()
        back[part, g] = ret[part, g]

    def returns(part):
        for k in range(1, NG):
            e, device = exp_from(k)
            ref = back.at[part, e]
            remote(ref, ref, ret_s.at[0], ret_r.at[part * NG + e], device).wait_recv()
        rows = back[part].astype(F32).reshape(E * C8, D).astype(BF16)
        return tn(picks, rows)

    def share_slots(part):
        at = 3 * part
        out = [
            remote(
                exp_in.at[part], all_ref.at[part, h], all_s.at[at], all_r.at[part * nh + h],
                (d, b, hy),
            ),
            remote(
                exp_in.at[part], all_ref.at[part, h], all_s.at[at + 1], all_r.at[part * nh + h],
                (d, b, hc),
            ),
            pltpu.make_async_copy(exp_in.at[part], all_ref.at[part, h], loc.at[4 + part]),
        ]
        for c in out:
            c.start()
        return out

    def got_slots(part, hh):
        ref = all_ref.at[part, hh]
        remote(ref, ref, all_s.at[0], all_r.at[part * nh + hh], (d, b, hc)).wait_recv()

    def pass_slots(part):
        got_slots(part, hy)
        ref = all_ref.at[part, hy]
        c = remote(ref, ref, all_s.at[3 * part + 2], all_r.at[part * nh + hy], (d, b, hc))
        c.start()
        return c

    dispatch(0, routed)
    logits = jnp.where(lane < E, nn(routed, router), -1e30)
    exps = jnp.exp(logits - jnp.max(logits, axis=-1, keepdims=True))
    probs = exps / jnp.sum(exps, axis=-1, keepdims=True)
    gate = jnp.sum(jnp.where(chosen, probs, 0.0), axis=-1, keepdims=True)
    dispatch(1, (gate * cot).astype(BF16))
    local[2].wait()
    local[3].wait()
    chunk = D
    chunks = z.FF // chunk

    arrivals(0)
    rows_in = exp_in[0].astype(F32).reshape(NG * C8, D).astype(BF16)
    out_acc[...] = jnp.zeros_like(out_acc)

    def forward_step(c, carry):
        at = pl.ds(pl.multiple_of(c * chunk, chunk), chunk)
        pre = nn(rows_in, win[:, at])
        pre_scr[:, at] = pre
        phi, _ = normal_parts(pre)
        out_acc[...] += nn((pre * phi).astype(BF16), wout[at, :])
        return carry

    lax.fori_loop(0, chunks, forward_step, 0)
    give_back(0, out_acc[...])

    arrivals(1)
    grad_out = exp_in[1].astype(F32).reshape(NG * C8, D).astype(BF16)
    gg_acc[...] = jnp.zeros_like(gg_acc)

    def backward_step(c, carry):
        at = pl.ds(pl.multiple_of(c * chunk, chunk), chunk)
        pre = pre_scr[:, at]
        phi, bell = normal_parts(pre)
        gh = nt(grad_out, wout[at, :]).astype(BF16).astype(F32)
        gp = (gh * (phi + pre * bell * INV_ROOT_TWO_PI)).astype(BF16)
        gg_acc[...] += nt(gp, win[:, at])
        return carry

    lax.fori_loop(0, chunks, backward_step, 0)
    give_back(1, gg_acc[...])
    moved = share_slots(0) + share_slots(1)

    expert_rows = returns(0)
    layer_ref[...] = (middle + gate * expert_rows).astype(BF16)
    grad_gate = jnp.sum(cot * expert_rows, axis=-1, keepdims=True)
    grad_probs = jnp.where(chosen, grad_gate, 0.0) + share
    inner = jnp.sum(probs * grad_probs, axis=-1, keepdims=True)
    grad_logits = (probs * (grad_probs - inner)).astype(BF16)
    from_router = nt(grad_logits, router)
    grad_routed = returns(1) + from_router
    scaled = grad_routed * gain
    mean = jnp.mean(scaled * middle, axis=-1, keepdims=True)
    gmid = cot + inverse * scaled - middle * (inverse * inverse * inverse) * mean
    gmid_ref[...] = gmid
    low_mid = gmid.astype(BF16)
    gatt = nt(low_mid, wo).astype(BF16)
    for n in range(HEAD_COUNT):
        gatt_ref[n] = gatt[:, n * HEAD_SIZE : (n + 1) * HEAD_SIZE]
    term = grad_routed * middle * inverse
    high = term.astype(BF16)
    rest = (term - high.astype(F32)).astype(BF16)
    ones = jnp.broadcast_to((lane == E).astype(BF16), (PT, LANES))
    small = tn(routed, grad_logits) + tn(high, ones) + tn(rest, ones)
    terms = jnp.concatenate([tn(att, low_mid), small], axis=1)
    for t in range(z.ndev):
        dwo_ref[t % nh, t // nh] = terms[t * z.R : (t + 1) * z.R].astype(BF16)

    passed = [pass_slots(0), pass_slots(1)]
    for part in range(2):
        for hh in (hc, hyc):
            got_slots(part, hh)
    for n, c in enumerate(moved):
        if n % 3 == 2:
            c.wait()
        else:
            c.wait_send()
    for c in passed:
        c.wait_send()
    for part in range(2):
        for k in range(1, NG):
            send_disp(part, k).wait_send()
            send_ret(part, k).wait_send()


def middle_part(z, att, x, wg, order, ids, w_in, w_out, cot):
    D, PT, NG, E, C8 = z.D, z.PT, z.NG, z.E, z.cap8
    dma = pltpu.SemaphoreType.DMA
    vmem = pl.BlockSpec(memory_space=pltpu.VMEM)
    hbm = pl.BlockSpec(memory_space=pl.ANY)
    return pl.pallas_call(
        functools.partial(middle_kernel, z),
        out_shape=(
            jax.ShapeDtypeStruct((PT, D), BF16),
            jax.ShapeDtypeStruct((PT, D), F32),
            jax.ShapeDtypeStruct((HEAD_COUNT, PT, HEAD_SIZE), BF16),
            jax.ShapeDtypeStruct((z.n_head, NG, z.R, D + LANES), BF16),
            jax.ShapeDtypeStruct((2, z.n_head, NG, C8, D), BF16),
        ),
        in_specs=[vmem, vmem, hbm, vmem, vmem, hbm, hbm, vmem],
        out_specs=(vmem, vmem, vmem, vmem, hbm),
        scratch_shapes=[
            pltpu.VMEM((D, z.FF), BF16),
            pltpu.VMEM((z.FF, D), BF16),
            pltpu.VMEM((z.ndev, z.R, D), BF16),
            pltpu.VMEM((z.ndev, z.R, LANES), BF16),
            pltpu.VMEM((2, E, C8, D), BF16),
            pltpu.VMEM((2, NG, C8, D), BF16),
            pltpu.VMEM((2, NG, C8, D), BF16),
            pltpu.VMEM((2, E, C8, D), BF16),
            pltpu.VMEM((E * C8, PT), F32),
            pltpu.VMEM((PT, D), BF16),
            pltpu.VMEM((NG * C8, z.FF), F32),
            pltpu.VMEM((NG * C8, D), F32),
            pltpu.VMEM((NG * C8, D), F32),
            dma((6,)),
            dma((2 * NG,)),
            dma((2 * NG,)),
            dma((2 * NG,)),
            dma((2 * NG,)),
            dma((6,)),
            dma((2 * z.n_head,)),
        ],
        compiler_params=pltpu.CompilerParams(
            collective_id=1, has_side_effects=True, vmem_limit_bytes=56 * 1024 * 1024
        ),
        name="experts_and_norms",
    )(att, x, wg, order, ids, w_in, w_out, cot)


def backward_kernel(
    z, gatt_ref, dwo_ref, normed_ref, qkv_ref, p_ref, attl_ref, wg_ref,
    wq_ref, wk_ref, wv_ref, x_ref, gmid_ref,
    gtok_ref, gain1_ref, gq_ref, gk_ref, gv_ref, go_ref, table_ref, gain2_ref, router_ref,
    w3, wfull, misc3, normed, qkv, probs, attl, k_t, do_in, grad_cat, dkv, dqkv, dw, dw3,
    diag, sub, far, dq_in, dw_in, first_in, second_src, second_in,
    loc, do_s, do_r, dq_s, dq_r, dw_s, dw_r, r1_s, r1_r, r2_s, r2_r,
):
    d, b, h = place()
    nb, nh, nd, ns, nv, NG = z.n_blk, z.n_head, z.n_dp, z.ns, z.ndev, z.NG
    D, R, PT, HS, E = z.D, z.R, z.PT, HEAD_SIZE, z.E
    s = b * nh + h
    me = d * ns + s
    g = d * nb + b
    hd = b * z.hb + jnp.minimum(h, z.hb - 1)
    active = h < z.hb

    def any_peer(k):
        t = lax.rem(me + k, nv)
        return t, (t // ns, lax.rem(t // nh, nb), lax.rem(t, nh))

    def greet(k, carry):
        signal(any_peer(k)[1])
        return carry

    lax.fori_loop(1, nv, greet, 0)
    local = [
        pltpu.make_async_copy(qkv_ref, qkv, loc.at[0]),
        pltpu.make_async_copy(attl_ref, attl, loc.at[1]),
        pltpu.make_async_copy(p_ref, probs, loc.at[2]),
        pltpu.make_async_copy(normed_ref, normed, loc.at[3]),
        pltpu.make_async_copy(wg_ref.at[:, :, pl.ds(0, 3 * D)], w3, loc.at[4]),
        pltpu.make_async_copy(wg_ref.at[:, :, pl.ds(4 * D, LANES)], misc3, loc.at[5]),
    ]
    for c in local:
        c.start()
    await_barrier(nv - 1)

    def send_do(n):
        hb, hh = n // z.hb, n % z.hb
        return remote(gatt_ref.at[n], do_in.at[s], do_s.at[n], do_r.at[s], (d, hb, hh))

    for n in range(HEAD_COUNT):
        mine = active & (hd == n)

        @pl.when(jnp.logical_not(mine))
        def _():
            send_do(n).start()

        @pl.when(mine)
        def _():
            do_in[s] = gatt_ref[n]

    def send_first(k):
        hh = lax.rem(h + k, nh)
        return remote(dwo_ref.at[hh], first_in.at[h], r1_s.at[k], r1_r.at[h], (d, b, hh))

    def group_peer(k):
        e = lax.rem(g + k, NG)
        return e, (e // nb, lax.rem(e, nb), h)

    def send_second(k):
        e, device = group_peer(k)
        return remote(second_src.at[e], second_in.at[g], r2_s.at[k], r2_r.at[g], device)

    for k in range(1, nh):
        send_first(k).start()
    first_in[h] = dwo_ref[h]

    def second_stage():
        for k in range(1, nh):
            hh = lax.rem(h + k, nh)
            remote(
                first_in.at[hh], first_in.at[hh], r1_s.at[0], r1_r.at[hh], (d, b, hh)
            ).wait_recv()

        def group_sum(e, carry):
            acc = first_in[0, e].astype(F32)
            for hh in range(1, nh):
                acc = acc + first_in[hh, e].astype(F32)
            second_src[e] = acc.astype(BF16)
            return carry

        lax.fori_loop(0, NG, group_sum, 0)
        for k in range(1, NG):
            send_second(k).start()
        second_in[g] = second_src[g]

    for c in local:
        c.wait()
    wfull[...] = flatten_rows(w3[...]).astype(BF16)
    gain = jnp.transpose(flatten_rows(misc3[...]))[E : E + 1, :]

    def send_dq(t):
        return remote(dqkv.at[t], dq_in.at[hd], dq_s.at[t], dq_r.at[hd], (d, t // nh, t % nh))

    def send_dw(k):
        t, device = any_peer(k)
        slot = d * HEAD_COUNT + hd
        return remote(dw3.at[t], dw_in.at[slot], dw_s.at[k], dw_r.at[slot], device)

    per = BLOCK // PT
    part_rows = BLOCK // 2

    @pl.when(active)
    def _():
        for j in range(z.nq):
            at = slice(j * BLOCK, (j + 1) * BLOCK)
            k_t[:, at] = jnp.transpose(qkv[at, HS : 2 * HS].astype(F32)).astype(BF16)
        dkv[...] = jnp.zeros_like(dkv)
        dw[...] = jnp.zeros_like(dw)
        diag[...] = jnp.zeros_like(diag)
        sub[...] = jnp.zeros_like(sub)
        far[...] = jnp.zeros_like(far)

        def got_do(k, carry):
            t = lax.rem(s + k, ns)
            remote(
                do_in.at[t], do_in.at[t], do_s.at[0], do_r.at[t],
                (d, t // nh, lax.rem(t, nh)),
            ).wait_recv()
            return carry

        lax.fori_loop(1, ns, got_do, 0)

    for i in reversed(range(z.nq)):
        if i == z.nq // 2:
            second_stage()

        @pl.when(active)
        def _():
            here = slice(i * BLOCK, (i + 1) * BLOCK)
            att = attl[here, :HS]
            inv = attl[here, HS:]
            do = do_in[i * per : (i + 1) * per].reshape(BLOCK, HS).astype(F32)
            do = (do * inv).astype(BF16)
            prod = do.astype(F32) * att
            high = prod.astype(BF16)
            rest = (prod - high.astype(F32)).astype(BF16)
            ones = jnp.ones((8, HS), BF16)
            delta = (nt(ones, high) + nt(ones, rest))[0:1, :]
            q = qkv[here, :HS]
            dq_t = jnp.zeros((HS, BLOCK), F32)
            for j in range(i + 1):
                for u in range(2):
                    at = slice(j * BLOCK + u * part_rows, j * BLOCK + (u + 1) * part_rows)
                    p = probs[i, at, :]
                    ds = p.astype(F32) * (nt(qkv[at, 2 * HS :], do) - delta)
                    low = ds.astype(BF16)
                    both = jnp.concatenate([nn(low, q), nn(p, do)], axis=1)
                    if j == i:
                        dkv[at, :] = both if i == z.nq - 1 else dkv[at, :] + both
                        diag[u * part_rows : (u + 1) * part_rows, :] += low.astype(F32)
                    else:
                        dkv[at, :] += both
                        if j == i - 1:
                            sub[u * part_rows : (u + 1) * part_rows, :] += low.astype(F32)
                        else:
                            far[...] += jnp.sum(
                                low.astype(F32).reshape(part_rows // 8, 8, BLOCK), axis=0
                            )
                    dq_t = dq_t + nn(k_t[:, at], low)
            dq = jnp.transpose(dq_t) * HS ** (-0.5)
            parts = jnp.concatenate([dq, dkv[here, :]], axis=1).astype(BF16)
            dw[...] += tn(normed[here, :], parts)
            dqkv[i * per : (i + 1) * per] = parts.reshape(per, PT, 3 * HS)
            for u in range(per):
                t = i * per + u

                @pl.when(t != s)
                def _():
                    send_dq(t).start()

                @pl.when(t == s)
                def _():
                    dq_in[hd] = dqkv[t]

    @pl.when(active)
    def _():
        jj = lax.broadcasted_iota(jnp.int32, (BLOCK, BLOCK), 0)
        ii = lax.broadcasted_iota(jnp.int32, (BLOCK, BLOCK), 1)
        lane = lax.broadcasted_iota(jnp.int32, (1, HS), 1)
        sums = jnp.zeros((1, HS), F32)
        half = BUCKETS // 2
        bounds = (0,) + LIMITS + (1 << 30,)
        tile_d, tile_s = diag[...], sub[...]

        def total(values):
            return jnp.sum(jnp.sum(values, axis=0, keepdims=True), axis=1, keepdims=True)

        for n in range(half):
            lo, hi = bounds[n], bounds[n + 1]
            dist = ii - jj
            part = total(
                jnp.where((dist >= lo) & (dist < hi), tile_d, 0.0)
                + jnp.where((dist + BLOCK >= lo) & (dist + BLOCK < hi), tile_s, 0.0)
            )
            if n == half - 1:
                part = part + total(far[...])
            sums = sums + jnp.where(lane == n, part, 0.0)
            if n > 0:
                part = total(jnp.where((-dist >= lo) & (-dist < hi), tile_d, 0.0))
                sums = sums + jnp.where(lane == half + n, part, 0.0)
        wide = jnp.concatenate([dw[...], jnp.broadcast_to(sums, (D, HS))], axis=1)
        split_rows(dw3, wide, R)

        def start_dw(k, carry):
            send_dw(k).start()
            return carry

        lax.fori_loop(1, nv, start_dw, 0)
        dw_in[d * HEAD_COUNT + hd] = dw3[me]

    for k in range(1, NG):
        e, device = group_peer(k)
        remote(second_in.at[e], second_in.at[e], r2_s.at[0], r2_r.at[e], device).wait_recv()
    acc = lax.fori_loop(
        0, NG, lambda t, a: a + second_in[t].astype(F32), jnp.zeros((R, D + LANES), F32)
    )
    go_ref[...] = acc[:, :D]
    router_ref[...] = acc[:, D : D + E]
    gain2_ref[...] = acc[:, D + E : D + E + 1]

    for n in range(HEAD_COUNT):

        @pl.when(jnp.logical_not(active & (hd == n)))
        def _():
            remote(
                dq_in.at[n], dq_in.at[n], dq_s.at[0], dq_r.at[n], (d, n // z.hb, n % z.hb)
            ).wait_recv()

        part = dq_in[n]
        for m in range(3):
            grad_cat[:, m * D + n * HS : m * D + (n + 1) * HS] = part[:, m * HS : (m + 1) * HS]
    grad_normed = nt(grad_cat[...], wfull[...])
    x = x_ref[...].astype(F32)
    inverse = lax.rsqrt(jnp.mean(x * x, axis=-1, keepdims=True) + EPSILON)
    scaled = grad_normed * gain
    mean = jnp.mean(scaled * x, axis=-1, keepdims=True)
    grad_in = inverse * scaled - x * (inverse * inverse * inverse) * mean
    gtok_ref[...] = (gmid_ref[...] + grad_in).astype(BF16)

    for dd in range(nd):
        for n in range(HEAD_COUNT):

            @pl.when(jnp.logical_not(active & (hd == n) & (d == dd)))
            def _():
                slot = dd * HEAD_COUNT + n
                remote(
                    dw_in.at[slot], dw_in.at[slot], dw_s.at[0], dw_r.at[slot],
                    (dd, n // z.hb, n % z.hb),
                ).wait_recv()

    lane = lax.broadcasted_iota(jnp.int32, (1, BUCKETS), 1)
    slot_lane = lax.broadcasted_iota(jnp.int32, (1, z.RL), 1)
    own_table = jnp.zeros((1, z.RL), F32)
    first = jnp.zeros((R, 1), F32)
    for n in range(HEAD_COUNT):
        part = dw_in[n].astype(F32)
        for dd in range(1, nd):
            part = part + dw_in[dd * HEAD_COUNT + n].astype(F32)
        at = slice(n * HS, (n + 1) * HS)
        for m, (out, w) in enumerate(((gq_ref, wq_ref), (gk_ref, wk_ref), (gv_ref, wv_ref))):
            cols = part[:, m * HS : (m + 1) * HS]
            out[:, at] = cols
            first = first + jnp.sum(cols * w[:, at].astype(F32), axis=-1, keepdims=True)
        line = part[0:1, 3 * HS : 3 * HS + BUCKETS]
        for k in range(z.RL):
            hit = lane + n * BUCKETS == me * z.RL + k
            value = jnp.sum(jnp.where(hit, line, 0.0), axis=1, keepdims=True)
            own_table = own_table + jnp.where(slot_lane == k, value, 0.0)
    own_gain = misc3[pl.ds(me, 1)].astype(F32).reshape(R, LANES)[:, E : E + 1]
    gain1_ref[...] = first / own_gain
    table_ref[...] = own_table

    for k in range(1, nh):
        send_first(k).wait_send()
    for k in range(1, NG):
        send_second(k).wait_send()
    for n in range(HEAD_COUNT):

        @pl.when(jnp.logical_not(active & (hd == n)))
        def _():
            send_do(n).wait_send()

    @pl.when(active)
    def _():
        for t in range(ns):

            @pl.when(t != s)
            def _():
                send_dq(t).wait_send()

        def sent_dw(k, carry):
            send_dw(k).wait_send()
            return carry

        lax.fori_loop(1, nv, sent_dw, 0)


def attention_backward(z, gatt, dwo, normed, qkv, probs, attl, wg, weights, x, gmid):
    D, R, PT, S, HS, E, NG = z.D, z.R, z.PT, z.S, HEAD_SIZE, z.E, z.NG
    dma = pltpu.SemaphoreType.DMA
    vmem = pl.BlockSpec(memory_space=pltpu.VMEM)
    hbm = pl.BlockSpec(memory_space=pl.ANY)
    return pl.pallas_call(
        functools.partial(backward_kernel, z),
        out_shape=(
            jax.ShapeDtypeStruct((PT, D), BF16),
            jax.ShapeDtypeStruct((R, 1), F32),
            jax.ShapeDtypeStruct((R, D), F32),
            jax.ShapeDtypeStruct((R, D), F32),
            jax.ShapeDtypeStruct((R, D), F32),
            jax.ShapeDtypeStruct((R, D), F32),
            jax.ShapeDtypeStruct((1, z.RL), F32),
            jax.ShapeDtypeStruct((R, 1), F32),
            jax.ShapeDtypeStruct((R, E), F32),
        ),
        in_specs=[vmem, vmem, hbm, hbm, hbm, hbm, hbm, vmem, vmem, vmem, vmem, vmem],
        out_specs=(vmem,) * 9,
        scratch_shapes=[
            pltpu.VMEM((z.ndev, R, 3 * D), BF16),
            pltpu.VMEM((D, 3 * D), BF16),
            pltpu.VMEM((z.ndev, R, LANES), BF16),
            pltpu.VMEM((S, D), BF16),
            pltpu.VMEM((S, 3 * HS), BF16),
            pltpu.VMEM((z.nq, S, BLOCK), BF16),
            pltpu.VMEM((S, 2 * HS), F32),
            pltpu.VMEM((HS, S), BF16),
            pltpu.VMEM((z.ns, PT, HS), BF16),
            pltpu.VMEM((PT, 3 * D), BF16),
            pltpu.VMEM((S, 2 * HS), F32),
            pltpu.VMEM((z.ns, PT, 3 * HS), BF16),
            pltpu.VMEM((D, 3 * HS), F32),
            pltpu.VMEM((z.ndev, R, 4 * HS), BF16),
            pltpu.VMEM((BLOCK, BLOCK), F32),
            pltpu.VMEM((BLOCK, BLOCK), F32),
            pltpu.VMEM((8, BLOCK), F32),
            pltpu.VMEM((HEAD_COUNT, PT, 3 * HS), BF16),
            pltpu.VMEM((z.n_dp * HEAD_COUNT, R, 4 * HS), BF16),
            pltpu.VMEM((z.n_head, NG, R, D + LANES), BF16),
            pltpu.VMEM((NG, R, D + LANES), BF16),
            pltpu.VMEM((NG, R, D + LANES), BF16),
            dma((6,)),
            dma((HEAD_COUNT,)),
            dma((z.ns,)),
            dma((z.ns,)),
            dma((HEAD_COUNT,)),
            dma((z.ndev,)),
            dma((z.n_dp * HEAD_COUNT,)),
            dma((z.n_head,)),
            dma((z.n_head,)),
            dma((NG,)),
            dma((NG,)),
        ],
        compiler_params=pltpu.CompilerParams(
            collective_id=2, has_side_effects=True, vmem_limit_bytes=58 * 1024 * 1024
        ),
        name="attention_backward",
    )(gatt, dwo, normed, qkv, probs, attl, wg, *weights, x, gmid)


def expert_kernel(z, slots_ref, win_ref, wout_ref, gin_ref, gout_ref, rows_in, rows_t, grad_out):
    @pl.when(pl.program_id(0) == 0)
    def _():
        for n in range(z.n_head):
            count = z.NG * z.cap8
            at = slice(n * count, (n + 1) * count)
            rows_in[at, :] = slots_ref[0, n].astype(F32).reshape(count, z.D).astype(BF16)
            grad_out[at, :] = slots_ref[1, n].astype(F32).reshape(count, z.D).astype(BF16)
        rows_t[...] = jnp.transpose(rows_in[...])

    w1 = win_ref[0]
    w2 = wout_ref[0]
    pre = nn(rows_in[...], w1)
    phi, bell = normal_parts(pre)
    hidden = (pre * phi).astype(BF16)
    gh = nt(grad_out[...], w2).astype(BF16).astype(F32)
    gp = (gh * (phi + pre * bell * INV_ROOT_TWO_PI)).astype(BF16)
    gin_ref[0] = nn(rows_t[...], gp)
    gout_ref[0] = tn(hidden, grad_out[...])


def expert_weights(z, slots, w_in, w_out):
    chunk = 512
    total = z.n_head * z.NG * z.cap8
    in_chunk = pl.BlockSpec((1, z.D, chunk), lambda i: (0, 0, i))
    out_chunk = pl.BlockSpec((1, chunk, z.D), lambda i: (0, i, 0))
    return pl.pallas_call(
        functools.partial(expert_kernel, z),
        grid=(z.FF // chunk,),
        out_shape=(
            jax.ShapeDtypeStruct((1, z.D, z.FF), F32),
            jax.ShapeDtypeStruct((1, z.FF, z.D), F32),
        ),
        in_specs=[pl.BlockSpec(memory_space=pltpu.VMEM), in_chunk, out_chunk],
        out_specs=(in_chunk, out_chunk),
        scratch_shapes=[
            pltpu.VMEM((total, z.D), BF16),
            pltpu.VMEM((z.D, total), BF16),
            pltpu.VMEM((total, z.D), BF16),
        ],
        compiler_params=pltpu.CompilerParams(
            dimension_semantics=("arbitrary",), vmem_limit_bytes=48 * 1024 * 1024
        ),
        name="expert_weight_grads",
    )(slots, w_in, w_out)


def local(
    sizes,
    tokens,
    order,
    expert_ids,
    norm1_gain,
    w_query,
    w_key,
    w_value,
    w_attn_out,
    rel_table,
    norm2_gain,
    w_router,
    w_in,
    w_out,
    cotangent,
):
    R, D = w_query.shape
    E = w_router.shape[1]
    z = Sizes(*sizes, R, D, E, w_in.shape[2], tokens.shape[1])
    rel = jnp.pad(rel_table, (0, R - rel_table.shape[0]))[None, :]
    gains = jnp.stack([norm1_gain, norm2_gain])
    row = np.arange(D)
    entries = np.where(row % R < z.RL, row // R * z.RL + row % R, -1).astype(np.int32)[None, :]
    ids = expert_ids.reshape(-1, z.PT)
    x = tokens.reshape(z.PT, D)
    cot = cotangent.reshape(z.PT, D)

    wg, normed, qkv, probs, attl, att = attention_forward(
        z,
        jnp.asarray(entries),
        x,
        (w_query, w_key, w_value, w_attn_out),
        w_router,
        gains.astype(F32),
        rel.astype(F32),
    )
    layer, gmid, gatt, dwo, slots = middle_part(z, att, x, wg, order, ids, w_in, w_out, cot)
    gtok, gain1, gq, gk, gv, go, table, gain2, router = attention_backward(
        z, gatt, dwo, normed, qkv, probs, attl, wg, (w_query, w_key, w_value), x, gmid
    )
    g_in, g_out = expert_weights(z, slots, w_in, w_out)
    return (
        layer.reshape(tokens.shape),
        gtok.reshape(tokens.shape),
        gain1.reshape(R),
        gq,
        gk,
        gv,
        go,
        table.reshape(z.RL),
        gain2.reshape(R),
        router,
        g_in,
        g_out,
    )


def solution(mesh):
    everywhere = ("dp", "blk", "head")
    rows, table = P(everywhere), P(everywhere, None)
    tokens = P("dp", ("blk", "head"), None)
    expert = P(("dp", "blk"), None, None)
    in_specs = (
        tokens,
        P("dp", ("blk", "head")),
        P(),
        rows,
        table,
        table,
        table,
        table,
        rows,
        rows,
        table,
        expert,
        expert,
        tokens,
    )
    out_specs = (
        tokens, tokens, rows, table, table, table, table, rows, rows, table, expert, expert
    )
    sizes = (mesh.shape["dp"], mesh.shape["blk"], mesh.shape["head"])
    return jax.shard_map(
        functools.partial(local, sizes),
        mesh=mesh,
        in_specs=in_specs,
        out_specs=out_specs,
        check_vma=False,
    )
```

```python
import functools
import itertools

import jax
import jax.numpy as jnp
import numpy as np
from jax import lax
from jax.experimental import pallas as pl
from jax.experimental.pallas import tpu as pltpu
from jax.sharding import PartitionSpec as P

HEAD_COUNT = 12
HEAD_SIZE = 64
BUCKETS = 32
BLOCK = 256
EPSILON = 1e-06
AUX_WEIGHT = 1.0
LIMITS = (1, 2, 3, 4, 5, 6, 7, 8, 12, 16, 23, 32, 46, 64, 91)
INV_ROOT_TWO = 0.7071067811865476
INV_ROOT_TWO_PI = 0.3989422804014327
LANES = 128
MESH = pl.DeviceIdType.MESH
F32 = jnp.float32
BF16 = jnp.bfloat16


def both_halves(values):
    n = values.shape[0] // 2
    return jnp.concatenate([values[:n], values[n:]], axis=1)


def line_order(b, nb):
    out = [(b, b >= 0)]
    for k in range(1, nb):
        out.append((b - k, b >= k))
        out.append((b + k, b + k < nb))
    return out


class Sends:
    def __init__(self, sems):
        self.sems, self.made = sems, []

    def put(self, src, dst, recv, device, cond=None):
        c = remote(src, dst, self.sems.at[len(self.made)], recv, device)
        self.made.append((c, cond))
        self.each(c.start, cond)

    def each(self, action, cond):
        if cond is None:
            action()
        else:
            pl.when(cond)(action)

    def finish(self):
        for c, cond in self.made:
            self.each(c.wait_send, cond)


class Sizes:
    def __init__(self, n_dp, n_blk, n_head, rows, width, experts, hidden, piece):
        self.n_dp, self.n_blk, self.n_head = n_dp, n_blk, n_head
        self.ndev = n_dp * n_blk * n_head
        self.ns = n_blk * n_head
        self.R, self.D, self.E, self.FF, self.PT = rows, width, experts, hidden, piece
        self.S = piece * self.ns
        self.nq = self.S // BLOCK
        self.hb = HEAD_COUNT // n_blk
        self.cap = (5 * piece + 4 * experts - 1) // (4 * experts)
        self.cap8 = (self.cap + 7) // 8 * 8
        self.NG = n_dp * n_blk
        self.RL = HEAD_COUNT * BUCKETS // self.ndev
        assert self.hb <= n_head and self.hb * n_blk == HEAD_COUNT
        assert experts == self.NG and n_head == 4


def nt(a, b):
    return lax.dot_general(a, b, (((1,), (1,)), ((), ())), preferred_element_type=F32)


def tn(a, b):
    return lax.dot_general(a, b, (((0,), (0,)), ((), ())), preferred_element_type=F32)


def nn(a, b):
    return jnp.dot(a, b, preferred_element_type=F32)


def place():
    return lax.axis_index("dp"), lax.axis_index("blk"), lax.axis_index("head")


def signal(device):
    pl.semaphore_signal(
        pltpu.get_barrier_semaphore(), inc=1, device_id=device, device_id_type=MESH
    )


def await_barrier(count):
    pl.semaphore_wait(pltpu.get_barrier_semaphore(), count)


def remote(src, dst, send, recv, device):
    return pltpu.make_async_remote_copy(
        src_ref=src, dst_ref=dst, send_sem=send, recv_sem=recv, device_id=device, device_id_type=MESH
    )


def flatten_rows(blocks):
    count, rows, lanes = blocks.shape
    wide = blocks.astype(F32)
    if rows % 8 == 0:
        return wide.reshape(count * rows, lanes)
    return jnp.concatenate([wide[i] for i in range(count)], axis=0)


def split_rows(dst_ref, values, rows):
    count = values.shape[0] // rows
    if rows % 8 == 0:
        dst_ref[...] = values.reshape(count, rows, values.shape[1]).astype(dst_ref.dtype)
    else:
        for i in range(count):
            dst_ref[i] = values[i * rows : (i + 1) * rows].astype(dst_ref.dtype)


def normal_parts(v):
    bell = jnp.exp(-0.5 * v * v)
    t = 1.0 / (1.0 + (0.3275911 * INV_ROOT_TWO) * jnp.abs(v))
    poly = t * (
        0.254829592
        + t * (-0.284496736 + t * (1.421413741 + t * (-1.453152027 + t * 1.061405429)))
    )
    tail = 0.5 * poly * bell
    return jnp.where(v >= 0, 1.0 - tail, tail), bell


def bias_tile(table, shift):
    j = lax.broadcasted_iota(jnp.int32, (BLOCK, BLOCK), 0)
    i = lax.broadcasted_iota(jnp.int32, (BLOCK, BLOCK), 1)
    dist = j - i + shift
    mag = jnp.abs(dist)
    half = BUCKETS // 2
    out = jnp.broadcast_to(table[0:1, 0:1], (BLOCK, BLOCK))
    for n, limit in enumerate(LIMITS):
        low = table[n + 1 : n + 2, 0:1]
        if shift == 0:
            high = table[half + n + 1 : half + n + 2, 0:1]
            out = jnp.where(mag >= limit, jnp.where(dist > 0, high, low), out)
        else:
            out = jnp.where(mag >= limit, low, out)
    return out


class Spread:
    def __init__(self, z, src, dst, send, recv, y_first, lanes):
        self.z, self.src, self.dst, self.recv = z, src, dst, recv
        self.sends, self.lanes = Sends(send), lanes
        d, b, h = place()
        self.at = (d, b, h)
        nh, nd = z.n_head, z.n_dp
        self.hy = lax.rem(h + 2, nh)
        self.hc = h + 1 - 2 * lax.rem(h, 2)
        self.hyc = lax.rem(self.hc + 2, nh)
        dto = [lax.rem(d + k, nd) for k in range(1, nd)]
        dfrom = [lax.rem(d + nd - k, nd) for k in range(1, nd)]
        ys = ([(d, self.hy)], [(d, self.hy)])
        xs = ([(p, h) for p in dto], [(p, h) for p in dfrom])
        self.first, self.second = (ys, xs) if y_first else (xs, ys)
        if y_first:
            self.second_slots = [(p, hh) for p in dfrom for hh in (h, self.hy)]
        else:
            self.second_slots = [(p, self.hy) for p in [d] + dfrom]
        self.core_slots = [(p, hh) for p in [d] + dfrom for hh in (self.hc, self.hyc)]

    def slot(self, dd, bb, hh):
        return (dd * self.z.n_blk + bb) * self.z.n_head + hh

    def ref(self, slot):
        return self.dst.at[slot, :, self.lanes]

    def put(self, src, slot, device, cond=None):
        self.sends.put(src, self.ref(slot), self.recv.at[slot], device, cond)

    def got(self, slot):
        d, b, h = self.at
        ref = self.ref(slot)
        remote(ref, ref, self.sends.sems.at[0], self.recv.at[slot], (d, b, self.hc)).wait_recv()

    def steps(self):
        d, b, h = self.at
        nb = self.z.n_blk

        def begin():
            mine = self.slot(d, b, h)
            self.put(self.src, mine, (d, b + 1, h), b + 1 < nb)
            self.put(self.src, mine, (d, b - 1, h), b >= 1)
            for dd, hh in self.first[0] + self.second[0] + [(d, self.hc)]:
                self.put(self.src, mine, (dd, b, hh))

        def line_arrival(k):
            for f, cond, to, more in (
                (b - k, b >= k, b + 1, b + 1 < nb),
                (b + k, b + k < nb, b - 1, b >= 1),
            ):
                slot = self.slot(d, f, h)
                pl.when(cond)(functools.partial(self.got, slot))
                if k < nb - 1:
                    self.put(self.ref(slot), slot, (d, to, h), cond & more)
                for dd, hh in self.first[0] + self.second[0] + [(d, self.hc)]:
                    self.put(self.ref(slot), slot, (dd, b, hh), cond)

        def first_arrival(p, f, cond):
            slot = self.slot(p[0], f, p[1])
            pl.when(cond)(functools.partial(self.got, slot))
            for dd, hh in self.second[0] + [(d, self.hc)]:
                self.put(self.ref(slot), slot, (dd, b, hh), cond)

        def second_arrival(p, f, cond):
            slot = self.slot(p[0], f, p[1])
            pl.when(cond)(functools.partial(self.got, slot))
            self.put(self.ref(slot), slot, (d, b, self.hc), cond)

        out = [begin]
        for k in range(1, nb):
            out.append(functools.partial(line_arrival, k))
        for p in self.first[1]:
            for f, cond in line_order(b, nb):
                out.append(functools.partial(first_arrival, p, f, cond))
        for p in self.second_slots:
            for f, cond in line_order(b, nb):
                out.append(functools.partial(second_arrival, p, f, cond))
        return out

    def finish(self):
        d, b, h = self.at
        for p in self.core_slots:
            for f in range(self.z.n_blk):
                self.got(self.slot(p[0], f, p[1]))
        self.sends.finish()


def spread_copies(z, y_first):
    nb, nd = z.n_blk, z.n_dp
    peers = 1 + nd - 1 + 1
    first = 1 if y_first else nd - 1
    second = peers - 1 - first
    second_slots = 2 * (nd - 1) if y_first else nd
    line = 2 * nb - 1
    return 2 + peers + (nb - 1) * 2 * (peers + 1) + first * line * (second + 1) + second_slots * line


def forward_kernel(
    z, entry_ref, x_ref, wq_ref, wk_ref, wv_ref, wo_ref, router_ref, rows_ref, rel_ref,
    wg_ref, normed_ref, qkv_ref, p_ref, attl_ref, att_out,
    w_own, slices, slices_in, xg, wh, bias_d, bias_s, normed, qkv, v_t, s_scr, p_scr, attl, att_scr,
    xs, xr, ss, sd, sr, was, war, wbs, wbr, ats, atr, loc,
):
    d, b, h = place()
    nb, nh, nd, ns, nv = z.n_blk, z.n_head, z.n_dp, z.ns, z.ndev
    D, R, E, PT, HS = z.D, z.R, z.E, z.PT, HEAD_SIZE
    s = b * nh + h
    me = d * ns + s
    hd = b * z.hb + jnp.minimum(h, z.hb - 1)
    active = h < z.hb
    hy = lax.rem(h + 2, nh)
    hc = h + 1 - 2 * lax.rem(h, 2)
    hyc = lax.rem(hc + 2, nh)

    def any_peer(k):
        t = lax.rem(me + k, nv)
        return t, (t // ns, lax.rem(t // nh, nb), lax.rem(t, nh))

    def greet(k, carry):
        signal(any_peer(k)[1])
        return carry

    lax.fori_loop(1, nv, greet, 0)

    eye = lax.broadcasted_iota(jnp.int32, (R, R), 0) == lax.broadcasted_iota(jnp.int32, (R, R), 1)
    row_of = lax.broadcasted_iota(jnp.int32, (LANES, R), 0)
    gains = jnp.where(
        row_of == E, rows_ref[0:1, :], jnp.where(row_of == E + 1, rows_ref[1:2, :], 0.0)
    )
    gains = jnp.where(row_of == E + 2, rel_ref[...], gains)
    misc = nt(eye.astype(BF16), gains.astype(BF16))
    lane = lax.broadcasted_iota(jnp.int32, (R, LANES), 1)
    w_own[:, 4 * D :] = misc.astype(BF16)
    w_own[:, 4 * D : 4 * D + E] = router_ref[...]
    for m, ref in enumerate((wq_ref, wk_ref, wv_ref, wo_ref)):
        w_own[:, m * D : (m + 1) * D] = ref[...]
    for n in range(HEAD_COUNT):
        at = slice(n * HS, (n + 1) * HS)
        slices[n] = jnp.concatenate(
            [wq_ref[:, at], wk_ref[:, at], wv_ref[:, at], misc[:, E : E + HS].astype(BF16)], axis=1
        )
    save_w = pltpu.make_async_copy(w_own, wg_ref.at[me], loc.at[0])
    save_w.start()
    await_barrier(nv - 1)

    def mine(n):
        return active & (hd == n)

    to_heads = Sends(ss)
    over_dp = Sends(sd)
    for n in range(HEAD_COUNT):
        to_heads.put(
            slices.at[n], slices_in.at[me], sr.at[me], (d, n // z.hb, n % z.hb),
            jnp.logical_not(mine(n)),
        )

    tokens = Sends(xs)
    pieces = 2
    rows_of = PT // pieces

    def xref(slot, c):
        return xg.at[slot, pl.ds(c * rows_of, rows_of)]

    def put(src, slot, c, device, cond=None):
        tokens.put(src, xref(slot, c), xr.at[slot * pieces + c], device, cond)

    def got(slot, c):
        ref = xref(slot, c)
        remote(ref, ref, xs.at[0], xr.at[slot * pieces + c], (d, b, hc)).wait_recv()

    for c in range(pieces):
        own = x_ref.at[pl.ds(c * rows_of, rows_of)]
        put(own, s, c, (d, b + 1, h), b + 1 < nb)
        put(own, s, c, (d, b - 1, h), b >= 1)
        put(own, s, c, (d, b, hy))
        put(own, s, c, (d, b, hc))
    xg[s] = x_ref[...]

    @pl.when(active)
    def _():
        slices_in[me] = slices[hd]

    for k in range(1, nb):
        for c in range(pieces):
            for f, cond, to, more in (
                (b - k, b >= k, b + 1, b + 1 < nb),
                (b + k, b + k < nb, b - 1, b >= 1),
            ):
                slot = f * nh + h
                pl.when(cond)(functools.partial(got, slot, c))
                if k < nb - 1:
                    put(xref(slot, c), slot, c, (d, to, h), cond & more)
                put(xref(slot, c), slot, c, (d, b, hy), cond)
                put(xref(slot, c), slot, c, (d, b, hc), cond)
        if k == 1:
            for m in range(ns):
                t = lax.rem(s + m, ns)
                slot = d * ns + t
                ref = slices_in.at[slot]
                if m > 0:
                    source = (d, t // nh, lax.rem(t, nh))
                    c = remote(ref, ref, ss.at[0], sr.at[slot], source)
                    pl.when(active)(c.wait_recv)
                for kd in range(1, nd):
                    over_dp.put(ref, ref, sr.at[slot], (lax.rem(d + kd, nd), b, h), active)

    for f, cond in line_order(b, nb):
        for c in range(pieces):
            slot = f * nh + hy
            pl.when(cond)(functools.partial(got, slot, c))
            put(xref(slot, c), slot, c, (d, b, hc), cond)

    cut = 2 * D
    part_a = Spread(
        z, w_own.at[:, pl.ds(0, cut)], wg_ref, was, war, True, pl.ds(0, cut)
    )
    part_b = Spread(
        z, w_own.at[:, pl.ds(cut, 2 * D + LANES)], wg_ref, wbs, wbr, False,
        pl.ds(cut, 2 * D + LANES),
    )
    spread_steps = [
        step
        for pair in itertools.zip_longest(part_b.steps(), part_a.steps())
        for step in pair
        if step is not None
    ]

    def run_steps(count):
        for _ in range(min(count, len(spread_steps))):
            spread_steps.pop(0)()

    run_steps(2)

    @pl.when(active)
    def _():
        for kd in range(1, nd):
            dd = lax.rem(d + kd, nd)

            def got_slice(t, carry):
                ref = slices_in.at[dd * ns + t]
                remote(ref, ref, ss.at[0], sr.at[dd * ns + t], (dd, b, h)).wait_recv()
                return carry

            lax.fori_loop(0, ns, got_slice, 0)

    for f in range(nb):
        for c in range(pieces):
            got(f * nh + hc, c)
            got(f * nh + hyc, c)

    rows = flatten_rows(slices_in[...])
    wh[:, : 2 * HS] = rows[:, : 2 * HS].astype(BF16)
    wh[:, :HS] = (rows[:, :HS] * HS ** (-0.5)).astype(BF16)
    wh[:, 2 * HS :] = rows[:, 2 * HS : 3 * HS].astype(BF16)
    gain = jnp.transpose(rows[:, LANES:])[HS : HS + 1, :]
    wanted = hd * BUCKETS + lax.broadcasted_iota(jnp.int32, (BUCKETS, D), 0)
    pick = (entry_ref[...] == wanted).astype(BF16)
    table = nn(pick, rows[:, LANES:].astype(BF16))[:, HS + 2 : HS + 3]
    bias_d[...] = bias_tile(table, 0)
    bias_s[...] = bias_tile(table, -BLOCK)
    far = table[BUCKETS // 2 - 1 : BUCKETS // 2, 0:1]
    per = BLOCK // PT
    half = BLOCK // 2

    def send_att(t):
        return remote(
            att_scr.at[t], att_out.at[hd], ats.at[t], atr.at[hd], (d, t // nh, t % nh)
        )

    for i in range(z.nq):
        run_steps(5)

        @pl.when(active)
        def _():
            here = slice(i * BLOCK, (i + 1) * BLOCK)
            x = xg[i * per : (i + 1) * per].reshape(BLOCK, D).astype(F32)
            inverse = lax.rsqrt(jnp.mean(x * x, axis=-1, keepdims=True) + EPSILON)
            low = (x * inverse * gain).astype(BF16)
            normed[here, :] = low
            mixed = nn(low, wh[...])
            qkv[here, :] = mixed.astype(BF16)
            v_t[:, here] = jnp.transpose(mixed[:, 2 * HS :]).astype(BF16)
            q = qkv[here, :HS]
            top = jnp.full((8, BLOCK), -1e30, F32)
            for j in range(i + 1):
                for u in range(2):
                    at = slice(j * BLOCK + u * half, j * BLOCK + (u + 1) * half)
                    part = slice(u * half, (u + 1) * half)
                    if j == i:
                        bias = bias_d[part, :]
                    elif j == i - 1:
                        bias = bias_s[part, :]
                    else:
                        bias = far
                    sc = nt(qkv[at, HS : 2 * HS], q) + bias
                    s_scr[at, :] = sc
                    top = jnp.maximum(top, jnp.max(sc.reshape(half // 8, 8, BLOCK), axis=0))
            top = jnp.max(top, axis=0, keepdims=True)
            total = jnp.zeros((8, BLOCK), F32)
            acc = jnp.zeros((HS, BLOCK), F32)
            for j in range(i + 1):
                for u in range(2):
                    at = slice(j * BLOCK + u * half, j * BLOCK + (u + 1) * half)
                    e = jnp.exp(s_scr[at, :] - top)
                    total = total + jnp.sum(e.reshape(half // 8, 8, BLOCK), axis=0)
                    p_scr[i, at, :] = e.astype(BF16)
                at = slice(j * BLOCK, (j + 1) * BLOCK)
                acc = acc + nn(v_t[:, at], p_scr[i, at, :])
            total = jnp.sum(total, axis=0, keepdims=True)
            both = jnp.concatenate([acc, jnp.broadcast_to(total, (HS, BLOCK))], axis=0)
            both = jnp.transpose(both)
            inv = 1.0 / both[:, HS:]
            att = (both[:, :HS] * inv).astype(BF16)
            attl[here, :] = jnp.concatenate([att.astype(F32), inv], axis=1)
            for u in range(per):
                att_scr[i * per + u] = both_halves(att[u * PT : (u + 1) * PT])
            to = slice(0, (i + 1) * BLOCK)
            pltpu.make_async_copy(p_scr.at[i, to], p_ref.at[i, to], loc.at[4 + i]).start()
            for u in range(per):
                t = i * per + u

                @pl.when(t != s)
                def _():
                    send_att(t).start()

                @pl.when(t == s)
                def _():
                    att_out[hd] = att_scr[t]

    @pl.when(active)
    def _():
        pltpu.make_async_copy(normed, normed_ref, loc.at[1]).start()
        pltpu.make_async_copy(qkv, qkv_ref, loc.at[2]).start()
        pltpu.make_async_copy(attl, attl_ref, loc.at[3]).start()

    run_steps(len(spread_steps))
    for n in range(HEAD_COUNT):

        @pl.when(jnp.logical_not(active & (hd == n)))
        def _():
            remote(
                att_out.at[n], att_out.at[n], ats.at[0], atr.at[n], (d, n // z.hb, n % z.hb)
            ).wait_recv()

    part_a.finish()
    part_b.finish()
    save_w.wait()
    tokens.finish()
    to_heads.finish()
    over_dp.finish()

    @pl.when(active)
    def _():
        pltpu.make_async_copy(normed, normed_ref, loc.at[1]).wait()
        pltpu.make_async_copy(qkv, qkv_ref, loc.at[2]).wait()
        pltpu.make_async_copy(attl, attl_ref, loc.at[3]).wait()
        for i in range(z.nq):
            to = slice(0, (i + 1) * BLOCK)
            pltpu.make_async_copy(p_scr.at[i, to], p_ref.at[i, to], loc.at[4 + i]).wait()
        for t in range(ns):

            @pl.when(t != s)
            def _():
                send_att(t).wait_send()


def attention_forward(z, entries, x, weights, router, rows, rel):
    D, S, HS, R, PT = z.D, z.S, HEAD_SIZE, z.R, z.PT
    nb = z.n_blk
    dma = pltpu.SemaphoreType.DMA
    vmem = pl.BlockSpec(memory_space=pltpu.VMEM)
    hbm = pl.BlockSpec(memory_space=pl.ANY)
    wide = 4 * D + LANES
    return pl.pallas_call(
        functools.partial(forward_kernel, z),
        out_shape=(
            jax.ShapeDtypeStruct((z.ndev, R, wide), BF16),
            jax.ShapeDtypeStruct((S, D), BF16),
            jax.ShapeDtypeStruct((S, 3 * HS), BF16),
            jax.ShapeDtypeStruct((z.nq, S, BLOCK), BF16),
            jax.ShapeDtypeStruct((S, 2 * HS), F32),
            jax.ShapeDtypeStruct((HEAD_COUNT, PT // 2, 2 * HS), BF16),
        ),
        in_specs=[vmem] * 9,
        out_specs=(hbm, hbm, hbm, hbm, hbm, vmem),
        scratch_shapes=[
            pltpu.VMEM((R, wide), BF16),
            pltpu.VMEM((HEAD_COUNT, R, 4 * HS), BF16),
            pltpu.VMEM((z.ndev, R, 4 * HS), BF16),
            pltpu.VMEM((z.ns, PT, D), BF16),
            pltpu.VMEM((D, 3 * HS), BF16),
            pltpu.VMEM((BLOCK, BLOCK), F32),
            pltpu.VMEM((BLOCK, BLOCK), F32),
            pltpu.VMEM((S, D), BF16),
            pltpu.VMEM((S, 3 * HS), BF16),
            pltpu.VMEM((HS, S), BF16),
            pltpu.VMEM((S, BLOCK), F32),
            pltpu.VMEM((z.nq, S, BLOCK), BF16),
            pltpu.VMEM((S, 2 * HS), F32),
            pltpu.VMEM((z.ns, PT // 2, 2 * HS), BF16),
            dma((2 * (4 + 6 * (nb - 1) + 2 * nb - 1),)),
            dma((2 * z.ns,)),
            dma((HEAD_COUNT,)),
            dma((z.ns * z.n_dp,)),
            dma((z.ndev,)),
            dma((spread_copies(z, True),)),
            dma((z.ndev,)),
            dma((spread_copies(z, False),)),
            dma((z.ndev,)),
            dma((z.ns,)),
            dma((HEAD_COUNT,)),
            dma((4 + z.nq,)),
        ],
        compiler_params=pltpu.CompilerParams(
            collective_id=0, has_side_effects=True, vmem_limit_bytes=48 * 1024 * 1024
        ),
        name="attention_forward",
    )(entries, x, *weights, router, rows, rel)


def middle_kernel(
    z, att_in, x_ref, w_ref, order_ref, ids_ref, win_ref, wout_ref, cot_ref,
    layer_ref, gmid_ref, gatt_ref, dwo_ref, all_ref,
    win, wout, wo3, misc3, disp, exp_in, ret, back, route, att_cat, pre_scr, out_acc, gg_acc,
    loc, dis_s, dis_r, ret_s, ret_r, all_s, all_r,
):
    d, b, h = place()
    nb, nh, nd, ns = z.n_blk, z.n_head, z.n_dp, z.ns
    D, E, PT, NG, C8 = z.D, z.E, z.PT, z.NG, z.cap8
    me = d * ns + b * nh + h
    g = d * nb + b
    hy = lax.rem(h + 2, nh)
    hc = h + 1 - 2 * lax.rem(h, 2)
    hyc = lax.rem(hc + 2, nh)

    def exp_peer(k):
        e = lax.rem(g + k, NG)
        return e, (e // nb, lax.rem(e, nb), h)

    def exp_from(k):
        e = lax.rem(g + NG - k, NG)
        return e, (e // nb, lax.rem(e, nb), h)

    for k in range(1, NG):
        signal(exp_peer(k)[1])
    signal((d, b, hy))
    signal((d, b, hc))
    local = [
        pltpu.make_async_copy(w_ref.at[:, :, pl.ds(3 * D, D)], wo3, loc.at[0]),
        pltpu.make_async_copy(w_ref.at[:, :, pl.ds(4 * D, LANES)], misc3, loc.at[1]),
        pltpu.make_async_copy(win_ref.at[0], win, loc.at[2]),
        pltpu.make_async_copy(wout_ref.at[0], wout, loc.at[3]),
    ]
    for c in local:
        c.start()

    ids_row = ids_ref[pl.ds(me, 1), :]
    order_row = order_ref[...]
    ids_col = jnp.transpose(jnp.broadcast_to(ids_row, (PT, PT)))
    order_col = jnp.transpose(jnp.broadcast_to(order_row, (PT, PT)))
    earlier = (order_col < order_row) & (ids_col == ids_row)
    rank = jnp.sum(earlier.astype(jnp.int32), axis=0, keepdims=True)
    slot = lax.broadcasted_iota(jnp.int32, (C8, PT), 0)
    base = (rank == slot) & (slot < z.cap)
    lane = lax.broadcasted_iota(jnp.int32, (1, LANES), 1)
    share = jnp.zeros((1, LANES), F32)
    ids_all = ids_ref[...]
    for e in range(E):
        route[e * C8 : (e + 1) * C8, :] = (base & (ids_row == e)).astype(F32)
        count = jnp.sum((ids_all == e).astype(F32), axis=1, keepdims=True)
        count = jnp.sum(count, axis=0, keepdims=True)
        share = share + jnp.where(lane == e, count, 0.0)
    share = share * (AUX_WEIGHT * E / (ids_all.shape[0] * ids_all.shape[1]))
    chosen = ids_col[:, :1] == lane
    picks = route[...].astype(BF16)

    x = x_ref[...].astype(F32)
    cot = cot_ref[...].astype(F32)
    for n in range(HEAD_COUNT):
        at = slice(n * HEAD_SIZE, (n + 1) * HEAD_SIZE)
        att_cat[: PT // 2, at] = att_in[n, :, :HEAD_SIZE]
        att_cat[PT // 2 :, at] = att_in[n, :, HEAD_SIZE:]
    att = att_cat[...]
    local[0].wait()
    local[1].wait()
    wo = flatten_rows(wo3[...]).astype(BF16)
    misc = flatten_rows(misc3[...])
    router = misc.astype(BF16)
    gain = jnp.transpose(misc)[E + 1 : E + 2, :]
    middle = x + nn(att, wo)
    inverse = lax.rsqrt(jnp.mean(middle * middle, axis=-1, keepdims=True) + EPSILON)
    routed = (middle * inverse * gain).astype(BF16)
    await_barrier(NG - 1 + 2)

    def send_disp(part, k):
        e, device = exp_peer(k)
        at = part * NG
        return remote(
            disp.at[part, e], exp_in.at[part, g], dis_s.at[at + k], dis_r.at[at + g], device
        )

    def dispatch(part, values):
        disp[part] = nn(picks, values).reshape(E, C8, D).astype(BF16)
        for k in range(1, NG):
            send_disp(part, k).start()
        exp_in[part, g] = disp[part, g]

    def arrivals(part):
        for k in range(1, NG):
            e, device = exp_from(k)
            ref = exp_in.at[part, e]
            remote(ref, ref, dis_s.at[0], dis_r.at[part * NG + e], device).wait_recv()

    def send_ret(part, k):
        e, device = exp_peer(k)
        at = part * NG
        return remote(
            ret.at[part, e], back.at[part, g], ret_s.at[at + k], ret_r.at[at + g], device
        )

    def give_back(part, values):
        ret[part] = values.reshape(NG, C8, D).astype(BF16)
        for k in range(1, NG):
            send_ret(part, k).start()
        back[part, g] = ret[part, g]

    def returns(part):
        for k in range(1, NG):
            e, device = exp_from(k)
            ref = back.at[part, e]
            remote(ref, ref, ret_s.at[0], ret_r.at[part * NG + e], device).wait_recv()
        rows = back[part].astype(F32).reshape(E * C8, D).astype(BF16)
        return tn(picks, rows)

    def share_slots(part):
        at = 3 * part
        out = [
            remote(
                exp_in.at[part], all_ref.at[part, h], all_s.at[at], all_r.at[part * nh + h],
                (d, b, hy),
            ),
            remote(
                exp_in.at[part], all_ref.at[part, h], all_s.at[at + 1], all_r.at[part * nh + h],
                (d, b, hc),
            ),
            pltpu.make_async_copy(exp_in.at[part], all_ref.at[part, h], loc.at[4 + part]),
        ]
        for c in out:
            c.start()
        return out

    def got_slots(part, hh):
        ref = all_ref.at[part, hh]
        remote(ref, ref, all_s.at[0], all_r.at[part * nh + hh], (d, b, hc)).wait_recv()

    def pass_slots(part):
        got_slots(part, hy)
        ref = all_ref.at[part, hy]
        c = remote(ref, ref, all_s.at[3 * part + 2], all_r.at[part * nh + hy], (d, b, hc))
        c.start()
        return c

    dispatch(0, routed)
    logits = jnp.where(lane < E, nn(routed, router), -1e30)
    exps = jnp.exp(logits - jnp.max(logits, axis=-1, keepdims=True))
    probs = exps / jnp.sum(exps, axis=-1, keepdims=True)
    gate = jnp.sum(jnp.where(chosen, probs, 0.0), axis=-1, keepdims=True)
    dispatch(1, (gate * cot).astype(BF16))
    local[2].wait()
    local[3].wait()
    chunk = D
    chunks = z.FF // chunk

    arrivals(0)
    rows_in = exp_in[0].astype(F32).reshape(NG * C8, D).astype(BF16)
    out_acc[...] = jnp.zeros_like(out_acc)

    def forward_step(c, carry):
        at = pl.ds(pl.multiple_of(c * chunk, chunk), chunk)
        pre = nn(rows_in, win[:, at])
        pre_scr[:, at] = pre
        phi, _ = normal_parts(pre)
        out_acc[...] += nn((pre * phi).astype(BF16), wout[at, :])
        return carry

    lax.fori_loop(0, chunks, forward_step, 0)
    give_back(0, out_acc[...])

    arrivals(1)
    grad_out = exp_in[1].astype(F32).reshape(NG * C8, D).astype(BF16)
    gg_acc[...] = jnp.zeros_like(gg_acc)

    def backward_step(c, carry):
        at = pl.ds(pl.multiple_of(c * chunk, chunk), chunk)
        pre = pre_scr[:, at]
        phi, bell = normal_parts(pre)
        gh = nt(grad_out, wout[at, :]).astype(BF16).astype(F32)
        gp = (gh * (phi + pre * bell * INV_ROOT_TWO_PI)).astype(BF16)
        gg_acc[...] += nt(gp, win[:, at])
        return carry

    lax.fori_loop(0, chunks, backward_step, 0)
    give_back(1, gg_acc[...])
    moved = share_slots(0) + share_slots(1)

    expert_rows = returns(0)
    layer_ref[...] = (middle + gate * expert_rows).astype(BF16)
    grad_gate = jnp.sum(cot * expert_rows, axis=-1, keepdims=True)
    grad_probs = jnp.where(chosen, grad_gate, 0.0) + share
    inner = jnp.sum(probs * grad_probs, axis=-1, keepdims=True)
    grad_logits = (probs * (grad_probs - inner)).astype(BF16)
    from_router = nt(grad_logits, router)
    grad_routed = returns(1) + from_router
    scaled = grad_routed * gain
    mean = jnp.mean(scaled * middle, axis=-1, keepdims=True)
    gmid = cot + inverse * scaled - middle * (inverse * inverse * inverse) * mean
    gmid_ref[...] = gmid
    low_mid = gmid.astype(BF16)
    gatt = nt(low_mid, wo).astype(BF16)
    for n in range(HEAD_COUNT):
        gatt_ref[n] = both_halves(gatt[:, n * HEAD_SIZE : (n + 1) * HEAD_SIZE])
    term = grad_routed * middle * inverse
    high = term.astype(BF16)
    rest = (term - high.astype(F32)).astype(BF16)
    ones = jnp.broadcast_to((lane == E).astype(BF16), (PT, LANES))
    small = tn(routed, grad_logits) + tn(high, ones) + tn(rest, ones)
    terms = jnp.concatenate([tn(att, low_mid), small], axis=1)
    for t in range(z.ndev):
        dwo_ref[t % nh, t // nh] = terms[t * z.R : (t + 1) * z.R].astype(BF16)

    passed = [pass_slots(0), pass_slots(1)]
    for part in range(2):
        for hh in (hc, hyc):
            got_slots(part, hh)
    for n, c in enumerate(moved):
        if n % 3 == 2:
            c.wait()
        else:
            c.wait_send()
    for c in passed:
        c.wait_send()
    for part in range(2):
        for k in range(1, NG):
            send_disp(part, k).wait_send()
            send_ret(part, k).wait_send()


def middle_part(z, att, x, wg, order, ids, w_in, w_out, cot):
    D, PT, NG, E, C8 = z.D, z.PT, z.NG, z.E, z.cap8
    dma = pltpu.SemaphoreType.DMA
    vmem = pl.BlockSpec(memory_space=pltpu.VMEM)
    hbm = pl.BlockSpec(memory_space=pl.ANY)
    return pl.pallas_call(
        functools.partial(middle_kernel, z),
        out_shape=(
            jax.ShapeDtypeStruct((PT, D), BF16),
            jax.ShapeDtypeStruct((PT, D), F32),
            jax.ShapeDtypeStruct((HEAD_COUNT, PT // 2, 2 * HEAD_SIZE), BF16),
            jax.ShapeDtypeStruct((z.n_head, NG, z.R, D + LANES), BF16),
            jax.ShapeDtypeStruct((2, z.n_head, NG, C8, D), BF16),
        ),
        in_specs=[vmem, vmem, hbm, vmem, vmem, hbm, hbm, vmem],
        out_specs=(vmem, vmem, vmem, vmem, hbm),
        scratch_shapes=[
            pltpu.VMEM((D, z.FF), BF16),
            pltpu.VMEM((z.FF, D), BF16),
            pltpu.VMEM((z.ndev, z.R, D), BF16),
            pltpu.VMEM((z.ndev, z.R, LANES), BF16),
            pltpu.VMEM((2, E, C8, D), BF16),
            pltpu.VMEM((2, NG, C8, D), BF16),
            pltpu.VMEM((2, NG, C8, D), BF16),
            pltpu.VMEM((2, E, C8, D), BF16),
            pltpu.VMEM((E * C8, PT), F32),
            pltpu.VMEM((PT, D), BF16),
            pltpu.VMEM((NG * C8, z.FF), F32),
            pltpu.VMEM((NG * C8, D), F32),
            pltpu.VMEM((NG * C8, D), F32),
            dma((6,)),
            dma((2 * NG,)),
            dma((2 * NG,)),
            dma((2 * NG,)),
            dma((2 * NG,)),
            dma((6,)),
            dma((2 * z.n_head,)),
        ],
        compiler_params=pltpu.CompilerParams(
            collective_id=1, has_side_effects=True, vmem_limit_bytes=56 * 1024 * 1024
        ),
        name="experts_and_norms",
    )(att, x, wg, order, ids, w_in, w_out, cot)


def backward_kernel(
    z, gatt_ref, dwo_ref, normed_ref, qkv_ref, p_ref, attl_ref, wg_ref,
    wq_ref, wk_ref, wv_ref, x_ref, gmid_ref,
    gtok_ref, gain1_ref, gq_ref, gk_ref, gv_ref, go_ref, table_ref, gain2_ref, router_ref,
    w3, wfull, misc3, normed, qkv, probs, attl, k_t, do_in, grad_cat, dkv, dqkv, dw, dw3,
    diag, sub, far, dq_in, dw_in, core_in, y_src, y_in, y_sum, dp_in, blk_src, blk_in,
    loc, do_s, do_r, dq_s, dq_r, dw_s, dw_r, r1_s, r1_r,
):
    d, b, h = place()
    nb, nh, nd, ns, nv, NG = z.n_blk, z.n_head, z.n_dp, z.ns, z.ndev, z.NG
    D, R, PT, HS, E = z.D, z.R, z.PT, HEAD_SIZE, z.E
    s = b * nh + h
    me = d * ns + s
    hd = b * z.hb + jnp.minimum(h, z.hb - 1)
    active = h < z.hb

    def any_peer(k):
        t = lax.rem(me + k, nv)
        return t, (t // ns, lax.rem(t // nh, nb), lax.rem(t, nh))

    def greet(k, carry):
        signal(any_peer(k)[1])
        return carry

    lax.fori_loop(1, nv, greet, 0)
    local = [
        pltpu.make_async_copy(qkv_ref, qkv, loc.at[0]),
        pltpu.make_async_copy(attl_ref, attl, loc.at[1]),
        pltpu.make_async_copy(p_ref, probs, loc.at[2]),
        pltpu.make_async_copy(normed_ref, normed, loc.at[3]),
        pltpu.make_async_copy(wg_ref.at[:, :, pl.ds(0, 3 * D)], w3, loc.at[4]),
        pltpu.make_async_copy(wg_ref.at[:, :, pl.ds(4 * D, LANES)], misc3, loc.at[5]),
    ]
    for c in local:
        c.start()
    await_barrier(nv - 1)

    def send_do(n):
        hb, hh = n // z.hb, n % z.hb
        return remote(gatt_ref.at[n], do_in.at[s], do_s.at[n], do_r.at[s], (d, hb, hh))

    for n in range(HEAD_COUNT):
        mine = active & (hd == n)

        @pl.when(jnp.logical_not(mine))
        def _():
            send_do(n).start()

        @pl.when(mine)
        def _():
            do_in[s] = gatt_ref[n]

    hy = lax.rem(h + 2, nh)
    hc = h + 1 - 2 * lax.rem(h, 2)
    hyc = lax.rem(hc + 2, nh)

    def sum_in(dst, src, terms, count):
        def body(e, carry):
            acc = src(e).astype(F32)
            for term in terms:
                acc = acc + term(e).astype(F32)
            dst[e] = acc.astype(BF16)
            return carry

        lax.fori_loop(0, count, body, 0)

    sums = Sends(r1_s)

    def got_sum(ref, k):
        remote(ref, ref, r1_s.at[0], r1_r.at[k], (d, b, hc)).wait_recv()

    def stage_core():
        sums.put(dwo_ref.at[hyc], core_in.at[0], r1_r.at[0], (d, b, hc))
        sums.put(dwo_ref.at[hc], core_in.at[1], r1_r.at[1], (d, b, hc))

    def stage_y():
        got_sum(core_in.at[0], 0)
        sum_in(y_src, lambda e: dwo_ref[hy, e], [lambda e: core_in[0, e]], NG)
        sums.put(y_src, y_in, r1_r.at[2], (d, b, hy))

    def stage_dp():
        got_sum(core_in.at[1], 1)
        got_sum(y_in, 2)
        sum_in(
            y_sum, lambda e: dwo_ref[h, e], [lambda e: core_in[1, e], lambda e: y_in[e]], NG
        )
        for k in range(1, nd):
            p = lax.rem(d + k, nd)
            sums.put(y_sum.at[pl.ds(p * nb, nb)], dp_in.at[d], r1_r.at[3 + d], (p, b, h))

    def stage_blk():
        others = [lax.rem(d + k, nd) for k in range(1, nd)]
        for p in others:
            got_sum(dp_in.at[p], 3 + p)

        def body(e, carry):
            acc = y_sum[d * nb + e].astype(F32)
            for p in others:
                acc = acc + dp_in[p, e].astype(F32)
            blk_src[e] = acc.astype(BF16)
            return carry

        lax.fori_loop(0, nb, body, 0)
        for k in range(1, nb):
            e = lax.rem(b + k, nb)
            sums.put(blk_src.at[e], blk_in.at[b], r1_r.at[3 + nd + b], (d, e, h))
        blk_in[b] = blk_src[b]

    stage_core()
    for c in local:
        c.wait()
    wfull[...] = flatten_rows(w3[...]).astype(BF16)
    gain = jnp.transpose(flatten_rows(misc3[...]))[E : E + 1, :]

    def send_dq(t):
        return remote(dqkv.at[t], dq_in.at[hd], dq_s.at[t], dq_r.at[hd], (d, t // nh, t % nh))

    def send_dw(k):
        t, device = any_peer(k)
        slot = d * HEAD_COUNT + hd
        return remote(dw3.at[t], dw_in.at[slot], dw_s.at[k], dw_r.at[slot], device)

    per = BLOCK // PT
    part_rows = BLOCK // 2

    @pl.when(active)
    def _():
        for j in range(z.nq):
            at = slice(j * BLOCK, (j + 1) * BLOCK)
            k_t[:, at] = jnp.transpose(qkv[at, HS : 2 * HS].astype(F32)).astype(BF16)
        dkv[...] = jnp.zeros_like(dkv)
        dw[...] = jnp.zeros_like(dw)
        diag[...] = jnp.zeros_like(diag)
        sub[...] = jnp.zeros_like(sub)
        far[...] = jnp.zeros_like(far)

        def got_do(k, carry):
            t = lax.rem(s + k, ns)
            remote(
                do_in.at[t], do_in.at[t], do_s.at[0], do_r.at[t],
                (d, t // nh, lax.rem(t, nh)),
            ).wait_recv()
            return carry

        lax.fori_loop(1, ns, got_do, 0)

    for i in reversed(range(z.nq)):
        if i == z.nq - 2:
            stage_y()
        if i == z.nq - 4:
            stage_dp()
        if i == 1:
            stage_blk()

        @pl.when(active)
        def _():
            here = slice(i * BLOCK, (i + 1) * BLOCK)
            att = attl[here, :HS]
            inv = attl[here, HS:]
            pairs = [do_in[i * per + u] for u in range(per)]
            do = jnp.concatenate(
                [half for p in pairs for half in (p[:, :HS], p[:, HS:])], axis=0
            ).astype(F32)
            do = (do * inv).astype(BF16)
            prod = do.astype(F32) * att
            high = prod.astype(BF16)
            rest = (prod - high.astype(F32)).astype(BF16)
            ones = jnp.ones((8, HS), BF16)
            delta = (nt(ones, high) + nt(ones, rest))[0:1, :]
            q = qkv[here, :HS]
            dq_t = jnp.zeros((HS, BLOCK), F32)
            for j in range(i + 1):
                for u in range(2):
                    at = slice(j * BLOCK + u * part_rows, j * BLOCK + (u + 1) * part_rows)
                    p = probs[i, at, :]
                    ds = p.astype(F32) * (nt(qkv[at, 2 * HS :], do) - delta)
                    low = ds.astype(BF16)
                    both = jnp.concatenate([nn(low, q), nn(p, do)], axis=1)
                    if j == i:
                        dkv[at, :] = both if i == z.nq - 1 else dkv[at, :] + both
                        diag[u * part_rows : (u + 1) * part_rows, :] += low.astype(F32)
                    else:
                        dkv[at, :] += both
                        if j == i - 1:
                            sub[u * part_rows : (u + 1) * part_rows, :] += low.astype(F32)
                        else:
                            far[...] += jnp.sum(
                                low.astype(F32).reshape(part_rows // 8, 8, BLOCK), axis=0
                            )
                    dq_t = dq_t + nn(k_t[:, at], low)
            dq = jnp.transpose(dq_t) * HS ** (-0.5)
            parts = jnp.concatenate([dq, dkv[here, :]], axis=1).astype(BF16)
            dw[...] += tn(normed[here, :], parts)
            for u in range(per):
                piece = parts[u * PT : (u + 1) * PT]
                dqkv[i * per + u, :PT] = piece[:, : 2 * HS]
                dqkv[i * per + u, PT:] = both_halves(piece[:, 2 * HS :])
            for u in range(per):
                t = i * per + u

                @pl.when(t != s)
                def _():
                    send_dq(t).start()

                @pl.when(t == s)
                def _():
                    dq_in[hd] = dqkv[t]

    @pl.when(active)
    def _():
        jj = lax.broadcasted_iota(jnp.int32, (BLOCK, BLOCK), 0)
        ii = lax.broadcasted_iota(jnp.int32, (BLOCK, BLOCK), 1)
        lane = lax.broadcasted_iota(jnp.int32, (1, HS), 1)
        sums = jnp.zeros((1, HS), F32)
        half = BUCKETS // 2
        bounds = (0,) + LIMITS + (1 << 30,)
        tile_d, tile_s = diag[...], sub[...]

        def total(values):
            return jnp.sum(jnp.sum(values, axis=0, keepdims=True), axis=1, keepdims=True)

        for n in range(half):
            lo, hi = bounds[n], bounds[n + 1]
            dist = ii - jj
            part = total(
                jnp.where((dist >= lo) & (dist < hi), tile_d, 0.0)
                + jnp.where((dist + BLOCK >= lo) & (dist + BLOCK < hi), tile_s, 0.0)
            )
            if n == half - 1:
                part = part + total(far[...])
            sums = sums + jnp.where(lane == n, part, 0.0)
            if n > 0:
                part = total(jnp.where((-dist >= lo) & (-dist < hi), tile_d, 0.0))
                sums = sums + jnp.where(lane == half + n, part, 0.0)
        wide = jnp.concatenate([dw[...], jnp.broadcast_to(sums, (D, HS))], axis=1)
        split_rows(dw3, wide, R)

        def start_dw(k, carry):
            send_dw(k).start()
            return carry

        lax.fori_loop(1, nv, start_dw, 0)
        dw_in[d * HEAD_COUNT + hd] = dw3[me]

    for k in range(1, nb):
        e = lax.rem(b + k, nb)
        got_sum(blk_in.at[e], 3 + nd + e)
    acc = blk_in[0].astype(F32)
    for e in range(1, nb):
        acc = acc + blk_in[e].astype(F32)
    go_ref[...] = acc[:, :D]
    router_ref[...] = acc[:, D : D + E]
    gain2_ref[...] = acc[:, D + E : D + E + 1]

    for n in range(HEAD_COUNT):

        @pl.when(jnp.logical_not(active & (hd == n)))
        def _():
            remote(
                dq_in.at[n], dq_in.at[n], dq_s.at[0], dq_r.at[n], (d, n // z.hb, n % z.hb)
            ).wait_recv()

        for m in range(2):
            grad_cat[:, m * D + n * HS : m * D + (n + 1) * HS] = dq_in[
                n, :PT, m * HS : (m + 1) * HS
            ]
        at = slice(2 * D + n * HS, 2 * D + (n + 1) * HS)
        grad_cat[: PT // 2, at] = dq_in[n, PT:, :HS]
        grad_cat[PT // 2 :, at] = dq_in[n, PT:, HS:]
    grad_normed = nt(grad_cat[...], wfull[...])
    x = x_ref[...].astype(F32)
    inverse = lax.rsqrt(jnp.mean(x * x, axis=-1, keepdims=True) + EPSILON)
    scaled = grad_normed * gain
    mean = jnp.mean(scaled * x, axis=-1, keepdims=True)
    grad_in = inverse * scaled - x * (inverse * inverse * inverse) * mean
    gtok_ref[...] = (gmid_ref[...] + grad_in).astype(BF16)

    for dd in range(nd):
        for n in range(HEAD_COUNT):

            @pl.when(jnp.logical_not(active & (hd == n) & (d == dd)))
            def _():
                slot = dd * HEAD_COUNT + n
                remote(
                    dw_in.at[slot], dw_in.at[slot], dw_s.at[0], dw_r.at[slot],
                    (dd, n // z.hb, n % z.hb),
                ).wait_recv()

    lane = lax.broadcasted_iota(jnp.int32, (1, BUCKETS), 1)
    slot_lane = lax.broadcasted_iota(jnp.int32, (1, z.RL), 1)
    own_table = jnp.zeros((1, z.RL), F32)
    first = jnp.zeros((R, 1), F32)
    for n in range(HEAD_COUNT):
        part = dw_in[n].astype(F32)
        for dd in range(1, nd):
            part = part + dw_in[dd * HEAD_COUNT + n].astype(F32)
        at = slice(n * HS, (n + 1) * HS)
        for m, (out, w) in enumerate(((gq_ref, wq_ref), (gk_ref, wk_ref), (gv_ref, wv_ref))):
            cols = part[:, m * HS : (m + 1) * HS]
            out[:, at] = cols
            first = first + jnp.sum(cols * w[:, at].astype(F32), axis=-1, keepdims=True)
        line = part[0:1, 3 * HS : 3 * HS + BUCKETS]
        for k in range(z.RL):
            hit = lane + n * BUCKETS == me * z.RL + k
            value = jnp.sum(jnp.where(hit, line, 0.0), axis=1, keepdims=True)
            own_table = own_table + jnp.where(slot_lane == k, value, 0.0)
    own_gain = misc3[pl.ds(me, 1)].astype(F32).reshape(R, LANES)[:, E : E + 1]
    gain1_ref[...] = first / own_gain
    table_ref[...] = own_table

    sums.finish()
    for n in range(HEAD_COUNT):

        @pl.when(jnp.logical_not(active & (hd == n)))
        def _():
            send_do(n).wait_send()

    @pl.when(active)
    def _():
        for t in range(ns):

            @pl.when(t != s)
            def _():
                send_dq(t).wait_send()

        def sent_dw(k, carry):
            send_dw(k).wait_send()
            return carry

        lax.fori_loop(1, nv, sent_dw, 0)


def attention_backward(z, gatt, dwo, normed, qkv, probs, attl, wg, weights, x, gmid):
    D, R, PT, S, HS, E, NG = z.D, z.R, z.PT, z.S, HEAD_SIZE, z.E, z.NG
    dma = pltpu.SemaphoreType.DMA
    vmem = pl.BlockSpec(memory_space=pltpu.VMEM)
    hbm = pl.BlockSpec(memory_space=pl.ANY)
    return pl.pallas_call(
        functools.partial(backward_kernel, z),
        out_shape=(
            jax.ShapeDtypeStruct((PT, D), BF16),
            jax.ShapeDtypeStruct((R, 1), F32),
            jax.ShapeDtypeStruct((R, D), F32),
            jax.ShapeDtypeStruct((R, D), F32),
            jax.ShapeDtypeStruct((R, D), F32),
            jax.ShapeDtypeStruct((R, D), F32),
            jax.ShapeDtypeStruct((1, z.RL), F32),
            jax.ShapeDtypeStruct((R, 1), F32),
            jax.ShapeDtypeStruct((R, E), F32),
        ),
        in_specs=[vmem, vmem, hbm, hbm, hbm, hbm, hbm, vmem, vmem, vmem, vmem, vmem],
        out_specs=(vmem,) * 9,
        scratch_shapes=[
            pltpu.VMEM((z.ndev, R, 3 * D), BF16),
            pltpu.VMEM((D, 3 * D), BF16),
            pltpu.VMEM((z.ndev, R, LANES), BF16),
            pltpu.VMEM((S, D), BF16),
            pltpu.VMEM((S, 3 * HS), BF16),
            pltpu.VMEM((z.nq, S, BLOCK), BF16),
            pltpu.VMEM((S, 2 * HS), F32),
            pltpu.VMEM((HS, S), BF16),
            pltpu.VMEM((z.ns, PT // 2, 2 * HS), BF16),
            pltpu.VMEM((PT, 3 * D), BF16),
            pltpu.VMEM((S, 2 * HS), F32),
            pltpu.VMEM((z.ns, PT + PT // 2, 2 * HS), BF16),
            pltpu.VMEM((D, 3 * HS), F32),
            pltpu.VMEM((z.ndev, R, 4 * HS), BF16),
            pltpu.VMEM((BLOCK, BLOCK), F32),
            pltpu.VMEM((BLOCK, BLOCK), F32),
            pltpu.VMEM((8, BLOCK), F32),
            pltpu.VMEM((HEAD_COUNT, PT + PT // 2, 2 * HS), BF16),
            pltpu.VMEM((z.n_dp * HEAD_COUNT, R, 4 * HS), BF16),
            pltpu.VMEM((2, NG, R, D + LANES), BF16),
            pltpu.VMEM((NG, R, D + LANES), BF16),
            pltpu.VMEM((NG, R, D + LANES), BF16),
            pltpu.VMEM((NG, R, D + LANES), BF16),
            pltpu.VMEM((z.n_dp, z.n_blk, R, D + LANES), BF16),
            pltpu.VMEM((z.n_blk, R, D + LANES), BF16),
            pltpu.VMEM((z.n_blk, R, D + LANES), BF16),
            dma((6,)),
            dma((HEAD_COUNT,)),
            dma((z.ns,)),
            dma((z.ns,)),
            dma((HEAD_COUNT,)),
            dma((z.ndev,)),
            dma((z.n_dp * HEAD_COUNT,)),
            dma((3 + z.n_dp - 1 + z.n_blk - 1,)),
            dma((3 + z.n_dp + z.n_blk,)),
        ],
        compiler_params=pltpu.CompilerParams(
            collective_id=2, has_side_effects=True, vmem_limit_bytes=58 * 1024 * 1024
        ),
        name="attention_backward",
    )(gatt, dwo, normed, qkv, probs, attl, wg, *weights, x, gmid)


def expert_kernel(z, slots_ref, win_ref, wout_ref, gin_ref, gout_ref, rows_in, rows_t, grad_out):
    @pl.when(pl.program_id(0) == 0)
    def _():
        for n in range(z.n_head):
            count = z.NG * z.cap8
            at = slice(n * count, (n + 1) * count)
            rows_in[at, :] = slots_ref[0, n].astype(F32).reshape(count, z.D).astype(BF16)
            grad_out[at, :] = slots_ref[1, n].astype(F32).reshape(count, z.D).astype(BF16)
        rows_t[...] = jnp.transpose(rows_in[...])

    w1 = win_ref[0]
    w2 = wout_ref[0]
    pre = nn(rows_in[...], w1)
    phi, bell = normal_parts(pre)
    hidden = (pre * phi).astype(BF16)
    gh = nt(grad_out[...], w2).astype(BF16).astype(F32)
    gp = (gh * (phi + pre * bell * INV_ROOT_TWO_PI)).astype(BF16)
    gin_ref[0] = nn(rows_t[...], gp)
    gout_ref[0] = tn(hidden, grad_out[...])


def expert_weights(z, slots, w_in, w_out):
    chunk = 512
    total = z.n_head * z.NG * z.cap8
    in_chunk = pl.BlockSpec((1, z.D, chunk), lambda i: (0, 0, i))
    out_chunk = pl.BlockSpec((1, chunk, z.D), lambda i: (0, i, 0))
    return pl.pallas_call(
        functools.partial(expert_kernel, z),
        grid=(z.FF // chunk,),
        out_shape=(
            jax.ShapeDtypeStruct((1, z.D, z.FF), F32),
            jax.ShapeDtypeStruct((1, z.FF, z.D), F32),
        ),
        in_specs=[pl.BlockSpec(memory_space=pltpu.VMEM), in_chunk, out_chunk],
        out_specs=(in_chunk, out_chunk),
        scratch_shapes=[
            pltpu.VMEM((total, z.D), BF16),
            pltpu.VMEM((z.D, total), BF16),
            pltpu.VMEM((total, z.D), BF16),
        ],
        compiler_params=pltpu.CompilerParams(
            dimension_semantics=("arbitrary",), vmem_limit_bytes=48 * 1024 * 1024
        ),
        name="expert_weight_grads",
    )(slots, w_in, w_out)


def local(
    sizes,
    tokens,
    order,
    expert_ids,
    norm1_gain,
    w_query,
    w_key,
    w_value,
    w_attn_out,
    rel_table,
    norm2_gain,
    w_router,
    w_in,
    w_out,
    cotangent,
):
    R, D = w_query.shape
    E = w_router.shape[1]
    z = Sizes(*sizes, R, D, E, w_in.shape[2], tokens.shape[1])
    rel = jnp.pad(rel_table, (0, R - rel_table.shape[0]))[None, :]
    gains = jnp.stack([norm1_gain, norm2_gain])
    row = np.arange(D)
    entries = np.where(row % R < z.RL, row // R * z.RL + row % R, -1).astype(np.int32)[None, :]
    ids = expert_ids.reshape(-1, z.PT)
    x = tokens.reshape(z.PT, D)
    cot = cotangent.reshape(z.PT, D)

    wg, normed, qkv, probs, attl, att = attention_forward(
        z,
        jnp.asarray(entries),
        x,
        (w_query, w_key, w_value, w_attn_out),
        w_router,
        gains.astype(F32),
        rel.astype(F32),
    )
    layer, gmid, gatt, dwo, slots = middle_part(z, att, x, wg, order, ids, w_in, w_out, cot)
    gtok, gain1, gq, gk, gv, go, table, gain2, router = attention_backward(
        z, gatt, dwo, normed, qkv, probs, attl, wg, (w_query, w_key, w_value), x, gmid
    )
    g_in, g_out = expert_weights(z, slots, w_in, w_out)
    return (
        layer.reshape(tokens.shape),
        gtok.reshape(tokens.shape),
        gain1.reshape(R),
        gq,
        gk,
        gv,
        go,
        table.reshape(z.RL),
        gain2.reshape(R),
        router,
        g_in,
        g_out,
    )


def solution(mesh):
    everywhere = ("dp", "blk", "head")
    rows, table = P(everywhere), P(everywhere, None)
    tokens = P("dp", ("blk", "head"), None)
    expert = P(("dp", "blk"), None, None)
    in_specs = (
        tokens,
        P("dp", ("blk", "head")),
        P(),
        rows,
        table,
        table,
        table,
        table,
        rows,
        rows,
        table,
        expert,
        expert,
        tokens,
    )
    out_specs = (
        tokens, tokens, rows, table, table, table, table, rows, rows, table, expert, expert
    )
    sizes = (mesh.shape["dp"], mesh.shape["blk"], mesh.shape["head"])
    return jax.shard_map(
        functools.partial(local, sizes),
        mesh=mesh,
        in_specs=in_specs,
        out_specs=out_specs,
        check_vma=False,
    )
```

```python
import functools
import itertools
import types

import jax
import jax.numpy as jnp
from jax import lax
from jax.experimental import pallas as pl
from jax.experimental.pallas import tpu as pltpu
from jax.sharding import PartitionSpec as P

HEAD_COUNT = 12
HEAD_SIZE = 64
BUCKETS = 32
BLOCK = 256
EPSILON = 1e-06
AUX_WEIGHT = 1.0
LIMITS = (1, 2, 3, 4, 5, 6, 7, 8, 12, 16, 23, 32, 46, 64, 91)
INV_ROOT_TWO = 0.7071067811865476
INV_ROOT_TWO_PI = 0.3989422804014327
LANES = 128
VMEM_LIMIT = 62 * 1024 * 1024
MESH = pl.DeviceIdType.MESH
F32 = jnp.float32
BF16 = jnp.bfloat16


def both_halves(values):
    n = values.shape[0] // 2
    return jnp.concatenate([values[:n], values[n:]], axis=1)


def line_order(b, nb):
    out = [(b, b >= 0)]
    for k in range(1, nb):
        out.append((b - k, b >= k))
        out.append((b + k, b + k < nb))
    return out


class Sends:
    def __init__(self, sems):
        self.sems, self.made = sems, []

    def put(self, src, dst, recv, device, cond=None):
        c = remote(src, dst, self.sems.at[len(self.made)], recv, device)
        self.made.append((c, cond))
        self.each(c.start, cond)

    def each(self, action, cond):
        if cond is None:
            action()
        else:
            pl.when(cond)(action)

    def finish(self):
        for c, cond in self.made:
            self.each(c.wait_send, cond)


class Sizes:
    def __init__(self, n_dp, n_blk, n_head, rows, width, experts, hidden, piece):
        self.n_dp, self.n_blk, self.n_head = n_dp, n_blk, n_head
        self.ndev = n_dp * n_blk * n_head
        self.ns = n_blk * n_head
        self.R, self.D, self.E, self.FF, self.PT = rows, width, experts, hidden, piece
        self.S = piece * self.ns
        self.nq = self.S // BLOCK
        self.hb = HEAD_COUNT // n_blk
        self.cap = (5 * piece + 4 * experts - 1) // (4 * experts)
        self.cap8 = (self.cap + 7) // 8 * 8
        self.NG = n_dp * n_blk
        self.RL = HEAD_COUNT * BUCKETS // self.ndev
        self.wide = 4 * width + LANES
        self.per = BLOCK // piece
        assert self.hb < n_head and self.hb * n_blk == HEAD_COUNT
        assert experts == self.NG and n_head == 4


    def holder(self, n):
        return n // self.hb, n % self.hb + n // self.hb % 2


def nt(a, b):
    return lax.dot_general(a, b, (((1,), (1,)), ((), ())), preferred_element_type=F32)


def tn(a, b):
    return lax.dot_general(a, b, (((0,), (0,)), ((), ())), preferred_element_type=F32)


def nn(a, b):
    return jnp.dot(a, b, preferred_element_type=F32)


def place():
    return lax.axis_index("dp"), lax.axis_index("blk"), lax.axis_index("head")


def signal(device):
    pl.semaphore_signal(
        pltpu.get_barrier_semaphore(), inc=1, device_id=device, device_id_type=MESH
    )


def await_barrier(count):
    pl.semaphore_wait(pltpu.get_barrier_semaphore(), count)


def remote(src, dst, send, recv, device):
    return pltpu.make_async_remote_copy(
        src_ref=src, dst_ref=dst, send_sem=send, recv_sem=recv, device_id=device, device_id_type=MESH
    )


def flatten_rows(blocks):
    count, rows, lanes = blocks.shape
    wide = blocks.astype(F32)
    if rows % 8 == 0:
        return wide.reshape(count * rows, lanes)
    return jnp.concatenate([wide[i] for i in range(count)], axis=0)


def split_rows(dst_ref, values, rows):
    count = values.shape[0] // rows
    if rows % 8 == 0:
        dst_ref[...] = values.reshape(count, rows, values.shape[1]).astype(dst_ref.dtype)
    else:
        for i in range(count):
            dst_ref[i] = values[i * rows : (i + 1) * rows].astype(dst_ref.dtype)


def normal_parts(v):
    bell = jnp.exp(-0.5 * v * v)
    t = 1.0 / (1.0 + (0.3275911 * INV_ROOT_TWO) * jnp.abs(v))
    poly = t * (
        0.254829592
        + t * (-0.284496736 + t * (1.421413741 + t * (-1.453152027 + t * 1.061405429)))
    )
    tail = 0.5 * poly * bell
    return jnp.where(v >= 0, 1.0 - tail, tail), bell


def bias_tile(table, shift):
    j = lax.broadcasted_iota(jnp.int32, (BLOCK, BLOCK), 0)
    i = lax.broadcasted_iota(jnp.int32, (BLOCK, BLOCK), 1)
    dist = j - i + shift
    mag = jnp.abs(dist)
    half = BUCKETS // 2
    out = jnp.broadcast_to(table[0:1, 0:1], (BLOCK, BLOCK))
    for n, limit in enumerate(LIMITS):
        low = table[n + 1 : n + 2, 0:1]
        if shift == 0:
            high = table[half + n + 1 : half + n + 2, 0:1]
            out = jnp.where(mag >= limit, jnp.where(dist > 0, high, low), out)
        else:
            out = jnp.where(mag >= limit, low, out)
    return out


class Spread:
    def __init__(self, z, src, dst, send, recv, y_first, lanes):
        self.z, self.src, self.dst, self.recv = z, src, dst, recv
        self.sends, self.lanes = Sends(send), lanes
        d, b, h = place()
        self.at = (d, b, h)
        nh, nd = z.n_head, z.n_dp
        self.hy = lax.rem(h + 2, nh)
        self.hc = h + 1 - 2 * lax.rem(h, 2)
        self.hyc = lax.rem(self.hc + 2, nh)
        dto = [lax.rem(d + k, nd) for k in range(1, nd)]
        dfrom = [lax.rem(d + nd - k, nd) for k in range(1, nd)]
        ys = ([(d, self.hy)], [(d, self.hy)])
        xs = ([(p, h) for p in dto], [(p, h) for p in dfrom])
        self.first, self.second = (ys, xs) if y_first else (xs, ys)
        if y_first:
            self.second_slots = [(p, hh) for p in dfrom for hh in (h, self.hy)]
        else:
            self.second_slots = [(p, self.hy) for p in [d] + dfrom]
        self.core_slots = [(p, hh) for p in [d] + dfrom for hh in (self.hc, self.hyc)]

    def slot(self, dd, bb, hh):
        return (dd * self.z.n_blk + bb) * self.z.n_head + hh

    def ref(self, slot):
        return self.dst.at[slot, :, self.lanes]

    def put(self, src, slot, device, cond=None):
        self.sends.put(src, self.ref(slot), self.recv.at[slot], device, cond)

    def got(self, slot):
        d, b, h = self.at
        ref = self.ref(slot)
        remote(ref, ref, self.sends.sems.at[0], self.recv.at[slot], (d, b, self.hc)).wait_recv()

    def steps(self):
        d, b, h = self.at
        nb = self.z.n_blk

        def begin():
            mine = self.slot(d, b, h)
            self.put(self.src, mine, (d, b + 1, h), b + 1 < nb)
            self.put(self.src, mine, (d, b - 1, h), b >= 1)
            for dd, hh in self.first[0] + self.second[0] + [(d, self.hc)]:
                self.put(self.src, mine, (dd, b, hh))

        def line_arrival(k):
            for f, cond, to, more in (
                (b - k, b >= k, b + 1, b + 1 < nb),
                (b + k, b + k < nb, b - 1, b >= 1),
            ):
                slot = self.slot(d, f, h)
                pl.when(cond)(functools.partial(self.got, slot))
                if k < nb - 1:
                    self.put(self.ref(slot), slot, (d, to, h), cond & more)
                for dd, hh in self.first[0] + self.second[0] + [(d, self.hc)]:
                    self.put(self.ref(slot), slot, (dd, b, hh), cond)

        def first_arrival(p, f, cond):
            slot = self.slot(p[0], f, p[1])
            pl.when(cond)(functools.partial(self.got, slot))
            for dd, hh in self.second[0] + [(d, self.hc)]:
                self.put(self.ref(slot), slot, (dd, b, hh), cond)

        def second_arrival(p, f, cond):
            slot = self.slot(p[0], f, p[1])
            pl.when(cond)(functools.partial(self.got, slot))
            self.put(self.ref(slot), slot, (d, b, self.hc), cond)

        out = [begin]
        for k in range(1, nb):
            out.append(functools.partial(line_arrival, k))
        for p in self.first[1]:
            for f, cond in line_order(b, nb):
                out.append(functools.partial(first_arrival, p, f, cond))
        for p in self.second_slots:
            for f, cond in line_order(b, nb):
                out.append(functools.partial(second_arrival, p, f, cond))
        return out

    def finish(self):
        d, b, h = self.at
        for p in self.core_slots:
            for f in range(self.z.n_blk):
                self.got(self.slot(p[0], f, p[1]))
        self.sends.finish()


def spread_copies(z, y_first):
    nb, nd = z.n_blk, z.n_dp
    peers = 1 + nd - 1 + 1
    first = 1 if y_first else nd - 1
    second = peers - 1 - first
    second_slots = 2 * (nd - 1) if y_first else nd
    line = 2 * nb - 1
    return 2 + peers + (nb - 1) * 2 * (peers + 1) + first * line * (second + 1) + second_slots * line


class Place:
    def __init__(self, z):
        self.d, self.b, self.h = d, b, h = place()
        self.s = b * z.n_head + h
        self.me = d * z.ns + self.s
        self.g = d * z.n_blk + b
        first = lax.rem(b, 2)
        self.active = (h >= first) & (h < first + z.hb)
        self.hd = b * z.hb + jnp.clip(h - first, 0, z.hb - 1)
        self.hy = lax.rem(h + 2, z.n_head)
        self.hc = h + 1 - 2 * lax.rem(h, 2)
        self.hyc = lax.rem(self.hc + 2, z.n_head)
        self.z = z

    def any_peer(self, k):
        z = self.z
        t = lax.rem(self.me + k, z.ndev)
        return t, (t // z.ns, lax.rem(t // z.n_head, z.n_blk), lax.rem(t, z.n_head))

    def in_sequence(self, t):
        return (self.d, t // self.z.n_head, lax.rem(t, self.z.n_head))

    def owns(self, n):
        return self.active & (self.hd == n)

    def group(self, k):
        z = self.z
        e = lax.rem(self.g + k, z.NG)
        return e, (e // z.n_blk, lax.rem(e, z.n_blk), self.h)


def layer_kernel(z, names, *refs):
    r = types.SimpleNamespace(**dict(zip(names, refs)))
    r.dkv = r.s_scr.at[:, pl.ds(0, 2 * HEAD_SIZE)]
    p = Place(z)

    def greet(k, carry):
        signal(p.any_peer(k)[1])
        return carry

    lax.fori_loop(1, z.ndev, greet, 0)
    D = z.D
    small = [
        pltpu.make_async_copy(ref, r.w_own.at[:, pl.ds(m * D, D)], r.in_sem.at[m])
        for m, ref in enumerate((r.wq_ref, r.wk_ref, r.wv_ref, r.wo_ref))
    ]
    small.append(pltpu.make_async_copy(r.x_ref, r.x_own, r.in_sem.at[4]))
    later = [
        pltpu.make_async_copy(r.cot_ref, r.cot, r.in_sem.at[5]),
        pltpu.make_async_copy(r.ids_ref, r.ids, r.in_sem.at[6]),
        pltpu.make_async_copy(r.win_ref.at[0], r.win, r.in_sem.at[7]),
        pltpu.make_async_copy(r.wout_ref.at[0], r.wout, r.in_sem.at[8]),
    ]
    for c in small + later:
        c.start()
    for c in small:
        c.wait()
    steps, finish_forward = forward_phase(z, r, p)
    for c in later:
        c.wait()
    finish_middle = middle_phase(z, r, p, steps)
    backward_phase(z, r, p, steps)
    finish_forward()
    finish_middle()


def forward_phase(z, r, p):
    d, b, h, s, me, hd, active = p.d, p.b, p.h, p.s, p.me, p.hd, p.active
    hy, hc, hyc = p.hy, p.hc, p.hyc
    nb, nh, nd, ns = z.n_blk, z.n_head, z.n_dp, z.ns
    D, R, E, PT, HS = z.D, z.R, z.E, z.PT, HEAD_SIZE

    eye = lax.broadcasted_iota(jnp.int32, (R, R), 0) == lax.broadcasted_iota(jnp.int32, (R, R), 1)
    row_of = lax.broadcasted_iota(jnp.int32, (LANES, R), 0)
    tail = jnp.zeros((LANES, R), F32)
    for n in range(3):
        tail = jnp.where(row_of == E + n, r.rows_ref[n : n + 1, :], tail)
    router_t = jnp.concatenate(
        [r.router_ref[...].astype(F32), jnp.zeros((LANES - E, R), F32)], axis=0
    )
    misc = nt(eye.astype(BF16), (tail + router_t).astype(BF16)).astype(BF16)
    r.w_own[:, 4 * D :] = misc
    for n in range(HEAD_COUNT):
        columns = [r.w_own[:, m * D + n * HS : m * D + (n + 1) * HS] for m in range(3)]
        r.slices[n] = jnp.concatenate(columns + [misc[:, E : E + HS]], axis=1)
    save_w = pltpu.make_async_copy(r.w_own, r.wg_ref.at[me], r.loc.at[0])
    save_w.start()
    await_barrier(z.ndev - 1)

    to_heads = Sends(r.sl_s)
    over_dp = Sends(r.sd_s)
    for n in range(HEAD_COUNT):
        hb, hh = z.holder(n)
        to_heads.put(
            r.slices.at[n], r.slices_in.at[me], r.sl_r.at[me], (d, hb, hh),
            jnp.logical_not(p.owns(n)),
        )

    tokens = Sends(r.x_s)
    pieces = 2
    rows_of = PT // pieces

    def xref(slot, c):
        return r.xg.at[slot, pl.ds(c * rows_of, rows_of)]

    def put(src, slot, c, device, cond=None):
        tokens.put(src, xref(slot, c), r.x_r.at[slot * pieces + c], device, cond)

    def got(slot, c):
        ref = xref(slot, c)
        remote(ref, ref, r.x_s.at[0], r.x_r.at[slot * pieces + c], (d, b, hc)).wait_recv()

    for c in range(pieces):
        own = r.x_own.at[pl.ds(c * rows_of, rows_of)]
        put(own, s, c, (d, b + 1, h), b + 1 < nb)
        put(own, s, c, (d, b - 1, h), b >= 1)
        put(own, s, c, (d, b, hy))
        put(own, s, c, (d, b, hc))
    r.xg[s] = r.x_own[...]

    @pl.when(active)
    def _():
        r.slices_in[me] = r.slices[hd]

    for k in range(1, nb):
        for c in range(pieces):
            for f, cond, to, more in (
                (b - k, b >= k, b + 1, b + 1 < nb),
                (b + k, b + k < nb, b - 1, b >= 1),
            ):
                slot = f * nh + h
                pl.when(cond)(functools.partial(got, slot, c))
                if k < nb - 1:
                    put(xref(slot, c), slot, c, (d, to, h), cond & more)
                put(xref(slot, c), slot, c, (d, b, hy), cond)
                put(xref(slot, c), slot, c, (d, b, hc), cond)
        if k == 1:
            for m in range(ns):
                t = lax.rem(s + m, ns)
                slot = d * ns + t
                ref = r.slices_in.at[slot]
                if m > 0:
                    c = remote(ref, ref, r.sl_s.at[0], r.sl_r.at[slot], p.in_sequence(t))
                    pl.when(active)(c.wait_recv)
                for kd in range(1, nd):
                    over_dp.put(ref, ref, r.sl_r.at[slot], (lax.rem(d + kd, nd), b, h), active)

    for f, cond in line_order(b, nb):
        for c in range(pieces):
            slot = f * nh + hy
            pl.when(cond)(functools.partial(got, slot, c))
            put(xref(slot, c), slot, c, (d, b, hc), cond)

    cuts = (3 * D, z.wide, False), (0, 3 * D // 2, True), (3 * D // 2, 3 * D, False)
    parts = [
        Spread(
            z, r.w_own.at[:, pl.ds(lo, hi - lo)], r.wg_ref,
            getattr(r, "w%d_s" % n), getattr(r, "w%d_r" % n), y_first, pl.ds(lo, hi - lo),
        )
        for n, (lo, hi, y_first) in enumerate(cuts)
    ]
    first, rest_a, rest_b = [part.steps() for part in parts]
    steps = []
    for k in range(nb):
        steps += [first.pop(0), rest_a.pop(0), rest_b.pop(0)]
    steps = Steps(steps + first, rest_a, rest_b, parts, save_w)

    steps.run(3)

    @pl.when(active)
    def _():
        for kd in range(1, nd):
            dd = lax.rem(d + kd, nd)

            def got_slice(t, carry):
                ref = r.slices_in.at[dd * ns + t]
                remote(ref, ref, r.sl_s.at[0], r.sl_r.at[dd * ns + t], (dd, b, h)).wait_recv()
                return carry

            lax.fori_loop(0, ns, got_slice, 0)

        rows = flatten_rows(r.slices_in[...])
        r.wh[:, : 2 * HS] = rows[:, : 2 * HS].astype(BF16)
        r.wh[:, :HS] = (rows[:, :HS] * HS ** (-0.5)).astype(BF16)
        r.wh[:, 2 * HS :] = rows[:, 2 * HS : 3 * HS].astype(BF16)
        r.gain1[...] = jnp.transpose(rows[:, LANES:])[HS : HS + 1, :]
        column = lax.broadcasted_iota(jnp.int32, (1, D), 1).astype(F32)
        owner = jnp.floor((column + 0.5) * (1.0 / R))
        place_of = column - owner * R
        entry = jnp.where(place_of < z.RL, owner * z.RL + place_of, -1.0)
        wanted = hd * BUCKETS + lax.broadcasted_iota(jnp.int32, (BUCKETS, D), 0)
        pick = (entry == wanted.astype(F32)).astype(BF16)
        table = nn(pick, rows[:, LANES:].astype(BF16))[:, HS + 2 : HS + 3]
        r.bias_d[...] = bias_tile(table, 0)
        r.bias_s[...] = bias_tile(table, -BLOCK)
        r.far_bias[...] = table[BUCKETS // 2 - 1 : BUCKETS // 2, 0:1]

    for f in range(nb):
        for c in range(pieces):
            got(f * nh + hc, c)
            got(f * nh + hyc, c)
    tokens.finish()
    per = z.per
    half = BLOCK // 2

    @pl.when(active)
    def _():
        for i in range(z.nq):
            here = slice(i * BLOCK, (i + 1) * BLOCK)
            x = r.xg[i * per : (i + 1) * per].reshape(BLOCK, D).astype(F32)
            inverse = lax.rsqrt(jnp.mean(x * x, axis=-1, keepdims=True) + EPSILON)
            low = (x * inverse * r.gain1[...]).astype(BF16)
            r.xg[i * per : (i + 1) * per] = low.reshape(per, PT, D)
            mixed = nn(low, r.wh[...])
            r.qkv[here, :] = mixed.astype(BF16)
            r.v_t[:, here] = jnp.transpose(mixed[:, 2 * HS :]).astype(BF16)
            r.k_t[:, here] = jnp.transpose(mixed[:, HS : 2 * HS]).astype(BF16)

    def send_att(t):
        return remote(
            r.att_src.at[t], r.att_in.at[hd], r.at_s.at[t], r.at_r.at[hd], (d, t // nh, t % nh)
        )

    low_rows, high_rows = range(z.nq // 2), range(z.nq // 2, z.nq)
    order = [i for pair in zip(reversed(high_rows), reversed(low_rows)) for i in pair]
    for i in order:
        steps.run(4)

        @pl.when(active)
        def _():
            here = slice(i * BLOCK, (i + 1) * BLOCK)
            q = r.qkv[here, :HS]
            top = jnp.full((8, BLOCK), -1e30, F32)
            far = r.far_bias[...]
            for j in range(i + 1):
                for u in range(2):
                    at = slice(j * BLOCK + u * half, j * BLOCK + (u + 1) * half)
                    part = slice(u * half, (u + 1) * half)
                    if j == i:
                        bias = r.bias_d[part, :]
                    elif j == i - 1:
                        bias = r.bias_s[part, :]
                    else:
                        bias = far
                    sc = nt(r.qkv[at, HS : 2 * HS], q) + bias
                    r.s_scr[at, :] = sc
                    top = jnp.maximum(top, jnp.max(sc.reshape(half // 8, 8, BLOCK), axis=0))
            top = jnp.max(top, axis=0, keepdims=True)
            total = jnp.zeros((8, BLOCK), F32)
            acc = jnp.zeros((HS, BLOCK), F32)
            for j in range(i + 1):
                for u in range(2):
                    at = slice(j * BLOCK + u * half, j * BLOCK + (u + 1) * half)
                    e = jnp.exp(r.s_scr[at, :] - top)
                    total = total + jnp.sum(e.reshape(half // 8, 8, BLOCK), axis=0)
                    r.probs[i, at, :] = e.astype(BF16)
                at = slice(j * BLOCK, (j + 1) * BLOCK)
                acc = acc + nn(r.v_t[:, at], r.probs[i, at, :])
            total = jnp.sum(total, axis=0, keepdims=True)
            both = jnp.concatenate([acc, jnp.broadcast_to(total, (HS, BLOCK))], axis=0)
            both = jnp.transpose(both)
            inv = 1.0 / both[:, HS:]
            att = (both[:, :HS] * inv).astype(BF16)
            r.attl[here, :] = jnp.concatenate([att.astype(F32), inv], axis=1)
            for u in range(per):
                t = i * per + u
                r.att_src[t] = both_halves(att[u * PT : (u + 1) * PT])

                @pl.when(t != s)
                def _():
                    send_att(t).start()

                @pl.when(t == s)
                def _():
                    r.att_in[hd] = r.att_src[t]

    def finish():
        to_heads.finish()
        over_dp.finish()

        @pl.when(active)
        def _():
            for t in range(ns):

                @pl.when(t != s)
                def _():
                    send_att(t).wait_send()

    return steps, finish


class Steps:
    def __init__(self, first, rest_a, rest_b, parts, save):
        self.first, self.parts, self.save = first, parts, save
        self.rest = [
            step
            for pair in itertools.zip_longest(rest_b, rest_a)
            for step in pair
            if step is not None
        ]

    def run(self, count):
        for _ in range(min(count, len(self.first))):
            self.first.pop(0)()

    def finish_first(self):
        self.run(len(self.first))
        self.parts[0].finish()
        self.save.wait()

    def run_rest(self, count):
        for _ in range(min(count, len(self.rest))):
            self.rest.pop(0)()

    def finish_rest(self):
        self.run_rest(len(self.rest))
        for part in self.parts[1:]:
            part.finish()


def middle_phase(z, r, p, steps):
    d, b, h, me, g, s = p.d, p.b, p.h, p.me, p.g, p.s
    hy, hc, hyc = p.hy, p.hc, p.hyc
    nb, nh, nd, ns = z.n_blk, z.n_head, z.n_dp, z.ns
    D, E, PT, NG, C8 = z.D, z.E, z.PT, z.NG, z.cap8

    ids_row = r.ids[pl.ds(me, 1), :]
    order_row = r.order_ref[...]
    ids_col = jnp.transpose(jnp.broadcast_to(ids_row, (PT, PT)))
    order_col = jnp.transpose(jnp.broadcast_to(order_row, (PT, PT)))
    earlier = (order_col < order_row) & (ids_col == ids_row)
    rank = jnp.sum(earlier.astype(jnp.int32), axis=0, keepdims=True)
    slot = lax.broadcasted_iota(jnp.int32, (C8, PT), 0)
    base = (rank == slot) & (slot < z.cap)
    lane = lax.broadcasted_iota(jnp.int32, (1, LANES), 1)
    share = jnp.zeros((1, LANES), F32)
    ids_all = r.ids[...]
    for e in range(E):
        r.route[e * C8 : (e + 1) * C8, :] = (base & (ids_row == e)).astype(F32)
        count = jnp.sum((ids_all == e).astype(F32), axis=1, keepdims=True)
        count = jnp.sum(count, axis=0, keepdims=True)
        share = share + jnp.where(lane == e, count, 0.0)
    share = share * (AUX_WEIGHT * E / (ids_all.shape[0] * ids_all.shape[1]))
    chosen = ids_col[:, :1] == lane
    picks = r.route[...].astype(BF16)
    x = r.x_own[...].astype(F32)
    cot = r.cot[...].astype(F32)

    steps.finish_first()
    load = [
        pltpu.make_async_copy(r.wg_ref.at[:, :, pl.ds(3 * D, D)], r.w3.at[0], r.loc.at[1]),
        pltpu.make_async_copy(r.wg_ref.at[:, :, pl.ds(4 * D, LANES)], r.misc3, r.loc.at[2]),
    ]
    for c in load:
        c.start()
    for c in load:
        c.wait()
    r.wo[...] = flatten_rows(r.w3[0]).astype(BF16)
    misc = flatten_rows(r.misc3[...])
    router = misc.astype(BF16)
    lines = jnp.transpose(misc)
    r.gain1[...] = lines[E : E + 1, :]
    gain = lines[E + 1 : E + 2, :]
    for n in range(HEAD_COUNT):
        hb, hh = z.holder(n)

        @pl.when(jnp.logical_not(p.owns(n)))
        def _():
            ref = r.att_in.at[n]
            remote(ref, ref, r.at_s.at[0], r.at_r.at[n], (d, hb, hh)).wait_recv()

        at = slice(n * HEAD_SIZE, (n + 1) * HEAD_SIZE)
        r.att_cat[: PT // 2, at] = r.att_in[n, :, :HEAD_SIZE]
        r.att_cat[PT // 2 :, at] = r.att_in[n, :, HEAD_SIZE:]
    att = r.att_cat[...]
    middle = x + nn(att, r.wo[...])
    inverse = lax.rsqrt(jnp.mean(middle * middle, axis=-1, keepdims=True) + EPSILON)
    routed = (middle * inverse * gain).astype(BF16)

    out = Sends(r.ex_s)

    def dispatch(part, values):
        r.disp[part] = nn(picks, values).reshape(E, C8, D).astype(BF16)
        for k in range(1, NG):
            e, device = p.group(k)
            out.put(r.disp.at[part, e], r.exp_in.at[part, g], r.ex_r.at[part * NG + g], device)
        r.exp_in[part, g] = r.disp[part, g]

    def arrivals(part):
        for k in range(1, NG):
            e, device = p.group(NG - k)
            ref = r.exp_in.at[part, e]
            remote(ref, ref, r.ex_s.at[0], r.ex_r.at[part * NG + e], device).wait_recv()

    def give_back(part, values):
        r.ret[part] = values.reshape(NG, C8, D).astype(BF16)
        for k in range(1, NG):
            e, device = p.group(k)
            out.put(r.ret.at[part, e], r.back.at[part, g], r.rt_r.at[part * NG + g], device)
        r.back[part, g] = r.ret[part, g]

    def returns(part):
        for k in range(1, NG):
            e, device = p.group(NG - k)
            ref = r.back.at[part, e]
            remote(ref, ref, r.ex_s.at[0], r.rt_r.at[part * NG + e], device).wait_recv()
        rows = r.back[part].astype(F32).reshape(E * C8, D).astype(BF16)
        return tn(picks, rows)

    copies = []

    def share_slots(part):
        src, dst, sem = r.exp_in.at[part], r.slots_ref.at[part, h], r.all_r.at[part * nh + h]
        out.put(src, dst, sem, (d, b, hy))
        out.put(src, dst, sem, (d, b, hc))
        c = pltpu.make_async_copy(src, dst, r.loc.at[3 + part])
        c.start()
        copies.append(c)

    def got_slots(part, hh):
        ref = r.slots_ref.at[part, hh]
        remote(ref, ref, r.ex_s.at[0], r.all_r.at[part * nh + hh], (d, b, hc)).wait_recv()

    def pass_slots(part):
        got_slots(part, hy)
        ref = r.slots_ref.at[part, hy]
        out.put(ref, ref, r.all_r.at[part * nh + hy], (d, b, hc))

    dispatch(0, routed)
    logits = jnp.where(lane < E, nn(routed, router), -1e30)
    exps = jnp.exp(logits - jnp.max(logits, axis=-1, keepdims=True))
    probs = exps / jnp.sum(exps, axis=-1, keepdims=True)
    gate = jnp.sum(jnp.where(chosen, probs, 0.0), axis=-1, keepdims=True)
    dispatch(1, (gate * cot).astype(BF16))
    chunk = D
    chunks = z.FF // chunk
    steps.run_rest(14)

    arrivals(0)
    rows_in = r.exp_in[0].astype(F32).reshape(NG * C8, D).astype(BF16)
    r.out_acc[...] = jnp.zeros_like(r.out_acc)

    def forward_step(c, carry):
        at = pl.ds(pl.multiple_of(c * chunk, chunk), chunk)
        pre = nn(rows_in, r.win[:, at])
        r.pre_scr[:, at] = pre
        phi, _ = normal_parts(pre)
        r.out_acc[...] += nn((pre * phi).astype(BF16), r.wout[at, :])
        return carry

    lax.fori_loop(0, chunks, forward_step, 0)
    give_back(0, r.out_acc[...])

    arrivals(1)
    grad_out = r.exp_in[1].astype(F32).reshape(NG * C8, D).astype(BF16)
    r.out_acc[...] = jnp.zeros_like(r.out_acc)

    def backward_step(c, carry):
        at = pl.ds(pl.multiple_of(c * chunk, chunk), chunk)
        pre = r.pre_scr[:, at]
        phi, bell = normal_parts(pre)
        gh = nt(grad_out, r.wout[at, :]).astype(BF16).astype(F32)
        gp = (gh * (phi + pre * bell * INV_ROOT_TWO_PI)).astype(BF16)
        r.out_acc[...] += nt(gp, r.win[:, at])
        return carry

    lax.fori_loop(0, chunks, backward_step, 0)
    give_back(1, r.out_acc[...])
    share_slots(0)
    share_slots(1)
    steps.run_rest(10)

    expert_rows = returns(0)
    r.layer_ref[...] = (middle + gate * expert_rows).astype(BF16)
    grad_gate = jnp.sum(cot * expert_rows, axis=-1, keepdims=True)
    grad_probs = jnp.where(chosen, grad_gate, 0.0) + share
    inner = jnp.sum(probs * grad_probs, axis=-1, keepdims=True)
    grad_logits = (probs * (grad_probs - inner)).astype(BF16)
    from_router = nt(grad_logits, router)
    grad_routed = returns(1) + from_router
    scaled = grad_routed * gain
    mean = jnp.mean(scaled * middle, axis=-1, keepdims=True)
    gmid = cot + inverse * scaled - middle * (inverse * inverse * inverse) * mean
    r.gmid[...] = gmid
    low_mid = gmid.astype(BF16)
    gatt = nt(low_mid, r.wo[...]).astype(BF16)

    for n in range(HEAD_COUNT):
        r.gatt[n] = both_halves(gatt[:, n * HEAD_SIZE : (n + 1) * HEAD_SIZE])
        hb, hh = z.holder(n)
        out.put(
            r.gatt.at[n], r.do_in.at[s], r.do_r.at[s], (d, hb, hh), jnp.logical_not(p.owns(n))
        )

        @pl.when(p.owns(n))
        def _():
            r.do_in[s] = r.gatt[n]

    term = grad_routed * middle * inverse
    high = term.astype(BF16)
    rest = (term - high.astype(F32)).astype(BF16)
    ones = jnp.broadcast_to((lane == E).astype(BF16), (PT, LANES))
    small = tn(routed, grad_logits) + tn(high, ones) + tn(rest, ones)
    terms = jnp.concatenate([tn(att, low_mid), small], axis=1)
    for t in range(z.ndev):
        r.dwo[t % nh, t // nh] = terms[t * z.R : (t + 1) * z.R].astype(BF16)
    pass_slots(0)
    pass_slots(1)

    def finish():
        for part in range(2):
            for hh in (hc, hyc):
                got_slots(part, hh)
        for c in copies:
            c.wait()
        out.finish()

    return finish


def backward_phase(z, r, p, steps):
    d, b, h, s, me, hd, active = p.d, p.b, p.h, p.s, p.me, p.hd, p.active
    hy, hc, hyc = p.hy, p.hc, p.hyc
    nb, nh, nd, ns, nv, NG = z.n_blk, z.n_head, z.n_dp, z.ns, z.ndev, z.NG
    D, R, PT, HS, E = z.D, z.R, z.PT, HEAD_SIZE, z.E

    def sum_in(dst, src, terms, count):
        def body(e, carry):
            acc = src(e).astype(F32)
            for term in terms:
                acc = acc + term(e).astype(F32)
            dst[e] = acc.astype(BF16)
            return carry

        lax.fori_loop(0, count, body, 0)

    sums = Sends(r.su_s)
    y_sum = r.core_in.at[0]

    def got_sum(ref, k):
        remote(ref, ref, r.su_s.at[0], r.su_r.at[k], (d, b, hc)).wait_recv()

    def stage_core():
        sums.put(r.dwo.at[hyc], r.core_in.at[0], r.su_r.at[0], (d, b, hc))
        sums.put(r.dwo.at[hc], r.core_in.at[1], r.su_r.at[1], (d, b, hc))

    def stage_y():
        got_sum(r.core_in.at[0], 0)
        sum_in(r.y_src, lambda e: r.dwo[hy, e], [lambda e: r.core_in[0, e]], NG)
        sums.put(r.y_src, r.y_in, r.su_r.at[2], (d, b, hy))

    def stage_dp():
        got_sum(r.core_in.at[1], 1)
        got_sum(r.y_in, 2)
        sum_in(
            y_sum, lambda e: r.dwo[h, e], [lambda e: r.core_in[1, e], lambda e: r.y_in[e]], NG
        )
        for k in range(1, nd):
            q = lax.rem(d + k, nd)
            sums.put(y_sum.at[pl.ds(q * nb, nb)], r.dp_in.at[d], r.su_r.at[3 + d], (q, b, h))

    def stage_blk():
        others = [lax.rem(d + k, nd) for k in range(1, nd)]
        for q in others:
            got_sum(r.dp_in.at[q], 3 + q)

        def body(e, carry):
            acc = y_sum[d * nb + e].astype(F32)
            for q in others:
                acc = acc + r.dp_in[q, e].astype(F32)
            r.blk_src[e] = acc.astype(BF16)
            return carry

        lax.fori_loop(0, nb, body, 0)
        for k in range(1, nb):
            e = lax.rem(b + k, nb)
            sums.put(r.blk_src.at[e], r.blk_in.at[b], r.su_r.at[3 + nd + b], (d, e, h))
        r.blk_in[b] = r.blk_src[b]

    stage_core()

    def send_dq(t):
        return remote(
            r.dqkv.at[t], r.dq_in.at[hd], r.dq_s.at[t], r.dq_r.at[hd], (d, t // nh, t % nh)
        )

    def send_dw(k):
        t, device = p.any_peer(k)
        slot = d * HEAD_COUNT + hd
        return remote(r.dw3.at[t], r.dw_in.at[slot], r.dw_s.at[k], r.dw_r.at[slot], device)

    per = z.per
    part_rows = BLOCK // 2

    @pl.when(active)
    def _():
        r.dkv[...] = jnp.zeros_like(r.dkv)
        r.dq_acc[...] = jnp.zeros_like(r.dq_acc)
        r.dw[...] = jnp.zeros_like(r.dw)
        r.diag[...] = jnp.zeros_like(r.diag)
        r.sub[...] = jnp.zeros_like(r.sub)
        r.far[...] = jnp.zeros_like(r.far)

        def got_do(k, carry):
            t = lax.rem(s + k, ns)
            ref = r.do_in.at[t]
            remote(ref, ref, r.ex_s.at[0], r.do_r.at[t], p.in_sequence(t)).wait_recv()
            return carry

        lax.fori_loop(1, ns, got_do, 0)
        ones = jnp.ones((8, HS), BF16)
        for i in range(z.nq):
            here = slice(i * BLOCK, (i + 1) * BLOCK)
            pairs = [r.do_in[i * per + u] for u in range(per)]
            do = jnp.concatenate(
                [side for pair in pairs for side in (pair[:, :HS], pair[:, HS:])], axis=0
            )
            do = (do.astype(F32) * r.attl[here, HS:]).astype(BF16)
            r.dos[here, :] = do
            prod = do.astype(F32) * r.attl[here, :HS]
            high = prod.astype(BF16)
            rest = (prod - high.astype(F32)).astype(BF16)
            r.delta[i] = nt(ones, high) + nt(ones, rest)

    def tile(i, j, u):
        at = slice(j * BLOCK + u * part_rows, j * BLOCK + (u + 1) * part_rows)
        here = slice(i * BLOCK, (i + 1) * BLOCK)
        pr = r.probs[i, at, :]
        do = r.dos[here, :]
        ds = pr.astype(F32) * (nt(r.qkv[at, 2 * HS :], do) - r.delta[i, 0:1, :])
        low = ds.astype(BF16)
        part = slice(u * part_rows, (u + 1) * part_rows)
        if j == i:
            r.diag[part, :] += low.astype(F32)
        elif j == i - 1:
            r.sub[part, :] += low.astype(F32)
        else:
            r.far[...] += jnp.sum(low.astype(F32).reshape(part_rows // 8, 8, BLOCK), axis=0)
        both = jnp.concatenate([nn(low, r.qkv[here, :HS]), nn(pr, do)], axis=1)
        return at, both, nn(r.k_t[:, at], low)

    def column(j, hi):
        for u in range(2):
            acc = jnp.zeros((part_rows, 2 * HS), F32)
            for i in range(j, hi + 1):
                at, both, dq = tile(i, j, u)
                acc = acc + both
                r.dq_acc[i] += dq
            r.dkv[at, :] += acc

    def row(i, lo):
        acc = jnp.zeros((HS, BLOCK), F32)
        for j in range(lo, i + 1):
            for u in range(2):
                at, both, dq = tile(i, j, u)
                r.dkv[at, :] += both
                acc = acc + dq
        r.dq_acc[i] += acc

    lo, hi = 0, z.nq - 1
    turn = 0
    while lo <= hi:
        if turn == 1:
            stage_y()
        if turn == 3:
            stage_dp()
        if turn == z.nq - 1:
            stage_blk()

        @pl.when(active)
        def _():
            if turn % 2 == 0:
                n = lo
                column(n, hi)
            else:
                n = hi
                row(n, lo)
            here = slice(n * BLOCK, (n + 1) * BLOCK)
            dq = jnp.transpose(r.dq_acc[n]) * HS ** (-0.5)
            parts = jnp.concatenate([dq, r.dkv[here, :]], axis=1).astype(BF16)
            r.dw[...] += tn(r.xg[n * per : (n + 1) * per].reshape(BLOCK, D), parts)
            for u in range(per):
                t = n * per + u
                piece = parts[u * PT : (u + 1) * PT]
                r.dqkv[t, :PT] = piece[:, : 2 * HS]
                r.dqkv[t, PT:] = both_halves(piece[:, 2 * HS :])

                @pl.when(t != s)
                def _():
                    send_dq(t).start()

                @pl.when(t == s)
                def _():
                    r.dq_in[hd] = r.dqkv[t]

        if turn % 2 == 0:
            lo += 1
        else:
            hi -= 1
        turn += 1
        steps.run_rest(6)

    @pl.when(active)
    def _():
        jj = lax.broadcasted_iota(jnp.int32, (BLOCK, BLOCK), 0)
        ii = lax.broadcasted_iota(jnp.int32, (BLOCK, BLOCK), 1)
        lane = lax.broadcasted_iota(jnp.int32, (1, HS), 1)
        sums_of = jnp.zeros((1, HS), F32)
        half = BUCKETS // 2
        bounds = (0,) + LIMITS + (1 << 30,)
        tile_d, tile_s = r.diag[...], r.sub[...]

        def total(values):
            return jnp.sum(jnp.sum(values, axis=0, keepdims=True), axis=1, keepdims=True)

        for n in range(half):
            near, beyond = bounds[n], bounds[n + 1]
            dist = ii - jj
            part = total(
                jnp.where((dist >= near) & (dist < beyond), tile_d, 0.0)
                + jnp.where((dist + BLOCK >= near) & (dist + BLOCK < beyond), tile_s, 0.0)
            )
            if n == half - 1:
                part = part + total(r.far[...])
            sums_of = sums_of + jnp.where(lane == n, part, 0.0)
            if n > 0:
                part = total(jnp.where((-dist >= near) & (-dist < beyond), tile_d, 0.0))
                sums_of = sums_of + jnp.where(lane == half + n, part, 0.0)
        wide = jnp.concatenate([r.dw[...], jnp.broadcast_to(sums_of, (D, HS))], axis=1)
        split_rows(r.dw3, wide, R)

        def start_dw(k, carry):
            send_dw(k).start()
            return carry

        lax.fori_loop(1, nv, start_dw, 0)
        r.dw_in[d * HEAD_COUNT + hd] = r.dw3[me]

    steps.finish_rest()
    load = [
        pltpu.make_async_copy(r.wg_ref.at[:, :, pl.ds(m * D, D)], r.w3.at[m], r.loc.at[5 + m])
        for m in range(3)
    ]
    for c in load:
        c.start()
    for m, c in enumerate(load):
        c.wait()
        r.wfull[:, m * D : (m + 1) * D] = flatten_rows(r.w3[m]).astype(BF16)

    for k in range(1, nb):
        e = lax.rem(b + k, nb)
        got_sum(r.blk_in.at[e], 3 + nd + e)
    acc = r.blk_in[0].astype(F32)
    for e in range(1, nb):
        acc = acc + r.blk_in[e].astype(F32)
    eye = lax.broadcasted_iota(jnp.int32, (R, R), 0) == lax.broadcasted_iota(jnp.int32, (R, R), 1)

    def as_row(column):
        return jnp.sum(jnp.where(eye, column, 0.0), axis=0, keepdims=True)

    r.go_ref[...] = acc[:, :D]
    r.router_out[...] = jnp.concatenate([as_row(acc[:, D + e : D + e + 1]) for e in range(E)], axis=0)
    r.gain2_ref[...] = as_row(acc[:, D + E : D + E + 1])

    for n in range(HEAD_COUNT):
        hb, hh = z.holder(n)

        @pl.when(jnp.logical_not(p.owns(n)))
        def _():
            ref = r.dq_in.at[n]
            remote(ref, ref, r.dq_s.at[0], r.dq_r.at[n], (d, hb, hh)).wait_recv()

        for m in range(2):
            r.grad_cat[:, m * D + n * HS : m * D + (n + 1) * HS] = r.dq_in[
                n, :PT, m * HS : (m + 1) * HS
            ]
        at = slice(2 * D + n * HS, 2 * D + (n + 1) * HS)
        r.grad_cat[: PT // 2, at] = r.dq_in[n, PT:, :HS]
        r.grad_cat[PT // 2 :, at] = r.dq_in[n, PT:, HS:]
    grad_normed = nt(r.grad_cat[...], r.wfull[...])
    x = r.x_own[...].astype(F32)
    inverse = lax.rsqrt(jnp.mean(x * x, axis=-1, keepdims=True) + EPSILON)
    scaled = grad_normed * r.gain1[...]
    mean = jnp.mean(scaled * x, axis=-1, keepdims=True)
    grad_in = inverse * scaled - x * (inverse * inverse * inverse) * mean
    r.gtok_ref[...] = (r.gmid[...] + grad_in).astype(BF16)

    for dd in range(nd):
        for n in range(HEAD_COUNT):
            hb, hh = z.holder(n)

            @pl.when(jnp.logical_not(p.owns(n) & (d == dd)))
            def _():
                ref = r.dw_in.at[dd * HEAD_COUNT + n]
                remote(
                    ref, ref, r.dw_s.at[0], r.dw_r.at[dd * HEAD_COUNT + n], (dd, hb, hh)
                ).wait_recv()

    lane = lax.broadcasted_iota(jnp.int32, (1, BUCKETS), 1)
    slot_lane = lax.broadcasted_iota(jnp.int32, (1, z.RL), 1)
    own_table = jnp.zeros((1, z.RL), F32)
    first = jnp.zeros((R, 1), F32)
    for n in range(HEAD_COUNT):
        part = r.dw_in[n].astype(F32)
        for dd in range(1, nd):
            part = part + r.dw_in[dd * HEAD_COUNT + n].astype(F32)
        for m, out in enumerate((r.gq_ref, r.gk_ref, r.gv_ref)):
            cols = part[:, m * HS : (m + 1) * HS]
            out[:, n * HS : (n + 1) * HS] = cols
            own = r.w_own[:, m * D + n * HS : m * D + (n + 1) * HS].astype(F32)
            first = first + jnp.sum(cols * own, axis=-1, keepdims=True)
        line = part[0:1, 3 * HS : 3 * HS + BUCKETS]
        for k in range(z.RL):
            hit = lane + n * BUCKETS == me * z.RL + k
            value = jnp.sum(jnp.where(hit, line, 0.0), axis=1, keepdims=True)
            own_table = own_table + jnp.where(slot_lane == k, value, 0.0)
    own_gain = r.w_own[:, 4 * D :].astype(F32)[:, E : E + 1]
    r.gain1_ref[...] = as_row(first / own_gain)
    r.table_ref[...] = own_table

    sums.finish()

    @pl.when(active)
    def _():
        for t in range(ns):

            @pl.when(t != s)
            def _():
                send_dq(t).wait_send()

        def sent_dw(k, carry):
            send_dw(k).wait_send()
            return carry

        lax.fori_loop(1, nv, sent_dw, 0)


def layer(z, x, order, ids, rows, weights, router_t, w_in, w_out, cot):
    D, R, PT, S, HS, E, NG, C8 = z.D, z.R, z.PT, z.S, HEAD_SIZE, z.E, z.NG, z.cap8
    nb, nd, nh, ns, nv = z.n_blk, z.n_dp, z.n_head, z.ns, z.ndev
    dma = pltpu.SemaphoreType.DMA
    vmem = pl.BlockSpec(memory_space=pltpu.VMEM)
    hbm = pl.BlockSpec(memory_space=pl.ANY)
    shape = jax.ShapeDtypeStruct
    inputs = {
        "x_ref": (x, hbm),
        "order_ref": (order, vmem),
        "ids_ref": (ids, hbm),
        "rows_ref": (rows, vmem),
        "wq_ref": (weights[0], hbm),
        "wk_ref": (weights[1], hbm),
        "wv_ref": (weights[2], hbm),
        "wo_ref": (weights[3], hbm),
        "router_ref": (router_t, vmem),
        "win_ref": (w_in, hbm),
        "wout_ref": (w_out, hbm),
        "cot_ref": (cot, hbm),
    }
    outputs = {
        "wg_ref": (shape((nv, R, z.wide), BF16), hbm),
        "slots_ref": (shape((2, nh, NG, C8, D), BF16), hbm),
        "layer_ref": (shape((PT, D), BF16), vmem),
        "gtok_ref": (shape((PT, D), BF16), vmem),
        "gain1_ref": (shape((1, R), F32), vmem),
        "gq_ref": (shape((R, D), F32), vmem),
        "gk_ref": (shape((R, D), F32), vmem),
        "gv_ref": (shape((R, D), F32), vmem),
        "go_ref": (shape((R, D), F32), vmem),
        "table_ref": (shape((1, z.RL), F32), vmem),
        "gain2_ref": (shape((1, R), F32), vmem),
        "router_out": (shape((E, R), F32), vmem),
    }
    V = pltpu.VMEM
    terms = D + LANES
    scratch = {
        "w_own": V((R, z.wide), BF16),
        "x_own": V((PT, D), BF16),
        "cot": V((PT, D), BF16),
        "ids": V(ids.shape, jnp.int32),
        "win": V((D, z.FF), BF16),
        "wout": V((z.FF, D), BF16),
        "slices": V((HEAD_COUNT, R, 4 * HS), BF16),
        "slices_in": V((nv, R, 4 * HS), BF16),
        "xg": V((ns, PT, D), BF16),
        "wh": V((D, 3 * HS), BF16),
        "gain1": V((1, D), F32),
        "far_bias": V((1, 1), F32),
        "bias_d": V((BLOCK, BLOCK), F32),
        "bias_s": V((BLOCK, BLOCK), F32),
        "qkv": V((S, 3 * HS), BF16),
        "v_t": V((HS, S), BF16),
        "k_t": V((HS, S), BF16),
        "s_scr": V((S, BLOCK), F32),
        "probs": V((z.nq, S, BLOCK), BF16),
        "attl": V((S, 2 * HS), F32),
        "att_src": V((ns, PT // 2, 2 * HS), BF16),
        "att_in": V((HEAD_COUNT, PT // 2, 2 * HS), BF16),
        "misc3": V((nv, R, LANES), BF16),
        "wo": V((D, D), BF16),
        "route": V((E * C8, PT), F32),
        "att_cat": V((PT, D), BF16),
        "disp": V((2, E, C8, D), BF16),
        "exp_in": V((2, NG, C8, D), BF16),
        "ret": V((2, NG, C8, D), BF16),
        "back": V((2, E, C8, D), BF16),
        "pre_scr": V((NG * C8, z.FF), F32),
        "out_acc": V((NG * C8, D), F32),
        "gmid": V((PT, D), F32),
        "gatt": V((HEAD_COUNT, PT // 2, 2 * HS), BF16),
        "do_in": V((ns, PT // 2, 2 * HS), BF16),
        "dwo": V((nh, NG, R, terms), BF16),
        "core_in": V((2, NG, R, terms), BF16),
        "y_src": V((NG, R, terms), BF16),
        "y_in": V((NG, R, terms), BF16),
        "dp_in": V((nd, nb, R, terms), BF16),
        "blk_src": V((nb, R, terms), BF16),
        "blk_in": V((nb, R, terms), BF16),
        "dos": V((S, HS), BF16),
        "delta": V((z.nq, 8, BLOCK), F32),
        "dq_acc": V((z.nq, HS, BLOCK), F32),
        "dw": V((D, 3 * HS), F32),
        "dw3": V((nv, R, 4 * HS), BF16),
        "diag": V((BLOCK, BLOCK), F32),
        "sub": V((BLOCK, BLOCK), F32),
        "far": V((8, BLOCK), F32),
        "dqkv": V((ns, PT + PT // 2, 2 * HS), BF16),
        "dq_in": V((HEAD_COUNT, PT + PT // 2, 2 * HS), BF16),
        "dw_in": V((nd * HEAD_COUNT, R, 4 * HS), BF16),
        "w3": V((3, nv, R, D), BF16),
        "wfull": V((D, 3 * D), BF16),
        "grad_cat": V((PT, 3 * D), BF16),
        "in_sem": dma((9,)),
        "loc": dma((8,)),
        "sl_s": dma((HEAD_COUNT,)),
        "sl_r": dma((nv,)),
        "sd_s": dma((ns * nd,)),
        "x_s": dma((2 * (4 + 6 * (nb - 1) + 2 * nb - 1),)),
        "x_r": dma((2 * ns,)),
        "w0_s": dma((spread_copies(z, False),)),
        "w0_r": dma((nv,)),
        "w1_s": dma((spread_copies(z, True),)),
        "w1_r": dma((nv,)),
        "w2_s": dma((spread_copies(z, False),)),
        "w2_r": dma((nv,)),
        "at_s": dma((ns,)),
        "at_r": dma((HEAD_COUNT,)),
        "ex_s": dma((4 * (NG - 1) + 6 + HEAD_COUNT,)),
        "ex_r": dma((2 * NG,)),
        "rt_r": dma((2 * NG,)),
        "all_r": dma((2 * nh,)),
        "do_r": dma((ns,)),
        "su_s": dma((3 + nd - 1 + nb - 1,)),
        "su_r": dma((3 + nd + nb,)),
        "dq_s": dma((ns,)),
        "dq_r": dma((HEAD_COUNT,)),
        "dw_s": dma((nv,)),
        "dw_r": dma((nd * HEAD_COUNT,)),
    }
    names = tuple(inputs) + tuple(outputs) + tuple(scratch)
    results = pl.pallas_call(
        functools.partial(layer_kernel, z, names),
        out_shape=tuple(v[0] for v in outputs.values()),
        in_specs=[v[1] for v in inputs.values()],
        out_specs=tuple(v[1] for v in outputs.values()),
        scratch_shapes=list(scratch.values()),
        compiler_params=pltpu.CompilerParams(
            collective_id=0, has_side_effects=True, vmem_limit_bytes=VMEM_LIMIT
        ),
        name="layer",
    )(*[v[0] for v in inputs.values()])
    return dict(zip(outputs, results))


PASSED = (
    "layer_ref", "gtok_ref", "gain1_ref", "gq_ref", "gk_ref", "gv_ref", "go_ref", "table_ref",
    "gain2_ref", "router_out",
)


def expert_kernel(z, slots_ref, win_ref, wout_ref, *refs):
    count = len(PASSED)
    passed_in, (gin_ref, gout_ref) = refs[:count], refs[count : count + 2]
    passed_out = refs[count + 2 : 2 * count + 2]
    rows_in, rows_t, grad_out, sem = refs[2 * count + 2 :]
    step = pl.program_id(0)

    def passing(n):
        return pltpu.make_async_copy(passed_in[n], passed_out[n], sem.at[n])

    @pl.when(step == 0)
    def _():
        for n in range(len(PASSED)):
            passing(n).start()
        for n in range(z.n_head):
            count = z.NG * z.cap8
            at = slice(n * count, (n + 1) * count)
            rows_in[at, :] = slots_ref[0, n].astype(F32).reshape(count, z.D).astype(BF16)
            grad_out[at, :] = slots_ref[1, n].astype(F32).reshape(count, z.D).astype(BF16)
        rows_t[...] = jnp.transpose(rows_in[...])

    w1 = win_ref[0]
    w2 = wout_ref[0]
    pre = nn(rows_in[...], w1)
    phi, bell = normal_parts(pre)
    hidden = (pre * phi).astype(BF16)
    gh = nt(grad_out[...], w2).astype(BF16).astype(F32)
    gp = (gh * (phi + pre * bell * INV_ROOT_TWO_PI)).astype(BF16)
    gin_ref[0] = nn(rows_t[...], gp)
    gout_ref[0] = tn(hidden, grad_out[...])

    @pl.when(step == pl.num_programs(0) - 1)
    def _():
        for n in range(len(PASSED)):
            passing(n).wait()


def expert_weights(z, slots, w_in, w_out, passed):
    chunk = 512
    hbm = pl.BlockSpec(memory_space=pl.ANY)
    total = z.n_head * z.NG * z.cap8
    in_chunk = pl.BlockSpec((1, z.D, chunk), lambda i: (0, 0, i))
    out_chunk = pl.BlockSpec((1, chunk, z.D), lambda i: (0, i, 0))
    return pl.pallas_call(
        functools.partial(expert_kernel, z),
        grid=(z.FF // chunk,),
        out_shape=(
            jax.ShapeDtypeStruct((1, z.D, z.FF), F32),
            jax.ShapeDtypeStruct((1, z.FF, z.D), F32),
        )
        + tuple(jax.ShapeDtypeStruct(a.shape, a.dtype) for a in passed),
        in_specs=[pl.BlockSpec(memory_space=pltpu.VMEM), in_chunk, out_chunk] + [hbm] * len(passed),
        out_specs=(in_chunk, out_chunk) + (hbm,) * len(passed),
        scratch_shapes=[
            pltpu.VMEM((total, z.D), BF16),
            pltpu.VMEM((z.D, total), BF16),
            pltpu.VMEM((total, z.D), BF16),
            pltpu.SemaphoreType.DMA((len(passed),)),
        ],
        compiler_params=pltpu.CompilerParams(
            dimension_semantics=("arbitrary",), vmem_limit_bytes=48 * 1024 * 1024
        ),
        name="expert_weight_grads",
    )(slots, w_in, w_out, *passed)


def local(
    sizes,
    tokens,
    order,
    expert_ids,
    norm1_gain,
    w_query,
    w_key,
    w_value,
    w_attn_out,
    rel_table,
    norm2_gain,
    w_router,
    w_in,
    w_out,
    cotangent,
):
    R, D = w_query.shape
    E = w_router.shape[1]
    z = Sizes(*sizes, R, D, E, w_in.shape[2], tokens.shape[1])
    rel = jnp.pad(rel_table, (0, R - rel_table.shape[0]))
    rows = jnp.stack([norm1_gain, norm2_gain, rel]).astype(F32)
    out = layer(
        z,
        tokens.reshape(z.PT, D),
        order,
        expert_ids.reshape(-1, z.PT),
        rows,
        (w_query, w_key, w_value, w_attn_out),
        w_router.T,
        w_in,
        w_out,
        cotangent.reshape(z.PT, D),
    )
    g_in, g_out, *rest = expert_weights(
        z, out["slots_ref"], w_in, w_out, [out[name] for name in PASSED]
    )
    layer_out, gtok, gain1, gq, gk, gv, go, table, gain2, router = rest
    return (
        layer_out.reshape(tokens.shape),
        gtok.reshape(tokens.shape),
        gain1.reshape(R),
        gq,
        gk,
        gv,
        go,
        table.reshape(z.RL),
        gain2.reshape(R),
        router.T,
        g_in,
        g_out,
    )


def solution(mesh):
    everywhere = ("dp", "blk", "head")
    rows, table = P(everywhere), P(everywhere, None)
    tokens = P("dp", ("blk", "head"), None)
    expert = P(("dp", "blk"), None, None)
    in_specs = (
        tokens,
        P("dp", ("blk", "head")),
        P(),
        rows,
        table,
        table,
        table,
        table,
        rows,
        rows,
        table,
        expert,
        expert,
        tokens,
    )
    out_specs = (
        tokens, tokens, rows, table, table, table, table, rows, rows, table, expert, expert
    )
    sizes = (mesh.shape["dp"], mesh.shape["blk"], mesh.shape["head"])
    return jax.shard_map(
        functools.partial(local, sizes),
        mesh=mesh,
        in_specs=in_specs,
        out_specs=out_specs,
        check_vma=False,
    )
```

```python
import functools
import itertools
import types

import jax
import jax.numpy as jnp
from jax import lax
from jax.experimental import pallas as pl
from jax.experimental.pallas import tpu as pltpu
from jax.sharding import PartitionSpec as P

HEAD_COUNT = 12
HEAD_SIZE = 64
BUCKETS = 32
BLOCK = 256
EPSILON = 1e-06
AUX_WEIGHT = 1.0
LIMITS = (1, 2, 3, 4, 5, 6, 7, 8, 12, 16, 23, 32, 46, 64, 91)
INV_ROOT_TWO = 0.7071067811865476
INV_ROOT_TWO_PI = 0.3989422804014327
LANES = 128
VMEM_LIMIT = 62 * 1024 * 1024
PASSED = (
    "layer_ref", "gtok_ref", "gain1_ref", "gq_ref", "gk_ref", "gv_ref", "go_ref", "table_ref",
    "gain2_ref", "router_out",
)
MESH = pl.DeviceIdType.MESH
F32 = jnp.float32
BF16 = jnp.bfloat16


def both_halves(values):
    n = values.shape[0] // 2
    return jnp.concatenate([values[:n], values[n:]], axis=1)


def line_order(b, nb):
    out = [(b, b >= 0)]
    for k in range(1, nb):
        out.append((b - k, b >= k))
        out.append((b + k, b + k < nb))
    return out


class Sends:
    def __init__(self, sems):
        self.sems, self.made = sems, []

    def put(self, src, dst, recv, device, cond=None):
        c = remote(src, dst, self.sems.at[len(self.made)], recv, device)
        self.made.append((c, cond))
        self.each(c.start, cond)

    def each(self, action, cond):
        if cond is None:
            action()
        else:
            pl.when(cond)(action)

    def finish(self):
        for c, cond in self.made:
            self.each(c.wait_send, cond)


class Sizes:
    def __init__(self, n_dp, n_blk, n_head, rows, width, experts, hidden, piece):
        self.n_dp, self.n_blk, self.n_head = n_dp, n_blk, n_head
        self.ndev = n_dp * n_blk * n_head
        self.ns = n_blk * n_head
        self.R, self.D, self.E, self.FF, self.PT = rows, width, experts, hidden, piece
        self.S = piece * self.ns
        self.nq = self.S // BLOCK
        self.hb = HEAD_COUNT // n_blk
        self.cap = (5 * piece + 4 * experts - 1) // (4 * experts)
        self.cap8 = (self.cap + 7) // 8 * 8
        self.NG = n_dp * n_blk
        self.RL = HEAD_COUNT * BUCKETS // self.ndev
        self.wide = 4 * width + LANES
        self.per = BLOCK // piece
        assert self.hb < n_head and self.hb * n_blk == HEAD_COUNT
        assert experts == self.NG and n_head == 4


    def holder(self, n):
        return n // self.hb, n % self.hb + n // self.hb % 2


def nt(a, b):
    return lax.dot_general(a, b, (((1,), (1,)), ((), ())), preferred_element_type=F32)


def tn(a, b):
    return lax.dot_general(a, b, (((0,), (0,)), ((), ())), preferred_element_type=F32)


def nn(a, b):
    return jnp.dot(a, b, preferred_element_type=F32)


def place():
    return lax.axis_index("dp"), lax.axis_index("blk"), lax.axis_index("head")


def signal(device):
    pl.semaphore_signal(
        pltpu.get_barrier_semaphore(), inc=1, device_id=device, device_id_type=MESH
    )


def await_barrier(count):
    pl.semaphore_wait(pltpu.get_barrier_semaphore(), count)


def remote(src, dst, send, recv, device):
    return pltpu.make_async_remote_copy(
        src_ref=src, dst_ref=dst, send_sem=send, recv_sem=recv, device_id=device, device_id_type=MESH
    )


def flatten_rows(blocks):
    count, rows, lanes = blocks.shape
    wide = blocks.astype(F32)
    if rows % 8 == 0:
        return wide.reshape(count * rows, lanes)
    return jnp.concatenate([wide[i] for i in range(count)], axis=0)


def split_rows(dst_ref, values, rows):
    count = values.shape[0] // rows
    if rows % 8 == 0:
        dst_ref[...] = values.reshape(count, rows, values.shape[1]).astype(dst_ref.dtype)
    else:
        for i in range(count):
            dst_ref[i] = values[i * rows : (i + 1) * rows].astype(dst_ref.dtype)


def activate(pre):
    phi, bell = normal_parts(pre)
    slope = phi + pre * bell * INV_ROOT_TWO_PI
    return (pre * phi).astype(BF16), slope.astype(BF16)


def grad_pre(grad_out, w, slope):
    hidden = nt(grad_out, w).astype(BF16).astype(F32)
    return (hidden * slope.astype(F32)).astype(BF16)


def normal_parts(v):
    bell = jnp.exp(-0.5 * v * v)
    t = 1.0 / (1.0 + (0.3275911 * INV_ROOT_TWO) * jnp.abs(v))
    poly = t * (
        0.254829592
        + t * (-0.284496736 + t * (1.421413741 + t * (-1.453152027 + t * 1.061405429)))
    )
    tail = 0.5 * poly * bell
    return jnp.where(v >= 0, 1.0 - tail, tail), bell


def bias_tile(table, shift):
    j = lax.broadcasted_iota(jnp.int32, (BLOCK, BLOCK), 0)
    i = lax.broadcasted_iota(jnp.int32, (BLOCK, BLOCK), 1)
    dist = j - i + shift
    mag = jnp.abs(dist)
    half = BUCKETS // 2
    out = jnp.broadcast_to(table[0:1, 0:1], (BLOCK, BLOCK))
    for n, limit in enumerate(LIMITS):
        low = table[n + 1 : n + 2, 0:1]
        if shift == 0:
            high = table[half + n + 1 : half + n + 2, 0:1]
            out = jnp.where(mag >= limit, jnp.where(dist > 0, high, low), out)
        else:
            out = jnp.where(mag >= limit, low, out)
    return out


class Spread:
    def __init__(self, z, src, dst, send, recv, y_first, lanes):
        self.z, self.src, self.dst, self.recv = z, src, dst, recv
        self.sends, self.lanes = Sends(send), lanes
        d, b, h = place()
        self.at = (d, b, h)
        nh, nd = z.n_head, z.n_dp
        self.hy = lax.rem(h + 2, nh)
        self.hc = h + 1 - 2 * lax.rem(h, 2)
        self.hyc = lax.rem(self.hc + 2, nh)
        dto = [lax.rem(d + k, nd) for k in range(1, nd)]
        dfrom = [lax.rem(d + nd - k, nd) for k in range(1, nd)]
        ys = ([(d, self.hy)], [(d, self.hy)])
        xs = ([(p, h) for p in dto], [(p, h) for p in dfrom])
        self.first, self.second = (ys, xs) if y_first else (xs, ys)
        if y_first:
            self.second_slots = [(p, hh) for p in dfrom for hh in (h, self.hy)]
        else:
            self.second_slots = [(p, self.hy) for p in [d] + dfrom]
        self.core_slots = [(p, hh) for p in [d] + dfrom for hh in (self.hc, self.hyc)]

    def slot(self, dd, bb, hh):
        return (dd * self.z.n_blk + bb) * self.z.n_head + hh

    def ref(self, slot):
        return self.dst.at[slot, :, self.lanes]

    def put(self, src, slot, device, cond=None):
        self.sends.put(src, self.ref(slot), self.recv.at[slot], device, cond)

    def got(self, slot):
        d, b, h = self.at
        ref = self.ref(slot)
        remote(ref, ref, self.sends.sems.at[0], self.recv.at[slot], (d, b, self.hc)).wait_recv()

    def steps(self):
        d, b, h = self.at
        nb = self.z.n_blk

        def begin():
            mine = self.slot(d, b, h)
            self.put(self.src, mine, (d, b + 1, h), b + 1 < nb)
            self.put(self.src, mine, (d, b - 1, h), b >= 1)
            for dd, hh in self.first[0] + self.second[0] + [(d, self.hc)]:
                self.put(self.src, mine, (dd, b, hh))

        def line_arrival(k):
            for f, cond, to, more in (
                (b - k, b >= k, b + 1, b + 1 < nb),
                (b + k, b + k < nb, b - 1, b >= 1),
            ):
                slot = self.slot(d, f, h)
                pl.when(cond)(functools.partial(self.got, slot))
                if k < nb - 1:
                    self.put(self.ref(slot), slot, (d, to, h), cond & more)
                for dd, hh in self.first[0] + self.second[0] + [(d, self.hc)]:
                    self.put(self.ref(slot), slot, (dd, b, hh), cond)

        def first_arrival(p, f, cond):
            slot = self.slot(p[0], f, p[1])
            pl.when(cond)(functools.partial(self.got, slot))
            for dd, hh in self.second[0] + [(d, self.hc)]:
                self.put(self.ref(slot), slot, (dd, b, hh), cond)

        def second_arrival(p, f, cond):
            slot = self.slot(p[0], f, p[1])
            pl.when(cond)(functools.partial(self.got, slot))
            self.put(self.ref(slot), slot, (d, b, self.hc), cond)

        out = [begin]
        for k in range(1, nb):
            out.append(functools.partial(line_arrival, k))
        for p in self.first[1]:
            for f, cond in line_order(b, nb):
                out.append(functools.partial(first_arrival, p, f, cond))
        for p in self.second_slots:
            for f, cond in line_order(b, nb):
                out.append(functools.partial(second_arrival, p, f, cond))
        return out

    def finish(self):
        d, b, h = self.at
        for p in self.core_slots:
            for f in range(self.z.n_blk):
                self.got(self.slot(p[0], f, p[1]))
        self.sends.finish()


def spread_copies(z, y_first):
    nb, nd = z.n_blk, z.n_dp
    peers = 1 + nd - 1 + 1
    first = 1 if y_first else nd - 1
    second = peers - 1 - first
    second_slots = 2 * (nd - 1) if y_first else nd
    line = 2 * nb - 1
    return 2 + peers + (nb - 1) * 2 * (peers + 1) + first * line * (second + 1) + second_slots * line


class Place:
    def __init__(self, z):
        self.d, self.b, self.h = d, b, h = place()
        self.s = b * z.n_head + h
        self.me = d * z.ns + self.s
        self.g = d * z.n_blk + b
        first = lax.rem(b, 2)
        self.active = (h >= first) & (h < first + z.hb)
        self.hd = b * z.hb + jnp.clip(h - first, 0, z.hb - 1)
        self.hy = lax.rem(h + 2, z.n_head)
        self.hc = h + 1 - 2 * lax.rem(h, 2)
        self.hyc = lax.rem(self.hc + 2, z.n_head)
        self.z = z

    def any_peer(self, k):
        z = self.z
        t = lax.rem(self.me + k, z.ndev)
        return t, (t // z.ns, lax.rem(t // z.n_head, z.n_blk), lax.rem(t, z.n_head))

    def in_sequence(self, t):
        return (self.d, t // self.z.n_head, lax.rem(t, self.z.n_head))

    def owns(self, n):
        return self.active & (self.hd == n)

    def group(self, k):
        z = self.z
        e = lax.rem(self.g + k, z.NG)
        return e, (e // z.n_blk, lax.rem(e, z.n_blk), self.h)


def written(r, *names):
    for name in names:
        short = name.replace("_ref", "").replace("_out", "") + "_v"
        c = pltpu.make_async_copy(
            getattr(r, short), getattr(r, name), r.out_sem.at[PASSED.index(name)]
        )
        c.start()
        r.outgoing.append(c)


def layer_kernel(z, names, *refs):
    r = types.SimpleNamespace(**dict(zip(names, refs)))
    r.dkv = r.s_scr.at[:, pl.ds(0, 2 * HEAD_SIZE)]
    r.outgoing = []
    p = Place(z)

    def greet(k, carry):
        signal(p.any_peer(k)[1])
        return carry

    lax.fori_loop(1, z.ndev, greet, 0)
    D = z.D
    small = [
        pltpu.make_async_copy(ref, r.w_own.at[:, pl.ds(m * D, D)], r.in_sem.at[m])
        for m, ref in enumerate((r.wq_ref, r.wk_ref, r.wv_ref, r.wo_ref))
    ]
    small.append(pltpu.make_async_copy(r.x_ref, r.x_own, r.in_sem.at[4]))
    later = [
        pltpu.make_async_copy(r.cot_ref, r.cot, r.in_sem.at[5]),
        pltpu.make_async_copy(r.ids_ref, r.ids, r.in_sem.at[6]),
        pltpu.make_async_copy(r.win_ref.at[0], r.win, r.in_sem.at[7]),
        pltpu.make_async_copy(r.wout_ref.at[0], r.wout, r.in_sem.at[8]),
    ]
    for c in small + later:
        c.start()
    for c in small:
        c.wait()
    steps, finish_forward = forward_phase(z, r, p)
    for c in later:
        c.wait()
    last_slots, finish_middle = middle_phase(z, r, p, steps)
    backward_phase(z, r, p, steps, last_slots)
    finish_forward()
    finish_middle()
    for c in r.outgoing:
        c.wait()


def forward_phase(z, r, p):
    d, b, h, s, me, hd, active = p.d, p.b, p.h, p.s, p.me, p.hd, p.active
    hy, hc, hyc = p.hy, p.hc, p.hyc
    nb, nh, nd, ns = z.n_blk, z.n_head, z.n_dp, z.ns
    D, R, E, PT, HS = z.D, z.R, z.E, z.PT, HEAD_SIZE

    eye = lax.broadcasted_iota(jnp.int32, (R, R), 0) == lax.broadcasted_iota(jnp.int32, (R, R), 1)
    row_of = lax.broadcasted_iota(jnp.int32, (LANES, R), 0)
    tail = jnp.zeros((LANES, R), F32)
    rel = jnp.concatenate([r.rel_ref[...].astype(F32), jnp.zeros((1, R - z.RL), F32)], axis=1)
    rows = r.gain1_in[...].astype(F32), r.gain2_in[...].astype(F32), rel
    for n in range(3):
        tail = jnp.where(row_of == E + n, rows[n], tail)
    router_t = jnp.concatenate(
        [r.router_ref[...].astype(F32), jnp.zeros((LANES - E, R), F32)], axis=0
    )
    misc = nt(eye.astype(BF16), (tail + router_t).astype(BF16)).astype(BF16)
    r.w_own[:, 4 * D :] = misc
    for n in range(HEAD_COUNT):
        columns = [r.w_own[:, m * D + n * HS : m * D + (n + 1) * HS] for m in range(3)]
        r.slices[n] = jnp.concatenate(columns + [misc[:, E : E + HS]], axis=1)
    save_w = pltpu.make_async_copy(r.w_own, r.wg_ref.at[me], r.loc.at[0])
    save_w.start()
    await_barrier(z.ndev - 1)

    to_heads = Sends(r.sl_s)
    over_dp = Sends(r.sd_s)
    for n in range(HEAD_COUNT):
        hb, hh = z.holder(n)
        to_heads.put(
            r.slices.at[n], r.slices_in.at[me], r.sl_r.at[me], (d, hb, hh),
            jnp.logical_not(p.owns(n)),
        )

    tokens = Sends(r.x_s)
    pieces = 2
    rows_of = PT // pieces

    def xref(slot, c):
        return r.xg.at[slot, pl.ds(c * rows_of, rows_of)]

    def put(src, slot, c, device, cond=None):
        tokens.put(src, xref(slot, c), r.x_r.at[slot * pieces + c], device, cond)

    def got(slot, c):
        ref = xref(slot, c)
        remote(ref, ref, r.x_s.at[0], r.x_r.at[slot * pieces + c], (d, b, hc)).wait_recv()

    for c in range(pieces):
        own = r.x_own.at[pl.ds(c * rows_of, rows_of)]
        put(own, s, c, (d, b + 1, h), b + 1 < nb)
        put(own, s, c, (d, b - 1, h), b >= 1)
        put(own, s, c, (d, b, hy))
        put(own, s, c, (d, b, hc))
    r.xg[s] = r.x_own[...]

    @pl.when(active)
    def _():
        r.slices_in[me] = r.slices[hd]

    for k in range(1, nb):
        for c in range(pieces):
            for f, cond, to, more in (
                (b - k, b >= k, b + 1, b + 1 < nb),
                (b + k, b + k < nb, b - 1, b >= 1),
            ):
                slot = f * nh + h
                pl.when(cond)(functools.partial(got, slot, c))
                if k < nb - 1:
                    put(xref(slot, c), slot, c, (d, to, h), cond & more)
                put(xref(slot, c), slot, c, (d, b, hy), cond)
                put(xref(slot, c), slot, c, (d, b, hc), cond)
        if k == 1:
            for m in range(ns):
                t = lax.rem(s + m, ns)
                slot = d * ns + t
                ref = r.slices_in.at[slot]
                if m > 0:
                    c = remote(ref, ref, r.sl_s.at[0], r.sl_r.at[slot], p.in_sequence(t))
                    pl.when(active)(c.wait_recv)
                for kd in range(1, nd):
                    over_dp.put(ref, ref, r.sl_r.at[slot], (lax.rem(d + kd, nd), b, h), active)

    for f, cond in line_order(b, nb):
        for c in range(pieces):
            slot = f * nh + hy
            pl.when(cond)(functools.partial(got, slot, c))
            put(xref(slot, c), slot, c, (d, b, hc), cond)

    cuts = (3 * D, z.wide, False), (0, 3 * D // 2, True), (3 * D // 2, 3 * D, False)
    parts = [
        Spread(
            z, r.w_own.at[:, pl.ds(lo, hi - lo)], r.wg_ref,
            getattr(r, "w%d_s" % n), getattr(r, "w%d_r" % n), y_first, pl.ds(lo, hi - lo),
        )
        for n, (lo, hi, y_first) in enumerate(cuts)
    ]
    first, rest_a, rest_b = [part.steps() for part in parts]
    steps = []
    for k in range(nb):
        steps += [first.pop(0), rest_a.pop(0), rest_b.pop(0)]
    steps = Steps(steps + first, rest_a, rest_b, parts, save_w)

    steps.run(3)

    @pl.when(active)
    def _():
        for kd in range(1, nd):
            dd = lax.rem(d + kd, nd)

            def got_slice(t, carry):
                ref = r.slices_in.at[dd * ns + t]
                remote(ref, ref, r.sl_s.at[0], r.sl_r.at[dd * ns + t], (dd, b, h)).wait_recv()
                return carry

            lax.fori_loop(0, ns, got_slice, 0)

        rows = flatten_rows(r.slices_in[...])
        r.wh[:, : 2 * HS] = rows[:, : 2 * HS].astype(BF16)
        r.wh[:, :HS] = (rows[:, :HS] * HS ** (-0.5)).astype(BF16)
        r.wh[:, 2 * HS :] = rows[:, 2 * HS : 3 * HS].astype(BF16)
        r.gain1[...] = jnp.transpose(rows[:, LANES:])[HS : HS + 1, :]
        column = lax.broadcasted_iota(jnp.int32, (1, D), 1).astype(F32)
        owner = jnp.floor((column + 0.5) * (1.0 / R))
        place_of = column - owner * R
        entry = jnp.where(place_of < z.RL, owner * z.RL + place_of, -1.0)
        wanted = hd * BUCKETS + lax.broadcasted_iota(jnp.int32, (BUCKETS, D), 0)
        pick = (entry == wanted.astype(F32)).astype(BF16)
        table = nn(pick, rows[:, LANES:].astype(BF16))[:, HS + 2 : HS + 3]
        r.bias_d[...] = bias_tile(table, 0)
        r.bias_s[...] = bias_tile(table, -BLOCK)
        r.far_bias[...] = table[BUCKETS // 2 - 1 : BUCKETS // 2, 0:1]

    for f in range(nb):
        for c in range(pieces):
            got(f * nh + hc, c)
            got(f * nh + hyc, c)
    tokens.finish()
    per = z.per
    half = BLOCK // 2

    @pl.when(active)
    def _():
        for i in range(z.nq):
            here = slice(i * BLOCK, (i + 1) * BLOCK)
            x = r.xg[i * per : (i + 1) * per].reshape(BLOCK, D).astype(F32)
            inverse = lax.rsqrt(jnp.mean(x * x, axis=-1, keepdims=True) + EPSILON)
            low = (x * inverse * r.gain1[...]).astype(BF16)
            r.xg[i * per : (i + 1) * per] = low.reshape(per, PT, D)
            mixed = nn(low, r.wh[...])
            r.qkv[here, :] = mixed.astype(BF16)
            r.v_t[:, here] = jnp.transpose(mixed[:, 2 * HS :]).astype(BF16)
            r.k_t[:, here] = jnp.transpose(mixed[:, HS : 2 * HS]).astype(BF16)

    def send_att(t):
        return remote(
            r.att_src.at[t], r.att_in.at[hd], r.at_s.at[t], r.at_r.at[hd], (d, t // nh, t % nh)
        )

    low_rows, high_rows = range(z.nq // 2), range(z.nq // 2, z.nq)
    order = [i for pair in zip(reversed(high_rows), reversed(low_rows)) for i in pair]
    for i in order:
        steps.run(4)

        @pl.when(active)
        def _():
            here = slice(i * BLOCK, (i + 1) * BLOCK)
            q = r.qkv[here, :HS]
            top = jnp.full((8, BLOCK), -1e30, F32)
            far = r.far_bias[...]
            for j in range(i + 1):
                for u in range(2):
                    at = slice(j * BLOCK + u * half, j * BLOCK + (u + 1) * half)
                    part = slice(u * half, (u + 1) * half)
                    if j == i:
                        bias = r.bias_d[part, :]
                    elif j == i - 1:
                        bias = r.bias_s[part, :]
                    else:
                        bias = far
                    sc = nt(r.qkv[at, HS : 2 * HS], q) + bias
                    r.s_scr[at, :] = sc
                    top = jnp.maximum(top, jnp.max(sc.reshape(half // 8, 8, BLOCK), axis=0))
            top = jnp.max(top, axis=0, keepdims=True)
            total = jnp.zeros((8, BLOCK), F32)
            acc = jnp.zeros((HS, BLOCK), F32)
            for j in range(i + 1):
                for u in range(2):
                    at = slice(j * BLOCK + u * half, j * BLOCK + (u + 1) * half)
                    e = jnp.exp(r.s_scr[at, :] - top)
                    total = total + jnp.sum(e.reshape(half // 8, 8, BLOCK), axis=0)
                    r.probs[i, at, :] = e.astype(BF16)
                at = slice(j * BLOCK, (j + 1) * BLOCK)
                acc = acc + nn(r.v_t[:, at], r.probs[i, at, :])
            total = jnp.sum(total, axis=0, keepdims=True)
            both = jnp.concatenate([acc, jnp.broadcast_to(total, (HS, BLOCK))], axis=0)
            both = jnp.transpose(both)
            inv = 1.0 / both[:, HS:]
            att = (both[:, :HS] * inv).astype(BF16)
            r.attl[here, :] = jnp.concatenate([att.astype(F32), inv], axis=1)
            for u in range(per):
                t = i * per + u
                r.att_src[t] = both_halves(att[u * PT : (u + 1) * PT])

                @pl.when(t != s)
                def _():
                    send_att(t).start()

                @pl.when(t == s)
                def _():
                    r.att_in[hd] = r.att_src[t]

    def finish():
        to_heads.finish()
        over_dp.finish()

        @pl.when(active)
        def _():
            for t in range(ns):

                @pl.when(t != s)
                def _():
                    send_att(t).wait_send()

    return steps, finish


class Steps:
    def __init__(self, first, rest_a, rest_b, parts, save):
        self.first, self.parts, self.save = first, parts, save
        self.rest = [
            step
            for pair in itertools.zip_longest(rest_b, rest_a)
            for step in pair
            if step is not None
        ]

    def run(self, count):
        for _ in range(min(count, len(self.first))):
            self.first.pop(0)()

    def finish_first(self):
        self.run(len(self.first))
        self.parts[0].finish()
        self.save.wait()

    def run_rest(self, count):
        for _ in range(min(count, len(self.rest))):
            self.rest.pop(0)()

    def finish_rest(self):
        self.run_rest(len(self.rest))
        for part in self.parts[1:]:
            part.finish()


def middle_phase(z, r, p, steps):
    d, b, h, me, g, s = p.d, p.b, p.h, p.me, p.g, p.s
    hy, hc, hyc = p.hy, p.hc, p.hyc
    nb, nh, nd, ns = z.n_blk, z.n_head, z.n_dp, z.ns
    D, E, PT, NG, C8 = z.D, z.E, z.PT, z.NG, z.cap8

    ids_row = r.ids[pl.ds(me, 1), :]
    order_row = r.order_ref[...]
    ids_col = jnp.transpose(jnp.broadcast_to(ids_row, (PT, PT)))
    order_col = jnp.transpose(jnp.broadcast_to(order_row, (PT, PT)))
    earlier = (order_col < order_row) & (ids_col == ids_row)
    rank = jnp.sum(earlier.astype(jnp.int32), axis=0, keepdims=True)
    slot = lax.broadcasted_iota(jnp.int32, (C8, PT), 0)
    base = (rank == slot) & (slot < z.cap)
    lane = lax.broadcasted_iota(jnp.int32, (1, LANES), 1)
    share = jnp.zeros((1, LANES), F32)
    ids_all = r.ids[...]
    for e in range(E):
        r.route[e * C8 : (e + 1) * C8, :] = (base & (ids_row == e)).astype(F32)
        count = jnp.sum((ids_all == e).astype(F32), axis=1, keepdims=True)
        count = jnp.sum(count, axis=0, keepdims=True)
        share = share + jnp.where(lane == e, count, 0.0)
    share = share * (AUX_WEIGHT * E / (ids_all.shape[0] * ids_all.shape[1]))
    chosen = ids_col[:, :1] == lane
    picks = r.route[...].astype(BF16)
    x = r.x_own[...].astype(F32)
    cot = r.cot[...].astype(F32)

    steps.finish_first()
    load = [
        pltpu.make_async_copy(r.wg_ref.at[:, :, pl.ds(3 * D, D)], r.w3.at[0], r.loc.at[1]),
        pltpu.make_async_copy(r.wg_ref.at[:, :, pl.ds(4 * D, LANES)], r.misc3, r.loc.at[2]),
    ]
    for c in load:
        c.start()
    for c in load:
        c.wait()
    r.wo[...] = flatten_rows(r.w3[0]).astype(BF16)
    misc = flatten_rows(r.misc3[...])
    router = misc.astype(BF16)
    lines = jnp.transpose(misc)
    r.gain1[...] = lines[E : E + 1, :]
    gain = lines[E + 1 : E + 2, :]
    for n in range(HEAD_COUNT):
        hb, hh = z.holder(n)

        @pl.when(jnp.logical_not(p.owns(n)))
        def _():
            ref = r.att_in.at[n]
            remote(ref, ref, r.at_s.at[0], r.at_r.at[n], (d, hb, hh)).wait_recv()

        at = slice(n * HEAD_SIZE, (n + 1) * HEAD_SIZE)
        r.att_cat[: PT // 2, at] = r.att_in[n, :, :HEAD_SIZE]
        r.att_cat[PT // 2 :, at] = r.att_in[n, :, HEAD_SIZE:]
    att = r.att_cat[...]
    middle = x + nn(att, r.wo[...])
    inverse = lax.rsqrt(jnp.mean(middle * middle, axis=-1, keepdims=True) + EPSILON)
    routed = (middle * inverse * gain).astype(BF16)

    out = Sends(r.ex_s)

    def dispatch(part, values):
        r.disp[part] = nn(picks, values).reshape(E, C8, D).astype(BF16)
        for k in range(1, NG):
            e, device = p.group(k)
            out.put(r.disp.at[part, e], r.exp_in.at[part, g], r.ex_r.at[part * NG + g], device)
        r.exp_in[part, g] = r.disp[part, g]

    def arrivals(part):
        for k in range(1, NG):
            e, device = p.group(NG - k)
            ref = r.exp_in.at[part, e]
            remote(ref, ref, r.ex_s.at[0], r.ex_r.at[part * NG + e], device).wait_recv()

    def give_back(part, values):
        r.ret[part] = values.reshape(NG, C8, D).astype(BF16)
        for k in range(1, NG):
            e, device = p.group(k)
            out.put(r.ret.at[part, e], r.back.at[part, g], r.rt_r.at[part * NG + g], device)
        r.back[part, g] = r.ret[part, g]

    def returns(part):
        for k in range(1, NG):
            e, device = p.group(NG - k)
            ref = r.back.at[part, e]
            remote(ref, ref, r.ex_s.at[0], r.rt_r.at[part * NG + e], device).wait_recv()
        rows = r.back[part].astype(F32).reshape(E * C8, D).astype(BF16)
        return tn(picks, rows)

    copies = []

    def share_slots(part):
        src, dst, sem = r.exp_in.at[part], r.slots_ref.at[part, h], r.all_r.at[part * nh + h]
        out.put(src, dst, sem, (d, b, hy))
        out.put(src, dst, sem, (d, b, hc))
        c = pltpu.make_async_copy(src, dst, r.loc.at[3 + part])
        c.start()
        copies.append(c)

    def got_slots(part, hh):
        ref = r.slots_ref.at[part, hh]
        remote(ref, ref, r.ex_s.at[0], r.all_r.at[part * nh + hh], (d, b, hc)).wait_recv()

    dispatch(0, routed)
    logits = jnp.where(lane < E, nn(routed, router), -1e30)
    exps = jnp.exp(logits - jnp.max(logits, axis=-1, keepdims=True))
    probs = exps / jnp.sum(exps, axis=-1, keepdims=True)
    gate = jnp.sum(jnp.where(chosen, probs, 0.0), axis=-1, keepdims=True)
    dispatch(1, (gate * cot).astype(BF16))
    chunk = D
    chunks = z.FF // chunk
    steps.run_rest(14)

    arrivals(0)
    share_slots(0)
    rows_in = r.exp_in[0].astype(F32).reshape(NG * C8, D).astype(BF16)
    r.out_acc[...] = jnp.zeros_like(r.out_acc)

    def forward_step(c, carry):
        at = pl.ds(pl.multiple_of(c * chunk, chunk), chunk)
        pre = nn(rows_in, r.win[:, at])
        hidden, r.slope[:, at] = activate(pre)
        r.hid[:, at] = hidden
        r.out_acc[...] += nn(hidden, r.wout[at, :])
        return carry

    lax.fori_loop(0, chunks, forward_step, 0)
    give_back(0, r.out_acc[...])

    arrivals(1)
    share_slots(1)
    grad_out = r.exp_in[1].astype(F32).reshape(NG * C8, D).astype(BF16)
    r.out_acc[...] = jnp.zeros_like(r.out_acc)

    def backward_step(c, carry):
        at = pl.ds(pl.multiple_of(c * chunk, chunk), chunk)
        gp = grad_pre(grad_out, r.wout[at, :], r.slope[:, at])
        r.slope[:, at] = gp
        r.out_acc[...] += nt(gp, r.win[:, at])
        return carry

    lax.fori_loop(0, chunks, backward_step, 0)
    give_back(1, r.out_acc[...])
    saves = []

    def save(hh):
        for n, (src, dst) in enumerate(((r.hid, r.hid_ref), (r.slope, r.gp_ref))):
            c = pltpu.make_async_copy(src, dst.at[hh], r.loc.at[8 + n])
            c.start()
            saves.append(c)

    def other_slots(hh, forward):
        for part in range(2):
            got_slots(part, hh)
            if forward:
                ref = r.slots_ref.at[part, hh]
                out.put(ref, ref, r.all_r.at[part * nh + hh], (d, b, hc))
        c = pltpu.make_async_copy(r.slots_ref.at[:, hh], r.act_in, r.loc.at[10])
        c.start()
        c.wait()
        while saves:
            saves.pop().wait()
        others_in = r.act_in[0].astype(F32).reshape(NG * C8, D).astype(BF16)
        others_grad = r.act_in[1].astype(F32).reshape(NG * C8, D).astype(BF16)

        def step(c, carry):
            at = pl.ds(pl.multiple_of(c * chunk, chunk), chunk)
            r.hid[:, at], slope = activate(nn(others_in, r.win[:, at]))
            r.slope[:, at] = grad_pre(others_grad, r.wout[at, :], slope)
            return carry

        lax.fori_loop(0, chunks, step, 0)
        save(hh)

    save(h)
    steps.run_rest(10)
    for c in copies:
        c.wait()
    other_slots(hc, False)

    expert_rows = returns(0)
    r.layer_v[...] = (middle + gate * expert_rows).astype(BF16)
    written(r, "layer_ref")
    grad_gate = jnp.sum(cot * expert_rows, axis=-1, keepdims=True)
    grad_probs = jnp.where(chosen, grad_gate, 0.0) + share
    inner = jnp.sum(probs * grad_probs, axis=-1, keepdims=True)
    grad_logits = (probs * (grad_probs - inner)).astype(BF16)
    from_router = nt(grad_logits, router)
    grad_routed = returns(1) + from_router
    scaled = grad_routed * gain
    mean = jnp.mean(scaled * middle, axis=-1, keepdims=True)
    gmid = cot + inverse * scaled - middle * (inverse * inverse * inverse) * mean
    r.gmid[...] = gmid
    low_mid = gmid.astype(BF16)
    gatt = nt(low_mid, r.wo[...]).astype(BF16)

    for n in range(HEAD_COUNT):
        r.gatt[n] = both_halves(gatt[:, n * HEAD_SIZE : (n + 1) * HEAD_SIZE])
        hb, hh = z.holder(n)
        out.put(
            r.gatt.at[n], r.do_in.at[s], r.do_r.at[s], (d, hb, hh), jnp.logical_not(p.owns(n))
        )

        @pl.when(p.owns(n))
        def _():
            r.do_in[s] = r.gatt[n]

    term = grad_routed * middle * inverse
    high = term.astype(BF16)
    rest = (term - high.astype(F32)).astype(BF16)
    ones = jnp.broadcast_to((lane == E).astype(BF16), (PT, LANES))
    small = tn(routed, grad_logits) + tn(high, ones) + tn(rest, ones)
    terms = jnp.concatenate([tn(att, low_mid), small], axis=1)
    for t in range(z.ndev):
        r.dwo[t % nh, t // nh] = terms[t * z.R : (t + 1) * z.R].astype(BF16)
    other_slots(hy, True)

    def finish():
        while saves:
            saves.pop().wait()
        out.finish()

    return functools.partial(other_slots, hyc, False), finish


def backward_phase(z, r, p, steps, last_slots):
    d, b, h, s, me, hd, active = p.d, p.b, p.h, p.s, p.me, p.hd, p.active
    hy, hc, hyc = p.hy, p.hc, p.hyc
    nb, nh, nd, ns, nv, NG = z.n_blk, z.n_head, z.n_dp, z.ns, z.ndev, z.NG
    D, R, PT, HS, E = z.D, z.R, z.PT, HEAD_SIZE, z.E

    def sum_in(dst, src, terms, count):
        def body(e, carry):
            acc = src(e).astype(F32)
            for term in terms:
                acc = acc + term(e).astype(F32)
            dst[e] = acc.astype(BF16)
            return carry

        lax.fori_loop(0, count, body, 0)

    sums = Sends(r.su_s)
    y_sum = r.core_in.at[0]

    def got_sum(ref, k):
        remote(ref, ref, r.su_s.at[0], r.su_r.at[k], (d, b, hc)).wait_recv()

    def stage_core():
        sums.put(r.dwo.at[hyc], r.core_in.at[0], r.su_r.at[0], (d, b, hc))
        sums.put(r.dwo.at[hc], r.core_in.at[1], r.su_r.at[1], (d, b, hc))

    def stage_y():
        got_sum(r.core_in.at[0], 0)
        sum_in(r.y_src, lambda e: r.dwo[hy, e], [lambda e: r.core_in[0, e]], NG)
        sums.put(r.y_src, r.y_in, r.su_r.at[2], (d, b, hy))

    def stage_dp():
        got_sum(r.core_in.at[1], 1)
        got_sum(r.y_in, 2)
        sum_in(
            y_sum, lambda e: r.dwo[h, e], [lambda e: r.core_in[1, e], lambda e: r.y_in[e]], NG
        )
        for k in range(1, nd):
            q = lax.rem(d + k, nd)
            sums.put(y_sum.at[pl.ds(q * nb, nb)], r.dp_in.at[d], r.su_r.at[3 + d], (q, b, h))

    def stage_blk():
        others = [lax.rem(d + k, nd) for k in range(1, nd)]
        for q in others:
            got_sum(r.dp_in.at[q], 3 + q)

        def body(e, carry):
            acc = y_sum[d * nb + e].astype(F32)
            for q in others:
                acc = acc + r.dp_in[q, e].astype(F32)
            r.blk_src[e] = acc.astype(BF16)
            return carry

        lax.fori_loop(0, nb, body, 0)
        for k in range(1, nb):
            e = lax.rem(b + k, nb)
            sums.put(r.blk_src.at[e], r.blk_in.at[b], r.su_r.at[3 + nd + b], (d, e, h))
        r.blk_in[b] = r.blk_src[b]

    stage_core()

    def send_dq(t):
        return remote(
            r.dqkv.at[t], r.dq_in.at[hd], r.dq_s.at[t], r.dq_r.at[hd], (d, t // nh, t % nh)
        )

    def send_dw(k):
        t, device = p.any_peer(k)
        slot = d * HEAD_COUNT + hd
        return remote(r.dw3.at[t], r.dw_in.at[slot], r.dw_s.at[k], r.dw_r.at[slot], device)

    per = z.per
    part_rows = BLOCK // 2

    @pl.when(active)
    def _():
        r.dkv[...] = jnp.zeros_like(r.dkv)
        r.dq_acc[...] = jnp.zeros_like(r.dq_acc)
        r.dw[...] = jnp.zeros_like(r.dw)
        r.diag[...] = jnp.zeros_like(r.diag)
        r.sub[...] = jnp.zeros_like(r.sub)
        r.far[...] = jnp.zeros_like(r.far)

        def got_do(k, carry):
            t = lax.rem(s + k, ns)
            ref = r.do_in.at[t]
            remote(ref, ref, r.ex_s.at[0], r.do_r.at[t], p.in_sequence(t)).wait_recv()
            return carry

        lax.fori_loop(1, ns, got_do, 0)
        ones = jnp.ones((8, HS), BF16)
        for i in range(z.nq):
            here = slice(i * BLOCK, (i + 1) * BLOCK)
            pairs = [r.do_in[i * per + u] for u in range(per)]
            do = jnp.concatenate(
                [side for pair in pairs for side in (pair[:, :HS], pair[:, HS:])], axis=0
            )
            do = (do.astype(F32) * r.attl[here, HS:]).astype(BF16)
            r.dos[here, :] = do
            prod = do.astype(F32) * r.attl[here, :HS]
            high = prod.astype(BF16)
            rest = (prod - high.astype(F32)).astype(BF16)
            r.delta[i] = nt(ones, high) + nt(ones, rest)

    def tile(i, j, u):
        at = slice(j * BLOCK + u * part_rows, j * BLOCK + (u + 1) * part_rows)
        here = slice(i * BLOCK, (i + 1) * BLOCK)
        pr = r.probs[i, at, :]
        do = r.dos[here, :]
        ds = pr.astype(F32) * (nt(r.qkv[at, 2 * HS :], do) - r.delta[i, 0:1, :])
        low = ds.astype(BF16)
        part = slice(u * part_rows, (u + 1) * part_rows)
        if j == i:
            r.diag[part, :] += low.astype(F32)
        elif j == i - 1:
            r.sub[part, :] += low.astype(F32)
        else:
            r.far[...] += jnp.sum(low.astype(F32).reshape(part_rows // 8, 8, BLOCK), axis=0)
        both = jnp.concatenate([nn(low, r.qkv[here, :HS]), nn(pr, do)], axis=1)
        return at, both, nn(r.k_t[:, at], low)

    def column(j, hi):
        for u in range(2):
            acc = jnp.zeros((part_rows, 2 * HS), F32)
            for i in range(j, hi + 1):
                at, both, dq = tile(i, j, u)
                acc = acc + both
                r.dq_acc[i] += dq
            r.dkv[at, :] += acc

    def row(i, lo):
        acc = jnp.zeros((HS, BLOCK), F32)
        for j in range(lo, i + 1):
            for u in range(2):
                at, both, dq = tile(i, j, u)
                r.dkv[at, :] += both
                acc = acc + dq
        r.dq_acc[i] += acc

    lo, hi = 0, z.nq - 1
    turn = 0
    while lo <= hi:
        if turn == 1:
            stage_y()
        if turn == 3:
            stage_dp()
        if turn == z.nq - 1:
            stage_blk()

        @pl.when(active)
        def _():
            if turn % 2 == 0:
                n = lo
                column(n, hi)
            else:
                n = hi
                row(n, lo)
            here = slice(n * BLOCK, (n + 1) * BLOCK)
            dq = jnp.transpose(r.dq_acc[n]) * HS ** (-0.5)
            parts = jnp.concatenate([dq, r.dkv[here, :]], axis=1).astype(BF16)
            r.dw[...] += tn(r.xg[n * per : (n + 1) * per].reshape(BLOCK, D), parts)
            for u in range(per):
                t = n * per + u
                piece = parts[u * PT : (u + 1) * PT]
                r.dqkv[t, :PT] = piece[:, : 2 * HS]
                r.dqkv[t, PT:] = both_halves(piece[:, 2 * HS :])

                @pl.when(t != s)
                def _():
                    send_dq(t).start()

                @pl.when(t == s)
                def _():
                    r.dq_in[hd] = r.dqkv[t]

        if turn % 2 == 0:
            lo += 1
        else:
            hi -= 1
        turn += 1
        steps.run_rest(6)

    @pl.when(active)
    def _():
        jj = lax.broadcasted_iota(jnp.int32, (BLOCK, BLOCK), 0)
        ii = lax.broadcasted_iota(jnp.int32, (BLOCK, BLOCK), 1)
        lane = lax.broadcasted_iota(jnp.int32, (1, HS), 1)
        sums_of = jnp.zeros((1, HS), F32)
        half = BUCKETS // 2
        bounds = (0,) + LIMITS + (1 << 30,)
        tile_d, tile_s = r.diag[...], r.sub[...]

        def total(values):
            return jnp.sum(jnp.sum(values, axis=0, keepdims=True), axis=1, keepdims=True)

        for n in range(half):
            near, beyond = bounds[n], bounds[n + 1]
            dist = ii - jj
            part = total(
                jnp.where((dist >= near) & (dist < beyond), tile_d, 0.0)
                + jnp.where((dist + BLOCK >= near) & (dist + BLOCK < beyond), tile_s, 0.0)
            )
            if n == half - 1:
                part = part + total(r.far[...])
            sums_of = sums_of + jnp.where(lane == n, part, 0.0)
            if n > 0:
                part = total(jnp.where((-dist >= near) & (-dist < beyond), tile_d, 0.0))
                sums_of = sums_of + jnp.where(lane == half + n, part, 0.0)
        wide = jnp.concatenate([r.dw[...], jnp.broadcast_to(sums_of, (D, HS))], axis=1)
        split_rows(r.dw3, wide, R)

        def start_dw(k, carry):
            send_dw(k).start()
            return carry

        lax.fori_loop(1, nv, start_dw, 0)
        r.dw_in[d * HEAD_COUNT + hd] = r.dw3[me]

    last_slots()
    steps.finish_rest()
    load = [
        pltpu.make_async_copy(r.wg_ref.at[:, :, pl.ds(m * D, D)], r.w3.at[m], r.loc.at[5 + m])
        for m in range(3)
    ]
    for c in load:
        c.start()
    for m, c in enumerate(load):
        c.wait()
        r.wfull[:, m * D : (m + 1) * D] = flatten_rows(r.w3[m]).astype(BF16)

    for k in range(1, nb):
        e = lax.rem(b + k, nb)
        got_sum(r.blk_in.at[e], 3 + nd + e)
    acc = r.blk_in[0].astype(F32)
    for e in range(1, nb):
        acc = acc + r.blk_in[e].astype(F32)
    eye = lax.broadcasted_iota(jnp.int32, (R, R), 0) == lax.broadcasted_iota(jnp.int32, (R, R), 1)

    def as_row(column):
        return jnp.sum(jnp.where(eye, column, 0.0), axis=0, keepdims=True)

    r.go_v[...] = acc[:, :D]
    r.router_v[...] = jnp.concatenate([as_row(acc[:, D + e : D + e + 1]) for e in range(E)], axis=0)
    r.gain2_v[...] = as_row(acc[:, D + E : D + E + 1])
    written(r, "go_ref", "router_out", "gain2_ref")

    for n in range(HEAD_COUNT):
        hb, hh = z.holder(n)

        @pl.when(jnp.logical_not(p.owns(n)))
        def _():
            ref = r.dq_in.at[n]
            remote(ref, ref, r.dq_s.at[0], r.dq_r.at[n], (d, hb, hh)).wait_recv()

        for m in range(2):
            r.grad_cat[:, m * D + n * HS : m * D + (n + 1) * HS] = r.dq_in[
                n, :PT, m * HS : (m + 1) * HS
            ]
        at = slice(2 * D + n * HS, 2 * D + (n + 1) * HS)
        r.grad_cat[: PT // 2, at] = r.dq_in[n, PT:, :HS]
        r.grad_cat[PT // 2 :, at] = r.dq_in[n, PT:, HS:]
    grad_normed = nt(r.grad_cat[...], r.wfull[...])
    x = r.x_own[...].astype(F32)
    inverse = lax.rsqrt(jnp.mean(x * x, axis=-1, keepdims=True) + EPSILON)
    scaled = grad_normed * r.gain1[...]
    mean = jnp.mean(scaled * x, axis=-1, keepdims=True)
    grad_in = inverse * scaled - x * (inverse * inverse * inverse) * mean
    r.gtok_v[...] = (r.gmid[...] + grad_in).astype(BF16)
    written(r, "gtok_ref")

    for dd in range(nd):
        for n in range(HEAD_COUNT):
            hb, hh = z.holder(n)

            @pl.when(jnp.logical_not(p.owns(n) & (d == dd)))
            def _():
                ref = r.dw_in.at[dd * HEAD_COUNT + n]
                remote(
                    ref, ref, r.dw_s.at[0], r.dw_r.at[dd * HEAD_COUNT + n], (dd, hb, hh)
                ).wait_recv()

    lane = lax.broadcasted_iota(jnp.int32, (1, BUCKETS), 1)
    slot_lane = lax.broadcasted_iota(jnp.int32, (1, z.RL), 1)
    own_table = jnp.zeros((1, z.RL), F32)
    first = jnp.zeros((R, 1), F32)
    for n in range(HEAD_COUNT):
        part = r.dw_in[n].astype(F32)
        for dd in range(1, nd):
            part = part + r.dw_in[dd * HEAD_COUNT + n].astype(F32)
        for m, out in enumerate((r.gq_v, r.gk_v, r.gv_v)):
            cols = part[:, m * HS : (m + 1) * HS]
            out[:, n * HS : (n + 1) * HS] = cols
            own = r.w_own[:, m * D + n * HS : m * D + (n + 1) * HS].astype(F32)
            first = first + jnp.sum(cols * own, axis=-1, keepdims=True)
        line = part[0:1, 3 * HS : 3 * HS + BUCKETS]
        for k in range(z.RL):
            hit = lane + n * BUCKETS == me * z.RL + k
            value = jnp.sum(jnp.where(hit, line, 0.0), axis=1, keepdims=True)
            own_table = own_table + jnp.where(slot_lane == k, value, 0.0)
    own_gain = r.w_own[:, 4 * D :].astype(F32)[:, E : E + 1]
    r.gain1_v[...] = as_row(first / own_gain)
    r.table_v[...] = own_table
    written(r, "gain1_ref", "gq_ref", "gk_ref", "gv_ref", "table_ref")

    sums.finish()

    @pl.when(active)
    def _():
        for t in range(ns):

            @pl.when(t != s)
            def _():
                send_dq(t).wait_send()

        def sent_dw(k, carry):
            send_dw(k).wait_send()
            return carry

        lax.fori_loop(1, nv, sent_dw, 0)


def layer(z, x, order, ids, rows, weights, router_t, w_in, w_out, cot):
    D, R, PT, S, HS, E, NG, C8 = z.D, z.R, z.PT, z.S, HEAD_SIZE, z.E, z.NG, z.cap8
    nb, nd, nh, ns, nv = z.n_blk, z.n_dp, z.n_head, z.ns, z.ndev
    dma = pltpu.SemaphoreType.DMA
    vmem = pl.BlockSpec(memory_space=pltpu.VMEM)
    hbm = pl.BlockSpec(memory_space=pltpu.HBM)
    shape = jax.ShapeDtypeStruct
    inputs = {
        "x_ref": (x, hbm),
        "order_ref": (order, vmem),
        "ids_ref": (ids, hbm),
        "gain1_in": (rows[0][None, :], vmem),
        "gain2_in": (rows[1][None, :], vmem),
        "rel_ref": (rows[2][None, :], vmem),
        "wq_ref": (weights[0], hbm),
        "wk_ref": (weights[1], hbm),
        "wv_ref": (weights[2], hbm),
        "wo_ref": (weights[3], hbm),
        "router_ref": (router_t, vmem),
        "win_ref": (w_in, hbm),
        "wout_ref": (w_out, hbm),
        "cot_ref": (cot, hbm),
    }
    outputs = {
        "wg_ref": (shape((nv, R, z.wide), BF16), hbm),
        "slots_ref": (shape((2, nh, NG, C8, D), BF16), hbm),
        "hid_ref": (shape((nh, NG * C8, z.FF), BF16), hbm),
        "gp_ref": (shape((nh, NG * C8, z.FF), BF16), hbm),
        "layer_ref": (shape((PT, D), BF16), hbm),
        "gtok_ref": (shape((PT, D), BF16), hbm),
        "gain1_ref": (shape((1, R), F32), hbm),
        "gq_ref": (shape((R, D), F32), hbm),
        "gk_ref": (shape((R, D), F32), hbm),
        "gv_ref": (shape((R, D), F32), hbm),
        "go_ref": (shape((R, D), F32), hbm),
        "table_ref": (shape((1, z.RL), F32), hbm),
        "gain2_ref": (shape((1, R), F32), hbm),
        "router_out": (shape((E, R), F32), hbm),
    }
    V = pltpu.VMEM
    terms = D + LANES
    scratch = {
        "w_own": V((R, z.wide), BF16),
        "x_own": V((PT, D), BF16),
        "cot": V((PT, D), BF16),
        "ids": V(ids.shape, jnp.int32),
        "win": V((D, z.FF), BF16),
        "wout": V((z.FF, D), BF16),
        "slices": V((HEAD_COUNT, R, 4 * HS), BF16),
        "slices_in": V((nv, R, 4 * HS), BF16),
        "xg": V((ns, PT, D), BF16),
        "wh": V((D, 3 * HS), BF16),
        "gain1": V((1, D), F32),
        "far_bias": V((1, 1), F32),
        "bias_d": V((BLOCK, BLOCK), F32),
        "bias_s": V((BLOCK, BLOCK), F32),
        "qkv": V((S, 3 * HS), BF16),
        "v_t": V((HS, S), BF16),
        "k_t": V((HS, S), BF16),
        "s_scr": V((S, BLOCK), F32),
        "probs": V((z.nq, S, BLOCK), BF16),
        "attl": V((S, 2 * HS), F32),
        "att_src": V((ns, PT // 2, 2 * HS), BF16),
        "att_in": V((HEAD_COUNT, PT // 2, 2 * HS), BF16),
        "misc3": V((nv, R, LANES), BF16),
        "wo": V((D, D), BF16),
        "route": V((E * C8, PT), F32),
        "att_cat": V((PT, D), BF16),
        "disp": V((2, E, C8, D), BF16),
        "exp_in": V((2, NG, C8, D), BF16),
        "ret": V((2, NG, C8, D), BF16),
        "back": V((2, E, C8, D), BF16),
        "hid": V((NG * C8, z.FF), BF16),
        "slope": V((NG * C8, z.FF), BF16),
        "act_in": V((2, NG, C8, D), BF16),
        "out_acc": V((NG * C8, D), F32),
        "gmid": V((PT, D), F32),
        "gatt": V((HEAD_COUNT, PT // 2, 2 * HS), BF16),
        "do_in": V((ns, PT // 2, 2 * HS), BF16),
        "dwo": V((nh, NG, R, terms), BF16),
        "core_in": V((2, NG, R, terms), BF16),
        "y_src": V((NG, R, terms), BF16),
        "y_in": V((NG, R, terms), BF16),
        "dp_in": V((nd, nb, R, terms), BF16),
        "blk_src": V((nb, R, terms), BF16),
        "blk_in": V((nb, R, terms), BF16),
        "dos": V((S, HS), BF16),
        "delta": V((z.nq, 8, BLOCK), F32),
        "dq_acc": V((z.nq, HS, BLOCK), F32),
        "dw": V((D, 3 * HS), F32),
        "dw3": V((nv, R, 4 * HS), BF16),
        "diag": V((BLOCK, BLOCK), F32),
        "sub": V((BLOCK, BLOCK), F32),
        "far": V((8, BLOCK), F32),
        "dqkv": V((ns, PT + PT // 2, 2 * HS), BF16),
        "dq_in": V((HEAD_COUNT, PT + PT // 2, 2 * HS), BF16),
        "dw_in": V((nd * HEAD_COUNT, R, 4 * HS), BF16),
        "w3": V((3, nv, R, D), BF16),
        "wfull": V((D, 3 * D), BF16),
        "grad_cat": V((PT, 3 * D), BF16),
        "layer_v": V((PT, D), BF16),
        "gtok_v": V((PT, D), BF16),
        "gain1_v": V((1, R), F32),
        "gq_v": V((R, D), F32),
        "gk_v": V((R, D), F32),
        "gv_v": V((R, D), F32),
        "go_v": V((R, D), F32),
        "table_v": V((1, z.RL), F32),
        "gain2_v": V((1, R), F32),
        "router_v": V((E, R), F32),
        "out_sem": dma((len(PASSED),)),
        "in_sem": dma((9,)),
        "loc": dma((11,)),
        "sl_s": dma((HEAD_COUNT,)),
        "sl_r": dma((nv,)),
        "sd_s": dma((ns * nd,)),
        "x_s": dma((2 * (4 + 6 * (nb - 1) + 2 * nb - 1),)),
        "x_r": dma((2 * ns,)),
        "w0_s": dma((spread_copies(z, False),)),
        "w0_r": dma((nv,)),
        "w1_s": dma((spread_copies(z, True),)),
        "w1_r": dma((nv,)),
        "w2_s": dma((spread_copies(z, False),)),
        "w2_r": dma((nv,)),
        "at_s": dma((ns,)),
        "at_r": dma((HEAD_COUNT,)),
        "ex_s": dma((4 * (NG - 1) + 6 + HEAD_COUNT,)),
        "ex_r": dma((2 * NG,)),
        "rt_r": dma((2 * NG,)),
        "all_r": dma((2 * nh,)),
        "do_r": dma((ns,)),
        "su_s": dma((3 + nd - 1 + nb - 1,)),
        "su_r": dma((3 + nd + nb,)),
        "dq_s": dma((ns,)),
        "dq_r": dma((HEAD_COUNT,)),
        "dw_s": dma((nv,)),
        "dw_r": dma((nd * HEAD_COUNT,)),
    }
    names = tuple(inputs) + tuple(outputs) + tuple(scratch)
    results = pl.pallas_call(
        functools.partial(layer_kernel, z, names),
        out_shape=tuple(v[0] for v in outputs.values()),
        in_specs=[v[1] for v in inputs.values()],
        out_specs=tuple(v[1] for v in outputs.values()),
        scratch_shapes=list(scratch.values()),
        compiler_params=pltpu.CompilerParams(
            collective_id=0, has_side_effects=True, vmem_limit_bytes=VMEM_LIMIT
        ),
        name="layer",
    )(*[v[0] for v in inputs.values()])
    return dict(zip(outputs, results))


def expert_kernel(z, slots_ref, hid_ref, gp_ref, *refs):
    count = len(PASSED)
    passed_in, (gin_ref, gout_ref) = refs[:count], refs[count : count + 2]
    passed_out = refs[count + 2 : 2 * count + 2]
    rows_t, grad_out, sem = refs[2 * count + 2 :]
    step = pl.program_id(0)

    def passing(n):
        return pltpu.make_async_copy(passed_in[n], passed_out[n], sem.at[n])

    @pl.when(step == 0)
    def _():
        for n in range(len(PASSED)):
            passing(n).start()
        count = z.NG * z.cap8
        for n in range(z.n_head):
            at = slice(n * count, (n + 1) * count)
            rows_in = slots_ref[0, n].astype(F32).reshape(count, z.D)
            rows_t[:, at] = jnp.transpose(rows_in).astype(BF16)
            grad_out[at, :] = slots_ref[1, n].astype(F32).reshape(count, z.D).astype(BF16)

    total = z.n_head * z.NG * z.cap8
    chunk = hid_ref.shape[2]
    gin_ref[0] = nn(rows_t[...], gp_ref[...].reshape(total, chunk))
    gout_ref[0] = tn(hid_ref[...].reshape(total, chunk), grad_out[...])

    @pl.when(step == pl.num_programs(0) - 1)
    def _():
        for n in range(len(PASSED)):
            passing(n).wait()


def expert_weights(z, slots, hid, gp, passed):
    chunk = 512
    hbm = pl.BlockSpec(memory_space=pltpu.HBM)
    total = z.n_head * z.NG * z.cap8
    in_chunk = pl.BlockSpec((1, z.D, chunk), lambda i: (0, 0, i))
    act_chunk = pl.BlockSpec((z.n_head, z.NG * z.cap8, chunk), lambda i: (0, 0, i))
    out_chunk = pl.BlockSpec((1, chunk, z.D), lambda i: (0, i, 0))
    return pl.pallas_call(
        functools.partial(expert_kernel, z),
        grid=(z.FF // chunk,),
        out_shape=(
            jax.ShapeDtypeStruct((1, z.D, z.FF), F32),
            jax.ShapeDtypeStruct((1, z.FF, z.D), F32),
        )
        + tuple(jax.ShapeDtypeStruct(a.shape, a.dtype) for a in passed),
        in_specs=[pl.BlockSpec(memory_space=pltpu.VMEM), act_chunk, act_chunk] + [hbm] * len(passed),
        out_specs=(in_chunk, out_chunk) + (hbm,) * len(passed),
        scratch_shapes=[
            pltpu.VMEM((z.D, total), BF16),
            pltpu.VMEM((total, z.D), BF16),
            pltpu.SemaphoreType.DMA((len(passed),)),
        ],
        compiler_params=pltpu.CompilerParams(
            dimension_semantics=("arbitrary",), vmem_limit_bytes=VMEM_LIMIT
        ),
        name="expert_weight_grads",
    )(slots, hid, gp, *passed)


def local(
    sizes,
    tokens,
    order,
    expert_ids,
    norm1_gain,
    w_query,
    w_key,
    w_value,
    w_attn_out,
    rel_table,
    norm2_gain,
    w_router,
    w_in,
    w_out,
    cotangent,
):
    R, D = w_query.shape
    E = w_router.shape[1]
    z = Sizes(*sizes, R, D, E, w_in.shape[2], tokens.shape[1])
    out = layer(
        z,
        tokens.reshape(z.PT, D),
        order,
        expert_ids.reshape(-1, z.PT),
        (norm1_gain, norm2_gain, rel_table),
        (w_query, w_key, w_value, w_attn_out),
        w_router.T,
        w_in,
        w_out,
        cotangent.reshape(z.PT, D),
    )
    g_in, g_out, *rest = expert_weights(
        z, out["slots_ref"], out["hid_ref"], out["gp_ref"], [out[name] for name in PASSED]
    )
    layer_out, gtok, gain1, gq, gk, gv, go, table, gain2, router = rest
    return (
        layer_out.reshape(tokens.shape),
        gtok.reshape(tokens.shape),
        gain1.reshape(R),
        gq,
        gk,
        gv,
        go,
        table.reshape(z.RL),
        gain2.reshape(R),
        router.T,
        g_in,
        g_out,
    )


def solution(mesh):
    everywhere = ("dp", "blk", "head")
    rows, table = P(everywhere), P(everywhere, None)
    tokens = P("dp", ("blk", "head"), None)
    expert = P(("dp", "blk"), None, None)
    in_specs = (
        tokens,
        P("dp", ("blk", "head")),
        P(),
        rows,
        table,
        table,
        table,
        table,
        rows,
        rows,
        table,
        expert,
        expert,
        tokens,
    )
    out_specs = (
        tokens, tokens, rows, table, table, table, table, rows, rows, table, expert, expert
    )
    sizes = (mesh.shape["dp"], mesh.shape["blk"], mesh.shape["head"])
    return jax.shard_map(
        functools.partial(local, sizes),
        mesh=mesh,
        in_specs=in_specs,
        out_specs=out_specs,
        check_vma=False,
    )
```

```python
import functools
import itertools
import types

import jax
import jax.numpy as jnp
from jax import lax
from jax.experimental import pallas as pl
from jax.experimental.pallas import tpu as pltpu
from jax.sharding import PartitionSpec as P

HEAD_COUNT = 12
HEAD_SIZE = 64
BUCKETS = 32
BLOCK = 256
EPSILON = 1e-06
AUX_WEIGHT = 1.0
LIMITS = (1, 2, 3, 4, 5, 6, 7, 8, 12, 16, 23, 32, 46, 64, 91)
INV_ROOT_TWO = 0.7071067811865476
INV_ROOT_TWO_PI = 0.3989422804014327
LANES = 128
VMEM_LIMIT = 62 * 1024 * 1024
PASSED = (
    "layer_ref", "gtok_ref", "gain1_ref", "gq_ref", "gk_ref", "gv_ref", "go_ref", "table_ref",
    "gain2_ref", "router_out",
)
MESH = pl.DeviceIdType.MESH
F32 = jnp.float32
BF16 = jnp.bfloat16


def both_halves(values):
    n = values.shape[0] // 2
    return jnp.concatenate([values[:n], values[n:]], axis=1)


def line_order(b, nb):
    out = [(b, b >= 0)]
    for k in range(1, nb):
        out.append((b - k, b >= k))
        out.append((b + k, b + k < nb))
    return out


class Sends:
    def __init__(self, sems):
        self.sems, self.made = sems, []

    def put(self, src, dst, recv, device, cond=None):
        c = remote(src, dst, self.sems.at[len(self.made)], recv, device)
        self.made.append((c, cond))
        self.each(c.start, cond)

    def each(self, action, cond):
        if cond is None:
            action()
        else:
            pl.when(cond)(action)

    def finish(self):
        for c, cond in self.made:
            self.each(c.wait_send, cond)


class Sizes:
    def __init__(self, n_dp, n_blk, n_head, rows, width, experts, hidden, piece):
        self.n_dp, self.n_blk, self.n_head = n_dp, n_blk, n_head
        self.ndev = n_dp * n_blk * n_head
        self.ns = n_blk * n_head
        self.R, self.D, self.E, self.FF, self.PT = rows, width, experts, hidden, piece
        self.S = piece * self.ns
        self.nq = self.S // BLOCK
        self.hb = HEAD_COUNT // n_blk
        self.cap = (5 * piece + 4 * experts - 1) // (4 * experts)
        self.cap8 = (self.cap + 7) // 8 * 8
        self.NG = n_dp * n_blk
        self.RL = HEAD_COUNT * BUCKETS // self.ndev
        self.wide = 4 * width + LANES
        self.per = BLOCK // piece
        assert self.hb < n_head and self.hb * n_blk == HEAD_COUNT
        assert experts == self.NG and n_head == 4


    def holder(self, n):
        return n // self.hb, n % self.hb + n // self.hb % 2


def nt(a, b):
    return lax.dot_general(a, b, (((1,), (1,)), ((), ())), preferred_element_type=F32)


def tn(a, b):
    return lax.dot_general(a, b, (((0,), (0,)), ((), ())), preferred_element_type=F32)


def nn(a, b):
    return jnp.dot(a, b, preferred_element_type=F32)


def place():
    return lax.axis_index("dp"), lax.axis_index("blk"), lax.axis_index("head")


def signal(device):
    pl.semaphore_signal(
        pltpu.get_barrier_semaphore(), inc=1, device_id=device, device_id_type=MESH
    )


def await_barrier(count):
    pl.semaphore_wait(pltpu.get_barrier_semaphore(), count)


def remote(src, dst, send, recv, device):
    return pltpu.make_async_remote_copy(
        src_ref=src, dst_ref=dst, send_sem=send, recv_sem=recv, device_id=device, device_id_type=MESH
    )


def flatten_rows(blocks):
    count, rows, lanes = blocks.shape
    wide = blocks.astype(F32)
    if rows % 8 == 0:
        return wide.reshape(count * rows, lanes)
    return jnp.concatenate([wide[i] for i in range(count)], axis=0)


def split_rows(dst_ref, values, rows):
    count = values.shape[0] // rows
    if rows % 8 == 0:
        dst_ref[...] = values.reshape(count, rows, values.shape[1]).astype(dst_ref.dtype)
    else:
        for i in range(count):
            dst_ref[i] = values[i * rows : (i + 1) * rows].astype(dst_ref.dtype)


def activate(pre):
    phi, bell = normal_parts(pre)
    slope = phi + pre * bell * INV_ROOT_TWO_PI
    return (pre * phi).astype(BF16), slope.astype(BF16)


def grad_pre(grad_out, w, slope):
    hidden = nt(grad_out, w).astype(BF16).astype(F32)
    return (hidden * slope.astype(F32)).astype(BF16)


def normal_parts(v):
    bell = jnp.exp(-0.5 * v * v)
    t = 1.0 / (1.0 + (0.3275911 * INV_ROOT_TWO) * jnp.abs(v))
    poly = t * (
        0.254829592
        + t * (-0.284496736 + t * (1.421413741 + t * (-1.453152027 + t * 1.061405429)))
    )
    tail = 0.5 * poly * bell
    return jnp.where(v >= 0, 1.0 - tail, tail), bell


def bias_tile(table, shift):
    j = lax.broadcasted_iota(jnp.int32, (BLOCK, BLOCK), 0)
    i = lax.broadcasted_iota(jnp.int32, (BLOCK, BLOCK), 1)
    dist = j - i + shift
    mag = jnp.abs(dist)
    half = BUCKETS // 2
    out = jnp.broadcast_to(table[0:1, 0:1], (BLOCK, BLOCK))
    for n, limit in enumerate(LIMITS):
        low = table[n + 1 : n + 2, 0:1]
        if shift == 0:
            high = table[half + n + 1 : half + n + 2, 0:1]
            out = jnp.where(mag >= limit, jnp.where(dist > 0, high, low), out)
        else:
            out = jnp.where(mag >= limit, low, out)
    return out


class Spread:
    def __init__(self, z, src, dst, send, recv, y_first, lanes):
        self.z, self.src, self.dst, self.recv = z, src, dst, recv
        self.sends, self.lanes = Sends(send), lanes
        d, b, h = place()
        self.at = (d, b, h)
        nh, nd = z.n_head, z.n_dp
        self.hy = lax.rem(h + 2, nh)
        self.hc = h + 1 - 2 * lax.rem(h, 2)
        self.hyc = lax.rem(self.hc + 2, nh)
        dto = [lax.rem(d + k, nd) for k in range(1, nd)]
        dfrom = [lax.rem(d + nd - k, nd) for k in range(1, nd)]
        ys = ([(d, self.hy)], [(d, self.hy)])
        xs = ([(p, h) for p in dto], [(p, h) for p in dfrom])
        self.first, self.second = (ys, xs) if y_first else (xs, ys)
        if y_first:
            self.second_slots = [(p, hh) for p in dfrom for hh in (h, self.hy)]
        else:
            self.second_slots = [(p, self.hy) for p in [d] + dfrom]
        self.core_slots = [(p, hh) for p in [d] + dfrom for hh in (self.hc, self.hyc)]

    def slot(self, dd, bb, hh):
        return (dd * self.z.n_blk + bb) * self.z.n_head + hh

    def ref(self, slot):
        return self.dst.at[slot, :, self.lanes]

    def put(self, src, slot, device, cond=None):
        self.sends.put(src, self.ref(slot), self.recv.at[slot], device, cond)

    def got(self, slot):
        d, b, h = self.at
        ref = self.ref(slot)
        remote(ref, ref, self.sends.sems.at[0], self.recv.at[slot], (d, b, self.hc)).wait_recv()

    def steps(self):
        d, b, h = self.at
        nb = self.z.n_blk

        def begin():
            mine = self.slot(d, b, h)
            self.put(self.src, mine, (d, b + 1, h), b + 1 < nb)
            self.put(self.src, mine, (d, b - 1, h), b >= 1)
            for dd, hh in self.first[0] + self.second[0] + [(d, self.hc)]:
                self.put(self.src, mine, (dd, b, hh))

        def line_arrival(k):
            for f, cond, to, more in (
                (b - k, b >= k, b + 1, b + 1 < nb),
                (b + k, b + k < nb, b - 1, b >= 1),
            ):
                slot = self.slot(d, f, h)
                pl.when(cond)(functools.partial(self.got, slot))
                if k < nb - 1:
                    self.put(self.ref(slot), slot, (d, to, h), cond & more)
                for dd, hh in self.first[0] + self.second[0] + [(d, self.hc)]:
                    self.put(self.ref(slot), slot, (dd, b, hh), cond)

        def first_arrival(p, f, cond):
            slot = self.slot(p[0], f, p[1])
            pl.when(cond)(functools.partial(self.got, slot))
            for dd, hh in self.second[0] + [(d, self.hc)]:
                self.put(self.ref(slot), slot, (dd, b, hh), cond)

        def second_arrival(p, f, cond):
            slot = self.slot(p[0], f, p[1])
            pl.when(cond)(functools.partial(self.got, slot))
            self.put(self.ref(slot), slot, (d, b, self.hc), cond)

        out = [begin]
        for k in range(1, nb):
            out.append(functools.partial(line_arrival, k))
        for p in self.first[1]:
            for f, cond in line_order(b, nb):
                out.append(functools.partial(first_arrival, p, f, cond))
        for p in self.second_slots:
            for f, cond in line_order(b, nb):
                out.append(functools.partial(second_arrival, p, f, cond))
        return out

    def finish(self):
        d, b, h = self.at
        for p in self.core_slots:
            for f in range(self.z.n_blk):
                self.got(self.slot(p[0], f, p[1]))
        self.sends.finish()


def spread_copies(z, y_first):
    nb, nd = z.n_blk, z.n_dp
    peers = 1 + nd - 1 + 1
    first = 1 if y_first else nd - 1
    second = peers - 1 - first
    second_slots = 2 * (nd - 1) if y_first else nd
    line = 2 * nb - 1
    return 2 + peers + (nb - 1) * 2 * (peers + 1) + first * line * (second + 1) + second_slots * line


class Place:
    def __init__(self, z):
        self.d, self.b, self.h = d, b, h = place()
        self.s = b * z.n_head + h
        self.me = d * z.ns + self.s
        self.g = d * z.n_blk + b
        first = lax.rem(b, 2)
        self.active = (h >= first) & (h < first + z.hb)
        self.hd = b * z.hb + jnp.clip(h - first, 0, z.hb - 1)
        self.hy = lax.rem(h + 2, z.n_head)
        self.hc = h + 1 - 2 * lax.rem(h, 2)
        self.hyc = lax.rem(self.hc + 2, z.n_head)
        self.z = z

    def any_peer(self, k):
        z = self.z
        t = lax.rem(self.me + k, z.ndev)
        return t, (t // z.ns, lax.rem(t // z.n_head, z.n_blk), lax.rem(t, z.n_head))

    def in_sequence(self, t):
        return (self.d, t // self.z.n_head, lax.rem(t, self.z.n_head))

    def owns(self, n):
        return self.active & (self.hd == n)

    def group(self, k):
        z = self.z
        e = lax.rem(self.g + k, z.NG)
        return e, (e // z.n_blk, lax.rem(e, z.n_blk), self.h)


def written(r, *names):
    for name in names:
        short = name.replace("_ref", "").replace("_out", "") + "_v"
        c = pltpu.make_async_copy(
            getattr(r, short), getattr(r, name), r.out_sem.at[PASSED.index(name)]
        )
        c.start()
        r.outgoing.append(c)


def layer_kernel(z, names, *refs):
    r = types.SimpleNamespace(**dict(zip(names, refs)))
    r.dkv = r.s_scr.at[:, pl.ds(0, 2 * HEAD_SIZE)]
    r.outgoing = []
    p = Place(z)

    def greet(k, carry):
        signal(p.any_peer(k)[1])
        return carry

    lax.fori_loop(1, z.ndev, greet, 0)
    D = z.D
    small = [
        pltpu.make_async_copy(ref, r.w_own.at[:, pl.ds(m * D, D)], r.in_sem.at[m])
        for m, ref in enumerate((r.wq_ref, r.wk_ref, r.wv_ref, r.wo_ref))
    ]
    small.append(pltpu.make_async_copy(r.x_ref, r.x_own, r.in_sem.at[4]))
    later = [
        pltpu.make_async_copy(r.cot_ref, r.cot, r.in_sem.at[5]),
        pltpu.make_async_copy(r.ids_ref, r.ids, r.in_sem.at[6]),
        pltpu.make_async_copy(r.win_ref.at[0], r.win, r.in_sem.at[7]),
        pltpu.make_async_copy(r.wout_ref.at[0], r.wout, r.in_sem.at[8]),
    ]
    for c in small + later:
        c.start()
    steps, finish_forward = forward_phase(z, r, p, small)
    for c in later:
        c.wait()
    last_slots, finish_middle = middle_phase(z, r, p, steps)
    backward_phase(z, r, p, steps, last_slots)
    finish_forward()
    finish_middle()
    for c in r.outgoing:
        c.wait()


def forward_phase(z, r, p, small):
    d, b, h, s, me, hd, active = p.d, p.b, p.h, p.s, p.me, p.hd, p.active
    hy, hc, hyc = p.hy, p.hc, p.hyc
    nb, nh, nd, ns = z.n_blk, z.n_head, z.n_dp, z.ns
    D, R, E, PT, HS = z.D, z.R, z.E, z.PT, HEAD_SIZE

    await_barrier(z.ndev - 1)
    small[4].wait()

    tokens = Sends(r.x_s)
    pieces = 2
    rows_of = PT // pieces

    def xref(slot, c):
        return r.xg.at[slot, pl.ds(c * rows_of, rows_of)]

    def put(src, slot, c, device, cond=None):
        tokens.put(src, xref(slot, c), r.x_r.at[slot * pieces + c], device, cond)

    def got(slot, c):
        ref = xref(slot, c)
        remote(ref, ref, r.x_s.at[0], r.x_r.at[slot * pieces + c], (d, b, hc)).wait_recv()

    for c in range(pieces):
        own = r.x_own.at[pl.ds(c * rows_of, rows_of)]
        put(own, s, c, (d, b + 1, h), b + 1 < nb)
        put(own, s, c, (d, b - 1, h), b >= 1)
        put(own, s, c, (d, b, hy))
        put(own, s, c, (d, b, hc))
    r.xg[s] = r.x_own[...]

    for c in small[:4]:
        c.wait()
    eye = lax.broadcasted_iota(jnp.int32, (R, R), 0) == lax.broadcasted_iota(jnp.int32, (R, R), 1)
    row_of = lax.broadcasted_iota(jnp.int32, (LANES, R), 0)
    tail = jnp.zeros((LANES, R), F32)
    rel = jnp.concatenate([r.rel_ref[...].astype(F32), jnp.zeros((1, R - z.RL), F32)], axis=1)
    rows = r.gain1_in[...].astype(F32), r.gain2_in[...].astype(F32), rel
    for n in range(3):
        tail = jnp.where(row_of == E + n, rows[n], tail)
    router_t = jnp.concatenate(
        [r.router_ref[...].astype(F32), jnp.zeros((LANES - E, R), F32)], axis=0
    )
    misc = nt(eye.astype(BF16), (tail + router_t).astype(BF16)).astype(BF16)
    r.w_own[:, 4 * D :] = misc
    for n in range(HEAD_COUNT):
        columns = [r.w_own[:, m * D + n * HS : m * D + (n + 1) * HS] for m in range(3)]
        r.slices[n] = jnp.concatenate(columns + [misc[:, E : E + HS]], axis=1)
    save_w = pltpu.make_async_copy(r.w_own, r.wg_ref.at[me], r.loc.at[0])
    save_w.start()
    to_heads = Sends(r.sl_s)
    over_dp = Sends(r.sd_s)
    for n in range(HEAD_COUNT):
        hb, hh = z.holder(n)
        to_heads.put(
            r.slices.at[n], r.slices_in.at[me], r.sl_r.at[me], (d, hb, hh),
            jnp.logical_not(p.owns(n)),
        )

    @pl.when(active)
    def _():
        r.slices_in[me] = r.slices[hd]

    for k in range(1, nb):
        for c in range(pieces):
            for f, cond, to, more in (
                (b - k, b >= k, b + 1, b + 1 < nb),
                (b + k, b + k < nb, b - 1, b >= 1),
            ):
                slot = f * nh + h
                pl.when(cond)(functools.partial(got, slot, c))
                if k < nb - 1:
                    put(xref(slot, c), slot, c, (d, to, h), cond & more)
                put(xref(slot, c), slot, c, (d, b, hy), cond)
                put(xref(slot, c), slot, c, (d, b, hc), cond)
        if k == 1:
            for m in range(ns):
                t = lax.rem(s + m, ns)
                slot = d * ns + t
                ref = r.slices_in.at[slot]
                if m > 0:
                    c = remote(ref, ref, r.sl_s.at[0], r.sl_r.at[slot], p.in_sequence(t))
                    pl.when(active)(c.wait_recv)
                for kd in range(1, nd):
                    over_dp.put(ref, ref, r.sl_r.at[slot], (lax.rem(d + kd, nd), b, h), active)

    for f, cond in line_order(b, nb):
        for c in range(pieces):
            slot = f * nh + hy
            pl.when(cond)(functools.partial(got, slot, c))
            put(xref(slot, c), slot, c, (d, b, hc), cond)

    cuts = (3 * D, z.wide, False), (0, 3 * D // 2, True), (3 * D // 2, 3 * D, False)
    parts = [
        Spread(
            z, r.w_own.at[:, pl.ds(lo, hi - lo)], r.wg_ref,
            getattr(r, "w%d_s" % n), getattr(r, "w%d_r" % n), y_first, pl.ds(lo, hi - lo),
        )
        for n, (lo, hi, y_first) in enumerate(cuts)
    ]
    first, rest_a, rest_b = [part.steps() for part in parts]
    steps = []
    for k in range(nb):
        steps += [first.pop(0), rest_a.pop(0), rest_b.pop(0)]
    steps = Steps(steps + first, rest_a, rest_b, parts, save_w)

    steps.run(3)

    @pl.when(active)
    def _():
        for kd in range(1, nd):
            dd = lax.rem(d + kd, nd)

            def got_slice(t, carry):
                ref = r.slices_in.at[dd * ns + t]
                remote(ref, ref, r.sl_s.at[0], r.sl_r.at[dd * ns + t], (dd, b, h)).wait_recv()
                return carry

            lax.fori_loop(0, ns, got_slice, 0)

        rows = flatten_rows(r.slices_in[...])
        r.wh[:, : 2 * HS] = rows[:, : 2 * HS].astype(BF16)
        r.wh[:, :HS] = (rows[:, :HS] * HS ** (-0.5)).astype(BF16)
        r.wh[:, 2 * HS :] = rows[:, 2 * HS : 3 * HS].astype(BF16)
        r.gain1[...] = jnp.transpose(rows[:, LANES:])[HS : HS + 1, :]
        column = lax.broadcasted_iota(jnp.int32, (1, D), 1).astype(F32)
        owner = jnp.floor((column + 0.5) * (1.0 / R))
        place_of = column - owner * R
        entry = jnp.where(place_of < z.RL, owner * z.RL + place_of, -1.0)
        wanted = hd * BUCKETS + lax.broadcasted_iota(jnp.int32, (BUCKETS, D), 0)
        pick = (entry == wanted.astype(F32)).astype(BF16)
        table = nn(pick, rows[:, LANES:].astype(BF16))[:, HS + 2 : HS + 3]
        r.bias_d[...] = bias_tile(table, 0)
        r.bias_s[...] = bias_tile(table, -BLOCK)
        r.far_bias[...] = table[BUCKETS // 2 - 1 : BUCKETS // 2, 0:1]

    for f in range(nb):
        for c in range(pieces):
            got(f * nh + hc, c)
            got(f * nh + hyc, c)
    tokens.finish()
    per = z.per
    half = BLOCK // 2

    @pl.when(active)
    def _():
        for i in range(z.nq):
            here = slice(i * BLOCK, (i + 1) * BLOCK)
            x = r.xg[i * per : (i + 1) * per].reshape(BLOCK, D).astype(F32)
            inverse = lax.rsqrt(jnp.mean(x * x, axis=-1, keepdims=True) + EPSILON)
            low = (x * inverse * r.gain1[...]).astype(BF16)
            r.xg[i * per : (i + 1) * per] = low.reshape(per, PT, D)
            mixed = nn(low, r.wh[...])
            r.qkv[here, :] = mixed.astype(BF16)
            r.v_t[:, here] = jnp.transpose(mixed[:, 2 * HS :]).astype(BF16)
            r.k_t[:, here] = jnp.transpose(mixed[:, HS : 2 * HS]).astype(BF16)

    def send_att(t):
        return remote(
            r.att_src.at[t], r.att_in.at[hd], r.at_s.at[t], r.at_r.at[hd], (d, t // nh, t % nh)
        )

    low_rows, high_rows = range(z.nq // 2), range(z.nq // 2, z.nq)
    order = [i for pair in zip(reversed(high_rows), reversed(low_rows)) for i in pair]
    for i in order:
        steps.run(4)

        @pl.when(active)
        def _():
            here = slice(i * BLOCK, (i + 1) * BLOCK)
            q = r.qkv[here, :HS]
            top = jnp.full((8, BLOCK), -1e30, F32)
            far = r.far_bias[...]
            for j in range(i + 1):
                for u in range(2):
                    at = slice(j * BLOCK + u * half, j * BLOCK + (u + 1) * half)
                    part = slice(u * half, (u + 1) * half)
                    if j == i:
                        bias = r.bias_d[part, :]
                    elif j == i - 1:
                        bias = r.bias_s[part, :]
                    else:
                        bias = far
                    sc = nt(r.qkv[at, HS : 2 * HS], q) + bias
                    r.s_scr[at, :] = sc
                    top = jnp.maximum(top, jnp.max(sc.reshape(half // 8, 8, BLOCK), axis=0))
            top = jnp.max(top, axis=0, keepdims=True)
            total = jnp.zeros((8, BLOCK), F32)
            acc = jnp.zeros((HS, BLOCK), F32)
            for j in range(i + 1):
                for u in range(2):
                    at = slice(j * BLOCK + u * half, j * BLOCK + (u + 1) * half)
                    e = jnp.exp(r.s_scr[at, :] - top)
                    total = total + jnp.sum(e.reshape(half // 8, 8, BLOCK), axis=0)
                    r.probs[i, at, :] = e.astype(BF16)
                at = slice(j * BLOCK, (j + 1) * BLOCK)
                acc = acc + nn(r.v_t[:, at], r.probs[i, at, :])
            total = jnp.sum(total, axis=0, keepdims=True)
            both = jnp.concatenate([acc, jnp.broadcast_to(total, (HS, BLOCK))], axis=0)
            both = jnp.transpose(both)
            inv = 1.0 / both[:, HS:]
            att = (both[:, :HS] * inv).astype(BF16)
            r.attl[here, :] = jnp.concatenate([att.astype(F32), inv], axis=1)
            for u in range(per):
                t = i * per + u
                r.att_src[t] = both_halves(att[u * PT : (u + 1) * PT])

                @pl.when(t != s)
                def _():
                    send_att(t).start()

                @pl.when(t == s)
                def _():
                    r.att_in[hd] = r.att_src[t]

    def finish():
        to_heads.finish()
        over_dp.finish()

        @pl.when(active)
        def _():
            for t in range(ns):

                @pl.when(t != s)
                def _():
                    send_att(t).wait_send()

    return steps, finish


class Steps:
    def __init__(self, first, rest_a, rest_b, parts, save):
        self.first, self.parts, self.save = first, parts, save
        self.rest = [
            step
            for pair in itertools.zip_longest(rest_b, rest_a)
            for step in pair
            if step is not None
        ]

    def run(self, count):
        for _ in range(min(count, len(self.first))):
            self.first.pop(0)()

    def finish_first(self):
        self.run(len(self.first))
        self.parts[0].finish()
        self.save.wait()

    def run_rest(self, count):
        for _ in range(min(count, len(self.rest))):
            self.rest.pop(0)()

    def finish_rest(self):
        self.run_rest(len(self.rest))
        for part in self.parts[1:]:
            part.finish()


def middle_phase(z, r, p, steps):
    d, b, h, me, g, s = p.d, p.b, p.h, p.me, p.g, p.s
    hy, hc, hyc = p.hy, p.hc, p.hyc
    nb, nh, nd, ns = z.n_blk, z.n_head, z.n_dp, z.ns
    D, E, PT, NG, C8 = z.D, z.E, z.PT, z.NG, z.cap8

    ids_row = r.ids[pl.ds(me, 1), :]
    order_row = r.order_ref[...]
    ids_col = jnp.transpose(jnp.broadcast_to(ids_row, (PT, PT)))
    order_col = jnp.transpose(jnp.broadcast_to(order_row, (PT, PT)))
    earlier = (order_col < order_row) & (ids_col == ids_row)
    rank = jnp.sum(earlier.astype(jnp.int32), axis=0, keepdims=True)
    slot = lax.broadcasted_iota(jnp.int32, (C8, PT), 0)
    base = (rank == slot) & (slot < z.cap)
    lane = lax.broadcasted_iota(jnp.int32, (1, LANES), 1)
    share = jnp.zeros((1, LANES), F32)
    ids_all = r.ids[...]
    for e in range(E):
        r.route[e * C8 : (e + 1) * C8, :] = (base & (ids_row == e)).astype(F32)
        count = jnp.sum((ids_all == e).astype(F32), axis=1, keepdims=True)
        count = jnp.sum(count, axis=0, keepdims=True)
        share = share + jnp.where(lane == e, count, 0.0)
    share = share * (AUX_WEIGHT * E / (ids_all.shape[0] * ids_all.shape[1]))
    chosen = ids_col[:, :1] == lane
    picks = r.route[...].astype(BF16)
    x = r.x_own[...].astype(F32)
    cot = r.cot[...].astype(F32)

    steps.finish_first()
    load = [
        pltpu.make_async_copy(r.wg_ref.at[:, :, pl.ds(3 * D, D)], r.w3.at[0], r.loc.at[1]),
        pltpu.make_async_copy(r.wg_ref.at[:, :, pl.ds(4 * D, LANES)], r.misc3, r.loc.at[2]),
    ]
    for c in load:
        c.start()
    for c in load:
        c.wait()
    r.wo[...] = flatten_rows(r.w3[0]).astype(BF16)
    misc = flatten_rows(r.misc3[...])
    router = misc.astype(BF16)
    lines = jnp.transpose(misc)
    r.gain1[...] = lines[E : E + 1, :]
    gain = lines[E + 1 : E + 2, :]
    for n in range(HEAD_COUNT):
        hb, hh = z.holder(n)

        @pl.when(jnp.logical_not(p.owns(n)))
        def _():
            ref = r.att_in.at[n]
            remote(ref, ref, r.at_s.at[0], r.at_r.at[n], (d, hb, hh)).wait_recv()

        at = slice(n * HEAD_SIZE, (n + 1) * HEAD_SIZE)
        r.att_cat[: PT // 2, at] = r.att_in[n, :, :HEAD_SIZE]
        r.att_cat[PT // 2 :, at] = r.att_in[n, :, HEAD_SIZE:]
    att = r.att_cat[...]
    middle = x + nn(att, r.wo[...])
    inverse = lax.rsqrt(jnp.mean(middle * middle, axis=-1, keepdims=True) + EPSILON)
    routed = (middle * inverse * gain).astype(BF16)

    out = Sends(r.ex_s)

    def dispatch(part, values):
        r.disp[part] = nn(picks, values).reshape(E, C8, D).astype(BF16)
        for k in range(1, NG):
            e, device = p.group(k)
            out.put(r.disp.at[part, e], r.exp_in.at[part, g], r.ex_r.at[part * NG + g], device)
        r.exp_in[part, g] = r.disp[part, g]

    def arrivals(part):
        for k in range(1, NG):
            e, device = p.group(NG - k)
            ref = r.exp_in.at[part, e]
            remote(ref, ref, r.ex_s.at[0], r.ex_r.at[part * NG + e], device).wait_recv()

    def give_back(part, values):
        r.ret[part] = values.reshape(NG, C8, D).astype(BF16)
        for k in range(1, NG):
            e, device = p.group(k)
            out.put(r.ret.at[part, e], r.back.at[part, g], r.rt_r.at[part * NG + g], device)
        r.back[part, g] = r.ret[part, g]

    def returns(part):
        for k in range(1, NG):
            e, device = p.group(NG - k)
            ref = r.back.at[part, e]
            remote(ref, ref, r.ex_s.at[0], r.rt_r.at[part * NG + e], device).wait_recv()
        rows = r.back[part].astype(F32).reshape(E * C8, D).astype(BF16)
        return tn(picks, rows)

    copies = []

    def share_slots(part):
        src, dst, sem = r.exp_in.at[part], r.slots_ref.at[part, h], r.all_r.at[part * nh + h]
        out.put(src, dst, sem, (d, b, hy))
        out.put(src, dst, sem, (d, b, hc))
        c = pltpu.make_async_copy(src, dst, r.loc.at[3 + part])
        c.start()
        copies.append(c)

    def got_slots(part, hh):
        ref = r.slots_ref.at[part, hh]
        remote(ref, ref, r.ex_s.at[0], r.all_r.at[part * nh + hh], (d, b, hc)).wait_recv()

    dispatch(0, routed)
    logits = jnp.where(lane < E, nn(routed, router), -1e30)
    exps = jnp.exp(logits - jnp.max(logits, axis=-1, keepdims=True))
    probs = exps / jnp.sum(exps, axis=-1, keepdims=True)
    gate = jnp.sum(jnp.where(chosen, probs, 0.0), axis=-1, keepdims=True)
    dispatch(1, (gate * cot).astype(BF16))
    chunk = D
    chunks = z.FF // chunk
    steps.run_rest(14)

    arrivals(0)
    share_slots(0)
    rows_in = r.exp_in[0].astype(F32).reshape(NG * C8, D).astype(BF16)
    r.out_acc[...] = jnp.zeros_like(r.out_acc)

    def forward_step(c, carry):
        at = pl.ds(pl.multiple_of(c * chunk, chunk), chunk)
        pre = nn(rows_in, r.win[:, at])
        hidden, r.slope[:, at] = activate(pre)
        r.hid[:, at] = hidden
        r.out_acc[...] += nn(hidden, r.wout[at, :])
        return carry

    lax.fori_loop(0, chunks, forward_step, 0)
    give_back(0, r.out_acc[...])

    arrivals(1)
    share_slots(1)
    grad_out = r.exp_in[1].astype(F32).reshape(NG * C8, D).astype(BF16)
    r.out_acc[...] = jnp.zeros_like(r.out_acc)

    def backward_step(c, carry):
        at = pl.ds(pl.multiple_of(c * chunk, chunk), chunk)
        gp = grad_pre(grad_out, r.wout[at, :], r.slope[:, at])
        r.slope[:, at] = gp
        r.out_acc[...] += nt(gp, r.win[:, at])
        return carry

    lax.fori_loop(0, chunks, backward_step, 0)
    give_back(1, r.out_acc[...])
    saves = []

    def save(hh):
        for n, (src, dst) in enumerate(((r.hid, r.hid_ref), (r.slope, r.gp_ref))):
            c = pltpu.make_async_copy(src, dst.at[hh], r.loc.at[8 + n])
            c.start()
            saves.append(c)

    def other_slots(hh, forward):
        for part in range(2):
            got_slots(part, hh)
            if forward:
                ref = r.slots_ref.at[part, hh]
                out.put(ref, ref, r.all_r.at[part * nh + hh], (d, b, hc))
        c = pltpu.make_async_copy(r.slots_ref.at[:, hh], r.act_in, r.loc.at[10])
        c.start()
        c.wait()
        while saves:
            saves.pop().wait()
        others_in = r.act_in[0].astype(F32).reshape(NG * C8, D).astype(BF16)
        others_grad = r.act_in[1].astype(F32).reshape(NG * C8, D).astype(BF16)

        def step(c, carry):
            at = pl.ds(pl.multiple_of(c * chunk, chunk), chunk)
            r.hid[:, at], slope = activate(nn(others_in, r.win[:, at]))
            r.slope[:, at] = grad_pre(others_grad, r.wout[at, :], slope)
            return carry

        lax.fori_loop(0, chunks, step, 0)
        save(hh)

    save(h)
    steps.run_rest(10)
    for c in copies:
        c.wait()
    other_slots(hc, False)

    expert_rows = returns(0)
    r.layer_v[...] = (middle + gate * expert_rows).astype(BF16)
    written(r, "layer_ref")
    grad_gate = jnp.sum(cot * expert_rows, axis=-1, keepdims=True)
    grad_probs = jnp.where(chosen, grad_gate, 0.0) + share
    inner = jnp.sum(probs * grad_probs, axis=-1, keepdims=True)
    grad_logits = (probs * (grad_probs - inner)).astype(BF16)
    from_router = nt(grad_logits, router)
    grad_routed = returns(1) + from_router
    scaled = grad_routed * gain
    mean = jnp.mean(scaled * middle, axis=-1, keepdims=True)
    gmid = cot + inverse * scaled - middle * (inverse * inverse * inverse) * mean
    r.gmid[...] = gmid
    low_mid = gmid.astype(BF16)
    gatt = nt(low_mid, r.wo[...]).astype(BF16)

    for n in range(HEAD_COUNT):
        r.gatt[n] = both_halves(gatt[:, n * HEAD_SIZE : (n + 1) * HEAD_SIZE])
        hb, hh = z.holder(n)
        out.put(
            r.gatt.at[n], r.do_in.at[s], r.do_r.at[s], (d, hb, hh), jnp.logical_not(p.owns(n))
        )

        @pl.when(p.owns(n))
        def _():
            r.do_in[s] = r.gatt[n]

    term = grad_routed * middle * inverse
    high = term.astype(BF16)
    rest = (term - high.astype(F32)).astype(BF16)
    ones = jnp.broadcast_to((lane == E).astype(BF16), (PT, LANES))
    small = tn(routed, grad_logits) + tn(high, ones) + tn(rest, ones)
    terms = jnp.concatenate([tn(att, low_mid), small], axis=1)
    for t in range(z.ndev):
        r.dwo[t % nh, t // nh] = terms[t * z.R : (t + 1) * z.R].astype(BF16)
    other_slots(hy, True)

    def finish():
        while saves:
            saves.pop().wait()
        out.finish()

    return functools.partial(other_slots, hyc, False), finish


def backward_phase(z, r, p, steps, last_slots):
    d, b, h, s, me, hd, active = p.d, p.b, p.h, p.s, p.me, p.hd, p.active
    hy, hc, hyc = p.hy, p.hc, p.hyc
    nb, nh, nd, ns, nv, NG = z.n_blk, z.n_head, z.n_dp, z.ns, z.ndev, z.NG
    D, R, PT, HS, E = z.D, z.R, z.PT, HEAD_SIZE, z.E

    def sum_in(dst, src, terms, count):
        def body(e, carry):
            acc = src(e).astype(F32)
            for term in terms:
                acc = acc + term(e).astype(F32)
            dst[e] = acc.astype(BF16)
            return carry

        lax.fori_loop(0, count, body, 0)

    sums = Sends(r.su_s)
    y_sum = r.core_in.at[0]

    def got_sum(ref, k):
        remote(ref, ref, r.su_s.at[0], r.su_r.at[k], (d, b, hc)).wait_recv()

    def stage_core():
        sums.put(r.dwo.at[hyc], r.core_in.at[0], r.su_r.at[0], (d, b, hc))
        sums.put(r.dwo.at[hc], r.core_in.at[1], r.su_r.at[1], (d, b, hc))

    def stage_y():
        got_sum(r.core_in.at[0], 0)
        sum_in(r.y_src, lambda e: r.dwo[hy, e], [lambda e: r.core_in[0, e]], NG)
        sums.put(r.y_src, r.y_in, r.su_r.at[2], (d, b, hy))

    def stage_dp():
        got_sum(r.core_in.at[1], 1)
        got_sum(r.y_in, 2)
        sum_in(
            y_sum, lambda e: r.dwo[h, e], [lambda e: r.core_in[1, e], lambda e: r.y_in[e]], NG
        )
        for k in range(1, nd):
            q = lax.rem(d + k, nd)
            sums.put(y_sum.at[pl.ds(q * nb, nb)], r.dp_in.at[d], r.su_r.at[3 + d], (q, b, h))

    def stage_blk():
        others = [lax.rem(d + k, nd) for k in range(1, nd)]
        for q in others:
            got_sum(r.dp_in.at[q], 3 + q)

        def body(e, carry):
            acc = y_sum[d * nb + e].astype(F32)
            for q in others:
                acc = acc + r.dp_in[q, e].astype(F32)
            r.blk_src[e] = acc.astype(BF16)
            return carry

        lax.fori_loop(0, nb, body, 0)
        for k in range(1, nb):
            e = lax.rem(b + k, nb)
            sums.put(r.blk_src.at[e], r.blk_in.at[b], r.su_r.at[3 + nd + b], (d, e, h))
        r.blk_in[b] = r.blk_src[b]

    stage_core()

    def send_dq(t):
        return remote(
            r.dqkv.at[t], r.dq_in.at[hd], r.dq_s.at[t], r.dq_r.at[hd], (d, t // nh, t % nh)
        )

    def send_dw(k):
        t, device = p.any_peer(k)
        slot = d * HEAD_COUNT + hd
        return remote(r.dw3.at[t], r.dw_in.at[slot], r.dw_s.at[k], r.dw_r.at[slot], device)

    per = z.per
    part_rows = BLOCK // 2

    @pl.when(active)
    def _():
        r.dkv[...] = jnp.zeros_like(r.dkv)
        r.dq_acc[...] = jnp.zeros_like(r.dq_acc)
        r.dw[...] = jnp.zeros_like(r.dw)
        r.diag[...] = jnp.zeros_like(r.diag)
        r.sub[...] = jnp.zeros_like(r.sub)
        r.far[...] = jnp.zeros_like(r.far)

        def got_do(k, carry):
            t = lax.rem(s + k, ns)
            ref = r.do_in.at[t]
            remote(ref, ref, r.ex_s.at[0], r.do_r.at[t], p.in_sequence(t)).wait_recv()
            return carry

        lax.fori_loop(1, ns, got_do, 0)
        ones = jnp.ones((8, HS), BF16)
        for i in range(z.nq):
            here = slice(i * BLOCK, (i + 1) * BLOCK)
            pairs = [r.do_in[i * per + u] for u in range(per)]
            do = jnp.concatenate(
                [side for pair in pairs for side in (pair[:, :HS], pair[:, HS:])], axis=0
            )
            do = (do.astype(F32) * r.attl[here, HS:]).astype(BF16)
            r.dos[here, :] = do
            prod = do.astype(F32) * r.attl[here, :HS]
            high = prod.astype(BF16)
            rest = (prod - high.astype(F32)).astype(BF16)
            r.delta[i] = nt(ones, high) + nt(ones, rest)

    def tile(i, j, u):
        at = slice(j * BLOCK + u * part_rows, j * BLOCK + (u + 1) * part_rows)
        here = slice(i * BLOCK, (i + 1) * BLOCK)
        pr = r.probs[i, at, :]
        do = r.dos[here, :]
        ds = pr.astype(F32) * (nt(r.qkv[at, 2 * HS :], do) - r.delta[i, 0:1, :])
        low = ds.astype(BF16)
        part = slice(u * part_rows, (u + 1) * part_rows)
        if j == i:
            r.diag[part, :] += low.astype(F32)
        elif j == i - 1:
            r.sub[part, :] += low.astype(F32)
        else:
            r.far[...] += jnp.sum(low.astype(F32).reshape(part_rows // 8, 8, BLOCK), axis=0)
        both = jnp.concatenate([nn(low, r.qkv[here, :HS]), nn(pr, do)], axis=1)
        return at, both, nn(r.k_t[:, at], low)

    def column(j, hi):
        for u in range(2):
            acc = jnp.zeros((part_rows, 2 * HS), F32)
            for i in range(j, hi + 1):
                at, both, dq = tile(i, j, u)
                acc = acc + both
                r.dq_acc[i] += dq
            r.dkv[at, :] += acc

    def row(i, lo):
        acc = jnp.zeros((HS, BLOCK), F32)
        for j in range(lo, i + 1):
            for u in range(2):
                at, both, dq = tile(i, j, u)
                r.dkv[at, :] += both
                acc = acc + dq
        r.dq_acc[i] += acc

    lo, hi = 0, z.nq - 1
    turn = 0
    while lo <= hi:
        if turn == 1:
            stage_y()
        if turn == 3:
            stage_dp()
        if turn == z.nq - 1:
            stage_blk()

        @pl.when(active)
        def _():
            if turn % 2 == 0:
                n = lo
                column(n, hi)
            else:
                n = hi
                row(n, lo)
            here = slice(n * BLOCK, (n + 1) * BLOCK)
            dq = jnp.transpose(r.dq_acc[n]) * HS ** (-0.5)
            parts = jnp.concatenate([dq, r.dkv[here, :]], axis=1).astype(BF16)
            r.dw[...] += tn(r.xg[n * per : (n + 1) * per].reshape(BLOCK, D), parts)
            for u in range(per):
                t = n * per + u
                piece = parts[u * PT : (u + 1) * PT]
                r.dqkv[t, :PT] = piece[:, : 2 * HS]
                r.dqkv[t, PT:] = both_halves(piece[:, 2 * HS :])

                @pl.when(t != s)
                def _():
                    send_dq(t).start()

                @pl.when(t == s)
                def _():
                    r.dq_in[hd] = r.dqkv[t]

        if turn % 2 == 0:
            lo += 1
        else:
            hi -= 1
        turn += 1
        steps.run_rest(6)

    @pl.when(active)
    def _():
        jj = lax.broadcasted_iota(jnp.int32, (BLOCK, BLOCK), 0)
        ii = lax.broadcasted_iota(jnp.int32, (BLOCK, BLOCK), 1)
        lane = lax.broadcasted_iota(jnp.int32, (1, HS), 1)
        sums_of = jnp.zeros((1, HS), F32)
        half = BUCKETS // 2
        bounds = (0,) + LIMITS + (1 << 30,)
        tile_d, tile_s = r.diag[...], r.sub[...]

        def total(values):
            return jnp.sum(jnp.sum(values, axis=0, keepdims=True), axis=1, keepdims=True)

        for n in range(half):
            near, beyond = bounds[n], bounds[n + 1]
            dist = ii - jj
            part = total(
                jnp.where((dist >= near) & (dist < beyond), tile_d, 0.0)
                + jnp.where((dist + BLOCK >= near) & (dist + BLOCK < beyond), tile_s, 0.0)
            )
            if n == half - 1:
                part = part + total(r.far[...])
            sums_of = sums_of + jnp.where(lane == n, part, 0.0)
            if n > 0:
                part = total(jnp.where((-dist >= near) & (-dist < beyond), tile_d, 0.0))
                sums_of = sums_of + jnp.where(lane == half + n, part, 0.0)
        wide = jnp.concatenate([r.dw[...], jnp.broadcast_to(sums_of, (D, HS))], axis=1)
        split_rows(r.dw3, wide, R)

        def start_dw(k, carry):
            send_dw(k).start()
            return carry

        lax.fori_loop(1, nv, start_dw, 0)
        r.dw_in[d * HEAD_COUNT + hd] = r.dw3[me]

    last_slots()
    steps.finish_rest()
    load = [
        pltpu.make_async_copy(r.wg_ref.at[:, :, pl.ds(m * D, D)], r.w3.at[m], r.loc.at[5 + m])
        for m in range(3)
    ]
    for c in load:
        c.start()
    for m, c in enumerate(load):
        c.wait()
        r.wfull[:, m * D : (m + 1) * D] = flatten_rows(r.w3[m]).astype(BF16)

    for k in range(1, nb):
        e = lax.rem(b + k, nb)
        got_sum(r.blk_in.at[e], 3 + nd + e)
    acc = r.blk_in[0].astype(F32)
    for e in range(1, nb):
        acc = acc + r.blk_in[e].astype(F32)
    eye = lax.broadcasted_iota(jnp.int32, (R, R), 0) == lax.broadcasted_iota(jnp.int32, (R, R), 1)

    def as_row(column):
        return jnp.sum(jnp.where(eye, column, 0.0), axis=0, keepdims=True)

    r.go_v[...] = acc[:, :D]
    r.router_v[...] = jnp.concatenate([as_row(acc[:, D + e : D + e + 1]) for e in range(E)], axis=0)
    r.gain2_v[...] = as_row(acc[:, D + E : D + E + 1])
    written(r, "go_ref", "router_out", "gain2_ref")

    for n in range(HEAD_COUNT):
        hb, hh = z.holder(n)

        @pl.when(jnp.logical_not(p.owns(n)))
        def _():
            ref = r.dq_in.at[n]
            remote(ref, ref, r.dq_s.at[0], r.dq_r.at[n], (d, hb, hh)).wait_recv()

        for m in range(2):
            r.grad_cat[:, m * D + n * HS : m * D + (n + 1) * HS] = r.dq_in[
                n, :PT, m * HS : (m + 1) * HS
            ]
        at = slice(2 * D + n * HS, 2 * D + (n + 1) * HS)
        r.grad_cat[: PT // 2, at] = r.dq_in[n, PT:, :HS]
        r.grad_cat[PT // 2 :, at] = r.dq_in[n, PT:, HS:]
    grad_normed = nt(r.grad_cat[...], r.wfull[...])
    x = r.x_own[...].astype(F32)
    inverse = lax.rsqrt(jnp.mean(x * x, axis=-1, keepdims=True) + EPSILON)
    scaled = grad_normed * r.gain1[...]
    mean = jnp.mean(scaled * x, axis=-1, keepdims=True)
    grad_in = inverse * scaled - x * (inverse * inverse * inverse) * mean
    r.gtok_v[...] = (r.gmid[...] + grad_in).astype(BF16)
    written(r, "gtok_ref")

    for dd in range(nd):
        for n in range(HEAD_COUNT):
            hb, hh = z.holder(n)

            @pl.when(jnp.logical_not(p.owns(n) & (d == dd)))
            def _():
                ref = r.dw_in.at[dd * HEAD_COUNT + n]
                remote(
                    ref, ref, r.dw_s.at[0], r.dw_r.at[dd * HEAD_COUNT + n], (dd, hb, hh)
                ).wait_recv()

    lane = lax.broadcasted_iota(jnp.int32, (1, BUCKETS), 1)
    slot_lane = lax.broadcasted_iota(jnp.int32, (1, z.RL), 1)
    own_table = jnp.zeros((1, z.RL), F32)
    first = jnp.zeros((R, 1), F32)
    for n in range(HEAD_COUNT):
        part = r.dw_in[n].astype(F32)
        for dd in range(1, nd):
            part = part + r.dw_in[dd * HEAD_COUNT + n].astype(F32)
        for m, out in enumerate((r.gq_v, r.gk_v, r.gv_v)):
            cols = part[:, m * HS : (m + 1) * HS]
            out[:, n * HS : (n + 1) * HS] = cols
            own = r.w_own[:, m * D + n * HS : m * D + (n + 1) * HS].astype(F32)
            first = first + jnp.sum(cols * own, axis=-1, keepdims=True)
        line = part[0:1, 3 * HS : 3 * HS + BUCKETS]
        for k in range(z.RL):
            hit = lane + n * BUCKETS == me * z.RL + k
            value = jnp.sum(jnp.where(hit, line, 0.0), axis=1, keepdims=True)
            own_table = own_table + jnp.where(slot_lane == k, value, 0.0)
    own_gain = r.w_own[:, 4 * D :].astype(F32)[:, E : E + 1]
    r.gain1_v[...] = as_row(first / own_gain)
    r.table_v[...] = own_table
    written(r, "gain1_ref", "gq_ref", "gk_ref", "gv_ref", "table_ref")

    sums.finish()

    @pl.when(active)
    def _():
        for t in range(ns):

            @pl.when(t != s)
            def _():
                send_dq(t).wait_send()

        def sent_dw(k, carry):
            send_dw(k).wait_send()
            return carry

        lax.fori_loop(1, nv, sent_dw, 0)


def layer(z, x, order, ids, rows, weights, router_t, w_in, w_out, cot):
    D, R, PT, S, HS, E, NG, C8 = z.D, z.R, z.PT, z.S, HEAD_SIZE, z.E, z.NG, z.cap8
    nb, nd, nh, ns, nv = z.n_blk, z.n_dp, z.n_head, z.ns, z.ndev
    dma = pltpu.SemaphoreType.DMA
    vmem = pl.BlockSpec(memory_space=pltpu.VMEM)
    hbm = pl.BlockSpec(memory_space=pltpu.HBM)
    shape = jax.ShapeDtypeStruct
    inputs = {
        "x_ref": (x, hbm),
        "order_ref": (order, vmem),
        "ids_ref": (ids, hbm),
        "gain1_in": (rows[0][None, :], vmem),
        "gain2_in": (rows[1][None, :], vmem),
        "rel_ref": (rows[2][None, :], vmem),
        "wq_ref": (weights[0], hbm),
        "wk_ref": (weights[1], hbm),
        "wv_ref": (weights[2], hbm),
        "wo_ref": (weights[3], hbm),
        "router_ref": (router_t, vmem),
        "win_ref": (w_in, hbm),
        "wout_ref": (w_out, hbm),
        "cot_ref": (cot, hbm),
    }
    outputs = {
        "wg_ref": (shape((nv, R, z.wide), BF16), hbm),
        "slots_ref": (shape((2, nh, NG, C8, D), BF16), hbm),
        "hid_ref": (shape((nh, NG * C8, z.FF), BF16), hbm),
        "gp_ref": (shape((nh, NG * C8, z.FF), BF16), hbm),
        "layer_ref": (shape((PT, D), BF16), hbm),
        "gtok_ref": (shape((PT, D), BF16), hbm),
        "gain1_ref": (shape((1, R), F32), hbm),
        "gq_ref": (shape((R, D), F32), hbm),
        "gk_ref": (shape((R, D), F32), hbm),
        "gv_ref": (shape((R, D), F32), hbm),
        "go_ref": (shape((R, D), F32), hbm),
        "table_ref": (shape((1, z.RL), F32), hbm),
        "gain2_ref": (shape((1, R), F32), hbm),
        "router_out": (shape((E, R), F32), hbm),
    }
    V = pltpu.VMEM
    terms = D + LANES
    scratch = {
        "w_own": V((R, z.wide), BF16),
        "x_own": V((PT, D), BF16),
        "cot": V((PT, D), BF16),
        "ids": V(ids.shape, jnp.int32),
        "win": V((D, z.FF), BF16),
        "wout": V((z.FF, D), BF16),
        "slices": V((HEAD_COUNT, R, 4 * HS), BF16),
        "slices_in": V((nv, R, 4 * HS), BF16),
        "xg": V((ns, PT, D), BF16),
        "wh": V((D, 3 * HS), BF16),
        "gain1": V((1, D), F32),
        "far_bias": V((1, 1), F32),
        "bias_d": V((BLOCK, BLOCK), F32),
        "bias_s": V((BLOCK, BLOCK), F32),
        "qkv": V((S, 3 * HS), BF16),
        "v_t": V((HS, S), BF16),
        "k_t": V((HS, S), BF16),
        "s_scr": V((S, BLOCK), F32),
        "probs": V((z.nq, S, BLOCK), BF16),
        "attl": V((S, 2 * HS), F32),
        "att_src": V((ns, PT // 2, 2 * HS), BF16),
        "att_in": V((HEAD_COUNT, PT // 2, 2 * HS), BF16),
        "misc3": V((nv, R, LANES), BF16),
        "wo": V((D, D), BF16),
        "route": V((E * C8, PT), F32),
        "att_cat": V((PT, D), BF16),
        "disp": V((2, E, C8, D), BF16),
        "exp_in": V((2, NG, C8, D), BF16),
        "ret": V((2, NG, C8, D), BF16),
        "back": V((2, E, C8, D), BF16),
        "hid": V((NG * C8, z.FF), BF16),
        "slope": V((NG * C8, z.FF), BF16),
        "act_in": V((2, NG, C8, D), BF16),
        "out_acc": V((NG * C8, D), F32),
        "gmid": V((PT, D), F32),
        "gatt": V((HEAD_COUNT, PT // 2, 2 * HS), BF16),
        "do_in": V((ns, PT // 2, 2 * HS), BF16),
        "dwo": V((nh, NG, R, terms), BF16),
        "core_in": V((2, NG, R, terms), BF16),
        "y_src": V((NG, R, terms), BF16),
        "y_in": V((NG, R, terms), BF16),
        "dp_in": V((nd, nb, R, terms), BF16),
        "blk_src": V((nb, R, terms), BF16),
        "blk_in": V((nb, R, terms), BF16),
        "dos": V((S, HS), BF16),
        "delta": V((z.nq, 8, BLOCK), F32),
        "dq_acc": V((z.nq, HS, BLOCK), F32),
        "dw": V((D, 3 * HS), F32),
        "dw3": V((nv, R, 4 * HS), BF16),
        "diag": V((BLOCK, BLOCK), F32),
        "sub": V((BLOCK, BLOCK), F32),
        "far": V((8, BLOCK), F32),
        "dqkv": V((ns, PT + PT // 2, 2 * HS), BF16),
        "dq_in": V((HEAD_COUNT, PT + PT // 2, 2 * HS), BF16),
        "dw_in": V((nd * HEAD_COUNT, R, 4 * HS), BF16),
        "w3": V((3, nv, R, D), BF16),
        "wfull": V((D, 3 * D), BF16),
        "grad_cat": V((PT, 3 * D), BF16),
        "layer_v": V((PT, D), BF16),
        "gtok_v": V((PT, D), BF16),
        "gain1_v": V((1, R), F32),
        "gq_v": V((R, D), F32),
        "gk_v": V((R, D), F32),
        "gv_v": V((R, D), F32),
        "go_v": V((R, D), F32),
        "table_v": V((1, z.RL), F32),
        "gain2_v": V((1, R), F32),
        "router_v": V((E, R), F32),
        "out_sem": dma((len(PASSED),)),
        "in_sem": dma((9,)),
        "loc": dma((11,)),
        "sl_s": dma((HEAD_COUNT,)),
        "sl_r": dma((nv,)),
        "sd_s": dma((ns * nd,)),
        "x_s": dma((2 * (4 + 6 * (nb - 1) + 2 * nb - 1),)),
        "x_r": dma((2 * ns,)),
        "w0_s": dma((spread_copies(z, False),)),
        "w0_r": dma((nv,)),
        "w1_s": dma((spread_copies(z, True),)),
        "w1_r": dma((nv,)),
        "w2_s": dma((spread_copies(z, False),)),
        "w2_r": dma((nv,)),
        "at_s": dma((ns,)),
        "at_r": dma((HEAD_COUNT,)),
        "ex_s": dma((4 * (NG - 1) + 6 + HEAD_COUNT,)),
        "ex_r": dma((2 * NG,)),
        "rt_r": dma((2 * NG,)),
        "all_r": dma((2 * nh,)),
        "do_r": dma((ns,)),
        "su_s": dma((3 + nd - 1 + nb - 1,)),
        "su_r": dma((3 + nd + nb,)),
        "dq_s": dma((ns,)),
        "dq_r": dma((HEAD_COUNT,)),
        "dw_s": dma((nv,)),
        "dw_r": dma((nd * HEAD_COUNT,)),
    }
    names = tuple(inputs) + tuple(outputs) + tuple(scratch)
    results = pl.pallas_call(
        functools.partial(layer_kernel, z, names),
        out_shape=tuple(v[0] for v in outputs.values()),
        in_specs=[v[1] for v in inputs.values()],
        out_specs=tuple(v[1] for v in outputs.values()),
        scratch_shapes=list(scratch.values()),
        compiler_params=pltpu.CompilerParams(
            collective_id=0, has_side_effects=True, vmem_limit_bytes=VMEM_LIMIT
        ),
        name="layer",
    )(*[v[0] for v in inputs.values()])
    return dict(zip(outputs, results))


def expert_kernel(z, slots_ref, hid_ref, gp_ref, *refs):
    count = len(PASSED)
    passed_in, (gin_ref, gout_ref) = refs[:count], refs[count : count + 2]
    passed_out = refs[count + 2 : 2 * count + 2]
    rows_t, grad_out = refs[2 * count + 2 :]
    step = pl.program_id(0)

    @pl.when(step == 0)
    def _():
        for src, dst in zip(passed_in, passed_out):
            dst[...] = src[...]
        count = z.NG * z.cap8
        for n in range(z.n_head):
            at = slice(n * count, (n + 1) * count)
            rows_in = slots_ref[0, n].astype(F32).reshape(count, z.D)
            rows_t[:, at] = jnp.transpose(rows_in).astype(BF16)
            grad_out[at, :] = slots_ref[1, n].astype(F32).reshape(count, z.D).astype(BF16)

    total = z.n_head * z.NG * z.cap8
    chunk = hid_ref.shape[2]
    gin_ref[0] = nn(rows_t[...], gp_ref[...].reshape(total, chunk))
    gout_ref[0] = tn(hid_ref[...].reshape(total, chunk), grad_out[...])


def expert_weights(z, slots, hid, gp, passed):
    chunk = 768
    vmem = pl.BlockSpec(memory_space=pltpu.VMEM)
    total = z.n_head * z.NG * z.cap8
    in_chunk = pl.BlockSpec((1, z.D, chunk), lambda i: (0, 0, i))
    act_chunk = pl.BlockSpec((z.n_head, z.NG * z.cap8, chunk), lambda i: (0, 0, i))
    out_chunk = pl.BlockSpec((1, chunk, z.D), lambda i: (0, i, 0))
    return pl.pallas_call(
        functools.partial(expert_kernel, z),
        grid=(z.FF // chunk,),
        out_shape=(
            jax.ShapeDtypeStruct((1, z.D, z.FF), F32),
            jax.ShapeDtypeStruct((1, z.FF, z.D), F32),
        )
        + tuple(jax.ShapeDtypeStruct(a.shape, a.dtype) for a in passed),
        in_specs=[pl.BlockSpec(memory_space=pltpu.VMEM), act_chunk, act_chunk] + [vmem] * len(passed),
        out_specs=(in_chunk, out_chunk) + (vmem,) * len(passed),
        scratch_shapes=[
            pltpu.VMEM((z.D, total), BF16),
            pltpu.VMEM((total, z.D), BF16),
        ],
        compiler_params=pltpu.CompilerParams(
            dimension_semantics=("arbitrary",), vmem_limit_bytes=VMEM_LIMIT
        ),
        name="expert_weight_grads",
    )(slots, hid, gp, *passed)


def local(
    sizes,
    tokens,
    order,
    expert_ids,
    norm1_gain,
    w_query,
    w_key,
    w_value,
    w_attn_out,
    rel_table,
    norm2_gain,
    w_router,
    w_in,
    w_out,
    cotangent,
):
    R, D = w_query.shape
    E = w_router.shape[1]
    z = Sizes(*sizes, R, D, E, w_in.shape[2], tokens.shape[1])
    out = layer(
        z,
        tokens.reshape(z.PT, D),
        order,
        expert_ids.reshape(-1, z.PT),
        (norm1_gain, norm2_gain, rel_table),
        (w_query, w_key, w_value, w_attn_out),
        w_router.T,
        w_in,
        w_out,
        cotangent.reshape(z.PT, D),
    )
    g_in, g_out, *rest = expert_weights(
        z, out["slots_ref"], out["hid_ref"], out["gp_ref"], [out[name] for name in PASSED]
    )
    layer_out, gtok, gain1, gq, gk, gv, go, table, gain2, router = rest
    return (
        layer_out.reshape(tokens.shape),
        gtok.reshape(tokens.shape),
        gain1.reshape(R),
        gq,
        gk,
        gv,
        go,
        table.reshape(z.RL),
        gain2.reshape(R),
        router.T,
        g_in,
        g_out,
    )


def solution(mesh):
    everywhere = ("dp", "blk", "head")
    rows, table = P(everywhere), P(everywhere, None)
    tokens = P("dp", ("blk", "head"), None)
    expert = P(("dp", "blk"), None, None)
    in_specs = (
        tokens,
        P("dp", ("blk", "head")),
        P(),
        rows,
        table,
        table,
        table,
        table,
        rows,
        rows,
        table,
        expert,
        expert,
        tokens,
    )
    out_specs = (
        tokens, tokens, rows, table, table, table, table, rows, rows, table, expert, expert
    )
    sizes = (mesh.shape["dp"], mesh.shape["blk"], mesh.shape["head"])
    return jax.shard_map(
        functools.partial(local, sizes),
        mesh=mesh,
        in_specs=in_specs,
        out_specs=out_specs,
        check_vma=False,
    )
```

```python
import functools
import itertools
import types

import jax
import jax.numpy as jnp
from jax import lax
from jax.experimental import pallas as pl
from jax.experimental.pallas import tpu as pltpu
from jax.sharding import PartitionSpec as P

HEAD_COUNT = 12
HEAD_SIZE = 64
BUCKETS = 32
BLOCK = 256
EPSILON = 1e-06
AUX_WEIGHT = 1.0
LIMITS = (1, 2, 3, 4, 5, 6, 7, 8, 12, 16, 23, 32, 46, 64, 91)
INV_ROOT_TWO = 0.7071067811865476
INV_ROOT_TWO_PI = 0.3989422804014327
LANES = 128
VMEM_LIMIT = 62 * 1024 * 1024
PASSED = (
    "layer_ref", "gtok_ref", "gain1_ref", "gq_ref", "gk_ref", "gv_ref", "go_ref", "table_ref",
    "gain2_ref", "router_out",
)
MESH = pl.DeviceIdType.MESH
F32 = jnp.float32
BF16 = jnp.bfloat16


def both_halves(values):
    n = values.shape[0] // 2
    return jnp.concatenate([values[:n], values[n:]], axis=1)


def line_order(b, nb):
    out = [(b, b >= 0)]
    for k in range(1, nb):
        out.append((b - k, b >= k))
        out.append((b + k, b + k < nb))
    return out


class Sends:
    def __init__(self, sems):
        self.sems, self.made = sems, []

    def put(self, src, dst, recv, device, cond=None):
        c = remote(src, dst, self.sems.at[len(self.made)], recv, device)
        self.made.append((c, cond))
        self.each(c.start, cond)

    def each(self, action, cond):
        if cond is None:
            action()
        else:
            pl.when(cond)(action)

    def finish(self):
        for c, cond in self.made:
            self.each(c.wait_send, cond)


class Sizes:
    def __init__(self, n_dp, n_blk, n_head, rows, width, experts, hidden, piece):
        self.n_dp, self.n_blk, self.n_head = n_dp, n_blk, n_head
        self.ndev = n_dp * n_blk * n_head
        self.ns = n_blk * n_head
        self.R, self.D, self.E, self.FF, self.PT = rows, width, experts, hidden, piece
        self.S = piece * self.ns
        self.nq = self.S // BLOCK
        self.hb = HEAD_COUNT // n_blk
        self.cap = (5 * piece + 4 * experts - 1) // (4 * experts)
        self.cap8 = (self.cap + 7) // 8 * 8
        self.NG = n_dp * n_blk
        self.RL = HEAD_COUNT * BUCKETS // self.ndev
        self.wide = 4 * width + LANES
        self.per = BLOCK // piece
        assert self.hb < n_head and self.hb * n_blk == HEAD_COUNT
        assert experts == self.NG and n_head == 4


    def holder(self, n):
        return n // self.hb, n % self.hb + n // self.hb % 2


def nt(a, b):
    return lax.dot_general(a, b, (((1,), (1,)), ((), ())), preferred_element_type=F32)


def tn(a, b):
    return lax.dot_general(a, b, (((0,), (0,)), ((), ())), preferred_element_type=F32)


def nn(a, b):
    return jnp.dot(a, b, preferred_element_type=F32)


def place():
    return lax.axis_index("dp"), lax.axis_index("blk"), lax.axis_index("head")


def signal(device):
    pl.semaphore_signal(
        pltpu.get_barrier_semaphore(), inc=1, device_id=device, device_id_type=MESH
    )


def await_barrier(count):
    pl.semaphore_wait(pltpu.get_barrier_semaphore(), count)


def remote(src, dst, send, recv, device):
    return pltpu.make_async_remote_copy(
        src_ref=src, dst_ref=dst, send_sem=send, recv_sem=recv, device_id=device, device_id_type=MESH
    )


def flatten_rows(blocks):
    count, rows, lanes = blocks.shape
    wide = blocks.astype(F32)
    if rows % 8 == 0:
        return wide.reshape(count * rows, lanes)
    return jnp.concatenate([wide[i] for i in range(count)], axis=0)


def split_rows(dst_ref, values, rows):
    count = values.shape[0] // rows
    if rows % 8 == 0:
        dst_ref[...] = values.reshape(count, rows, values.shape[1]).astype(dst_ref.dtype)
    else:
        for i in range(count):
            dst_ref[i] = values[i * rows : (i + 1) * rows].astype(dst_ref.dtype)


def activate(pre):
    phi, bell = normal_parts(pre)
    slope = phi + pre * bell * INV_ROOT_TWO_PI
    return (pre * phi).astype(BF16), slope.astype(BF16)


def grad_pre(grad_out, w, slope):
    hidden = nt(grad_out, w).astype(BF16).astype(F32)
    return (hidden * slope.astype(F32)).astype(BF16)


def normal_parts(v):
    bell = jnp.exp(-0.5 * v * v)
    t = 1.0 / (1.0 + (0.3275911 * INV_ROOT_TWO) * jnp.abs(v))
    poly = t * (
        0.254829592
        + t * (-0.284496736 + t * (1.421413741 + t * (-1.453152027 + t * 1.061405429)))
    )
    tail = 0.5 * poly * bell
    return jnp.where(v >= 0, 1.0 - tail, tail), bell


def bias_tile(table, shift):
    j = lax.broadcasted_iota(jnp.int32, (BLOCK, BLOCK), 0)
    i = lax.broadcasted_iota(jnp.int32, (BLOCK, BLOCK), 1)
    dist = j - i + shift
    mag = jnp.abs(dist)
    half = BUCKETS // 2
    out = jnp.broadcast_to(table[0:1, 0:1], (BLOCK, BLOCK))
    for n, limit in enumerate(LIMITS):
        low = table[n + 1 : n + 2, 0:1]
        if shift == 0:
            high = table[half + n + 1 : half + n + 2, 0:1]
            out = jnp.where(mag >= limit, jnp.where(dist > 0, high, low), out)
        else:
            out = jnp.where(mag >= limit, low, out)
    return out


def bucket_sums(tile, shift):
    row = lax.broadcasted_iota(jnp.int32, (BLOCK, BLOCK), 0)
    column = lax.broadcasted_iota(jnp.int32, (BLOCK, BLOCK), 1)
    turn = (row + column == BLOCK - 1).astype(BF16)
    high = tile.astype(BF16)
    rest = (tile - high.astype(F32)).astype(BF16)
    turned = nn(turn, high) + nn(turn, rest)
    wide = jnp.concatenate([turned, jnp.zeros((BLOCK, BLOCK), F32)], axis=1)
    skewed = pltpu.roll(wide, 0, 1, stride=1, stride_axis=0)
    line = jnp.sum(skewed.reshape(BLOCK // 8, 8, 2 * BLOCK), axis=0)
    behind = lax.broadcasted_iota(jnp.int32, (2 * BLOCK, HEAD_SIZE), 0) - (BLOCK - 1) + shift
    bucket = jnp.zeros((2 * BLOCK, HEAD_SIZE), jnp.int32)
    for limit in LIMITS:
        bucket = bucket + (jnp.abs(behind) >= limit).astype(jnp.int32)
    bucket = bucket + jnp.where(behind < 0, BUCKETS // 2, 0)
    hot = bucket == lax.broadcasted_iota(jnp.int32, (2 * BLOCK, HEAD_SIZE), 1)
    parts = jnp.dot(
        line, hot.astype(F32), precision=lax.Precision.HIGHEST, preferred_element_type=F32
    )
    return jnp.sum(parts, axis=0, keepdims=True)


class Spread:
    def __init__(self, z, src, dst, send, recv, y_first, lanes):
        self.z, self.src, self.dst, self.recv = z, src, dst, recv
        self.sends, self.lanes = Sends(send), lanes
        d, b, h = place()
        self.at = (d, b, h)
        nh, nd = z.n_head, z.n_dp
        self.hy = lax.rem(h + 2, nh)
        self.hc = h + 1 - 2 * lax.rem(h, 2)
        self.hyc = lax.rem(self.hc + 2, nh)
        dto = [lax.rem(d + k, nd) for k in range(1, nd)]
        dfrom = [lax.rem(d + nd - k, nd) for k in range(1, nd)]
        ys = ([(d, self.hy)], [(d, self.hy)])
        xs = ([(p, h) for p in dto], [(p, h) for p in dfrom])
        self.first, self.second = (ys, xs) if y_first else (xs, ys)
        if y_first:
            self.second_slots = [(p, hh) for p in dfrom for hh in (h, self.hy)]
        else:
            self.second_slots = [(p, self.hy) for p in [d] + dfrom]
        self.core_slots = [(p, hh) for p in [d] + dfrom for hh in (self.hc, self.hyc)]

    def slot(self, dd, bb, hh):
        return (dd * self.z.n_blk + bb) * self.z.n_head + hh

    def ref(self, slot):
        return self.dst.at[slot, :, self.lanes]

    def put(self, src, slot, device, cond=None):
        self.sends.put(src, self.ref(slot), self.recv.at[slot], device, cond)

    def got(self, slot):
        d, b, h = self.at
        ref = self.ref(slot)
        remote(ref, ref, self.sends.sems.at[0], self.recv.at[slot], (d, b, self.hc)).wait_recv()

    def steps(self):
        d, b, h = self.at
        nb = self.z.n_blk

        def begin():
            mine = self.slot(d, b, h)
            self.put(self.src, mine, (d, b + 1, h), b + 1 < nb)
            self.put(self.src, mine, (d, b - 1, h), b >= 1)
            for dd, hh in self.first[0] + self.second[0] + [(d, self.hc)]:
                self.put(self.src, mine, (dd, b, hh))

        def line_arrival(k):
            for f, cond, to, more in (
                (b - k, b >= k, b + 1, b + 1 < nb),
                (b + k, b + k < nb, b - 1, b >= 1),
            ):
                slot = self.slot(d, f, h)
                pl.when(cond)(functools.partial(self.got, slot))
                if k < nb - 1:
                    self.put(self.ref(slot), slot, (d, to, h), cond & more)
                for dd, hh in self.first[0] + self.second[0] + [(d, self.hc)]:
                    self.put(self.ref(slot), slot, (dd, b, hh), cond)

        def first_arrival(p, f, cond):
            slot = self.slot(p[0], f, p[1])
            pl.when(cond)(functools.partial(self.got, slot))
            for dd, hh in self.second[0] + [(d, self.hc)]:
                self.put(self.ref(slot), slot, (dd, b, hh), cond)

        def second_arrival(p, f, cond):
            slot = self.slot(p[0], f, p[1])
            pl.when(cond)(functools.partial(self.got, slot))
            self.put(self.ref(slot), slot, (d, b, self.hc), cond)

        out = [begin]
        for k in range(1, nb):
            out.append(functools.partial(line_arrival, k))
        for p in self.first[1]:
            for f, cond in line_order(b, nb):
                out.append(functools.partial(first_arrival, p, f, cond))
        for p in self.second_slots:
            for f, cond in line_order(b, nb):
                out.append(functools.partial(second_arrival, p, f, cond))
        return out

    def finish(self):
        d, b, h = self.at
        for p in self.core_slots:
            for f in range(self.z.n_blk):
                self.got(self.slot(p[0], f, p[1]))
        self.sends.finish()


def spread_copies(z, y_first):
    nb, nd = z.n_blk, z.n_dp
    peers = 1 + nd - 1 + 1
    first = 1 if y_first else nd - 1
    second = peers - 1 - first
    second_slots = 2 * (nd - 1) if y_first else nd
    line = 2 * nb - 1
    return 2 + peers + (nb - 1) * 2 * (peers + 1) + first * line * (second + 1) + second_slots * line


class Place:
    def __init__(self, z):
        self.d, self.b, self.h = d, b, h = place()
        self.s = b * z.n_head + h
        self.me = d * z.ns + self.s
        self.g = d * z.n_blk + b
        first = lax.rem(b, 2)
        self.active = (h >= first) & (h < first + z.hb)
        self.hd = b * z.hb + jnp.clip(h - first, 0, z.hb - 1)
        self.hy = lax.rem(h + 2, z.n_head)
        self.hc = h + 1 - 2 * lax.rem(h, 2)
        self.hyc = lax.rem(self.hc + 2, z.n_head)
        self.z = z

    def any_peer(self, k):
        z = self.z
        t = lax.rem(self.me + k, z.ndev)
        return t, (t // z.ns, lax.rem(t // z.n_head, z.n_blk), lax.rem(t, z.n_head))

    def in_sequence(self, t):
        return (self.d, t // self.z.n_head, lax.rem(t, self.z.n_head))

    def owns(self, n):
        return self.active & (self.hd == n)

    def group(self, k):
        z = self.z
        e = lax.rem(self.g + k, z.NG)
        return e, (e // z.n_blk, lax.rem(e, z.n_blk), self.h)


def written(r, *names):
    for name in names:
        short = name.replace("_ref", "").replace("_out", "") + "_v"
        c = pltpu.make_async_copy(
            getattr(r, short), getattr(r, name), r.out_sem.at[PASSED.index(name)]
        )
        c.start()
        r.outgoing.append(c)


def layer_kernel(z, names, *refs):
    r = types.SimpleNamespace(**dict(zip(names, refs)))
    r.dkv = r.s_scr.at[:, pl.ds(0, 2 * HEAD_SIZE)]
    r.outgoing = []
    p = Place(z)

    def greet(k, carry):
        signal(p.any_peer(k)[1])
        return carry

    lax.fori_loop(1, z.ndev, greet, 0)
    D = z.D
    small = [
        pltpu.make_async_copy(ref, r.w_own.at[:, pl.ds(m * D, D)], r.in_sem.at[m])
        for m, ref in enumerate((r.wq_ref, r.wk_ref, r.wv_ref, r.wo_ref))
    ]
    small.append(pltpu.make_async_copy(r.x_ref, r.x_own, r.in_sem.at[4]))
    later = [
        pltpu.make_async_copy(r.cot_ref, r.cot, r.in_sem.at[5]),
        pltpu.make_async_copy(r.ids_ref, r.ids, r.in_sem.at[6]),
        pltpu.make_async_copy(r.win_ref.at[0], r.win, r.in_sem.at[7]),
        pltpu.make_async_copy(r.wout_ref.at[0], r.wout, r.in_sem.at[8]),
    ]
    for c in small + later:
        c.start()
    steps, finish_forward = forward_phase(z, r, p, small)
    for c in later:
        c.wait()
    last_slots, finish_middle = middle_phase(z, r, p, steps)
    backward_phase(z, r, p, steps, last_slots)
    finish_forward()
    finish_middle()
    for c in r.outgoing:
        c.wait()


def forward_phase(z, r, p, small):
    d, b, h, s, me, hd, active = p.d, p.b, p.h, p.s, p.me, p.hd, p.active
    hy, hc, hyc = p.hy, p.hc, p.hyc
    nb, nh, nd, ns = z.n_blk, z.n_head, z.n_dp, z.ns
    D, R, E, PT, HS = z.D, z.R, z.E, z.PT, HEAD_SIZE

    await_barrier(z.ndev - 1)
    small[4].wait()

    tokens = Sends(r.x_s)
    pieces = 2
    rows_of = PT // pieces

    def xref(slot, c):
        return r.xg.at[slot, pl.ds(c * rows_of, rows_of)]

    def put(src, slot, c, device, cond=None):
        tokens.put(src, xref(slot, c), r.x_r.at[slot * pieces + c], device, cond)

    def got(slot, c):
        ref = xref(slot, c)
        remote(ref, ref, r.x_s.at[0], r.x_r.at[slot * pieces + c], (d, b, hc)).wait_recv()

    for c in range(pieces):
        own = r.x_own.at[pl.ds(c * rows_of, rows_of)]
        put(own, s, c, (d, b + 1, h), b + 1 < nb)
        put(own, s, c, (d, b - 1, h), b >= 1)
        put(own, s, c, (d, b, hy))
        put(own, s, c, (d, b, hc))
    r.xg[s] = r.x_own[...]

    for c in small[:4]:
        c.wait()
    eye = lax.broadcasted_iota(jnp.int32, (R, R), 0) == lax.broadcasted_iota(jnp.int32, (R, R), 1)
    row_of = lax.broadcasted_iota(jnp.int32, (LANES, R), 0)
    tail = jnp.zeros((LANES, R), F32)
    rel = jnp.concatenate([r.rel_ref[...].astype(F32), jnp.zeros((1, R - z.RL), F32)], axis=1)
    rows = r.gain1_in[...].astype(F32), r.gain2_in[...].astype(F32), rel
    for n in range(3):
        tail = jnp.where(row_of == E + n, rows[n], tail)
    router_t = jnp.concatenate(
        [r.router_ref[...].astype(F32), jnp.zeros((LANES - E, R), F32)], axis=0
    )
    misc = nt(eye.astype(BF16), (tail + router_t).astype(BF16)).astype(BF16)
    r.w_own[:, 4 * D :] = misc
    for n in range(HEAD_COUNT):
        columns = [r.w_own[:, m * D + n * HS : m * D + (n + 1) * HS] for m in range(3)]
        r.slices[n] = jnp.concatenate(columns + [misc[:, E : E + HS]], axis=1)
    save_w = pltpu.make_async_copy(r.w_own, r.wg_ref.at[me], r.loc.at[0])
    save_w.start()
    to_heads = Sends(r.sl_s)
    over_dp = Sends(r.sd_s)
    for n in range(HEAD_COUNT):
        hb, hh = z.holder(n)
        to_heads.put(
            r.slices.at[n], r.slices_in.at[me], r.sl_r.at[me], (d, hb, hh),
            jnp.logical_not(p.owns(n)),
        )

    @pl.when(active)
    def _():
        r.slices_in[me] = r.slices[hd]

    for k in range(1, nb):
        for c in range(pieces):
            for f, cond, to, more in (
                (b - k, b >= k, b + 1, b + 1 < nb),
                (b + k, b + k < nb, b - 1, b >= 1),
            ):
                slot = f * nh + h
                pl.when(cond)(functools.partial(got, slot, c))
                if k < nb - 1:
                    put(xref(slot, c), slot, c, (d, to, h), cond & more)
                put(xref(slot, c), slot, c, (d, b, hy), cond)
                put(xref(slot, c), slot, c, (d, b, hc), cond)
        if k == 1:
            for m in range(ns):
                t = lax.rem(s + m, ns)
                slot = d * ns + t
                ref = r.slices_in.at[slot]
                if m > 0:
                    c = remote(ref, ref, r.sl_s.at[0], r.sl_r.at[slot], p.in_sequence(t))
                    pl.when(active)(c.wait_recv)
                for kd in range(1, nd):
                    over_dp.put(ref, ref, r.sl_r.at[slot], (lax.rem(d + kd, nd), b, h), active)

    for f, cond in line_order(b, nb):
        for c in range(pieces):
            slot = f * nh + hy
            pl.when(cond)(functools.partial(got, slot, c))
            put(xref(slot, c), slot, c, (d, b, hc), cond)

    cuts = (3 * D, z.wide, False), (0, 3 * D // 2, True), (3 * D // 2, 3 * D, False)
    parts = [
        Spread(
            z, r.w_own.at[:, pl.ds(lo, hi - lo)], r.wg_ref,
            getattr(r, "w%d_s" % n), getattr(r, "w%d_r" % n), y_first, pl.ds(lo, hi - lo),
        )
        for n, (lo, hi, y_first) in enumerate(cuts)
    ]
    first, rest_a, rest_b = [part.steps() for part in parts]
    steps = []
    for k in range(nb):
        steps += [first.pop(0), rest_a.pop(0), rest_b.pop(0)]
    steps = Steps(steps + first, rest_a, rest_b, parts, save_w)

    steps.run(3)

    @pl.when(active)
    def _():
        for kd in range(1, nd):
            dd = lax.rem(d + kd, nd)

            def got_slice(t, carry):
                ref = r.slices_in.at[dd * ns + t]
                remote(ref, ref, r.sl_s.at[0], r.sl_r.at[dd * ns + t], (dd, b, h)).wait_recv()
                return carry

            lax.fori_loop(0, ns, got_slice, 0)

        rows = flatten_rows(r.slices_in[...])
        r.wh[:, : 2 * HS] = rows[:, : 2 * HS].astype(BF16)
        r.wh[:, :HS] = (rows[:, :HS] * HS ** (-0.5)).astype(BF16)
        r.wh[:, 2 * HS :] = rows[:, 2 * HS : 3 * HS].astype(BF16)
        r.gain1[...] = jnp.transpose(rows[:, LANES:])[HS : HS + 1, :]
        column = lax.broadcasted_iota(jnp.int32, (1, D), 1).astype(F32)
        owner = jnp.floor((column + 0.5) * (1.0 / R))
        place_of = column - owner * R
        entry = jnp.where(place_of < z.RL, owner * z.RL + place_of, -1.0)
        wanted = hd * BUCKETS + lax.broadcasted_iota(jnp.int32, (BUCKETS, D), 0)
        pick = (entry == wanted.astype(F32)).astype(BF16)
        table = nn(pick, rows[:, LANES:].astype(BF16))[:, HS + 2 : HS + 3]
        r.bias_d[...] = bias_tile(table, 0)
        r.bias_s[...] = bias_tile(table, -BLOCK)
        r.far_bias[...] = table[BUCKETS // 2 - 1 : BUCKETS // 2, 0:1]

    for f in range(nb):
        for c in range(pieces):
            got(f * nh + hc, c)
            got(f * nh + hyc, c)
    tokens.finish()
    per = z.per
    half = BLOCK // 2

    @pl.when(active)
    def _():
        for i in range(z.nq):
            here = slice(i * BLOCK, (i + 1) * BLOCK)
            x = r.xg[i * per : (i + 1) * per].reshape(BLOCK, D).astype(F32)
            inverse = lax.rsqrt(jnp.mean(x * x, axis=-1, keepdims=True) + EPSILON)
            low = (x * inverse * r.gain1[...]).astype(BF16)
            r.xg[i * per : (i + 1) * per] = low.reshape(per, PT, D)
            mixed = nn(low, r.wh[...])
            r.qkv[here, :] = mixed.astype(BF16)
            r.v_t[:, here] = jnp.transpose(mixed[:, 2 * HS :]).astype(BF16)
            r.k_t[:, here] = jnp.transpose(mixed[:, HS : 2 * HS]).astype(BF16)

    def send_att(t):
        return remote(
            r.att_src.at[t], r.att_in.at[hd], r.at_s.at[t], r.at_r.at[hd], (d, t // nh, t % nh)
        )

    low_rows, high_rows = range(z.nq // 2), range(z.nq // 2, z.nq)
    order = [i for pair in zip(reversed(high_rows), reversed(low_rows)) for i in pair]
    for i in order:
        steps.run(4)

        @pl.when(active)
        def _():
            here = slice(i * BLOCK, (i + 1) * BLOCK)
            q = r.qkv[here, :HS]
            top = jnp.full((8, BLOCK), -1e30, F32)
            far = r.far_bias[...]
            for j in range(i + 1):
                for u in range(2):
                    at = slice(j * BLOCK + u * half, j * BLOCK + (u + 1) * half)
                    part = slice(u * half, (u + 1) * half)
                    if j == i:
                        bias = r.bias_d[part, :]
                    elif j == i - 1:
                        bias = r.bias_s[part, :]
                    else:
                        bias = far
                    sc = nt(r.qkv[at, HS : 2 * HS], q) + bias
                    r.s_scr[at, :] = sc
                    top = jnp.maximum(top, jnp.max(sc.reshape(half // 8, 8, BLOCK), axis=0))
            top = jnp.max(top, axis=0, keepdims=True)
            total = jnp.zeros((8, BLOCK), F32)
            acc = jnp.zeros((HS, BLOCK), F32)
            for j in range(i + 1):
                for u in range(2):
                    at = slice(j * BLOCK + u * half, j * BLOCK + (u + 1) * half)
                    e = jnp.exp(r.s_scr[at, :] - top)
                    total = total + jnp.sum(e.reshape(half // 8, 8, BLOCK), axis=0)
                    r.probs[i, at, :] = e.astype(BF16)
                at = slice(j * BLOCK, (j + 1) * BLOCK)
                acc = acc + nn(r.v_t[:, at], r.probs[i, at, :])
            total = jnp.sum(total, axis=0, keepdims=True)
            both = jnp.concatenate([acc, jnp.broadcast_to(total, (HS, BLOCK))], axis=0)
            both = jnp.transpose(both)
            inv = 1.0 / both[:, HS:]
            att = (both[:, :HS] * inv).astype(BF16)
            r.attl[here, :] = jnp.concatenate([att.astype(F32), inv], axis=1)
            for u in range(per):
                t = i * per + u
                r.att_src[t] = both_halves(att[u * PT : (u + 1) * PT])

                @pl.when(t != s)
                def _():
                    send_att(t).start()

                @pl.when(t == s)
                def _():
                    r.att_in[hd] = r.att_src[t]

    def finish():
        to_heads.finish()
        over_dp.finish()

        @pl.when(active)
        def _():
            for t in range(ns):

                @pl.when(t != s)
                def _():
                    send_att(t).wait_send()

    return steps, finish


class Steps:
    def __init__(self, first, rest_a, rest_b, parts, save):
        self.first, self.parts, self.save = first, parts, save
        self.rest = [
            step
            for pair in itertools.zip_longest(rest_b, rest_a)
            for step in pair
            if step is not None
        ]

    def run(self, count):
        for _ in range(min(count, len(self.first))):
            self.first.pop(0)()

    def finish_first(self):
        self.run(len(self.first))
        self.parts[0].finish()
        self.save.wait()

    def run_rest(self, count):
        for _ in range(min(count, len(self.rest))):
            self.rest.pop(0)()

    def finish_rest(self):
        self.run_rest(len(self.rest))
        for part in self.parts[1:]:
            part.finish()


def middle_phase(z, r, p, steps):
    d, b, h, me, g, s = p.d, p.b, p.h, p.me, p.g, p.s
    hy, hc, hyc = p.hy, p.hc, p.hyc
    nb, nh, nd, ns = z.n_blk, z.n_head, z.n_dp, z.ns
    D, E, PT, NG, C8 = z.D, z.E, z.PT, z.NG, z.cap8

    ids_row = r.ids[pl.ds(me, 1), :]
    order_row = r.order_ref[...]
    ids_col = jnp.transpose(jnp.broadcast_to(ids_row, (PT, PT)))
    order_col = jnp.transpose(jnp.broadcast_to(order_row, (PT, PT)))
    earlier = (order_col < order_row) & (ids_col == ids_row)
    rank = jnp.sum(earlier.astype(jnp.int32), axis=0, keepdims=True)
    slot = lax.broadcasted_iota(jnp.int32, (C8, PT), 0)
    base = (rank == slot) & (slot < z.cap)
    lane = lax.broadcasted_iota(jnp.int32, (1, LANES), 1)
    share = jnp.zeros((1, LANES), F32)
    ids_all = r.ids[...]
    for e in range(E):
        r.route[e * C8 : (e + 1) * C8, :] = (base & (ids_row == e)).astype(F32)
        count = jnp.sum((ids_all == e).astype(F32), axis=1, keepdims=True)
        count = jnp.sum(count, axis=0, keepdims=True)
        share = share + jnp.where(lane == e, count, 0.0)
    share = share * (AUX_WEIGHT * E / (ids_all.shape[0] * ids_all.shape[1]))
    chosen = ids_col[:, :1] == lane
    picks = r.route[...].astype(BF16)
    x = r.x_own[...].astype(F32)
    cot = r.cot[...].astype(F32)

    steps.finish_first()
    load = [
        pltpu.make_async_copy(r.wg_ref.at[:, :, pl.ds(3 * D, D)], r.w3.at[0], r.loc.at[1]),
        pltpu.make_async_copy(r.wg_ref.at[:, :, pl.ds(4 * D, LANES)], r.misc3, r.loc.at[2]),
    ]
    for c in load:
        c.start()
    for c in load:
        c.wait()
    r.wo[...] = flatten_rows(r.w3[0]).astype(BF16)
    misc = flatten_rows(r.misc3[...])
    router = misc.astype(BF16)
    lines = jnp.transpose(misc)
    r.gain1[...] = lines[E : E + 1, :]
    gain = lines[E + 1 : E + 2, :]
    for n in range(HEAD_COUNT):
        hb, hh = z.holder(n)

        @pl.when(jnp.logical_not(p.owns(n)))
        def _():
            ref = r.att_in.at[n]
            remote(ref, ref, r.at_s.at[0], r.at_r.at[n], (d, hb, hh)).wait_recv()

        at = slice(n * HEAD_SIZE, (n + 1) * HEAD_SIZE)
        r.att_cat[: PT // 2, at] = r.att_in[n, :, :HEAD_SIZE]
        r.att_cat[PT // 2 :, at] = r.att_in[n, :, HEAD_SIZE:]
    att = r.att_cat[...]
    middle = x + nn(att, r.wo[...])
    inverse = lax.rsqrt(jnp.mean(middle * middle, axis=-1, keepdims=True) + EPSILON)
    routed = (middle * inverse * gain).astype(BF16)

    out = Sends(r.ex_s)

    def dispatch(part, values):
        r.disp[part] = nn(picks, values).reshape(E, C8, D).astype(BF16)
        for k in range(1, NG):
            e, device = p.group(k)
            out.put(r.disp.at[part, e], r.exp_in.at[part, g], r.ex_r.at[part * NG + g], device)
        r.exp_in[part, g] = r.disp[part, g]

    def arrivals(part):
        for k in range(1, NG):
            e, device = p.group(NG - k)
            ref = r.exp_in.at[part, e]
            remote(ref, ref, r.ex_s.at[0], r.ex_r.at[part * NG + e], device).wait_recv()

    def give_back(part, values):
        r.ret[part] = values.reshape(NG, C8, D).astype(BF16)
        for k in range(1, NG):
            e, device = p.group(k)
            out.put(r.ret.at[part, e], r.back.at[part, g], r.rt_r.at[part * NG + g], device)
        r.back[part, g] = r.ret[part, g]

    def returns(part):
        for k in range(1, NG):
            e, device = p.group(NG - k)
            ref = r.back.at[part, e]
            remote(ref, ref, r.ex_s.at[0], r.rt_r.at[part * NG + e], device).wait_recv()
        rows = r.back[part].astype(F32).reshape(E * C8, D).astype(BF16)
        return tn(picks, rows)

    copies = []

    def share_slots(part):
        src, dst, sem = r.exp_in.at[part], r.slots_ref.at[part, h], r.all_r.at[part * nh + h]
        out.put(src, dst, sem, (d, b, hy))
        out.put(src, dst, sem, (d, b, hc))
        c = pltpu.make_async_copy(src, dst, r.loc.at[3 + part])
        c.start()
        copies.append(c)

    def got_slots(part, hh):
        ref = r.slots_ref.at[part, hh]
        remote(ref, ref, r.ex_s.at[0], r.all_r.at[part * nh + hh], (d, b, hc)).wait_recv()

    dispatch(0, routed)
    logits = jnp.where(lane < E, nn(routed, router), -1e30)
    exps = jnp.exp(logits - jnp.max(logits, axis=-1, keepdims=True))
    probs = exps / jnp.sum(exps, axis=-1, keepdims=True)
    gate = jnp.sum(jnp.where(chosen, probs, 0.0), axis=-1, keepdims=True)
    dispatch(1, (gate * cot).astype(BF16))
    chunk = D
    chunks = z.FF // chunk
    steps.run_rest(14)

    arrivals(0)
    share_slots(0)
    rows_in = r.exp_in[0].astype(F32).reshape(NG * C8, D).astype(BF16)
    r.out_acc[...] = jnp.zeros_like(r.out_acc)

    def forward_step(c, carry):
        at = pl.ds(pl.multiple_of(c * chunk, chunk), chunk)
        pre = nn(rows_in, r.win[:, at])
        hidden, r.slope[:, at] = activate(pre)
        r.hid[:, at] = hidden
        r.out_acc[...] += nn(hidden, r.wout[at, :])
        return carry

    lax.fori_loop(0, chunks, forward_step, 0)
    give_back(0, r.out_acc[...])

    arrivals(1)
    share_slots(1)
    grad_out = r.exp_in[1].astype(F32).reshape(NG * C8, D).astype(BF16)
    r.out_acc[...] = jnp.zeros_like(r.out_acc)

    def backward_step(c, carry):
        at = pl.ds(pl.multiple_of(c * chunk, chunk), chunk)
        gp = grad_pre(grad_out, r.wout[at, :], r.slope[:, at])
        r.slope[:, at] = gp
        r.out_acc[...] += nt(gp, r.win[:, at])
        return carry

    lax.fori_loop(0, chunks, backward_step, 0)
    give_back(1, r.out_acc[...])
    saves = []

    def save(hh):
        for n, (src, dst) in enumerate(((r.hid, r.hid_ref), (r.slope, r.gp_ref))):
            c = pltpu.make_async_copy(src, dst.at[hh], r.loc.at[8 + n])
            c.start()
            saves.append(c)

    def other_slots(hh, forward):
        for part in range(2):
            got_slots(part, hh)
            if forward:
                ref = r.slots_ref.at[part, hh]
                out.put(ref, ref, r.all_r.at[part * nh + hh], (d, b, hc))
        c = pltpu.make_async_copy(r.slots_ref.at[:, hh], r.act_in, r.loc.at[10])
        c.start()
        c.wait()
        while saves:
            saves.pop().wait()
        others_in = r.act_in[0].astype(F32).reshape(NG * C8, D).astype(BF16)
        others_grad = r.act_in[1].astype(F32).reshape(NG * C8, D).astype(BF16)

        def step(c, carry):
            at = pl.ds(pl.multiple_of(c * chunk, chunk), chunk)
            r.hid[:, at], slope = activate(nn(others_in, r.win[:, at]))
            r.slope[:, at] = grad_pre(others_grad, r.wout[at, :], slope)
            return carry

        lax.fori_loop(0, chunks, step, 0)
        save(hh)

    save(h)
    steps.run_rest(10)
    for c in copies:
        c.wait()
    other_slots(hc, False)

    expert_rows = returns(0)
    r.layer_v[...] = (middle + gate * expert_rows).astype(BF16)
    written(r, "layer_ref")
    grad_gate = jnp.sum(cot * expert_rows, axis=-1, keepdims=True)
    grad_probs = jnp.where(chosen, grad_gate, 0.0) + share
    inner = jnp.sum(probs * grad_probs, axis=-1, keepdims=True)
    grad_logits = (probs * (grad_probs - inner)).astype(BF16)
    from_router = nt(grad_logits, router)
    grad_routed = returns(1) + from_router
    scaled = grad_routed * gain
    mean = jnp.mean(scaled * middle, axis=-1, keepdims=True)
    gmid = cot + inverse * scaled - middle * (inverse * inverse * inverse) * mean
    r.gmid[...] = gmid
    low_mid = gmid.astype(BF16)
    gatt = nt(low_mid, r.wo[...]).astype(BF16)

    for n in range(HEAD_COUNT):
        r.gatt[n] = both_halves(gatt[:, n * HEAD_SIZE : (n + 1) * HEAD_SIZE])
        hb, hh = z.holder(n)
        out.put(
            r.gatt.at[n], r.do_in.at[s], r.do_r.at[s], (d, hb, hh), jnp.logical_not(p.owns(n))
        )

        @pl.when(p.owns(n))
        def _():
            r.do_in[s] = r.gatt[n]

    term = grad_routed * middle * inverse
    high = term.astype(BF16)
    rest = (term - high.astype(F32)).astype(BF16)
    ones = jnp.broadcast_to((lane == E).astype(BF16), (PT, LANES))
    small = tn(routed, grad_logits) + tn(high, ones) + tn(rest, ones)
    terms = jnp.concatenate([tn(att, low_mid), small], axis=1)
    for t in range(z.ndev):
        r.dwo[t % nh, t // nh] = terms[t * z.R : (t + 1) * z.R].astype(BF16)
    other_slots(hy, True)

    def finish():
        while saves:
            saves.pop().wait()
        out.finish()

    return functools.partial(other_slots, hyc, False), finish


def backward_phase(z, r, p, steps, last_slots):
    d, b, h, s, me, hd, active = p.d, p.b, p.h, p.s, p.me, p.hd, p.active
    hy, hc, hyc = p.hy, p.hc, p.hyc
    nb, nh, nd, ns, nv, NG = z.n_blk, z.n_head, z.n_dp, z.ns, z.ndev, z.NG
    D, R, PT, HS, E = z.D, z.R, z.PT, HEAD_SIZE, z.E

    def sum_in(dst, src, terms, count):
        def body(e, carry):
            acc = src(e).astype(F32)
            for term in terms:
                acc = acc + term(e).astype(F32)
            dst[e] = acc.astype(BF16)
            return carry

        lax.fori_loop(0, count, body, 0)

    sums = Sends(r.su_s)
    y_sum = r.core_in.at[0]

    def got_sum(ref, k):
        remote(ref, ref, r.su_s.at[0], r.su_r.at[k], (d, b, hc)).wait_recv()

    def stage_core():
        sums.put(r.dwo.at[hyc], r.core_in.at[0], r.su_r.at[0], (d, b, hc))
        sums.put(r.dwo.at[hc], r.core_in.at[1], r.su_r.at[1], (d, b, hc))

    def stage_y():
        got_sum(r.core_in.at[0], 0)
        sum_in(r.y_src, lambda e: r.dwo[hy, e], [lambda e: r.core_in[0, e]], NG)
        sums.put(r.y_src, r.y_in, r.su_r.at[2], (d, b, hy))

    def stage_dp():
        got_sum(r.core_in.at[1], 1)
        got_sum(r.y_in, 2)
        sum_in(
            y_sum, lambda e: r.dwo[h, e], [lambda e: r.core_in[1, e], lambda e: r.y_in[e]], NG
        )
        for k in range(1, nd):
            q = lax.rem(d + k, nd)
            sums.put(y_sum.at[pl.ds(q * nb, nb)], r.dp_in.at[d], r.su_r.at[3 + d], (q, b, h))

    def stage_blk():
        others = [lax.rem(d + k, nd) for k in range(1, nd)]
        for q in others:
            got_sum(r.dp_in.at[q], 3 + q)

        def body(e, carry):
            acc = y_sum[d * nb + e].astype(F32)
            for q in others:
                acc = acc + r.dp_in[q, e].astype(F32)
            r.blk_src[e] = acc.astype(BF16)
            return carry

        lax.fori_loop(0, nb, body, 0)
        for k in range(1, nb):
            e = lax.rem(b + k, nb)
            sums.put(r.blk_src.at[e], r.blk_in.at[b], r.su_r.at[3 + nd + b], (d, e, h))
        r.blk_in[b] = r.blk_src[b]

    stage_core()

    def send_dq(t):
        return remote(
            r.dqkv.at[t], r.dq_in.at[hd], r.dq_s.at[t], r.dq_r.at[hd], (d, t // nh, t % nh)
        )

    def send_dw(k):
        t, device = p.any_peer(k)
        slot = d * HEAD_COUNT + hd
        return remote(r.dw3.at[t], r.dw_in.at[slot], r.dw_s.at[k], r.dw_r.at[slot], device)

    per = z.per
    part_rows = BLOCK // 2

    @pl.when(active)
    def _():
        r.dkv[...] = jnp.zeros_like(r.dkv)
        r.dq_acc[...] = jnp.zeros_like(r.dq_acc)
        r.dw[...] = jnp.zeros_like(r.dw)
        r.diag[...] = jnp.zeros_like(r.diag)
        r.sub[...] = jnp.zeros_like(r.sub)
        r.far[...] = jnp.zeros_like(r.far)

        def got_do(k, carry):
            t = lax.rem(s + k, ns)
            ref = r.do_in.at[t]
            remote(ref, ref, r.ex_s.at[0], r.do_r.at[t], p.in_sequence(t)).wait_recv()
            return carry

        lax.fori_loop(1, ns, got_do, 0)
        ones = jnp.ones((8, HS), BF16)
        for i in range(z.nq):
            here = slice(i * BLOCK, (i + 1) * BLOCK)
            pairs = [r.do_in[i * per + u] for u in range(per)]
            do = jnp.concatenate(
                [side for pair in pairs for side in (pair[:, :HS], pair[:, HS:])], axis=0
            )
            do = (do.astype(F32) * r.attl[here, HS:]).astype(BF16)
            r.dos[here, :] = do
            prod = do.astype(F32) * r.attl[here, :HS]
            high = prod.astype(BF16)
            rest = (prod - high.astype(F32)).astype(BF16)
            r.delta[i] = nt(ones, high) + nt(ones, rest)

    def tile(i, j, u):
        at = slice(j * BLOCK + u * part_rows, j * BLOCK + (u + 1) * part_rows)
        here = slice(i * BLOCK, (i + 1) * BLOCK)
        pr = r.probs[i, at, :]
        do = r.dos[here, :]
        ds = pr.astype(F32) * (nt(r.qkv[at, 2 * HS :], do) - r.delta[i, 0:1, :])
        low = ds.astype(BF16)
        part = slice(u * part_rows, (u + 1) * part_rows)
        if j == i:
            r.diag[part, :] += low.astype(F32)
        elif j == i - 1:
            r.sub[part, :] += low.astype(F32)
        else:
            r.far[...] += jnp.sum(low.astype(F32).reshape(part_rows // 8, 8, BLOCK), axis=0)
        both = jnp.concatenate([nn(low, r.qkv[here, :HS]), nn(pr, do)], axis=1)
        return at, both, nn(r.k_t[:, at], low)

    def column(j, hi):
        for u in range(2):
            acc = jnp.zeros((part_rows, 2 * HS), F32)
            for i in range(j, hi + 1):
                at, both, dq = tile(i, j, u)
                acc = acc + both
                r.dq_acc[i] += dq
            r.dkv[at, :] += acc

    def row(i, lo):
        acc = jnp.zeros((HS, BLOCK), F32)
        for j in range(lo, i + 1):
            for u in range(2):
                at, both, dq = tile(i, j, u)
                r.dkv[at, :] += both
                acc = acc + dq
        r.dq_acc[i] += acc

    lo, hi = 0, z.nq - 1
    turn = 0
    while lo <= hi:
        if turn == 1:
            stage_y()
        if turn == 3:
            stage_dp()
        if turn == z.nq - 1:
            stage_blk()

        @pl.when(active)
        def _():
            if turn % 2 == 0:
                n = lo
                column(n, hi)
            else:
                n = hi
                row(n, lo)
            here = slice(n * BLOCK, (n + 1) * BLOCK)
            dq = jnp.transpose(r.dq_acc[n]) * HS ** (-0.5)
            parts = jnp.concatenate([dq, r.dkv[here, :]], axis=1).astype(BF16)
            r.dw[...] += tn(r.xg[n * per : (n + 1) * per].reshape(BLOCK, D), parts)
            for u in range(per):
                t = n * per + u
                piece = parts[u * PT : (u + 1) * PT]
                r.dqkv[t, :PT] = piece[:, : 2 * HS]
                r.dqkv[t, PT:] = both_halves(piece[:, 2 * HS :])

                @pl.when(t != s)
                def _():
                    send_dq(t).start()

                @pl.when(t == s)
                def _():
                    r.dq_in[hd] = r.dqkv[t]

        if turn % 2 == 0:
            lo += 1
        else:
            hi -= 1
        turn += 1
        steps.run_rest(6)

    @pl.when(active)
    def _():
        lane = lax.broadcasted_iota(jnp.int32, (1, HS), 1)
        half = BUCKETS // 2
        sums_of = bucket_sums(r.diag[...], 0) + bucket_sums(r.sub[...], BLOCK)
        beyond = jnp.sum(jnp.sum(r.far[...], axis=0, keepdims=True), axis=1, keepdims=True)
        sums_of = sums_of + jnp.where(lane == half - 1, beyond, 0.0)
        wide = jnp.concatenate([r.dw[...], jnp.broadcast_to(sums_of, (D, HS))], axis=1)
        split_rows(r.dw3, wide, R)

        def start_dw(k, carry):
            send_dw(k).start()
            return carry

        lax.fori_loop(1, nv, start_dw, 0)
        r.dw_in[d * HEAD_COUNT + hd] = r.dw3[me]

    last_slots()
    steps.finish_rest()
    load = [
        pltpu.make_async_copy(r.wg_ref.at[:, :, pl.ds(m * D, D)], r.w3.at[m], r.loc.at[5 + m])
        for m in range(3)
    ]
    for c in load:
        c.start()
    for m, c in enumerate(load):
        c.wait()
        r.wfull[:, m * D : (m + 1) * D] = flatten_rows(r.w3[m]).astype(BF16)

    for k in range(1, nb):
        e = lax.rem(b + k, nb)
        got_sum(r.blk_in.at[e], 3 + nd + e)
    acc = r.blk_in[0].astype(F32)
    for e in range(1, nb):
        acc = acc + r.blk_in[e].astype(F32)
    eye = lax.broadcasted_iota(jnp.int32, (R, R), 0) == lax.broadcasted_iota(jnp.int32, (R, R), 1)

    def as_row(column):
        return jnp.sum(jnp.where(eye, column, 0.0), axis=0, keepdims=True)

    r.go_v[...] = acc[:, :D]
    r.router_v[...] = jnp.concatenate([as_row(acc[:, D + e : D + e + 1]) for e in range(E)], axis=0)
    r.gain2_v[...] = as_row(acc[:, D + E : D + E + 1])
    written(r, "go_ref", "router_out", "gain2_ref")

    for n in range(HEAD_COUNT):
        hb, hh = z.holder(n)

        @pl.when(jnp.logical_not(p.owns(n)))
        def _():
            ref = r.dq_in.at[n]
            remote(ref, ref, r.dq_s.at[0], r.dq_r.at[n], (d, hb, hh)).wait_recv()

        for m in range(2):
            r.grad_cat[:, m * D + n * HS : m * D + (n + 1) * HS] = r.dq_in[
                n, :PT, m * HS : (m + 1) * HS
            ]
        at = slice(2 * D + n * HS, 2 * D + (n + 1) * HS)
        r.grad_cat[: PT // 2, at] = r.dq_in[n, PT:, :HS]
        r.grad_cat[PT // 2 :, at] = r.dq_in[n, PT:, HS:]
    grad_normed = nt(r.grad_cat[...], r.wfull[...])
    x = r.x_own[...].astype(F32)
    inverse = lax.rsqrt(jnp.mean(x * x, axis=-1, keepdims=True) + EPSILON)
    scaled = grad_normed * r.gain1[...]
    mean = jnp.mean(scaled * x, axis=-1, keepdims=True)
    grad_in = inverse * scaled - x * (inverse * inverse * inverse) * mean
    r.gtok_v[...] = (r.gmid[...] + grad_in).astype(BF16)
    written(r, "gtok_ref")

    for dd in range(nd):
        for n in range(HEAD_COUNT):
            hb, hh = z.holder(n)

            @pl.when(jnp.logical_not(p.owns(n) & (d == dd)))
            def _():
                ref = r.dw_in.at[dd * HEAD_COUNT + n]
                remote(
                    ref, ref, r.dw_s.at[0], r.dw_r.at[dd * HEAD_COUNT + n], (dd, hb, hh)
                ).wait_recv()

    first = jnp.zeros((R, HS), F32)
    lines = []
    for n in range(HEAD_COUNT):
        part = r.dw_in[n].astype(F32)
        for dd in range(1, nd):
            part = part + r.dw_in[dd * HEAD_COUNT + n].astype(F32)
        for m, out in enumerate((r.gq_v, r.gk_v, r.gv_v)):
            cols = part[:, m * HS : (m + 1) * HS]
            out[:, n * HS : (n + 1) * HS] = cols
            own = r.w_own[:, m * D + n * HS : m * D + (n + 1) * HS].astype(F32)
            first = first + cols * own
        lines.append(part[0:1, 3 * HS : 3 * HS + BUCKETS])
    first = jnp.sum(first, axis=-1, keepdims=True)
    table = jnp.concatenate(lines, axis=0)
    entry = lax.broadcasted_iota(jnp.int32, table.shape, 0) * BUCKETS + lax.broadcasted_iota(
        jnp.int32, table.shape, 1
    )
    slot_lane = lax.broadcasted_iota(jnp.int32, (1, z.RL), 1)
    own_table = jnp.zeros((1, z.RL), F32)
    for k in range(z.RL):
        value = jnp.sum(jnp.where(entry == me * z.RL + k, table, 0.0), axis=0, keepdims=True)
        value = jnp.sum(value, axis=1, keepdims=True)
        own_table = own_table + jnp.where(slot_lane == k, value, 0.0)
    own_gain = r.w_own[:, 4 * D :].astype(F32)[:, E : E + 1]
    r.gain1_v[...] = as_row(first / own_gain)
    r.table_v[...] = own_table
    written(r, "gain1_ref", "gq_ref", "gk_ref", "gv_ref", "table_ref")

    sums.finish()

    @pl.when(active)
    def _():
        for t in range(ns):

            @pl.when(t != s)
            def _():
                send_dq(t).wait_send()

        def sent_dw(k, carry):
            send_dw(k).wait_send()
            return carry

        lax.fori_loop(1, nv, sent_dw, 0)


def layer(z, x, order, ids, rows, weights, router_t, w_in, w_out, cot):
    D, R, PT, S, HS, E, NG, C8 = z.D, z.R, z.PT, z.S, HEAD_SIZE, z.E, z.NG, z.cap8
    nb, nd, nh, ns, nv = z.n_blk, z.n_dp, z.n_head, z.ns, z.ndev
    dma = pltpu.SemaphoreType.DMA
    vmem = pl.BlockSpec(memory_space=pltpu.VMEM)
    hbm = pl.BlockSpec(memory_space=pltpu.HBM)
    shape = jax.ShapeDtypeStruct
    inputs = {
        "x_ref": (x, hbm),
        "order_ref": (order, vmem),
        "ids_ref": (ids, hbm),
        "gain1_in": (rows[0][None, :], vmem),
        "gain2_in": (rows[1][None, :], vmem),
        "rel_ref": (rows[2][None, :], vmem),
        "wq_ref": (weights[0], hbm),
        "wk_ref": (weights[1], hbm),
        "wv_ref": (weights[2], hbm),
        "wo_ref": (weights[3], hbm),
        "router_ref": (router_t, vmem),
        "win_ref": (w_in, hbm),
        "wout_ref": (w_out, hbm),
        "cot_ref": (cot, hbm),
    }
    outputs = {
        "wg_ref": (shape((nv, R, z.wide), BF16), hbm),
        "slots_ref": (shape((2, nh, NG, C8, D), BF16), hbm),
        "hid_ref": (shape((nh, NG * C8, z.FF), BF16), hbm),
        "gp_ref": (shape((nh, NG * C8, z.FF), BF16), hbm),
        "layer_ref": (shape((PT, D), BF16), hbm),
        "gtok_ref": (shape((PT, D), BF16), hbm),
        "gain1_ref": (shape((1, R), F32), hbm),
        "gq_ref": (shape((R, D), F32), hbm),
        "gk_ref": (shape((R, D), F32), hbm),
        "gv_ref": (shape((R, D), F32), hbm),
        "go_ref": (shape((R, D), F32), hbm),
        "table_ref": (shape((1, z.RL), F32), hbm),
        "gain2_ref": (shape((1, R), F32), hbm),
        "router_out": (shape((E, R), F32), hbm),
    }
    V = pltpu.VMEM
    terms = D + LANES
    scratch = {
        "w_own": V((R, z.wide), BF16),
        "x_own": V((PT, D), BF16),
        "cot": V((PT, D), BF16),
        "ids": V(ids.shape, jnp.int32),
        "win": V((D, z.FF), BF16),
        "wout": V((z.FF, D), BF16),
        "slices": V((HEAD_COUNT, R, 4 * HS), BF16),
        "slices_in": V((nv, R, 4 * HS), BF16),
        "xg": V((ns, PT, D), BF16),
        "wh": V((D, 3 * HS), BF16),
        "gain1": V((1, D), F32),
        "far_bias": V((1, 1), F32),
        "bias_d": V((BLOCK, BLOCK), F32),
        "bias_s": V((BLOCK, BLOCK), F32),
        "qkv": V((S, 3 * HS), BF16),
        "v_t": V((HS, S), BF16),
        "k_t": V((HS, S), BF16),
        "s_scr": V((S, BLOCK), F32),
        "probs": V((z.nq, S, BLOCK), BF16),
        "attl": V((S, 2 * HS), F32),
        "att_src": V((ns, PT // 2, 2 * HS), BF16),
        "att_in": V((HEAD_COUNT, PT // 2, 2 * HS), BF16),
        "misc3": V((nv, R, LANES), BF16),
        "wo": V((D, D), BF16),
        "route": V((E * C8, PT), F32),
        "att_cat": V((PT, D), BF16),
        "disp": V((2, E, C8, D), BF16),
        "exp_in": V((2, NG, C8, D), BF16),
        "ret": V((2, NG, C8, D), BF16),
        "back": V((2, E, C8, D), BF16),
        "hid": V((NG * C8, z.FF), BF16),
        "slope": V((NG * C8, z.FF), BF16),
        "act_in": V((2, NG, C8, D), BF16),
        "out_acc": V((NG * C8, D), F32),
        "gmid": V((PT, D), F32),
        "gatt": V((HEAD_COUNT, PT // 2, 2 * HS), BF16),
        "do_in": V((ns, PT // 2, 2 * HS), BF16),
        "dwo": V((nh, NG, R, terms), BF16),
        "core_in": V((2, NG, R, terms), BF16),
        "y_src": V((NG, R, terms), BF16),
        "y_in": V((NG, R, terms), BF16),
        "dp_in": V((nd, nb, R, terms), BF16),
        "blk_src": V((nb, R, terms), BF16),
        "blk_in": V((nb, R, terms), BF16),
        "dos": V((S, HS), BF16),
        "delta": V((z.nq, 8, BLOCK), F32),
        "dq_acc": V((z.nq, HS, BLOCK), F32),
        "dw": V((D, 3 * HS), F32),
        "dw3": V((nv, R, 4 * HS), BF16),
        "diag": V((BLOCK, BLOCK), F32),
        "sub": V((BLOCK, BLOCK), F32),
        "far": V((8, BLOCK), F32),
        "dqkv": V((ns, PT + PT // 2, 2 * HS), BF16),
        "dq_in": V((HEAD_COUNT, PT + PT // 2, 2 * HS), BF16),
        "dw_in": V((nd * HEAD_COUNT, R, 4 * HS), BF16),
        "w3": V((3, nv, R, D), BF16),
        "wfull": V((D, 3 * D), BF16),
        "grad_cat": V((PT, 3 * D), BF16),
        "layer_v": V((PT, D), BF16),
        "gtok_v": V((PT, D), BF16),
        "gain1_v": V((1, R), F32),
        "gq_v": V((R, D), F32),
        "gk_v": V((R, D), F32),
        "gv_v": V((R, D), F32),
        "go_v": V((R, D), F32),
        "table_v": V((1, z.RL), F32),
        "gain2_v": V((1, R), F32),
        "router_v": V((E, R), F32),
        "out_sem": dma((len(PASSED),)),
        "in_sem": dma((9,)),
        "loc": dma((11,)),
        "sl_s": dma((HEAD_COUNT,)),
        "sl_r": dma((nv,)),
        "sd_s": dma((ns * nd,)),
        "x_s": dma((2 * (4 + 6 * (nb - 1) + 2 * nb - 1),)),
        "x_r": dma((2 * ns,)),
        "w0_s": dma((spread_copies(z, False),)),
        "w0_r": dma((nv,)),
        "w1_s": dma((spread_copies(z, True),)),
        "w1_r": dma((nv,)),
        "w2_s": dma((spread_copies(z, False),)),
        "w2_r": dma((nv,)),
        "at_s": dma((ns,)),
        "at_r": dma((HEAD_COUNT,)),
        "ex_s": dma((4 * (NG - 1) + 6 + HEAD_COUNT,)),
        "ex_r": dma((2 * NG,)),
        "rt_r": dma((2 * NG,)),
        "all_r": dma((2 * nh,)),
        "do_r": dma((ns,)),
        "su_s": dma((3 + nd - 1 + nb - 1,)),
        "su_r": dma((3 + nd + nb,)),
        "dq_s": dma((ns,)),
        "dq_r": dma((HEAD_COUNT,)),
        "dw_s": dma((nv,)),
        "dw_r": dma((nd * HEAD_COUNT,)),
    }
    names = tuple(inputs) + tuple(outputs) + tuple(scratch)
    results = pl.pallas_call(
        functools.partial(layer_kernel, z, names),
        out_shape=tuple(v[0] for v in outputs.values()),
        in_specs=[v[1] for v in inputs.values()],
        out_specs=tuple(v[1] for v in outputs.values()),
        scratch_shapes=list(scratch.values()),
        compiler_params=pltpu.CompilerParams(
            collective_id=0, has_side_effects=True, vmem_limit_bytes=VMEM_LIMIT
        ),
        name="layer",
    )(*[v[0] for v in inputs.values()])
    return dict(zip(outputs, results))


def expert_kernel(z, slots_ref, hid_ref, gp_ref, *refs):
    count = len(PASSED)
    passed_in, (gin_ref, gout_ref) = refs[:count], refs[count : count + 2]
    passed_out = refs[count + 2 : 2 * count + 2]
    rows_t, grad_out = refs[2 * count + 2 :]
    step = pl.program_id(0)

    @pl.when(step == 0)
    def _():
        for src, dst in zip(passed_in, passed_out):
            dst[...] = src[...]
        count = z.NG * z.cap8
        for n in range(z.n_head):
            at = slice(n * count, (n + 1) * count)
            rows_in = slots_ref[0, n].astype(F32).reshape(count, z.D)
            rows_t[:, at] = jnp.transpose(rows_in).astype(BF16)
            grad_out[at, :] = slots_ref[1, n].astype(F32).reshape(count, z.D).astype(BF16)

    total = z.n_head * z.NG * z.cap8
    chunk = hid_ref.shape[2]
    gin_ref[0] = nn(rows_t[...], gp_ref[...].reshape(total, chunk))
    gout_ref[0] = tn(hid_ref[...].reshape(total, chunk), grad_out[...])


def expert_weights(z, slots, hid, gp, passed):
    chunk = 768
    vmem = pl.BlockSpec(memory_space=pltpu.VMEM)
    total = z.n_head * z.NG * z.cap8
    in_chunk = pl.BlockSpec((1, z.D, chunk), lambda i: (0, 0, i))
    act_chunk = pl.BlockSpec((z.n_head, z.NG * z.cap8, chunk), lambda i: (0, 0, i))
    out_chunk = pl.BlockSpec((1, chunk, z.D), lambda i: (0, i, 0))
    return pl.pallas_call(
        functools.partial(expert_kernel, z),
        grid=(z.FF // chunk,),
        out_shape=(
            jax.ShapeDtypeStruct((1, z.D, z.FF), F32),
            jax.ShapeDtypeStruct((1, z.FF, z.D), F32),
        )
        + tuple(jax.ShapeDtypeStruct(a.shape, a.dtype) for a in passed),
        in_specs=[pl.BlockSpec(memory_space=pltpu.VMEM), act_chunk, act_chunk] + [vmem] * len(passed),
        out_specs=(in_chunk, out_chunk) + (vmem,) * len(passed),
        scratch_shapes=[
            pltpu.VMEM((z.D, total), BF16),
            pltpu.VMEM((total, z.D), BF16),
        ],
        compiler_params=pltpu.CompilerParams(
            dimension_semantics=("arbitrary",), vmem_limit_bytes=VMEM_LIMIT
        ),
        name="expert_weight_grads",
    )(slots, hid, gp, *passed)


def local(
    sizes,
    tokens,
    order,
    expert_ids,
    norm1_gain,
    w_query,
    w_key,
    w_value,
    w_attn_out,
    rel_table,
    norm2_gain,
    w_router,
    w_in,
    w_out,
    cotangent,
):
    R, D = w_query.shape
    E = w_router.shape[1]
    z = Sizes(*sizes, R, D, E, w_in.shape[2], tokens.shape[1])
    out = layer(
        z,
        tokens.reshape(z.PT, D),
        order,
        expert_ids.reshape(-1, z.PT),
        (norm1_gain, norm2_gain, rel_table),
        (w_query, w_key, w_value, w_attn_out),
        w_router.T,
        w_in,
        w_out,
        cotangent.reshape(z.PT, D),
    )
    g_in, g_out, *rest = expert_weights(
        z, out["slots_ref"], out["hid_ref"], out["gp_ref"], [out[name] for name in PASSED]
    )
    layer_out, gtok, gain1, gq, gk, gv, go, table, gain2, router = rest
    return (
        layer_out.reshape(tokens.shape),
        gtok.reshape(tokens.shape),
        gain1.reshape(R),
        gq,
        gk,
        gv,
        go,
        table.reshape(z.RL),
        gain2.reshape(R),
        router.T,
        g_in,
        g_out,
    )


def solution(mesh):
    everywhere = ("dp", "blk", "head")
    rows, table = P(everywhere), P(everywhere, None)
    tokens = P("dp", ("blk", "head"), None)
    expert = P(("dp", "blk"), None, None)
    in_specs = (
        tokens,
        P("dp", ("blk", "head")),
        P(),
        rows,
        table,
        table,
        table,
        table,
        rows,
        rows,
        table,
        expert,
        expert,
        tokens,
    )
    out_specs = (
        tokens, tokens, rows, table, table, table, table, rows, rows, table, expert, expert
    )
    sizes = (mesh.shape["dp"], mesh.shape["blk"], mesh.shape["head"])
    return jax.shard_map(
        functools.partial(local, sizes),
        mesh=mesh,
        in_specs=in_specs,
        out_specs=out_specs,
        check_vma=False,
    )
```

```python
import functools
import itertools
import types

import jax
import jax.numpy as jnp
from jax import lax
from jax.experimental import pallas as pl
from jax.experimental.pallas import tpu as pltpu
from jax.sharding import PartitionSpec as P

HEAD_COUNT = 12
HEAD_SIZE = 64
BUCKETS = 32
BLOCK = 256
EPSILON = 1e-06
AUX_WEIGHT = 1.0
LIMITS = (1, 2, 3, 4, 5, 6, 7, 8, 12, 16, 23, 32, 46, 64, 91)
INV_ROOT_TWO = 0.7071067811865476
INV_ROOT_TWO_PI = 0.3989422804014327
LANES = 128
VMEM_LIMIT = 62 * 1024 * 1024
PASSED = (
    "layer_ref", "gtok_ref", "gain1_ref", "gq_ref", "gk_ref", "gv_ref", "go_ref", "table_ref",
    "gain2_ref", "router_out",
)
MESH = pl.DeviceIdType.MESH
F32 = jnp.float32
BF16 = jnp.bfloat16


def both_halves(values):
    n = values.shape[0] // 2
    return jnp.concatenate([values[:n], values[n:]], axis=1)


def line_order(b, nb):
    out = [(b, b >= 0)]
    for k in range(1, nb):
        out.append((b - k, b >= k))
        out.append((b + k, b + k < nb))
    return out


class Sends:
    def __init__(self, sems):
        self.sems, self.made = sems, []

    def put(self, src, dst, recv, device, cond=None):
        c = remote(src, dst, self.sems.at[len(self.made)], recv, device)
        self.made.append((c, cond))
        self.each(c.start, cond)

    def each(self, action, cond):
        if cond is None:
            action()
        else:
            pl.when(cond)(action)

    def finish(self):
        for c, cond in self.made:
            self.each(c.wait_send, cond)


class Sizes:
    def __init__(self, n_dp, n_blk, n_head, rows, width, experts, hidden, piece):
        self.n_dp, self.n_blk, self.n_head = n_dp, n_blk, n_head
        self.ndev = n_dp * n_blk * n_head
        self.ns = n_blk * n_head
        self.R, self.D, self.E, self.FF, self.PT = rows, width, experts, hidden, piece
        self.S = piece * self.ns
        self.nq = self.S // BLOCK
        self.hb = HEAD_COUNT // n_blk
        self.cap = (5 * piece + 4 * experts - 1) // (4 * experts)
        self.cap8 = (self.cap + 7) // 8 * 8
        self.NG = n_dp * n_blk
        self.RL = HEAD_COUNT * BUCKETS // self.ndev
        self.wide = 4 * width + LANES
        self.per = BLOCK // piece
        assert self.hb < n_head and self.hb * n_blk == HEAD_COUNT
        assert experts == self.NG and n_head == 4


    def holder(self, n):
        return n // self.hb, n % self.hb + n // self.hb % 2


def nt(a, b):
    return lax.dot_general(a, b, (((1,), (1,)), ((), ())), preferred_element_type=F32)


def tn(a, b):
    return lax.dot_general(a, b, (((0,), (0,)), ((), ())), preferred_element_type=F32)


def nn(a, b):
    return jnp.dot(a, b, preferred_element_type=F32)


def place():
    return lax.axis_index("dp"), lax.axis_index("blk"), lax.axis_index("head")


def signal(device):
    pl.semaphore_signal(
        pltpu.get_barrier_semaphore(), inc=1, device_id=device, device_id_type=MESH
    )


def await_barrier(count):
    pl.semaphore_wait(pltpu.get_barrier_semaphore(), count)


def remote(src, dst, send, recv, device):
    return pltpu.make_async_remote_copy(
        src_ref=src, dst_ref=dst, send_sem=send, recv_sem=recv, device_id=device, device_id_type=MESH
    )


def flatten_rows(blocks):
    count, rows, lanes = blocks.shape
    wide = blocks.astype(F32)
    if rows % 8 == 0:
        return wide.reshape(count * rows, lanes)
    return jnp.concatenate([wide[i] for i in range(count)], axis=0)


def split_rows(dst_ref, values, rows):
    count = values.shape[0] // rows
    if rows % 8 == 0:
        dst_ref[...] = values.reshape(count, rows, values.shape[1]).astype(dst_ref.dtype)
    else:
        for i in range(count):
            dst_ref[i] = values[i * rows : (i + 1) * rows].astype(dst_ref.dtype)


def activate(pre):
    phi, bell = normal_parts(pre)
    slope = phi + pre * bell * INV_ROOT_TWO_PI
    return (pre * phi).astype(BF16), slope.astype(BF16)


def grad_pre(grad_out, w, slope):
    hidden = nt(grad_out, w).astype(BF16).astype(F32)
    return (hidden * slope.astype(F32)).astype(BF16)


def normal_parts(v):
    bell = jnp.exp(-0.5 * v * v)
    t = 1.0 / (1.0 + (0.3275911 * INV_ROOT_TWO) * jnp.abs(v))
    poly = t * (
        0.254829592
        + t * (-0.284496736 + t * (1.421413741 + t * (-1.453152027 + t * 1.061405429)))
    )
    tail = 0.5 * poly * bell
    return jnp.where(v >= 0, 1.0 - tail, tail), bell


def bias_tile(table, shift):
    j = lax.broadcasted_iota(jnp.int32, (BLOCK, BLOCK), 0)
    i = lax.broadcasted_iota(jnp.int32, (BLOCK, BLOCK), 1)
    dist = j - i + shift
    mag = jnp.abs(dist)
    half = BUCKETS // 2
    out = jnp.broadcast_to(table[0:1, 0:1], (BLOCK, BLOCK))
    for n, limit in enumerate(LIMITS):
        low = table[n + 1 : n + 2, 0:1]
        if shift == 0:
            high = table[half + n + 1 : half + n + 2, 0:1]
            out = jnp.where(mag >= limit, jnp.where(dist > 0, high, low), out)
        else:
            out = jnp.where(mag >= limit, low, out)
    return out


def bucket_sums(tile, shift):
    row = lax.broadcasted_iota(jnp.int32, (BLOCK, BLOCK), 0)
    column = lax.broadcasted_iota(jnp.int32, (BLOCK, BLOCK), 1)
    turn = (row + column == BLOCK - 1).astype(BF16)
    high = tile.astype(BF16)
    rest = (tile - high.astype(F32)).astype(BF16)
    turned = nn(turn, high) + nn(turn, rest)
    wide = jnp.concatenate([turned, jnp.zeros((BLOCK, BLOCK), F32)], axis=1)
    skewed = pltpu.roll(wide, 0, 1, stride=1, stride_axis=0)
    line = jnp.sum(skewed.reshape(BLOCK // 8, 8, 2 * BLOCK), axis=0)
    behind = lax.broadcasted_iota(jnp.int32, (2 * BLOCK, HEAD_SIZE), 0) - (BLOCK - 1) + shift
    bucket = jnp.zeros((2 * BLOCK, HEAD_SIZE), jnp.int32)
    for limit in LIMITS:
        bucket = bucket + (jnp.abs(behind) >= limit).astype(jnp.int32)
    bucket = bucket + jnp.where(behind < 0, BUCKETS // 2, 0)
    hot = bucket == lax.broadcasted_iota(jnp.int32, (2 * BLOCK, HEAD_SIZE), 1)
    parts = jnp.dot(
        line, hot.astype(F32), precision=lax.Precision.HIGHEST, preferred_element_type=F32
    )
    return jnp.sum(parts, axis=0, keepdims=True)


class Spread:
    def __init__(self, z, src, dst, send, recv, y_first, lanes):
        self.z, self.src, self.dst, self.recv = z, src, dst, recv
        self.sends, self.lanes = Sends(send), lanes
        d, b, h = place()
        self.at = (d, b, h)
        nh, nd = z.n_head, z.n_dp
        self.hy = lax.rem(h + 2, nh)
        self.hc = h + 1 - 2 * lax.rem(h, 2)
        self.hyc = lax.rem(self.hc + 2, nh)
        dto = [lax.rem(d + k, nd) for k in range(1, nd)]
        dfrom = [lax.rem(d + nd - k, nd) for k in range(1, nd)]
        ys = ([(d, self.hy)], [(d, self.hy)])
        xs = ([(p, h) for p in dto], [(p, h) for p in dfrom])
        self.first, self.second = (ys, xs) if y_first else (xs, ys)
        if y_first:
            self.second_slots = [(p, hh) for p in dfrom for hh in (h, self.hy)]
        else:
            self.second_slots = [(p, self.hy) for p in [d] + dfrom]
        self.core_slots = [(p, hh) for p in [d] + dfrom for hh in (self.hc, self.hyc)]

    def slot(self, dd, bb, hh):
        return (dd * self.z.n_blk + bb) * self.z.n_head + hh

    def ref(self, slot):
        return self.dst.at[slot, :, self.lanes]

    def put(self, src, slot, device, cond=None):
        self.sends.put(src, self.ref(slot), self.recv.at[slot], device, cond)

    def got(self, slot):
        d, b, h = self.at
        ref = self.ref(slot)
        remote(ref, ref, self.sends.sems.at[0], self.recv.at[slot], (d, b, self.hc)).wait_recv()

    def steps(self):
        d, b, h = self.at
        nb = self.z.n_blk

        def begin():
            mine = self.slot(d, b, h)
            self.put(self.src, mine, (d, b + 1, h), b + 1 < nb)
            self.put(self.src, mine, (d, b - 1, h), b >= 1)
            for dd, hh in self.first[0] + self.second[0] + [(d, self.hc)]:
                self.put(self.src, mine, (dd, b, hh))

        def line_arrival(k):
            for f, cond, to, more in (
                (b - k, b >= k, b + 1, b + 1 < nb),
                (b + k, b + k < nb, b - 1, b >= 1),
            ):
                slot = self.slot(d, f, h)
                pl.when(cond)(functools.partial(self.got, slot))
                if k < nb - 1:
                    self.put(self.ref(slot), slot, (d, to, h), cond & more)
                for dd, hh in self.first[0] + self.second[0] + [(d, self.hc)]:
                    self.put(self.ref(slot), slot, (dd, b, hh), cond)

        def first_arrival(p, f, cond):
            slot = self.slot(p[0], f, p[1])
            pl.when(cond)(functools.partial(self.got, slot))
            for dd, hh in self.second[0] + [(d, self.hc)]:
                self.put(self.ref(slot), slot, (dd, b, hh), cond)

        def second_arrival(p, f, cond):
            slot = self.slot(p[0], f, p[1])
            pl.when(cond)(functools.partial(self.got, slot))
            self.put(self.ref(slot), slot, (d, b, self.hc), cond)

        out = [begin]
        for k in range(1, nb):
            out.append(functools.partial(line_arrival, k))
        for p in self.first[1]:
            for f, cond in line_order(b, nb):
                out.append(functools.partial(first_arrival, p, f, cond))
        for p in self.second_slots:
            for f, cond in line_order(b, nb):
                out.append(functools.partial(second_arrival, p, f, cond))
        return out

    def finish(self):
        d, b, h = self.at
        for p in self.core_slots:
            for f in range(self.z.n_blk):
                self.got(self.slot(p[0], f, p[1]))
        self.sends.finish()


def spread_copies(z, y_first):
    nb, nd = z.n_blk, z.n_dp
    peers = 1 + nd - 1 + 1
    first = 1 if y_first else nd - 1
    second = peers - 1 - first
    second_slots = 2 * (nd - 1) if y_first else nd
    line = 2 * nb - 1
    return 2 + peers + (nb - 1) * 2 * (peers + 1) + first * line * (second + 1) + second_slots * line


class Place:
    def __init__(self, z):
        self.d, self.b, self.h = d, b, h = place()
        self.s = b * z.n_head + h
        self.me = d * z.ns + self.s
        self.g = d * z.n_blk + b
        first = lax.rem(b, 2)
        self.active = (h >= first) & (h < first + z.hb)
        self.hd = b * z.hb + jnp.clip(h - first, 0, z.hb - 1)
        self.hy = lax.rem(h + 2, z.n_head)
        self.hc = h + 1 - 2 * lax.rem(h, 2)
        self.hyc = lax.rem(self.hc + 2, z.n_head)
        self.z = z

    def any_peer(self, k):
        z = self.z
        t = lax.rem(self.me + k, z.ndev)
        return t, (t // z.ns, lax.rem(t // z.n_head, z.n_blk), lax.rem(t, z.n_head))

    def in_sequence(self, t):
        return (self.d, t // self.z.n_head, lax.rem(t, self.z.n_head))

    def owns(self, n):
        return self.active & (self.hd == n)

    def group(self, k):
        z = self.z
        e = lax.rem(self.g + k, z.NG)
        return e, (e // z.n_blk, lax.rem(e, z.n_blk), self.h)


def written(r, *names):
    for name in names:
        short = name.replace("_ref", "").replace("_out", "") + "_v"
        c = pltpu.make_async_copy(
            getattr(r, short), getattr(r, name), r.out_sem.at[PASSED.index(name)]
        )
        c.start()
        r.outgoing.append(c)


def layer_kernel(z, names, *refs):
    r = types.SimpleNamespace(**dict(zip(names, refs)))
    r.dkv = r.s_scr.at[:, pl.ds(0, 2 * HEAD_SIZE)]
    r.outgoing = []
    p = Place(z)

    def greet(k, carry):
        signal(p.any_peer(k)[1])
        return carry

    lax.fori_loop(1, z.ndev, greet, 0)
    D = z.D
    small = [
        pltpu.make_async_copy(ref, r.w_own.at[:, pl.ds(m * D, D)], r.in_sem.at[m])
        for m, ref in enumerate((r.wq_ref, r.wk_ref, r.wv_ref, r.wo_ref))
    ]
    small.append(pltpu.make_async_copy(r.x_ref, r.x_own, r.in_sem.at[4]))
    later = [
        pltpu.make_async_copy(r.cot_ref, r.cot, r.in_sem.at[5]),
        pltpu.make_async_copy(r.ids_ref, r.ids, r.in_sem.at[6]),
        pltpu.make_async_copy(r.win_ref.at[0], r.win, r.in_sem.at[7]),
        pltpu.make_async_copy(r.wout_ref.at[0], r.wout, r.in_sem.at[8]),
    ]
    for c in small + later:
        c.start()
    steps, finish_forward = forward_phase(z, r, p, small)
    for c in later:
        c.wait()
    last_slots, finish_middle = middle_phase(z, r, p, steps)
    backward_phase(z, r, p, steps, last_slots)
    finish_forward()
    finish_middle()
    for c in r.outgoing:
        c.wait()


def forward_phase(z, r, p, small):
    d, b, h, s, me, hd, active = p.d, p.b, p.h, p.s, p.me, p.hd, p.active
    hy, hc, hyc = p.hy, p.hc, p.hyc
    nb, nh, nd, ns = z.n_blk, z.n_head, z.n_dp, z.ns
    D, R, E, PT, HS = z.D, z.R, z.E, z.PT, HEAD_SIZE

    await_barrier(z.ndev - 1)
    small[4].wait()

    tokens = Sends(r.x_s)
    pieces = 2
    rows_of = PT // pieces

    def xref(slot, c):
        return r.xg.at[slot, pl.ds(c * rows_of, rows_of)]

    def put(src, slot, c, device, cond=None):
        tokens.put(src, xref(slot, c), r.x_r.at[slot * pieces + c], device, cond)

    def got(slot, c):
        ref = xref(slot, c)
        remote(ref, ref, r.x_s.at[0], r.x_r.at[slot * pieces + c], (d, b, hc)).wait_recv()

    for c in range(pieces):
        own = r.x_own.at[pl.ds(c * rows_of, rows_of)]
        put(own, s, c, (d, b + 1, h), b + 1 < nb)
        put(own, s, c, (d, b - 1, h), b >= 1)
        put(own, s, c, (d, b, hy))
        put(own, s, c, (d, b, hc))
    r.xg[s] = r.x_own[...]

    for c in small[:4]:
        c.wait()
    eye = lax.broadcasted_iota(jnp.int32, (R, R), 0) == lax.broadcasted_iota(jnp.int32, (R, R), 1)
    row_of = lax.broadcasted_iota(jnp.int32, (LANES, R), 0)
    tail = jnp.zeros((LANES, R), F32)
    rel = jnp.concatenate([r.rel_ref[...].astype(F32), jnp.zeros((1, R - z.RL), F32)], axis=1)
    rows = r.gain1_in[...].astype(F32), r.gain2_in[...].astype(F32), rel
    for n in range(3):
        tail = jnp.where(row_of == E + n, rows[n], tail)
    router_t = jnp.concatenate(
        [r.router_ref[...].astype(F32), jnp.zeros((LANES - E, R), F32)], axis=0
    )
    misc = nt(eye.astype(BF16), (tail + router_t).astype(BF16)).astype(BF16)
    r.w_own[:, 4 * D :] = misc
    for n in range(HEAD_COUNT):
        columns = [r.w_own[:, m * D + n * HS : m * D + (n + 1) * HS] for m in range(3)]
        r.slices[n] = jnp.concatenate(columns + [misc[:, E : E + HS]], axis=1)
    save_w = pltpu.make_async_copy(r.w_own, r.wg_ref.at[me], r.loc.at[0])
    save_w.start()
    to_heads = Sends(r.sl_s)
    over_dp = Sends(r.sd_s)
    for n in range(HEAD_COUNT):
        hb, hh = z.holder(n)
        to_heads.put(
            r.slices.at[n], r.slices_in.at[me], r.sl_r.at[me], (d, hb, hh),
            jnp.logical_not(p.owns(n)),
        )

    @pl.when(active)
    def _():
        r.slices_in[me] = r.slices[hd]

    for k in range(1, nb):
        for c in range(pieces):
            for f, cond, to, more in (
                (b - k, b >= k, b + 1, b + 1 < nb),
                (b + k, b + k < nb, b - 1, b >= 1),
            ):
                slot = f * nh + h
                pl.when(cond)(functools.partial(got, slot, c))
                if k < nb - 1:
                    put(xref(slot, c), slot, c, (d, to, h), cond & more)
                put(xref(slot, c), slot, c, (d, b, hy), cond)
                put(xref(slot, c), slot, c, (d, b, hc), cond)
        if k == 1:
            for m in range(ns):
                t = lax.rem(s + m, ns)
                slot = d * ns + t
                ref = r.slices_in.at[slot]
                if m > 0:
                    c = remote(ref, ref, r.sl_s.at[0], r.sl_r.at[slot], p.in_sequence(t))
                    pl.when(active)(c.wait_recv)
                for kd in range(1, nd):
                    over_dp.put(ref, ref, r.sl_r.at[slot], (lax.rem(d + kd, nd), b, h), active)

    for f, cond in line_order(b, nb):
        for c in range(pieces):
            slot = f * nh + hy
            pl.when(cond)(functools.partial(got, slot, c))
            put(xref(slot, c), slot, c, (d, b, hc), cond)

    cuts = (3 * D, z.wide, False), (0, 3 * D // 2, True), (3 * D // 2, 3 * D, False)
    parts = [
        Spread(
            z, r.w_own.at[:, pl.ds(lo, hi - lo)], r.wg_ref,
            getattr(r, "w%d_s" % n), getattr(r, "w%d_r" % n), y_first, pl.ds(lo, hi - lo),
        )
        for n, (lo, hi, y_first) in enumerate(cuts)
    ]
    first, rest_a, rest_b = [part.steps() for part in parts]
    steps = []
    for k in range(nb):
        steps += [first.pop(0), rest_a.pop(0), rest_b.pop(0)]
    steps = Steps(steps + first, rest_a, rest_b, parts, save_w)

    steps.run(3)

    @pl.when(active)
    def _():
        for kd in range(1, nd):
            dd = lax.rem(d + kd, nd)

            def got_slice(t, carry):
                ref = r.slices_in.at[dd * ns + t]
                remote(ref, ref, r.sl_s.at[0], r.sl_r.at[dd * ns + t], (dd, b, h)).wait_recv()
                return carry

            lax.fori_loop(0, ns, got_slice, 0)

        rows = flatten_rows(r.slices_in[...])
        r.wh[:, : 2 * HS] = rows[:, : 2 * HS].astype(BF16)
        r.wh[:, :HS] = (rows[:, :HS] * HS ** (-0.5)).astype(BF16)
        r.wh[:, 2 * HS :] = rows[:, 2 * HS : 3 * HS].astype(BF16)
        r.gain1[...] = jnp.transpose(rows[:, LANES:])[HS : HS + 1, :]
        column = lax.broadcasted_iota(jnp.int32, (1, D), 1).astype(F32)
        owner = jnp.floor((column + 0.5) * (1.0 / R))
        place_of = column - owner * R
        entry = jnp.where(place_of < z.RL, owner * z.RL + place_of, -1.0)
        wanted = hd * BUCKETS + lax.broadcasted_iota(jnp.int32, (BUCKETS, D), 0)
        pick = (entry == wanted.astype(F32)).astype(BF16)
        table = nn(pick, rows[:, LANES:].astype(BF16))[:, HS + 2 : HS + 3]
        r.bias_d[...] = bias_tile(table, 0)
        r.bias_s[...] = bias_tile(table, -BLOCK)
        r.far_bias[...] = table[BUCKETS // 2 - 1 : BUCKETS // 2, 0:1]

    for f in range(nb):
        for c in range(pieces):
            got(f * nh + hc, c)
            got(f * nh + hyc, c)
    tokens.finish()
    per = z.per
    half = BLOCK // 2

    @pl.when(active)
    def _():
        def project(i, carry):
            here = pl.ds(pl.multiple_of(i * BLOCK, BLOCK), BLOCK)
            own = pl.ds(i * per, per)
            x = r.xg[own].reshape(BLOCK, D).astype(F32)
            inverse = lax.rsqrt(jnp.mean(x * x, axis=-1, keepdims=True) + EPSILON)
            low = (x * inverse * r.gain1[...]).astype(BF16)
            r.xg[own] = low.reshape(per, PT, D)
            mixed = nn(low, r.wh[...])
            r.qkv[here, :] = mixed.astype(BF16)
            r.v_t[:, here] = jnp.transpose(mixed[:, 2 * HS :]).astype(BF16)
            r.k_t[:, here] = jnp.transpose(mixed[:, HS : 2 * HS]).astype(BF16)
            return carry

        lax.fori_loop(0, z.nq, project, 0)

    def send_att(t):
        return remote(
            r.att_src.at[t], r.att_in.at[hd], r.at_s.at[t], r.at_r.at[hd], (d, t // nh, t % nh)
        )

    low_rows, high_rows = range(z.nq // 2), range(z.nq // 2, z.nq)
    order = [i for pair in zip(reversed(high_rows), reversed(low_rows)) for i in pair]
    for i in order:
        steps.run(4)

        @pl.when(active)
        def _():
            here = slice(i * BLOCK, (i + 1) * BLOCK)
            q = r.qkv[here, :HS]
            top = jnp.full((8, BLOCK), -1e30, F32)
            far = r.far_bias[...]
            for j in range(i + 1):
                for u in range(2):
                    at = slice(j * BLOCK + u * half, j * BLOCK + (u + 1) * half)
                    part = slice(u * half, (u + 1) * half)
                    if j == i:
                        bias = r.bias_d[part, :]
                    elif j == i - 1:
                        bias = r.bias_s[part, :]
                    else:
                        bias = far
                    sc = nt(r.qkv[at, HS : 2 * HS], q) + bias
                    r.s_scr[at, :] = sc
                    top = jnp.maximum(top, jnp.max(sc.reshape(half // 8, 8, BLOCK), axis=0))
            top = jnp.max(top, axis=0, keepdims=True)
            total = jnp.zeros((8, BLOCK), F32)
            acc = jnp.zeros((HS, BLOCK), F32)
            for j in range(i + 1):
                for u in range(2):
                    at = slice(j * BLOCK + u * half, j * BLOCK + (u + 1) * half)
                    e = jnp.exp(r.s_scr[at, :] - top)
                    total = total + jnp.sum(e.reshape(half // 8, 8, BLOCK), axis=0)
                    r.probs[i, at, :] = e.astype(BF16)
                at = slice(j * BLOCK, (j + 1) * BLOCK)
                acc = acc + nn(r.v_t[:, at], r.probs[i, at, :])
            total = jnp.sum(total, axis=0, keepdims=True)
            both = jnp.concatenate([acc, jnp.broadcast_to(total, (HS, BLOCK))], axis=0)
            both = jnp.transpose(both)
            inv = 1.0 / both[:, HS:]
            att = (both[:, :HS] * inv).astype(BF16)
            r.attl[here, :] = jnp.concatenate([att.astype(F32), inv], axis=1)
            for u in range(per):
                t = i * per + u
                r.att_src[t] = both_halves(att[u * PT : (u + 1) * PT])

                @pl.when(t != s)
                def _():
                    send_att(t).start()

                @pl.when(t == s)
                def _():
                    r.att_in[hd] = r.att_src[t]

    def finish():
        to_heads.finish()
        over_dp.finish()

        @pl.when(active)
        def _():
            for t in range(ns):

                @pl.when(t != s)
                def _():
                    send_att(t).wait_send()

    return steps, finish


class Steps:
    def __init__(self, first, rest_a, rest_b, parts, save):
        self.first, self.parts, self.save = first, parts, save
        self.rest = [
            step
            for pair in itertools.zip_longest(rest_b, rest_a)
            for step in pair
            if step is not None
        ]

    def run(self, count):
        for _ in range(min(count, len(self.first))):
            self.first.pop(0)()

    def finish_first(self):
        self.run(len(self.first))
        self.parts[0].finish()
        self.save.wait()

    def run_rest(self, count):
        for _ in range(min(count, len(self.rest))):
            self.rest.pop(0)()

    def finish_rest(self):
        self.run_rest(len(self.rest))
        for part in self.parts[1:]:
            part.finish()


def middle_phase(z, r, p, steps):
    d, b, h, me, g, s = p.d, p.b, p.h, p.me, p.g, p.s
    hy, hc, hyc = p.hy, p.hc, p.hyc
    nb, nh, nd, ns = z.n_blk, z.n_head, z.n_dp, z.ns
    D, E, PT, NG, C8 = z.D, z.E, z.PT, z.NG, z.cap8

    ids_row = r.ids[pl.ds(me, 1), :]
    order_row = r.order_ref[...]
    ids_col = jnp.transpose(jnp.broadcast_to(ids_row, (PT, PT)))
    order_col = jnp.transpose(jnp.broadcast_to(order_row, (PT, PT)))
    earlier = (order_col < order_row) & (ids_col == ids_row)
    rank = jnp.sum(earlier.astype(jnp.int32), axis=0, keepdims=True)
    slot = lax.broadcasted_iota(jnp.int32, (C8, PT), 0)
    base = (rank == slot) & (slot < z.cap)
    lane = lax.broadcasted_iota(jnp.int32, (1, LANES), 1)
    share = jnp.zeros((1, LANES), F32)
    ids_all = r.ids[...]
    for e in range(E):
        r.route[e * C8 : (e + 1) * C8, :] = (base & (ids_row == e)).astype(F32)
        count = jnp.sum((ids_all == e).astype(F32), axis=1, keepdims=True)
        count = jnp.sum(count, axis=0, keepdims=True)
        share = share + jnp.where(lane == e, count, 0.0)
    share = share * (AUX_WEIGHT * E / (ids_all.shape[0] * ids_all.shape[1]))
    chosen = ids_col[:, :1] == lane
    picks = r.route[...].astype(BF16)
    x = r.x_own[...].astype(F32)
    cot = r.cot[...].astype(F32)

    steps.finish_first()
    load = [
        pltpu.make_async_copy(r.wg_ref.at[:, :, pl.ds(3 * D, D)], r.w3.at[0], r.loc.at[1]),
        pltpu.make_async_copy(r.wg_ref.at[:, :, pl.ds(4 * D, LANES)], r.misc3, r.loc.at[2]),
    ]
    for c in load:
        c.start()
    for c in load:
        c.wait()
    r.wo[...] = flatten_rows(r.w3[0]).astype(BF16)
    misc = flatten_rows(r.misc3[...])
    router = misc.astype(BF16)
    lines = jnp.transpose(misc)
    r.gain1[...] = lines[E : E + 1, :]
    gain = lines[E + 1 : E + 2, :]
    for n in range(HEAD_COUNT):
        hb, hh = z.holder(n)

        @pl.when(jnp.logical_not(p.owns(n)))
        def _():
            ref = r.att_in.at[n]
            remote(ref, ref, r.at_s.at[0], r.at_r.at[n], (d, hb, hh)).wait_recv()

        at = slice(n * HEAD_SIZE, (n + 1) * HEAD_SIZE)
        r.att_cat[: PT // 2, at] = r.att_in[n, :, :HEAD_SIZE]
        r.att_cat[PT // 2 :, at] = r.att_in[n, :, HEAD_SIZE:]
    att = r.att_cat[...]
    middle = x + nn(att, r.wo[...])
    inverse = lax.rsqrt(jnp.mean(middle * middle, axis=-1, keepdims=True) + EPSILON)
    routed = (middle * inverse * gain).astype(BF16)

    out = Sends(r.ex_s)

    def dispatch(part, values):
        r.disp[part] = nn(picks, values).reshape(E, C8, D).astype(BF16)
        for k in range(1, NG):
            e, device = p.group(k)
            out.put(r.disp.at[part, e], r.exp_in.at[part, g], r.ex_r.at[part * NG + g], device)
        r.exp_in[part, g] = r.disp[part, g]

    def arrivals(part):
        for k in range(1, NG):
            e, device = p.group(NG - k)
            ref = r.exp_in.at[part, e]
            remote(ref, ref, r.ex_s.at[0], r.ex_r.at[part * NG + e], device).wait_recv()

    def give_back(part, values):
        r.ret[part] = values.reshape(NG, C8, D).astype(BF16)
        for k in range(1, NG):
            e, device = p.group(k)
            out.put(r.ret.at[part, e], r.back.at[part, g], r.rt_r.at[part * NG + g], device)
        r.back[part, g] = r.ret[part, g]

    def returns(part):
        for k in range(1, NG):
            e, device = p.group(NG - k)
            ref = r.back.at[part, e]
            remote(ref, ref, r.ex_s.at[0], r.rt_r.at[part * NG + e], device).wait_recv()
        rows = r.back[part].astype(F32).reshape(E * C8, D).astype(BF16)
        return tn(picks, rows)

    copies = []

    def share_slots(part):
        src, dst, sem = r.exp_in.at[part], r.slots_ref.at[part, h], r.all_r.at[part * nh + h]
        out.put(src, dst, sem, (d, b, hy))
        out.put(src, dst, sem, (d, b, hc))
        c = pltpu.make_async_copy(src, dst, r.loc.at[3 + part])
        c.start()
        copies.append(c)

    def got_slots(part, hh):
        ref = r.slots_ref.at[part, hh]
        remote(ref, ref, r.ex_s.at[0], r.all_r.at[part * nh + hh], (d, b, hc)).wait_recv()

    dispatch(0, routed)
    logits = jnp.where(lane < E, nn(routed, router), -1e30)
    exps = jnp.exp(logits - jnp.max(logits, axis=-1, keepdims=True))
    probs = exps / jnp.sum(exps, axis=-1, keepdims=True)
    gate = jnp.sum(jnp.where(chosen, probs, 0.0), axis=-1, keepdims=True)
    dispatch(1, (gate * cot).astype(BF16))
    chunk = D // 2
    chunks = z.FF // chunk
    steps.run_rest(14)

    arrivals(0)
    share_slots(0)
    rows_in = r.exp_in[0].astype(F32).reshape(NG * C8, D).astype(BF16)
    r.out_acc[...] = jnp.zeros_like(r.out_acc)

    def forward_step(c, carry):
        at = pl.ds(pl.multiple_of(c * chunk, chunk), chunk)
        pre = nn(rows_in, r.win[:, at])
        hidden, r.slope[:, at] = activate(pre)
        r.hid[:, at] = hidden
        r.out_acc[...] += nn(hidden, r.wout[at, :])
        return carry

    lax.fori_loop(0, chunks, forward_step, 0)
    give_back(0, r.out_acc[...])

    arrivals(1)
    share_slots(1)
    grad_out = r.exp_in[1].astype(F32).reshape(NG * C8, D).astype(BF16)
    r.out_acc[...] = jnp.zeros_like(r.out_acc)

    def backward_step(c, carry):
        at = pl.ds(pl.multiple_of(c * chunk, chunk), chunk)
        gp = grad_pre(grad_out, r.wout[at, :], r.slope[:, at])
        r.slope[:, at] = gp
        r.out_acc[...] += nt(gp, r.win[:, at])
        return carry

    lax.fori_loop(0, chunks, backward_step, 0)
    give_back(1, r.out_acc[...])
    saves = []

    def save(hh):
        for n, (src, dst) in enumerate(((r.hid, r.hid_ref), (r.slope, r.gp_ref))):
            c = pltpu.make_async_copy(src, dst.at[hh], r.loc.at[8 + n])
            c.start()
            saves.append(c)

    def other_slots(hh, forward):
        for part in range(2):
            got_slots(part, hh)
            if forward:
                ref = r.slots_ref.at[part, hh]
                out.put(ref, ref, r.all_r.at[part * nh + hh], (d, b, hc))
        c = pltpu.make_async_copy(r.slots_ref.at[:, hh], r.act_in, r.loc.at[10])
        c.start()
        c.wait()
        while saves:
            saves.pop().wait()
        others_in = r.act_in[0].astype(F32).reshape(NG * C8, D).astype(BF16)
        others_grad = r.act_in[1].astype(F32).reshape(NG * C8, D).astype(BF16)

        def step(c, carry):
            at = pl.ds(pl.multiple_of(c * chunk, chunk), chunk)
            r.hid[:, at], slope = activate(nn(others_in, r.win[:, at]))
            r.slope[:, at] = grad_pre(others_grad, r.wout[at, :], slope)
            return carry

        lax.fori_loop(0, chunks, step, 0)
        save(hh)

    save(h)
    steps.run_rest(10)
    for c in copies:
        c.wait()
    other_slots(hc, False)

    expert_rows = returns(0)
    r.layer_v[...] = (middle + gate * expert_rows).astype(BF16)
    written(r, "layer_ref")
    grad_gate = jnp.sum(cot * expert_rows, axis=-1, keepdims=True)
    grad_probs = jnp.where(chosen, grad_gate, 0.0) + share
    inner = jnp.sum(probs * grad_probs, axis=-1, keepdims=True)
    grad_logits = (probs * (grad_probs - inner)).astype(BF16)
    from_router = nt(grad_logits, router)
    grad_routed = returns(1) + from_router
    scaled = grad_routed * gain
    mean = jnp.mean(scaled * middle, axis=-1, keepdims=True)
    gmid = cot + inverse * scaled - middle * (inverse * inverse * inverse) * mean
    r.gmid[...] = gmid
    low_mid = gmid.astype(BF16)
    gatt = nt(low_mid, r.wo[...]).astype(BF16)

    for n in range(HEAD_COUNT):
        r.gatt[n] = both_halves(gatt[:, n * HEAD_SIZE : (n + 1) * HEAD_SIZE])
        hb, hh = z.holder(n)
        out.put(
            r.gatt.at[n], r.do_in.at[s], r.do_r.at[s], (d, hb, hh), jnp.logical_not(p.owns(n))
        )

        @pl.when(p.owns(n))
        def _():
            r.do_in[s] = r.gatt[n]

    term = grad_routed * middle * inverse
    high = term.astype(BF16)
    rest = (term - high.astype(F32)).astype(BF16)
    ones = jnp.broadcast_to((lane == E).astype(BF16), (PT, LANES))
    small = tn(routed, grad_logits) + tn(high, ones) + tn(rest, ones)
    terms = jnp.concatenate([tn(att, low_mid), small], axis=1)
    for t in range(z.ndev):
        r.dwo[t % nh, t // nh] = terms[t * z.R : (t + 1) * z.R].astype(BF16)
    other_slots(hy, True)

    def finish():
        while saves:
            saves.pop().wait()
        out.finish()

    return functools.partial(other_slots, hyc, False), finish


def backward_phase(z, r, p, steps, last_slots):
    d, b, h, s, me, hd, active = p.d, p.b, p.h, p.s, p.me, p.hd, p.active
    hy, hc, hyc = p.hy, p.hc, p.hyc
    nb, nh, nd, ns, nv, NG = z.n_blk, z.n_head, z.n_dp, z.ns, z.ndev, z.NG
    D, R, PT, HS, E = z.D, z.R, z.PT, HEAD_SIZE, z.E

    def sum_in(dst, src, terms, count):
        def body(e, carry):
            acc = src(e).astype(F32)
            for term in terms:
                acc = acc + term(e).astype(F32)
            dst[e] = acc.astype(BF16)
            return carry

        lax.fori_loop(0, count, body, 0)

    sums = Sends(r.su_s)
    y_sum = r.core_in.at[0]

    def got_sum(ref, k):
        remote(ref, ref, r.su_s.at[0], r.su_r.at[k], (d, b, hc)).wait_recv()

    def stage_core():
        sums.put(r.dwo.at[hyc], r.core_in.at[0], r.su_r.at[0], (d, b, hc))
        sums.put(r.dwo.at[hc], r.core_in.at[1], r.su_r.at[1], (d, b, hc))

    def stage_y():
        got_sum(r.core_in.at[0], 0)
        sum_in(r.y_src, lambda e: r.dwo[hy, e], [lambda e: r.core_in[0, e]], NG)
        sums.put(r.y_src, r.y_in, r.su_r.at[2], (d, b, hy))

    def stage_dp():
        got_sum(r.core_in.at[1], 1)
        got_sum(r.y_in, 2)
        sum_in(
            y_sum, lambda e: r.dwo[h, e], [lambda e: r.core_in[1, e], lambda e: r.y_in[e]], NG
        )
        for k in range(1, nd):
            q = lax.rem(d + k, nd)
            sums.put(y_sum.at[pl.ds(q * nb, nb)], r.dp_in.at[d], r.su_r.at[3 + d], (q, b, h))

    def stage_blk():
        others = [lax.rem(d + k, nd) for k in range(1, nd)]
        for q in others:
            got_sum(r.dp_in.at[q], 3 + q)

        def body(e, carry):
            acc = y_sum[d * nb + e].astype(F32)
            for q in others:
                acc = acc + r.dp_in[q, e].astype(F32)
            r.blk_src[e] = acc.astype(BF16)
            return carry

        lax.fori_loop(0, nb, body, 0)
        for k in range(1, nb):
            e = lax.rem(b + k, nb)
            sums.put(r.blk_src.at[e], r.blk_in.at[b], r.su_r.at[3 + nd + b], (d, e, h))
        r.blk_in[b] = r.blk_src[b]

    stage_core()

    def send_dq(t):
        return remote(
            r.dqkv.at[t], r.dq_in.at[hd], r.dq_s.at[t], r.dq_r.at[hd], (d, t // nh, t % nh)
        )

    def send_dw(k):
        t, device = p.any_peer(k)
        slot = d * HEAD_COUNT + hd
        return remote(r.dw3.at[t], r.dw_in.at[slot], r.dw_s.at[k], r.dw_r.at[slot], device)

    per = z.per
    part_rows = BLOCK // 2

    @pl.when(active)
    def _():
        r.dkv[...] = jnp.zeros_like(r.dkv)
        r.dq_acc[...] = jnp.zeros_like(r.dq_acc)
        r.dw[...] = jnp.zeros_like(r.dw)
        r.diag[...] = jnp.zeros_like(r.diag)
        r.sub[...] = jnp.zeros_like(r.sub)
        r.far[...] = jnp.zeros_like(r.far)

        def got_do(k, carry):
            t = lax.rem(s + k, ns)
            ref = r.do_in.at[t]
            remote(ref, ref, r.ex_s.at[0], r.do_r.at[t], p.in_sequence(t)).wait_recv()
            return carry

        lax.fori_loop(1, ns, got_do, 0)
        ones = jnp.ones((8, HS), BF16)

        def prepare(i, carry):
            here = pl.ds(pl.multiple_of(i * BLOCK, BLOCK), BLOCK)
            pairs = [r.do_in[i * per + u] for u in range(per)]
            do = jnp.concatenate(
                [side for pair in pairs for side in (pair[:, :HS], pair[:, HS:])], axis=0
            )
            do = (do.astype(F32) * r.attl[here, HS:]).astype(BF16)
            r.dos[here, :] = do
            prod = do.astype(F32) * r.attl[here, :HS]
            high = prod.astype(BF16)
            rest = (prod - high.astype(F32)).astype(BF16)
            r.delta[i] = nt(ones, high) + nt(ones, rest)
            return carry

        lax.fori_loop(0, z.nq, prepare, 0)

    def tile(i, j, u):
        at = slice(j * BLOCK + u * part_rows, j * BLOCK + (u + 1) * part_rows)
        here = slice(i * BLOCK, (i + 1) * BLOCK)
        pr = r.probs[i, at, :]
        do = r.dos[here, :]
        ds = pr.astype(F32) * (nt(r.qkv[at, 2 * HS :], do) - r.delta[i, 0:1, :])
        low = ds.astype(BF16)
        part = slice(u * part_rows, (u + 1) * part_rows)
        if j == i:
            r.diag[part, :] += low.astype(F32)
        elif j == i - 1:
            r.sub[part, :] += low.astype(F32)
        else:
            r.far[...] += jnp.sum(low.astype(F32).reshape(part_rows // 8, 8, BLOCK), axis=0)
        both = jnp.concatenate([nn(low, r.qkv[here, :HS]), nn(pr, do)], axis=1)
        return at, both, nn(r.k_t[:, at], low)

    def column(j, hi):
        for u in range(2):
            acc = jnp.zeros((part_rows, 2 * HS), F32)
            for i in range(j, hi + 1):
                at, both, dq = tile(i, j, u)
                acc = acc + both
                r.dq_acc[i] += dq
            r.dkv[at, :] += acc

    def row(i, lo):
        acc = jnp.zeros((HS, BLOCK), F32)
        for j in range(lo, i + 1):
            for u in range(2):
                at, both, dq = tile(i, j, u)
                r.dkv[at, :] += both
                acc = acc + dq
        r.dq_acc[i] += acc

    lo, hi = 0, z.nq - 1
    turn = 0
    while lo <= hi:
        if turn == 1:
            stage_y()
        if turn == 3:
            stage_dp()
        if turn == z.nq - 1:
            stage_blk()

        @pl.when(active)
        def _():
            if turn % 2 == 0:
                n = lo
                column(n, hi)
            else:
                n = hi
                row(n, lo)
            here = slice(n * BLOCK, (n + 1) * BLOCK)
            dq = jnp.transpose(r.dq_acc[n]) * HS ** (-0.5)
            parts = jnp.concatenate([dq, r.dkv[here, :]], axis=1).astype(BF16)
            r.dw[...] += tn(r.xg[n * per : (n + 1) * per].reshape(BLOCK, D), parts)
            for u in range(per):
                t = n * per + u
                piece = parts[u * PT : (u + 1) * PT]
                r.dqkv[t, :PT] = piece[:, : 2 * HS]
                r.dqkv[t, PT:] = both_halves(piece[:, 2 * HS :])

                @pl.when(t != s)
                def _():
                    send_dq(t).start()

                @pl.when(t == s)
                def _():
                    r.dq_in[hd] = r.dqkv[t]

        if turn % 2 == 0:
            lo += 1
        else:
            hi -= 1
        turn += 1
        steps.run_rest(6)

    @pl.when(active)
    def _():
        lane = lax.broadcasted_iota(jnp.int32, (1, HS), 1)
        half = BUCKETS // 2
        sums_of = bucket_sums(r.diag[...], 0) + bucket_sums(r.sub[...], BLOCK)
        beyond = jnp.sum(jnp.sum(r.far[...], axis=0, keepdims=True), axis=1, keepdims=True)
        sums_of = sums_of + jnp.where(lane == half - 1, beyond, 0.0)
        wide = jnp.concatenate([r.dw[...], jnp.broadcast_to(sums_of, (D, HS))], axis=1)
        split_rows(r.dw3, wide, R)

        def start_dw(k, carry):
            send_dw(k).start()
            return carry

        lax.fori_loop(1, nv, start_dw, 0)
        r.dw_in[d * HEAD_COUNT + hd] = r.dw3[me]

    last_slots()
    steps.finish_rest()
    load = [
        pltpu.make_async_copy(r.wg_ref.at[:, :, pl.ds(m * D, D)], r.w3.at[m], r.loc.at[5 + m])
        for m in range(3)
    ]
    for c in load:
        c.start()
    for m, c in enumerate(load):
        c.wait()
        r.wfull[:, m * D : (m + 1) * D] = flatten_rows(r.w3[m]).astype(BF16)

    for k in range(1, nb):
        e = lax.rem(b + k, nb)
        got_sum(r.blk_in.at[e], 3 + nd + e)
    acc = r.blk_in[0].astype(F32)
    for e in range(1, nb):
        acc = acc + r.blk_in[e].astype(F32)
    eye = lax.broadcasted_iota(jnp.int32, (R, R), 0) == lax.broadcasted_iota(jnp.int32, (R, R), 1)

    def as_row(column):
        return jnp.sum(jnp.where(eye, column, 0.0), axis=0, keepdims=True)

    r.go_v[...] = acc[:, :D]
    r.router_v[...] = jnp.concatenate([as_row(acc[:, D + e : D + e + 1]) for e in range(E)], axis=0)
    r.gain2_v[...] = as_row(acc[:, D + E : D + E + 1])
    written(r, "go_ref", "router_out", "gain2_ref")

    for n in range(HEAD_COUNT):
        hb, hh = z.holder(n)

        @pl.when(jnp.logical_not(p.owns(n)))
        def _():
            ref = r.dq_in.at[n]
            remote(ref, ref, r.dq_s.at[0], r.dq_r.at[n], (d, hb, hh)).wait_recv()

        for m in range(2):
            r.grad_cat[:, m * D + n * HS : m * D + (n + 1) * HS] = r.dq_in[
                n, :PT, m * HS : (m + 1) * HS
            ]
        at = slice(2 * D + n * HS, 2 * D + (n + 1) * HS)
        r.grad_cat[: PT // 2, at] = r.dq_in[n, PT:, :HS]
        r.grad_cat[PT // 2 :, at] = r.dq_in[n, PT:, HS:]
    grad_normed = nt(r.grad_cat[...], r.wfull[...])
    x = r.x_own[...].astype(F32)
    inverse = lax.rsqrt(jnp.mean(x * x, axis=-1, keepdims=True) + EPSILON)
    scaled = grad_normed * r.gain1[...]
    mean = jnp.mean(scaled * x, axis=-1, keepdims=True)
    grad_in = inverse * scaled - x * (inverse * inverse * inverse) * mean
    r.gtok_v[...] = (r.gmid[...] + grad_in).astype(BF16)
    written(r, "gtok_ref")

    for dd in range(nd):
        for n in range(HEAD_COUNT):
            hb, hh = z.holder(n)

            @pl.when(jnp.logical_not(p.owns(n) & (d == dd)))
            def _():
                ref = r.dw_in.at[dd * HEAD_COUNT + n]
                remote(
                    ref, ref, r.dw_s.at[0], r.dw_r.at[dd * HEAD_COUNT + n], (dd, hb, hh)
                ).wait_recv()

    first = jnp.zeros((R, HS), F32)
    lines = []
    for n in range(HEAD_COUNT):
        part = r.dw_in[n].astype(F32)
        for dd in range(1, nd):
            part = part + r.dw_in[dd * HEAD_COUNT + n].astype(F32)
        for m, out in enumerate((r.gq_v, r.gk_v, r.gv_v)):
            cols = part[:, m * HS : (m + 1) * HS]
            out[:, n * HS : (n + 1) * HS] = cols
            own = r.w_own[:, m * D + n * HS : m * D + (n + 1) * HS].astype(F32)
            first = first + cols * own
        lines.append(part[0:1, 3 * HS : 3 * HS + BUCKETS])
    first = jnp.sum(first, axis=-1, keepdims=True)
    table = jnp.concatenate(lines, axis=0)
    entry = lax.broadcasted_iota(jnp.int32, table.shape, 0) * BUCKETS + lax.broadcasted_iota(
        jnp.int32, table.shape, 1
    )
    slot_lane = lax.broadcasted_iota(jnp.int32, (1, z.RL), 1)
    own_table = jnp.zeros((1, z.RL), F32)
    for k in range(z.RL):
        value = jnp.sum(jnp.where(entry == me * z.RL + k, table, 0.0), axis=0, keepdims=True)
        value = jnp.sum(value, axis=1, keepdims=True)
        own_table = own_table + jnp.where(slot_lane == k, value, 0.0)
    own_gain = r.w_own[:, 4 * D :].astype(F32)[:, E : E + 1]
    r.gain1_v[...] = as_row(first / own_gain)
    r.table_v[...] = own_table
    written(r, "gain1_ref", "gq_ref", "gk_ref", "gv_ref", "table_ref")

    sums.finish()

    @pl.when(active)
    def _():
        for t in range(ns):

            @pl.when(t != s)
            def _():
                send_dq(t).wait_send()

        def sent_dw(k, carry):
            send_dw(k).wait_send()
            return carry

        lax.fori_loop(1, nv, sent_dw, 0)


def layer(z, x, order, ids, rows, weights, router_t, w_in, w_out, cot):
    D, R, PT, S, HS, E, NG, C8 = z.D, z.R, z.PT, z.S, HEAD_SIZE, z.E, z.NG, z.cap8
    nb, nd, nh, ns, nv = z.n_blk, z.n_dp, z.n_head, z.ns, z.ndev
    dma = pltpu.SemaphoreType.DMA
    vmem = pl.BlockSpec(memory_space=pltpu.VMEM)
    hbm = pl.BlockSpec(memory_space=pltpu.HBM)
    shape = jax.ShapeDtypeStruct
    inputs = {
        "x_ref": (x, hbm),
        "order_ref": (order, vmem),
        "ids_ref": (ids, hbm),
        "gain1_in": (rows[0][None, :], vmem),
        "gain2_in": (rows[1][None, :], vmem),
        "rel_ref": (rows[2][None, :], vmem),
        "wq_ref": (weights[0], hbm),
        "wk_ref": (weights[1], hbm),
        "wv_ref": (weights[2], hbm),
        "wo_ref": (weights[3], hbm),
        "router_ref": (router_t, vmem),
        "win_ref": (w_in, hbm),
        "wout_ref": (w_out, hbm),
        "cot_ref": (cot, hbm),
    }
    outputs = {
        "wg_ref": (shape((nv, R, z.wide), BF16), hbm),
        "slots_ref": (shape((2, nh, NG, C8, D), BF16), hbm),
        "hid_ref": (shape((nh, NG * C8, z.FF), BF16), hbm),
        "gp_ref": (shape((nh, NG * C8, z.FF), BF16), hbm),
        "layer_ref": (shape((PT, D), BF16), hbm),
        "gtok_ref": (shape((PT, D), BF16), hbm),
        "gain1_ref": (shape((1, R), F32), hbm),
        "gq_ref": (shape((R, D), F32), hbm),
        "gk_ref": (shape((R, D), F32), hbm),
        "gv_ref": (shape((R, D), F32), hbm),
        "go_ref": (shape((R, D), F32), hbm),
        "table_ref": (shape((1, z.RL), F32), hbm),
        "gain2_ref": (shape((1, R), F32), hbm),
        "router_out": (shape((E, R), F32), hbm),
    }
    V = pltpu.VMEM
    terms = D + LANES
    scratch = {
        "w_own": V((R, z.wide), BF16),
        "x_own": V((PT, D), BF16),
        "cot": V((PT, D), BF16),
        "ids": V(ids.shape, jnp.int32),
        "win": V((D, z.FF), BF16),
        "wout": V((z.FF, D), BF16),
        "slices": V((HEAD_COUNT, R, 4 * HS), BF16),
        "slices_in": V((nv, R, 4 * HS), BF16),
        "xg": V((ns, PT, D), BF16),
        "wh": V((D, 3 * HS), BF16),
        "gain1": V((1, D), F32),
        "far_bias": V((1, 1), F32),
        "bias_d": V((BLOCK, BLOCK), F32),
        "bias_s": V((BLOCK, BLOCK), F32),
        "qkv": V((S, 3 * HS), BF16),
        "v_t": V((HS, S), BF16),
        "k_t": V((HS, S), BF16),
        "s_scr": V((S, BLOCK), F32),
        "probs": V((z.nq, S, BLOCK), BF16),
        "attl": V((S, 2 * HS), F32),
        "att_src": V((ns, PT // 2, 2 * HS), BF16),
        "att_in": V((HEAD_COUNT, PT // 2, 2 * HS), BF16),
        "misc3": V((nv, R, LANES), BF16),
        "wo": V((D, D), BF16),
        "route": V((E * C8, PT), F32),
        "att_cat": V((PT, D), BF16),
        "disp": V((2, E, C8, D), BF16),
        "exp_in": V((2, NG, C8, D), BF16),
        "ret": V((2, NG, C8, D), BF16),
        "back": V((2, E, C8, D), BF16),
        "hid": V((NG * C8, z.FF), BF16),
        "slope": V((NG * C8, z.FF), BF16),
        "act_in": V((2, NG, C8, D), BF16),
        "out_acc": V((NG * C8, D), F32),
        "gmid": V((PT, D), F32),
        "gatt": V((HEAD_COUNT, PT // 2, 2 * HS), BF16),
        "do_in": V((ns, PT // 2, 2 * HS), BF16),
        "dwo": V((nh, NG, R, terms), BF16),
        "core_in": V((2, NG, R, terms), BF16),
        "y_src": V((NG, R, terms), BF16),
        "y_in": V((NG, R, terms), BF16),
        "dp_in": V((nd, nb, R, terms), BF16),
        "blk_src": V((nb, R, terms), BF16),
        "blk_in": V((nb, R, terms), BF16),
        "dos": V((S, HS), BF16),
        "delta": V((z.nq, 8, BLOCK), F32),
        "dq_acc": V((z.nq, HS, BLOCK), F32),
        "dw": V((D, 3 * HS), F32),
        "dw3": V((nv, R, 4 * HS), BF16),
        "diag": V((BLOCK, BLOCK), F32),
        "sub": V((BLOCK, BLOCK), F32),
        "far": V((8, BLOCK), F32),
        "dqkv": V((ns, PT + PT // 2, 2 * HS), BF16),
        "dq_in": V((HEAD_COUNT, PT + PT // 2, 2 * HS), BF16),
        "dw_in": V((nd * HEAD_COUNT, R, 4 * HS), BF16),
        "w3": V((3, nv, R, D), BF16),
        "wfull": V((D, 3 * D), BF16),
        "grad_cat": V((PT, 3 * D), BF16),
        "layer_v": V((PT, D), BF16),
        "gtok_v": V((PT, D), BF16),
        "gain1_v": V((1, R), F32),
        "gq_v": V((R, D), F32),
        "gk_v": V((R, D), F32),
        "gv_v": V((R, D), F32),
        "go_v": V((R, D), F32),
        "table_v": V((1, z.RL), F32),
        "gain2_v": V((1, R), F32),
        "router_v": V((E, R), F32),
        "out_sem": dma((len(PASSED),)),
        "in_sem": dma((9,)),
        "loc": dma((11,)),
        "sl_s": dma((HEAD_COUNT,)),
        "sl_r": dma((nv,)),
        "sd_s": dma((ns * nd,)),
        "x_s": dma((2 * (4 + 6 * (nb - 1) + 2 * nb - 1),)),
        "x_r": dma((2 * ns,)),
        "w0_s": dma((spread_copies(z, False),)),
        "w0_r": dma((nv,)),
        "w1_s": dma((spread_copies(z, True),)),
        "w1_r": dma((nv,)),
        "w2_s": dma((spread_copies(z, False),)),
        "w2_r": dma((nv,)),
        "at_s": dma((ns,)),
        "at_r": dma((HEAD_COUNT,)),
        "ex_s": dma((4 * (NG - 1) + 6 + HEAD_COUNT,)),
        "ex_r": dma((2 * NG,)),
        "rt_r": dma((2 * NG,)),
        "all_r": dma((2 * nh,)),
        "do_r": dma((ns,)),
        "su_s": dma((3 + nd - 1 + nb - 1,)),
        "su_r": dma((3 + nd + nb,)),
        "dq_s": dma((ns,)),
        "dq_r": dma((HEAD_COUNT,)),
        "dw_s": dma((nv,)),
        "dw_r": dma((nd * HEAD_COUNT,)),
    }
    names = tuple(inputs) + tuple(outputs) + tuple(scratch)
    results = pl.pallas_call(
        functools.partial(layer_kernel, z, names),
        out_shape=tuple(v[0] for v in outputs.values()),
        in_specs=[v[1] for v in inputs.values()],
        out_specs=tuple(v[1] for v in outputs.values()),
        scratch_shapes=list(scratch.values()),
        compiler_params=pltpu.CompilerParams(
            collective_id=0, has_side_effects=True, vmem_limit_bytes=VMEM_LIMIT
        ),
        name="layer",
    )(*[v[0] for v in inputs.values()])
    return dict(zip(outputs, results))


def expert_kernel(z, slots_ref, hid_ref, gp_ref, *refs):
    count = len(PASSED)
    passed_in, (gin_ref, gout_ref) = refs[:count], refs[count : count + 2]
    passed_out = refs[count + 2 : 2 * count + 2]
    rows_t, grad_out = refs[2 * count + 2 :]
    step = pl.program_id(0)

    @pl.when(step == 0)
    def _():
        for src, dst in zip(passed_in, passed_out):
            dst[...] = src[...]
        count = z.NG * z.cap8
        for n in range(z.n_head):
            at = slice(n * count, (n + 1) * count)
            rows_in = slots_ref[0, n].astype(F32).reshape(count, z.D)
            rows_t[:, at] = jnp.transpose(rows_in).astype(BF16)
            grad_out[at, :] = slots_ref[1, n].astype(F32).reshape(count, z.D).astype(BF16)

    total = z.n_head * z.NG * z.cap8
    chunk = hid_ref.shape[2]
    gin_ref[0] = nn(rows_t[...], gp_ref[...].reshape(total, chunk))
    gout_ref[0] = tn(hid_ref[...].reshape(total, chunk), grad_out[...])


def expert_weights(z, slots, hid, gp, passed):
    chunk = 768
    vmem = pl.BlockSpec(memory_space=pltpu.VMEM)
    total = z.n_head * z.NG * z.cap8
    in_chunk = pl.BlockSpec((1, z.D, chunk), lambda i: (0, 0, i))
    act_chunk = pl.BlockSpec((z.n_head, z.NG * z.cap8, chunk), lambda i: (0, 0, i))
    out_chunk = pl.BlockSpec((1, chunk, z.D), lambda i: (0, i, 0))
    return pl.pallas_call(
        functools.partial(expert_kernel, z),
        grid=(z.FF // chunk,),
        out_shape=(
            jax.ShapeDtypeStruct((1, z.D, z.FF), F32),
            jax.ShapeDtypeStruct((1, z.FF, z.D), F32),
        )
        + tuple(jax.ShapeDtypeStruct(a.shape, a.dtype) for a in passed),
        in_specs=[pl.BlockSpec(memory_space=pltpu.VMEM), act_chunk, act_chunk] + [vmem] * len(passed),
        out_specs=(in_chunk, out_chunk) + (vmem,) * len(passed),
        scratch_shapes=[
            pltpu.VMEM((z.D, total), BF16),
            pltpu.VMEM((total, z.D), BF16),
        ],
        compiler_params=pltpu.CompilerParams(
            dimension_semantics=("arbitrary",), vmem_limit_bytes=VMEM_LIMIT
        ),
        name="expert_weight_grads",
    )(slots, hid, gp, *passed)


def local(
    sizes,
    tokens,
    order,
    expert_ids,
    norm1_gain,
    w_query,
    w_key,
    w_value,
    w_attn_out,
    rel_table,
    norm2_gain,
    w_router,
    w_in,
    w_out,
    cotangent,
):
    R, D = w_query.shape
    E = w_router.shape[1]
    z = Sizes(*sizes, R, D, E, w_in.shape[2], tokens.shape[1])
    out = layer(
        z,
        tokens.reshape(z.PT, D),
        order,
        expert_ids.reshape(-1, z.PT),
        (norm1_gain, norm2_gain, rel_table),
        (w_query, w_key, w_value, w_attn_out),
        w_router.T,
        w_in,
        w_out,
        cotangent.reshape(z.PT, D),
    )
    g_in, g_out, *rest = expert_weights(
        z, out["slots_ref"], out["hid_ref"], out["gp_ref"], [out[name] for name in PASSED]
    )
    layer_out, gtok, gain1, gq, gk, gv, go, table, gain2, router = rest
    return (
        layer_out.reshape(tokens.shape),
        gtok.reshape(tokens.shape),
        gain1.reshape(R),
        gq,
        gk,
        gv,
        go,
        table.reshape(z.RL),
        gain2.reshape(R),
        router.T,
        g_in,
        g_out,
    )


def solution(mesh):
    everywhere = ("dp", "blk", "head")
    rows, table = P(everywhere), P(everywhere, None)
    tokens = P("dp", ("blk", "head"), None)
    expert = P(("dp", "blk"), None, None)
    in_specs = (
        tokens,
        P("dp", ("blk", "head")),
        P(),
        rows,
        table,
        table,
        table,
        table,
        rows,
        rows,
        table,
        expert,
        expert,
        tokens,
    )
    out_specs = (
        tokens, tokens, rows, table, table, table, table, rows, rows, table, expert, expert
    )
    sizes = (mesh.shape["dp"], mesh.shape["blk"], mesh.shape["head"])
    return jax.shard_map(
        functools.partial(local, sizes),
        mesh=mesh,
        in_specs=in_specs,
        out_specs=out_specs,
        check_vma=False,
    )
```

```python
import functools
import itertools
import types

import jax
import jax.numpy as jnp
from jax import lax
from jax.experimental import pallas as pl
from jax.experimental.pallas import tpu as pltpu
from jax.sharding import PartitionSpec as P

HEAD_COUNT = 12
HEAD_SIZE = 64
BUCKETS = 32
BLOCK = 256
EPSILON = 1e-06
AUX_WEIGHT = 1.0
LIMITS = (1, 2, 3, 4, 5, 6, 7, 8, 12, 16, 23, 32, 46, 64, 91)
INV_ROOT_TWO = 0.7071067811865476
INV_ROOT_TWO_PI = 0.3989422804014327
LANES = 128
VMEM_LIMIT = 62 * 1024 * 1024
PASSED = (
    "layer_ref", "gtok_ref", "gain1_ref", "gq_ref", "gk_ref", "gv_ref", "go_ref", "table_ref",
    "gain2_ref", "router_out",
)
MESH = pl.DeviceIdType.MESH
F32 = jnp.float32
BF16 = jnp.bfloat16


def both_halves(values):
    n = values.shape[0] // 2
    return jnp.concatenate([values[:n], values[n:]], axis=1)


def line_order(b, nb):
    out = [(b, b >= 0)]
    for k in range(1, nb):
        out.append((b - k, b >= k))
        out.append((b + k, b + k < nb))
    return out


class Sends:
    def __init__(self, sems):
        self.sems, self.made = sems, []

    def put(self, src, dst, recv, device, cond=None):
        c = remote(src, dst, self.sems.at[len(self.made)], recv, device)
        self.made.append((c, cond))
        self.each(c.start, cond)

    def each(self, action, cond):
        if cond is None:
            action()
        else:
            pl.when(cond)(action)

    def finish(self):
        for c, cond in self.made:
            self.each(c.wait_send, cond)


class Sizes:
    def __init__(self, n_dp, n_blk, n_head, rows, width, experts, hidden, piece):
        self.n_dp, self.n_blk, self.n_head = n_dp, n_blk, n_head
        self.ndev = n_dp * n_blk * n_head
        self.ns = n_blk * n_head
        self.R, self.D, self.E, self.FF, self.PT = rows, width, experts, hidden, piece
        self.S = piece * self.ns
        self.nq = self.S // BLOCK
        self.hb = HEAD_COUNT // n_blk
        self.cap = (5 * piece + 4 * experts - 1) // (4 * experts)
        self.cap8 = (self.cap + 7) // 8 * 8
        self.NG = n_dp * n_blk
        self.RL = HEAD_COUNT * BUCKETS // self.ndev
        self.wide = 4 * width + LANES
        self.per = BLOCK // piece
        assert self.hb < n_head and self.hb * n_blk == HEAD_COUNT
        assert experts == self.NG and n_head == 4


    def holder(self, n):
        return n // self.hb, n % self.hb + n // self.hb % 2


def nt(a, b):
    return lax.dot_general(a, b, (((1,), (1,)), ((), ())), preferred_element_type=F32)


def tn(a, b):
    return lax.dot_general(a, b, (((0,), (0,)), ((), ())), preferred_element_type=F32)


def nn(a, b):
    return jnp.dot(a, b, preferred_element_type=F32)


def place():
    return lax.axis_index("dp"), lax.axis_index("blk"), lax.axis_index("head")


def signal(device):
    pl.semaphore_signal(
        pltpu.get_barrier_semaphore(), inc=1, device_id=device, device_id_type=MESH
    )


def await_barrier(count):
    pl.semaphore_wait(pltpu.get_barrier_semaphore(), count)


def remote(src, dst, send, recv, device):
    return pltpu.make_async_remote_copy(
        src_ref=src, dst_ref=dst, send_sem=send, recv_sem=recv, device_id=device, device_id_type=MESH
    )


def flatten_rows(blocks):
    count, rows, lanes = blocks.shape
    wide = blocks.astype(F32)
    if rows % 8 == 0:
        return wide.reshape(count * rows, lanes)
    return jnp.concatenate([wide[i] for i in range(count)], axis=0)


def split_rows(dst_ref, values, rows):
    count = values.shape[0] // rows
    if rows % 8 == 0:
        dst_ref[...] = values.reshape(count, rows, values.shape[1]).astype(dst_ref.dtype)
    else:
        for i in range(count):
            dst_ref[i] = values[i * rows : (i + 1) * rows].astype(dst_ref.dtype)


def activate(pre):
    phi, bell = normal_parts(pre)
    slope = phi + pre * bell * INV_ROOT_TWO_PI
    return (pre * phi).astype(BF16), slope.astype(BF16)


def grad_pre(grad_out, w, slope):
    hidden = nt(grad_out, w).astype(BF16).astype(F32)
    return (hidden * slope.astype(F32)).astype(BF16)


def normal_parts(v):
    bell = jnp.exp(-0.5 * v * v)
    t = 1.0 / (1.0 + (0.3275911 * INV_ROOT_TWO) * jnp.abs(v))
    poly = t * (
        0.254829592
        + t * (-0.284496736 + t * (1.421413741 + t * (-1.453152027 + t * 1.061405429)))
    )
    tail = 0.5 * poly * bell
    return jnp.where(v >= 0, 1.0 - tail, tail), bell


def bias_tile(table, shift):
    j = lax.broadcasted_iota(jnp.int32, (BLOCK, BLOCK), 0)
    i = lax.broadcasted_iota(jnp.int32, (BLOCK, BLOCK), 1)
    dist = j - i + shift
    mag = jnp.abs(dist)
    half = BUCKETS // 2
    out = jnp.broadcast_to(table[0:1, 0:1], (BLOCK, BLOCK))
    for n, limit in enumerate(LIMITS):
        low = table[n + 1 : n + 2, 0:1]
        if shift == 0:
            high = table[half + n + 1 : half + n + 2, 0:1]
            out = jnp.where(mag >= limit, jnp.where(dist > 0, high, low), out)
        else:
            out = jnp.where(mag >= limit, low, out)
    return out


def bucket_sums(tile, shift):
    row = lax.broadcasted_iota(jnp.int32, (BLOCK, BLOCK), 0)
    column = lax.broadcasted_iota(jnp.int32, (BLOCK, BLOCK), 1)
    turn = (row + column == BLOCK - 1).astype(BF16)
    high = tile.astype(BF16)
    rest = (tile - high.astype(F32)).astype(BF16)
    turned = nn(turn, high) + nn(turn, rest)
    wide = jnp.concatenate([turned, jnp.zeros((BLOCK, BLOCK), F32)], axis=1)
    skewed = pltpu.roll(wide, 0, 1, stride=1, stride_axis=0)
    line = jnp.sum(skewed.reshape(BLOCK // 8, 8, 2 * BLOCK), axis=0)
    behind = lax.broadcasted_iota(jnp.int32, (2 * BLOCK, HEAD_SIZE), 0) - (BLOCK - 1) + shift
    bucket = jnp.zeros((2 * BLOCK, HEAD_SIZE), jnp.int32)
    for limit in LIMITS:
        bucket = bucket + (jnp.abs(behind) >= limit).astype(jnp.int32)
    bucket = bucket + jnp.where(behind < 0, BUCKETS // 2, 0)
    hot = bucket == lax.broadcasted_iota(jnp.int32, (2 * BLOCK, HEAD_SIZE), 1)
    parts = jnp.dot(
        line, hot.astype(F32), precision=lax.Precision.HIGHEST, preferred_element_type=F32
    )
    return jnp.sum(parts, axis=0, keepdims=True)


class Spread:
    def __init__(self, z, src, dst, send, recv, y_first, lanes):
        self.z, self.src, self.dst, self.recv = z, src, dst, recv
        self.sends, self.lanes = Sends(send), lanes
        d, b, h = place()
        self.at = (d, b, h)
        nh, nd = z.n_head, z.n_dp
        self.hy = lax.rem(h + 2, nh)
        self.hc = h + 1 - 2 * lax.rem(h, 2)
        self.hyc = lax.rem(self.hc + 2, nh)
        dto = [lax.rem(d + k, nd) for k in range(1, nd)]
        dfrom = [lax.rem(d + nd - k, nd) for k in range(1, nd)]
        ys = ([(d, self.hy)], [(d, self.hy)])
        xs = ([(p, h) for p in dto], [(p, h) for p in dfrom])
        self.first, self.second = (ys, xs) if y_first else (xs, ys)
        if y_first:
            self.second_slots = [(p, hh) for p in dfrom for hh in (h, self.hy)]
        else:
            self.second_slots = [(p, self.hy) for p in [d] + dfrom]
        self.core_slots = [(p, hh) for p in [d] + dfrom for hh in (self.hc, self.hyc)]

    def slot(self, dd, bb, hh):
        return (dd * self.z.n_blk + bb) * self.z.n_head + hh

    def ref(self, slot):
        return self.dst.at[slot, :, self.lanes]

    def put(self, src, slot, device, cond=None):
        self.sends.put(src, self.ref(slot), self.recv.at[slot], device, cond)

    def got(self, slot):
        d, b, h = self.at
        ref = self.ref(slot)
        remote(ref, ref, self.sends.sems.at[0], self.recv.at[slot], (d, b, self.hc)).wait_recv()

    def steps(self):
        d, b, h = self.at
        nb = self.z.n_blk

        def begin():
            mine = self.slot(d, b, h)
            self.put(self.src, mine, (d, b + 1, h), b + 1 < nb)
            self.put(self.src, mine, (d, b - 1, h), b >= 1)
            for dd, hh in self.first[0] + self.second[0] + [(d, self.hc)]:
                self.put(self.src, mine, (dd, b, hh))

        def line_arrival(k):
            for f, cond, to, more in (
                (b - k, b >= k, b + 1, b + 1 < nb),
                (b + k, b + k < nb, b - 1, b >= 1),
            ):
                slot = self.slot(d, f, h)
                pl.when(cond)(functools.partial(self.got, slot))
                if k < nb - 1:
                    self.put(self.ref(slot), slot, (d, to, h), cond & more)
                for dd, hh in self.first[0] + self.second[0] + [(d, self.hc)]:
                    self.put(self.ref(slot), slot, (dd, b, hh), cond)

        def first_arrival(p, f, cond):
            slot = self.slot(p[0], f, p[1])
            pl.when(cond)(functools.partial(self.got, slot))
            for dd, hh in self.second[0] + [(d, self.hc)]:
                self.put(self.ref(slot), slot, (dd, b, hh), cond)

        def second_arrival(p, f, cond):
            slot = self.slot(p[0], f, p[1])
            pl.when(cond)(functools.partial(self.got, slot))
            self.put(self.ref(slot), slot, (d, b, self.hc), cond)

        out = [begin]
        for k in range(1, nb):
            out.append(functools.partial(line_arrival, k))
        for p in self.first[1]:
            for f, cond in line_order(b, nb):
                out.append(functools.partial(first_arrival, p, f, cond))
        for p in self.second_slots:
            for f, cond in line_order(b, nb):
                out.append(functools.partial(second_arrival, p, f, cond))
        return out

    def finish(self):
        d, b, h = self.at
        for p in self.core_slots:
            for f in range(self.z.n_blk):
                self.got(self.slot(p[0], f, p[1]))
        self.sends.finish()


def spread_copies(z, y_first):
    nb, nd = z.n_blk, z.n_dp
    peers = 1 + nd - 1 + 1
    first = 1 if y_first else nd - 1
    second = peers - 1 - first
    second_slots = 2 * (nd - 1) if y_first else nd
    line = 2 * nb - 1
    return 2 + peers + (nb - 1) * 2 * (peers + 1) + first * line * (second + 1) + second_slots * line


class Place:
    def __init__(self, z):
        self.d, self.b, self.h = d, b, h = place()
        self.s = b * z.n_head + h
        self.me = d * z.ns + self.s
        self.g = d * z.n_blk + b
        first = lax.rem(b, 2)
        self.active = (h >= first) & (h < first + z.hb)
        self.hd = b * z.hb + jnp.clip(h - first, 0, z.hb - 1)
        self.hy = lax.rem(h + 2, z.n_head)
        self.hc = h + 1 - 2 * lax.rem(h, 2)
        self.hyc = lax.rem(self.hc + 2, z.n_head)
        self.z = z

    def any_peer(self, k):
        z = self.z
        t = lax.rem(self.me + k, z.ndev)
        return t, (t // z.ns, lax.rem(t // z.n_head, z.n_blk), lax.rem(t, z.n_head))

    def in_sequence(self, t):
        return (self.d, t // self.z.n_head, lax.rem(t, self.z.n_head))

    def owns(self, n):
        return self.active & (self.hd == n)

    def group(self, k):
        z = self.z
        e = lax.rem(self.g + k, z.NG)
        return e, (e // z.n_blk, lax.rem(e, z.n_blk), self.h)


def written(r, *names):
    for name in names:
        short = name.replace("_ref", "").replace("_out", "") + "_v"
        c = pltpu.make_async_copy(
            getattr(r, short), getattr(r, name), r.out_sem.at[PASSED.index(name)]
        )
        c.start()
        r.outgoing.append(c)


def layer_kernel(z, names, *refs):
    r = types.SimpleNamespace(**dict(zip(names, refs)))
    r.dkv = r.s_scr.at[:, pl.ds(0, 2 * HEAD_SIZE)]
    r.outgoing = []
    p = Place(z)

    def greet(k, carry):
        signal(p.any_peer(k)[1])
        return carry

    lax.fori_loop(1, z.ndev, greet, 0)
    D = z.D
    small = [
        pltpu.make_async_copy(ref, r.w_own.at[:, pl.ds(m * D, D)], r.in_sem.at[m])
        for m, ref in enumerate((r.wq_ref, r.wk_ref, r.wv_ref, r.wo_ref))
    ]
    small.append(pltpu.make_async_copy(r.x_ref, r.x_own, r.in_sem.at[4]))
    later = [
        pltpu.make_async_copy(r.cot_ref, r.cot, r.in_sem.at[5]),
        pltpu.make_async_copy(r.ids_ref, r.ids, r.in_sem.at[6]),
        pltpu.make_async_copy(r.win_ref.at[0], r.win, r.in_sem.at[7]),
        pltpu.make_async_copy(r.wout_ref.at[0], r.wout, r.in_sem.at[8]),
    ]
    for c in small + later:
        c.start()
    steps, finish_forward = forward_phase(z, r, p, small)
    for c in later:
        c.wait()
    last_slots, finish_middle = middle_phase(z, r, p, steps)
    backward_phase(z, r, p, steps, last_slots)
    finish_forward()
    finish_middle()
    for c in r.outgoing:
        c.wait()


def forward_phase(z, r, p, small):
    d, b, h, s, me, hd, active = p.d, p.b, p.h, p.s, p.me, p.hd, p.active
    hy, hc, hyc = p.hy, p.hc, p.hyc
    nb, nh, nd, ns = z.n_blk, z.n_head, z.n_dp, z.ns
    D, R, E, PT, HS = z.D, z.R, z.E, z.PT, HEAD_SIZE

    await_barrier(z.ndev - 1)
    small[4].wait()

    tokens = Sends(r.x_s)
    pieces = 2
    rows_of = PT // pieces

    def xref(slot, c):
        return r.xg.at[slot, pl.ds(c * rows_of, rows_of)]

    def put(src, slot, c, device, cond=None):
        tokens.put(src, xref(slot, c), r.x_r.at[slot * pieces + c], device, cond)

    def got(slot, c):
        ref = xref(slot, c)
        remote(ref, ref, r.x_s.at[0], r.x_r.at[slot * pieces + c], (d, b, hc)).wait_recv()

    for c in range(pieces):
        own = r.x_own.at[pl.ds(c * rows_of, rows_of)]
        put(own, s, c, (d, b + 1, h), b + 1 < nb)
        put(own, s, c, (d, b - 1, h), b >= 1)
        put(own, s, c, (d, b, hy))
        put(own, s, c, (d, b, hc))
    r.xg[s] = r.x_own[...]

    for c in small[:4]:
        c.wait()
    eye = lax.broadcasted_iota(jnp.int32, (R, R), 0) == lax.broadcasted_iota(jnp.int32, (R, R), 1)
    row_of = lax.broadcasted_iota(jnp.int32, (LANES, R), 0)
    tail = jnp.zeros((LANES, R), F32)
    rel = jnp.concatenate([r.rel_ref[...].astype(F32), jnp.zeros((1, R - z.RL), F32)], axis=1)
    rows = r.gain1_in[...].astype(F32), r.gain2_in[...].astype(F32), rel
    for n in range(3):
        tail = jnp.where(row_of == E + n, rows[n], tail)
    router_t = jnp.concatenate(
        [r.router_ref[...].astype(F32), jnp.zeros((LANES - E, R), F32)], axis=0
    )
    misc = nt(eye.astype(BF16), (tail + router_t).astype(BF16)).astype(BF16)
    r.w_own[:, 4 * D :] = misc
    for n in range(HEAD_COUNT):
        columns = [r.w_own[:, m * D + n * HS : m * D + (n + 1) * HS] for m in range(3)]
        r.slices[n] = jnp.concatenate(columns + [misc[:, E : E + HS]], axis=1)
    save_w = pltpu.make_async_copy(r.w_own, r.wg_ref.at[me], r.loc.at[0])
    save_w.start()
    to_heads = Sends(r.sl_s)
    over_dp = Sends(r.sd_s)
    for n in range(HEAD_COUNT):
        hb, hh = z.holder(n)
        to_heads.put(
            r.slices.at[n], r.slices_in.at[me], r.sl_r.at[me], (d, hb, hh),
            jnp.logical_not(p.owns(n)),
        )

    @pl.when(active)
    def _():
        r.slices_in[me] = r.slices[hd]

    for k in range(1, nb):
        for c in range(pieces):
            for f, cond, to, more in (
                (b - k, b >= k, b + 1, b + 1 < nb),
                (b + k, b + k < nb, b - 1, b >= 1),
            ):
                slot = f * nh + h
                pl.when(cond)(functools.partial(got, slot, c))
                if k < nb - 1:
                    put(xref(slot, c), slot, c, (d, to, h), cond & more)
                put(xref(slot, c), slot, c, (d, b, hy), cond)
                put(xref(slot, c), slot, c, (d, b, hc), cond)
        if k == 1:
            for m in range(ns):
                t = lax.rem(s + m, ns)
                slot = d * ns + t
                ref = r.slices_in.at[slot]
                if m > 0:
                    c = remote(ref, ref, r.sl_s.at[0], r.sl_r.at[slot], p.in_sequence(t))
                    pl.when(active)(c.wait_recv)
                for kd in range(1, nd):
                    over_dp.put(ref, ref, r.sl_r.at[slot], (lax.rem(d + kd, nd), b, h), active)

    for f, cond in line_order(b, nb):
        for c in range(pieces):
            slot = f * nh + hy
            pl.when(cond)(functools.partial(got, slot, c))
            put(xref(slot, c), slot, c, (d, b, hc), cond)

    cuts = (3 * D, z.wide, False), (0, 3 * D // 2, True), (3 * D // 2, 3 * D, False)
    parts = [
        Spread(
            z, r.w_own.at[:, pl.ds(lo, hi - lo)], r.wg_ref,
            getattr(r, "w%d_s" % n), getattr(r, "w%d_r" % n), y_first, pl.ds(lo, hi - lo),
        )
        for n, (lo, hi, y_first) in enumerate(cuts)
    ]
    first, rest_a, rest_b = [part.steps() for part in parts]
    steps = []
    for k in range(nb):
        steps += [first.pop(0), rest_a.pop(0), rest_b.pop(0)]
    steps = Steps(steps + first, rest_a, rest_b, parts, save_w)

    steps.run(3)

    @pl.when(active)
    def _():
        for kd in range(1, nd):
            dd = lax.rem(d + kd, nd)

            def got_slice(t, carry):
                ref = r.slices_in.at[dd * ns + t]
                remote(ref, ref, r.sl_s.at[0], r.sl_r.at[dd * ns + t], (dd, b, h)).wait_recv()
                return carry

            lax.fori_loop(0, ns, got_slice, 0)

        rows = flatten_rows(r.slices_in[...])
        r.wh[:, : 2 * HS] = rows[:, : 2 * HS].astype(BF16)
        r.wh[:, :HS] = (rows[:, :HS] * HS ** (-0.5)).astype(BF16)
        r.wh[:, 2 * HS :] = rows[:, 2 * HS : 3 * HS].astype(BF16)
        r.gain1[...] = jnp.transpose(rows[:, LANES:])[HS : HS + 1, :]
        column = lax.broadcasted_iota(jnp.int32, (1, D), 1).astype(F32)
        owner = jnp.floor((column + 0.5) * (1.0 / R))
        place_of = column - owner * R
        entry = jnp.where(place_of < z.RL, owner * z.RL + place_of, -1.0)
        wanted = hd * BUCKETS + lax.broadcasted_iota(jnp.int32, (BUCKETS, D), 0)
        pick = (entry == wanted.astype(F32)).astype(BF16)
        table = nn(pick, rows[:, LANES:].astype(BF16))[:, HS + 2 : HS + 3]
        r.bias_d[...] = bias_tile(table, 0)
        r.bias_s[...] = bias_tile(table, -BLOCK)
        r.far_bias[...] = table[BUCKETS // 2 - 1 : BUCKETS // 2, 0:1]

    for f in range(nb):
        for c in range(pieces):
            got(f * nh + hc, c)
            got(f * nh + hyc, c)
    tokens.finish()
    per = z.per
    half = BLOCK // 2

    @pl.when(active)
    def _():
        def project(i, carry):
            here = pl.ds(pl.multiple_of(i * BLOCK, BLOCK), BLOCK)
            own = pl.ds(i * per, per)
            x = r.xg[own].reshape(BLOCK, D).astype(F32)
            inverse = lax.rsqrt(jnp.mean(x * x, axis=-1, keepdims=True) + EPSILON)
            low = (x * inverse * r.gain1[...]).astype(BF16)
            r.xg[own] = low.reshape(per, PT, D)
            mixed = nn(low, r.wh[...])
            r.qkv[here, :] = mixed.astype(BF16)
            r.v_t[:, here] = jnp.transpose(mixed[:, 2 * HS :]).astype(BF16)
            r.k_t[:, here] = jnp.transpose(mixed[:, HS : 2 * HS]).astype(BF16)
            return carry

        lax.fori_loop(0, z.nq, project, 0)

    def send_att(t):
        return remote(
            r.att_src.at[t], r.att_in.at[hd], r.at_s.at[t], r.at_r.at[hd], (d, t // nh, t % nh)
        )

    low_rows, high_rows = range(z.nq // 2), range(z.nq // 2, z.nq)
    order = [i for pair in zip(reversed(high_rows), reversed(low_rows)) for i in pair]
    for i in order:
        steps.run(4)

        @pl.when(active)
        def _():
            here = slice(i * BLOCK, (i + 1) * BLOCK)
            q = r.qkv[here, :HS]
            top = jnp.full((8, BLOCK), -1e30, F32)
            far = r.far_bias[...]
            for j in range(i + 1):
                for u in range(2):
                    at = slice(j * BLOCK + u * half, j * BLOCK + (u + 1) * half)
                    part = slice(u * half, (u + 1) * half)
                    if j == i:
                        bias = r.bias_d[part, :]
                    elif j == i - 1:
                        bias = r.bias_s[part, :]
                    else:
                        bias = far
                    sc = nt(r.qkv[at, HS : 2 * HS], q) + bias
                    r.s_scr[at, :] = sc
                    top = jnp.maximum(top, jnp.max(sc.reshape(half // 8, 8, BLOCK), axis=0))
            top = jnp.max(top, axis=0, keepdims=True)
            total = jnp.zeros((8, BLOCK), F32)
            acc = jnp.zeros((HS, BLOCK), F32)
            for j in range(i + 1):
                for u in range(2):
                    at = slice(j * BLOCK + u * half, j * BLOCK + (u + 1) * half)
                    e = jnp.exp(r.s_scr[at, :] - top)
                    total = total + jnp.sum(e.reshape(half // 8, 8, BLOCK), axis=0)
                    r.probs[i, at, :] = e.astype(BF16)
                at = slice(j * BLOCK, (j + 1) * BLOCK)
                acc = acc + nn(r.v_t[:, at], r.probs[i, at, :])
            total = jnp.sum(total, axis=0, keepdims=True)
            both = jnp.concatenate([acc, jnp.broadcast_to(total, (HS, BLOCK))], axis=0)
            both = jnp.transpose(both)
            inv = 1.0 / both[:, HS:]
            att = (both[:, :HS] * inv).astype(BF16)
            r.attl[here, :] = jnp.concatenate([att.astype(F32), inv], axis=1)
            for u in range(per):
                t = i * per + u
                r.att_src[t] = both_halves(att[u * PT : (u + 1) * PT])

                @pl.when(t != s)
                def _():
                    send_att(t).start()

                @pl.when(t == s)
                def _():
                    r.att_in[hd] = r.att_src[t]

    def finish():
        to_heads.finish()
        over_dp.finish()

        @pl.when(active)
        def _():
            for t in range(ns):

                @pl.when(t != s)
                def _():
                    send_att(t).wait_send()

    return steps, finish


class Steps:
    def __init__(self, first, rest_a, rest_b, parts, save):
        self.first, self.parts, self.save = first, parts, save
        self.rest = [
            step
            for pair in itertools.zip_longest(rest_b, rest_a)
            for step in pair
            if step is not None
        ]

    def run(self, count):
        for _ in range(min(count, len(self.first))):
            self.first.pop(0)()

    def finish_first(self):
        self.run(len(self.first))
        self.parts[0].finish()
        self.save.wait()

    def run_rest(self, count):
        for _ in range(min(count, len(self.rest))):
            self.rest.pop(0)()

    def finish_rest(self):
        self.run_rest(len(self.rest))
        for part in self.parts[1:]:
            part.finish()


def middle_phase(z, r, p, steps):
    d, b, h, me, g, s = p.d, p.b, p.h, p.me, p.g, p.s
    hy, hc, hyc = p.hy, p.hc, p.hyc
    nb, nh, nd, ns = z.n_blk, z.n_head, z.n_dp, z.ns
    D, E, PT, NG, C8 = z.D, z.E, z.PT, z.NG, z.cap8

    ids_row = r.ids[pl.ds(me, 1), :]
    order_row = r.order_ref[...]
    ids_col = jnp.transpose(jnp.broadcast_to(ids_row, (PT, PT)))
    order_col = jnp.transpose(jnp.broadcast_to(order_row, (PT, PT)))
    earlier = (order_col < order_row) & (ids_col == ids_row)
    rank = jnp.sum(earlier.astype(jnp.int32), axis=0, keepdims=True)
    slot = lax.broadcasted_iota(jnp.int32, (C8, PT), 0)
    base = (rank == slot) & (slot < z.cap)
    lane = lax.broadcasted_iota(jnp.int32, (1, LANES), 1)
    share = jnp.zeros((1, LANES), F32)
    ids_all = r.ids[...]
    for e in range(E):
        r.route[e * C8 : (e + 1) * C8, :] = (base & (ids_row == e)).astype(F32)
        count = jnp.sum((ids_all == e).astype(F32), axis=1, keepdims=True)
        count = jnp.sum(count, axis=0, keepdims=True)
        share = share + jnp.where(lane == e, count, 0.0)
    share = share * (AUX_WEIGHT * E / (ids_all.shape[0] * ids_all.shape[1]))
    chosen = ids_col[:, :1] == lane
    picks = r.route[...].astype(BF16)
    x = r.x_own[...].astype(F32)
    cot = r.cot[...].astype(F32)

    steps.finish_first()
    load = [
        pltpu.make_async_copy(r.wg_ref.at[:, :, pl.ds(3 * D, D)], r.w3.at[0], r.loc.at[1]),
        pltpu.make_async_copy(r.wg_ref.at[:, :, pl.ds(4 * D, LANES)], r.misc3, r.loc.at[2]),
    ]
    for c in load:
        c.start()
    for c in load:
        c.wait()
    r.wo[...] = flatten_rows(r.w3[0]).astype(BF16)
    misc = flatten_rows(r.misc3[...])
    router = misc.astype(BF16)
    lines = jnp.transpose(misc)
    r.gain1[...] = lines[E : E + 1, :]
    gain = lines[E + 1 : E + 2, :]
    for n in range(HEAD_COUNT):
        hb, hh = z.holder(n)

        @pl.when(jnp.logical_not(p.owns(n)))
        def _():
            ref = r.att_in.at[n]
            remote(ref, ref, r.at_s.at[0], r.at_r.at[n], (d, hb, hh)).wait_recv()

        at = slice(n * HEAD_SIZE, (n + 1) * HEAD_SIZE)
        r.att_cat[: PT // 2, at] = r.att_in[n, :, :HEAD_SIZE]
        r.att_cat[PT // 2 :, at] = r.att_in[n, :, HEAD_SIZE:]
    att = r.att_cat[...]
    middle = x + nn(att, r.wo[...])
    inverse = lax.rsqrt(jnp.mean(middle * middle, axis=-1, keepdims=True) + EPSILON)
    routed = (middle * inverse * gain).astype(BF16)

    out = Sends(r.ex_s)

    def dispatch(part, values):
        r.disp[part] = nn(picks, values).reshape(E, C8, D).astype(BF16)
        for k in range(1, NG):
            e, device = p.group(k)
            out.put(r.disp.at[part, e], r.exp_in.at[part, g], r.ex_r.at[part * NG + g], device)
        r.exp_in[part, g] = r.disp[part, g]

    def arrivals(part):
        for k in range(1, NG):
            e, device = p.group(NG - k)
            ref = r.exp_in.at[part, e]
            remote(ref, ref, r.ex_s.at[0], r.ex_r.at[part * NG + e], device).wait_recv()

    def give_back(part, values):
        r.ret[part] = values.reshape(NG, C8, D).astype(BF16)
        for k in range(1, NG):
            e, device = p.group(k)
            out.put(r.ret.at[part, e], r.back.at[part, g], r.rt_r.at[part * NG + g], device)
        r.back[part, g] = r.ret[part, g]

    def returns(part):
        for k in range(1, NG):
            e, device = p.group(NG - k)
            ref = r.back.at[part, e]
            remote(ref, ref, r.ex_s.at[0], r.rt_r.at[part * NG + e], device).wait_recv()
        rows = r.back[part].astype(F32).reshape(E * C8, D).astype(BF16)
        return tn(picks, rows)

    copies = []

    def share_slots(part):
        src, dst, sem = r.exp_in.at[part], r.slots_ref.at[part, h], r.all_r.at[part * nh + h]
        out.put(src, dst, sem, (d, b, hy))
        out.put(src, dst, sem, (d, b, hc))
        c = pltpu.make_async_copy(src, dst, r.loc.at[3 + part])
        c.start()
        copies.append(c)

    def got_slots(part, hh):
        ref = r.slots_ref.at[part, hh]
        remote(ref, ref, r.ex_s.at[0], r.all_r.at[part * nh + hh], (d, b, hc)).wait_recv()

    dispatch(0, routed)
    logits = jnp.where(lane < E, nn(routed, router), -1e30)
    exps = jnp.exp(logits - jnp.max(logits, axis=-1, keepdims=True))
    probs = exps / jnp.sum(exps, axis=-1, keepdims=True)
    gate = jnp.sum(jnp.where(chosen, probs, 0.0), axis=-1, keepdims=True)
    dispatch(1, (gate * cot).astype(BF16))
    chunk = D
    chunks = z.FF // chunk
    piece = D // 2
    steps.run_rest(14)

    arrivals(0)
    share_slots(0)
    rows_in = r.exp_in[0].astype(F32).reshape(NG * C8, D).astype(BF16)
    r.out_acc[...] = jnp.zeros_like(r.out_acc)

    def forward_step(c, carry):
        at = pl.ds(pl.multiple_of(c * chunk, chunk), chunk)
        pre = nn(rows_in, r.win[:, at])
        hidden, r.slope[:, at] = activate(pre)
        r.hid[:, at] = hidden
        r.out_acc[...] += nn(hidden, r.wout[at, :])
        return carry

    lax.fori_loop(0, chunks, forward_step, 0)
    give_back(0, r.out_acc[...])

    arrivals(1)
    share_slots(1)
    grad_out = r.exp_in[1].astype(F32).reshape(NG * C8, D).astype(BF16)
    r.out_acc[...] = jnp.zeros_like(r.out_acc)

    def backward_step(c, carry):
        at = pl.ds(pl.multiple_of(c * chunk, chunk), chunk)
        gp = grad_pre(grad_out, r.wout[at, :], r.slope[:, at])
        r.slope[:, at] = gp
        r.out_acc[...] += nt(gp, r.win[:, at])
        return carry

    lax.fori_loop(0, chunks, backward_step, 0)
    give_back(1, r.out_acc[...])
    saves = []

    def save(hh):
        for n, (src, dst) in enumerate(((r.hid, r.hid_ref), (r.slope, r.gp_ref))):
            c = pltpu.make_async_copy(src, dst.at[hh], r.loc.at[8 + n])
            c.start()
            saves.append(c)

    def other_slots(hh, forward):
        for part in range(2):
            got_slots(part, hh)
            if forward:
                ref = r.slots_ref.at[part, hh]
                out.put(ref, ref, r.all_r.at[part * nh + hh], (d, b, hc))
        c = pltpu.make_async_copy(r.slots_ref.at[:, hh], r.act_in, r.loc.at[10])
        c.start()
        c.wait()
        while saves:
            saves.pop().wait()
        others_in = r.act_in[0].astype(F32).reshape(NG * C8, D).astype(BF16)
        others_grad = r.act_in[1].astype(F32).reshape(NG * C8, D).astype(BF16)

        def step(c, carry):
            at = pl.ds(pl.multiple_of(c * piece, piece), piece)
            r.hid[:, at], slope = activate(nn(others_in, r.win[:, at]))
            r.slope[:, at] = grad_pre(others_grad, r.wout[at, :], slope)
            return carry

        lax.fori_loop(0, z.FF // piece, step, 0)
        save(hh)

    save(h)
    steps.run_rest(10)
    for c in copies:
        c.wait()
    other_slots(hc, False)

    expert_rows = returns(0)
    r.layer_v[...] = (middle + gate * expert_rows).astype(BF16)
    written(r, "layer_ref")
    grad_gate = jnp.sum(cot * expert_rows, axis=-1, keepdims=True)
    grad_probs = jnp.where(chosen, grad_gate, 0.0) + share
    inner = jnp.sum(probs * grad_probs, axis=-1, keepdims=True)
    grad_logits = (probs * (grad_probs - inner)).astype(BF16)
    from_router = nt(grad_logits, router)
    grad_routed = returns(1) + from_router
    scaled = grad_routed * gain
    mean = jnp.mean(scaled * middle, axis=-1, keepdims=True)
    gmid = cot + inverse * scaled - middle * (inverse * inverse * inverse) * mean
    r.gmid[...] = gmid
    low_mid = gmid.astype(BF16)
    gatt = nt(low_mid, r.wo[...]).astype(BF16)

    for n in range(HEAD_COUNT):
        r.gatt[n] = both_halves(gatt[:, n * HEAD_SIZE : (n + 1) * HEAD_SIZE])
        hb, hh = z.holder(n)
        out.put(
            r.gatt.at[n], r.do_in.at[s], r.do_r.at[s], (d, hb, hh), jnp.logical_not(p.owns(n))
        )

        @pl.when(p.owns(n))
        def _():
            r.do_in[s] = r.gatt[n]

    term = grad_routed * middle * inverse
    high = term.astype(BF16)
    rest = (term - high.astype(F32)).astype(BF16)
    ones = jnp.broadcast_to((lane == E).astype(BF16), (PT, LANES))
    small = tn(routed, grad_logits) + tn(high, ones) + tn(rest, ones)
    terms = jnp.concatenate([tn(att, low_mid), small], axis=1)
    for t in range(z.ndev):
        r.dwo[t % nh, t // nh] = terms[t * z.R : (t + 1) * z.R].astype(BF16)
    other_slots(hy, True)

    def finish():
        while saves:
            saves.pop().wait()
        out.finish()

    return functools.partial(other_slots, hyc, False), finish


def backward_phase(z, r, p, steps, last_slots):
    d, b, h, s, me, hd, active = p.d, p.b, p.h, p.s, p.me, p.hd, p.active
    hy, hc, hyc = p.hy, p.hc, p.hyc
    nb, nh, nd, ns, nv, NG = z.n_blk, z.n_head, z.n_dp, z.ns, z.ndev, z.NG
    D, R, PT, HS, E = z.D, z.R, z.PT, HEAD_SIZE, z.E

    def sum_in(dst, src, terms, count):
        def body(e, carry):
            acc = src(e).astype(F32)
            for term in terms:
                acc = acc + term(e).astype(F32)
            dst[e] = acc.astype(BF16)
            return carry

        lax.fori_loop(0, count, body, 0)

    sums = Sends(r.su_s)
    y_sum = r.core_in.at[0]

    def got_sum(ref, k):
        remote(ref, ref, r.su_s.at[0], r.su_r.at[k], (d, b, hc)).wait_recv()

    def stage_core():
        sums.put(r.dwo.at[hyc], r.core_in.at[0], r.su_r.at[0], (d, b, hc))
        sums.put(r.dwo.at[hc], r.core_in.at[1], r.su_r.at[1], (d, b, hc))

    def stage_y():
        got_sum(r.core_in.at[0], 0)
        sum_in(r.y_src, lambda e: r.dwo[hy, e], [lambda e: r.core_in[0, e]], NG)
        sums.put(r.y_src, r.y_in, r.su_r.at[2], (d, b, hy))

    def stage_dp():
        got_sum(r.core_in.at[1], 1)
        got_sum(r.y_in, 2)
        sum_in(
            y_sum, lambda e: r.dwo[h, e], [lambda e: r.core_in[1, e], lambda e: r.y_in[e]], NG
        )
        for k in range(1, nd):
            q = lax.rem(d + k, nd)
            sums.put(y_sum.at[pl.ds(q * nb, nb)], r.dp_in.at[d], r.su_r.at[3 + d], (q, b, h))

    def stage_blk():
        others = [lax.rem(d + k, nd) for k in range(1, nd)]
        for q in others:
            got_sum(r.dp_in.at[q], 3 + q)

        def body(e, carry):
            acc = y_sum[d * nb + e].astype(F32)
            for q in others:
                acc = acc + r.dp_in[q, e].astype(F32)
            r.blk_src[e] = acc.astype(BF16)
            return carry

        lax.fori_loop(0, nb, body, 0)
        for k in range(1, nb):
            e = lax.rem(b + k, nb)
            sums.put(r.blk_src.at[e], r.blk_in.at[b], r.su_r.at[3 + nd + b], (d, e, h))
        r.blk_in[b] = r.blk_src[b]

    stage_core()

    def send_dq(t):
        return remote(
            r.dqkv.at[t], r.dq_in.at[hd], r.dq_s.at[t], r.dq_r.at[hd], (d, t // nh, t % nh)
        )

    def send_dw(k):
        t, device = p.any_peer(k)
        slot = d * HEAD_COUNT + hd
        return remote(r.dw3.at[t], r.dw_in.at[slot], r.dw_s.at[k], r.dw_r.at[slot], device)

    per = z.per
    part_rows = BLOCK // 2

    @pl.when(active)
    def _():
        r.dkv[...] = jnp.zeros_like(r.dkv)
        r.dq_acc[...] = jnp.zeros_like(r.dq_acc)
        r.dw[...] = jnp.zeros_like(r.dw)
        r.diag[...] = jnp.zeros_like(r.diag)
        r.sub[...] = jnp.zeros_like(r.sub)
        r.far[...] = jnp.zeros_like(r.far)

        def got_do(k, carry):
            t = lax.rem(s + k, ns)
            ref = r.do_in.at[t]
            remote(ref, ref, r.ex_s.at[0], r.do_r.at[t], p.in_sequence(t)).wait_recv()
            return carry

        lax.fori_loop(1, ns, got_do, 0)
        ones = jnp.ones((8, HS), BF16)

        def prepare(i, carry):
            here = pl.ds(pl.multiple_of(i * BLOCK, BLOCK), BLOCK)
            pairs = [r.do_in[i * per + u] for u in range(per)]
            do = jnp.concatenate(
                [side for pair in pairs for side in (pair[:, :HS], pair[:, HS:])], axis=0
            )
            do = (do.astype(F32) * r.attl[here, HS:]).astype(BF16)
            r.dos[here, :] = do
            prod = do.astype(F32) * r.attl[here, :HS]
            high = prod.astype(BF16)
            rest = (prod - high.astype(F32)).astype(BF16)
            r.delta[i] = nt(ones, high) + nt(ones, rest)
            return carry

        lax.fori_loop(0, z.nq, prepare, 0)

    def tile(i, j, u):
        at = slice(j * BLOCK + u * part_rows, j * BLOCK + (u + 1) * part_rows)
        here = slice(i * BLOCK, (i + 1) * BLOCK)
        pr = r.probs[i, at, :]
        do = r.dos[here, :]
        ds = pr.astype(F32) * (nt(r.qkv[at, 2 * HS :], do) - r.delta[i, 0:1, :])
        low = ds.astype(BF16)
        part = slice(u * part_rows, (u + 1) * part_rows)
        if j == i:
            r.diag[part, :] += low.astype(F32)
        elif j == i - 1:
            r.sub[part, :] += low.astype(F32)
        else:
            r.far[...] += jnp.sum(low.astype(F32).reshape(part_rows // 8, 8, BLOCK), axis=0)
        both = jnp.concatenate([nn(low, r.qkv[here, :HS]), nn(pr, do)], axis=1)
        return at, both, nn(r.k_t[:, at], low)

    def column(j, hi):
        for u in range(2):
            acc = jnp.zeros((part_rows, 2 * HS), F32)
            for i in range(j, hi + 1):
                at, both, dq = tile(i, j, u)
                acc = acc + both
                r.dq_acc[i] += dq
            r.dkv[at, :] += acc

    def row(i, lo):
        acc = jnp.zeros((HS, BLOCK), F32)
        for j in range(lo, i + 1):
            for u in range(2):
                at, both, dq = tile(i, j, u)
                r.dkv[at, :] += both
                acc = acc + dq
        r.dq_acc[i] += acc

    lo, hi = 0, z.nq - 1
    turn = 0
    while lo <= hi:
        if turn == 1:
            stage_y()
        if turn == 3:
            stage_dp()
        if turn == z.nq - 1:
            stage_blk()

        @pl.when(active)
        def _():
            if turn % 2 == 0:
                n = lo
                column(n, hi)
            else:
                n = hi
                row(n, lo)
            here = slice(n * BLOCK, (n + 1) * BLOCK)
            dq = jnp.transpose(r.dq_acc[n]) * HS ** (-0.5)
            parts = jnp.concatenate([dq, r.dkv[here, :]], axis=1).astype(BF16)
            r.dw[...] += tn(r.xg[n * per : (n + 1) * per].reshape(BLOCK, D), parts)
            for u in range(per):
                t = n * per + u
                piece = parts[u * PT : (u + 1) * PT]
                r.dqkv[t, :PT] = piece[:, : 2 * HS]
                r.dqkv[t, PT:] = both_halves(piece[:, 2 * HS :])

                @pl.when(t != s)
                def _():
                    send_dq(t).start()

                @pl.when(t == s)
                def _():
                    r.dq_in[hd] = r.dqkv[t]

        if turn % 2 == 0:
            lo += 1
        else:
            hi -= 1
        turn += 1
        steps.run_rest(6)

    @pl.when(active)
    def _():
        lane = lax.broadcasted_iota(jnp.int32, (1, HS), 1)
        half = BUCKETS // 2
        sums_of = bucket_sums(r.diag[...], 0) + bucket_sums(r.sub[...], BLOCK)
        beyond = jnp.sum(jnp.sum(r.far[...], axis=0, keepdims=True), axis=1, keepdims=True)
        sums_of = sums_of + jnp.where(lane == half - 1, beyond, 0.0)
        wide = jnp.concatenate([r.dw[...], jnp.broadcast_to(sums_of, (D, HS))], axis=1)
        split_rows(r.dw3, wide, R)

        def start_dw(k, carry):
            send_dw(k).start()
            return carry

        lax.fori_loop(1, nv, start_dw, 0)
        r.dw_in[d * HEAD_COUNT + hd] = r.dw3[me]

    last_slots()
    steps.finish_rest()
    load = [
        pltpu.make_async_copy(r.wg_ref.at[:, :, pl.ds(m * D, D)], r.w3.at[m], r.loc.at[5 + m])
        for m in range(3)
    ]
    for c in load:
        c.start()
    for m, c in enumerate(load):
        c.wait()
        r.wfull[:, m * D : (m + 1) * D] = flatten_rows(r.w3[m]).astype(BF16)

    for k in range(1, nb):
        e = lax.rem(b + k, nb)
        got_sum(r.blk_in.at[e], 3 + nd + e)
    acc = r.blk_in[0].astype(F32)
    for e in range(1, nb):
        acc = acc + r.blk_in[e].astype(F32)
    eye = lax.broadcasted_iota(jnp.int32, (R, R), 0) == lax.broadcasted_iota(jnp.int32, (R, R), 1)

    def as_row(column):
        return jnp.sum(jnp.where(eye, column, 0.0), axis=0, keepdims=True)

    r.go_v[...] = acc[:, :D]
    r.router_v[...] = jnp.concatenate([as_row(acc[:, D + e : D + e + 1]) for e in range(E)], axis=0)
    r.gain2_v[...] = as_row(acc[:, D + E : D + E + 1])
    written(r, "go_ref", "router_out", "gain2_ref")

    for n in range(HEAD_COUNT):
        hb, hh = z.holder(n)

        @pl.when(jnp.logical_not(p.owns(n)))
        def _():
            ref = r.dq_in.at[n]
            remote(ref, ref, r.dq_s.at[0], r.dq_r.at[n], (d, hb, hh)).wait_recv()

        for m in range(2):
            r.grad_cat[:, m * D + n * HS : m * D + (n + 1) * HS] = r.dq_in[
                n, :PT, m * HS : (m + 1) * HS
            ]
        at = slice(2 * D + n * HS, 2 * D + (n + 1) * HS)
        r.grad_cat[: PT // 2, at] = r.dq_in[n, PT:, :HS]
        r.grad_cat[PT // 2 :, at] = r.dq_in[n, PT:, HS:]
    grad_normed = nt(r.grad_cat[...], r.wfull[...])
    x = r.x_own[...].astype(F32)
    inverse = lax.rsqrt(jnp.mean(x * x, axis=-1, keepdims=True) + EPSILON)
    scaled = grad_normed * r.gain1[...]
    mean = jnp.mean(scaled * x, axis=-1, keepdims=True)
    grad_in = inverse * scaled - x * (inverse * inverse * inverse) * mean
    r.gtok_v[...] = (r.gmid[...] + grad_in).astype(BF16)
    written(r, "gtok_ref")

    for dd in range(nd):
        for n in range(HEAD_COUNT):
            hb, hh = z.holder(n)

            @pl.when(jnp.logical_not(p.owns(n) & (d == dd)))
            def _():
                ref = r.dw_in.at[dd * HEAD_COUNT + n]
                remote(
                    ref, ref, r.dw_s.at[0], r.dw_r.at[dd * HEAD_COUNT + n], (dd, hb, hh)
                ).wait_recv()

    first = jnp.zeros((R, HS), F32)
    lines = []
    for n in range(HEAD_COUNT):
        part = r.dw_in[n].astype(F32)
        for dd in range(1, nd):
            part = part + r.dw_in[dd * HEAD_COUNT + n].astype(F32)
        for m, out in enumerate((r.gq_v, r.gk_v, r.gv_v)):
            cols = part[:, m * HS : (m + 1) * HS]
            out[:, n * HS : (n + 1) * HS] = cols
            own = r.w_own[:, m * D + n * HS : m * D + (n + 1) * HS].astype(F32)
            first = first + cols * own
        lines.append(part[0:1, 3 * HS : 3 * HS + BUCKETS])
    first = jnp.sum(first, axis=-1, keepdims=True)
    table = jnp.concatenate(lines, axis=0)
    entry = lax.broadcasted_iota(jnp.int32, table.shape, 0) * BUCKETS + lax.broadcasted_iota(
        jnp.int32, table.shape, 1
    )
    slot_lane = lax.broadcasted_iota(jnp.int32, (1, z.RL), 1)
    own_table = jnp.zeros((1, z.RL), F32)
    for k in range(z.RL):
        value = jnp.sum(jnp.where(entry == me * z.RL + k, table, 0.0), axis=0, keepdims=True)
        value = jnp.sum(value, axis=1, keepdims=True)
        own_table = own_table + jnp.where(slot_lane == k, value, 0.0)
    own_gain = r.w_own[:, 4 * D :].astype(F32)[:, E : E + 1]
    r.gain1_v[...] = as_row(first / own_gain)
    r.table_v[...] = own_table
    written(r, "gain1_ref", "gq_ref", "gk_ref", "gv_ref", "table_ref")

    sums.finish()

    @pl.when(active)
    def _():
        for t in range(ns):

            @pl.when(t != s)
            def _():
                send_dq(t).wait_send()

        def sent_dw(k, carry):
            send_dw(k).wait_send()
            return carry

        lax.fori_loop(1, nv, sent_dw, 0)


def layer(z, x, order, ids, rows, weights, router_t, w_in, w_out, cot):
    D, R, PT, S, HS, E, NG, C8 = z.D, z.R, z.PT, z.S, HEAD_SIZE, z.E, z.NG, z.cap8
    nb, nd, nh, ns, nv = z.n_blk, z.n_dp, z.n_head, z.ns, z.ndev
    dma = pltpu.SemaphoreType.DMA
    vmem = pl.BlockSpec(memory_space=pltpu.VMEM)
    hbm = pl.BlockSpec(memory_space=pltpu.HBM)
    shape = jax.ShapeDtypeStruct
    inputs = {
        "x_ref": (x, hbm),
        "order_ref": (order, vmem),
        "ids_ref": (ids, hbm),
        "gain1_in": (rows[0][None, :], vmem),
        "gain2_in": (rows[1][None, :], vmem),
        "rel_ref": (rows[2][None, :], vmem),
        "wq_ref": (weights[0], hbm),
        "wk_ref": (weights[1], hbm),
        "wv_ref": (weights[2], hbm),
        "wo_ref": (weights[3], hbm),
        "router_ref": (router_t, vmem),
        "win_ref": (w_in, hbm),
        "wout_ref": (w_out, hbm),
        "cot_ref": (cot, hbm),
    }
    outputs = {
        "wg_ref": (shape((nv, R, z.wide), BF16), hbm),
        "slots_ref": (shape((2, nh, NG, C8, D), BF16), hbm),
        "hid_ref": (shape((nh, NG * C8, z.FF), BF16), hbm),
        "gp_ref": (shape((nh, NG * C8, z.FF), BF16), hbm),
        "layer_ref": (shape((PT, D), BF16), hbm),
        "gtok_ref": (shape((PT, D), BF16), hbm),
        "gain1_ref": (shape((1, R), F32), hbm),
        "gq_ref": (shape((R, D), F32), hbm),
        "gk_ref": (shape((R, D), F32), hbm),
        "gv_ref": (shape((R, D), F32), hbm),
        "go_ref": (shape((R, D), F32), hbm),
        "table_ref": (shape((1, z.RL), F32), hbm),
        "gain2_ref": (shape((1, R), F32), hbm),
        "router_out": (shape((E, R), F32), hbm),
    }
    V = pltpu.VMEM
    terms = D + LANES
    scratch = {
        "w_own": V((R, z.wide), BF16),
        "x_own": V((PT, D), BF16),
        "cot": V((PT, D), BF16),
        "ids": V(ids.shape, jnp.int32),
        "win": V((D, z.FF), BF16),
        "wout": V((z.FF, D), BF16),
        "slices": V((HEAD_COUNT, R, 4 * HS), BF16),
        "slices_in": V((nv, R, 4 * HS), BF16),
        "xg": V((ns, PT, D), BF16),
        "wh": V((D, 3 * HS), BF16),
        "gain1": V((1, D), F32),
        "far_bias": V((1, 1), F32),
        "bias_d": V((BLOCK, BLOCK), F32),
        "bias_s": V((BLOCK, BLOCK), F32),
        "qkv": V((S, 3 * HS), BF16),
        "v_t": V((HS, S), BF16),
        "k_t": V((HS, S), BF16),
        "s_scr": V((S, BLOCK), F32),
        "probs": V((z.nq, S, BLOCK), BF16),
        "attl": V((S, 2 * HS), F32),
        "att_src": V((ns, PT // 2, 2 * HS), BF16),
        "att_in": V((HEAD_COUNT, PT // 2, 2 * HS), BF16),
        "misc3": V((nv, R, LANES), BF16),
        "wo": V((D, D), BF16),
        "route": V((E * C8, PT), F32),
        "att_cat": V((PT, D), BF16),
        "disp": V((2, E, C8, D), BF16),
        "exp_in": V((2, NG, C8, D), BF16),
        "ret": V((2, NG, C8, D), BF16),
        "back": V((2, E, C8, D), BF16),
        "hid": V((NG * C8, z.FF), BF16),
        "slope": V((NG * C8, z.FF), BF16),
        "act_in": V((2, NG, C8, D), BF16),
        "out_acc": V((NG * C8, D), F32),
        "gmid": V((PT, D), F32),
        "gatt": V((HEAD_COUNT, PT // 2, 2 * HS), BF16),
        "do_in": V((ns, PT // 2, 2 * HS), BF16),
        "dwo": V((nh, NG, R, terms), BF16),
        "core_in": V((2, NG, R, terms), BF16),
        "y_src": V((NG, R, terms), BF16),
        "y_in": V((NG, R, terms), BF16),
        "dp_in": V((nd, nb, R, terms), BF16),
        "blk_src": V((nb, R, terms), BF16),
        "blk_in": V((nb, R, terms), BF16),
        "dos": V((S, HS), BF16),
        "delta": V((z.nq, 8, BLOCK), F32),
        "dq_acc": V((z.nq, HS, BLOCK), F32),
        "dw": V((D, 3 * HS), F32),
        "dw3": V((nv, R, 4 * HS), BF16),
        "diag": V((BLOCK, BLOCK), F32),
        "sub": V((BLOCK, BLOCK), F32),
        "far": V((8, BLOCK), F32),
        "dqkv": V((ns, PT + PT // 2, 2 * HS), BF16),
        "dq_in": V((HEAD_COUNT, PT + PT // 2, 2 * HS), BF16),
        "dw_in": V((nd * HEAD_COUNT, R, 4 * HS), BF16),
        "w3": V((3, nv, R, D), BF16),
        "wfull": V((D, 3 * D), BF16),
        "grad_cat": V((PT, 3 * D), BF16),
        "layer_v": V((PT, D), BF16),
        "gtok_v": V((PT, D), BF16),
        "gain1_v": V((1, R), F32),
        "gq_v": V((R, D), F32),
        "gk_v": V((R, D), F32),
        "gv_v": V((R, D), F32),
        "go_v": V((R, D), F32),
        "table_v": V((1, z.RL), F32),
        "gain2_v": V((1, R), F32),
        "router_v": V((E, R), F32),
        "out_sem": dma((len(PASSED),)),
        "in_sem": dma((9,)),
        "loc": dma((11,)),
        "sl_s": dma((HEAD_COUNT,)),
        "sl_r": dma((nv,)),
        "sd_s": dma((ns * nd,)),
        "x_s": dma((2 * (4 + 6 * (nb - 1) + 2 * nb - 1),)),
        "x_r": dma((2 * ns,)),
        "w0_s": dma((spread_copies(z, False),)),
        "w0_r": dma((nv,)),
        "w1_s": dma((spread_copies(z, True),)),
        "w1_r": dma((nv,)),
        "w2_s": dma((spread_copies(z, False),)),
        "w2_r": dma((nv,)),
        "at_s": dma((ns,)),
        "at_r": dma((HEAD_COUNT,)),
        "ex_s": dma((4 * (NG - 1) + 6 + HEAD_COUNT,)),
        "ex_r": dma((2 * NG,)),
        "rt_r": dma((2 * NG,)),
        "all_r": dma((2 * nh,)),
        "do_r": dma((ns,)),
        "su_s": dma((3 + nd - 1 + nb - 1,)),
        "su_r": dma((3 + nd + nb,)),
        "dq_s": dma((ns,)),
        "dq_r": dma((HEAD_COUNT,)),
        "dw_s": dma((nv,)),
        "dw_r": dma((nd * HEAD_COUNT,)),
    }
    names = tuple(inputs) + tuple(outputs) + tuple(scratch)
    results = pl.pallas_call(
        functools.partial(layer_kernel, z, names),
        out_shape=tuple(v[0] for v in outputs.values()),
        in_specs=[v[1] for v in inputs.values()],
        out_specs=tuple(v[1] for v in outputs.values()),
        scratch_shapes=list(scratch.values()),
        compiler_params=pltpu.CompilerParams(
            collective_id=0, has_side_effects=True, vmem_limit_bytes=VMEM_LIMIT
        ),
        name="layer",
    )(*[v[0] for v in inputs.values()])
    return dict(zip(outputs, results))


def expert_kernel(z, slots_ref, hid_ref, gp_ref, *refs):
    count = len(PASSED)
    passed_in, (gin_ref, gout_ref) = refs[:count], refs[count : count + 2]
    passed_out = refs[count + 2 : 2 * count + 2]
    rows_t, grad_out = refs[2 * count + 2 :]
    step = pl.program_id(0)

    @pl.when(step == 0)
    def _():
        for src, dst in zip(passed_in, passed_out):
            dst[...] = src[...]
        count = z.NG * z.cap8
        for n in range(z.n_head):
            at = slice(n * count, (n + 1) * count)
            rows_in = slots_ref[0, n].astype(F32).reshape(count, z.D)
            rows_t[:, at] = jnp.transpose(rows_in).astype(BF16)
            grad_out[at, :] = slots_ref[1, n].astype(F32).reshape(count, z.D).astype(BF16)

    total = z.n_head * z.NG * z.cap8
    chunk = hid_ref.shape[2]
    gin_ref[0] = nn(rows_t[...], gp_ref[...].reshape(total, chunk))
    gout_ref[0] = tn(hid_ref[...].reshape(total, chunk), grad_out[...])


def expert_weights(z, slots, hid, gp, passed):
    chunk = 768
    vmem = pl.BlockSpec(memory_space=pltpu.VMEM)
    total = z.n_head * z.NG * z.cap8
    in_chunk = pl.BlockSpec((1, z.D, chunk), lambda i: (0, 0, i))
    act_chunk = pl.BlockSpec((z.n_head, z.NG * z.cap8, chunk), lambda i: (0, 0, i))
    out_chunk = pl.BlockSpec((1, chunk, z.D), lambda i: (0, i, 0))
    return pl.pallas_call(
        functools.partial(expert_kernel, z),
        grid=(z.FF // chunk,),
        out_shape=(
            jax.ShapeDtypeStruct((1, z.D, z.FF), F32),
            jax.ShapeDtypeStruct((1, z.FF, z.D), F32),
        )
        + tuple(jax.ShapeDtypeStruct(a.shape, a.dtype) for a in passed),
        in_specs=[pl.BlockSpec(memory_space=pltpu.VMEM), act_chunk, act_chunk] + [vmem] * len(passed),
        out_specs=(in_chunk, out_chunk) + (vmem,) * len(passed),
        scratch_shapes=[
            pltpu.VMEM((z.D, total), BF16),
            pltpu.VMEM((total, z.D), BF16),
        ],
        compiler_params=pltpu.CompilerParams(
            dimension_semantics=("arbitrary",), vmem_limit_bytes=VMEM_LIMIT
        ),
        name="expert_weight_grads",
    )(slots, hid, gp, *passed)


def local(
    sizes,
    tokens,
    order,
    expert_ids,
    norm1_gain,
    w_query,
    w_key,
    w_value,
    w_attn_out,
    rel_table,
    norm2_gain,
    w_router,
    w_in,
    w_out,
    cotangent,
):
    R, D = w_query.shape
    E = w_router.shape[1]
    z = Sizes(*sizes, R, D, E, w_in.shape[2], tokens.shape[1])
    out = layer(
        z,
        tokens.reshape(z.PT, D),
        order,
        expert_ids.reshape(-1, z.PT),
        (norm1_gain, norm2_gain, rel_table),
        (w_query, w_key, w_value, w_attn_out),
        w_router.T,
        w_in,
        w_out,
        cotangent.reshape(z.PT, D),
    )
    g_in, g_out, *rest = expert_weights(
        z, out["slots_ref"], out["hid_ref"], out["gp_ref"], [out[name] for name in PASSED]
    )
    layer_out, gtok, gain1, gq, gk, gv, go, table, gain2, router = rest
    return (
        layer_out.reshape(tokens.shape),
        gtok.reshape(tokens.shape),
        gain1.reshape(R),
        gq,
        gk,
        gv,
        go,
        table.reshape(z.RL),
        gain2.reshape(R),
        router.T,
        g_in,
        g_out,
    )


def solution(mesh):
    everywhere = ("dp", "blk", "head")
    rows, table = P(everywhere), P(everywhere, None)
    tokens = P("dp", ("blk", "head"), None)
    expert = P(("dp", "blk"), None, None)
    in_specs = (
        tokens,
        P("dp", ("blk", "head")),
        P(),
        rows,
        table,
        table,
        table,
        table,
        rows,
        rows,
        table,
        expert,
        expert,
        tokens,
    )
    out_specs = (
        tokens, tokens, rows, table, table, table, table, rows, rows, table, expert, expert
    )
    sizes = (mesh.shape["dp"], mesh.shape["blk"], mesh.shape["head"])
    return jax.shard_map(
        functools.partial(local, sizes),
        mesh=mesh,
        in_specs=in_specs,
        out_specs=out_specs,
        check_vma=False,
    )
```
